32 devices in a mesh: rep: 4 (over y, x), shard: 8 (over z, core).
Axes of the slice: x: 2, y: 2, z: 4, core: 2. Of those that a mesh axis runs over, the one named last changes fastest.
Arguments:
- tokens: bfloat16 [4096, 960], P(('rep', 'shard')), may hold values from -6 to 6
- lengths: int32 [4, 6], P('rep'), may hold values from 0 to 1024, as said below
- norm_one: bfloat16 [960], P('shard'), may hold values from 0.099609375 to 1.8984375
- w_query: bfloat16 [960, 960], P('shard'), may hold values from -0.1875 to 0.1875
- w_key: bfloat16 [960, 320], P('shard'), may hold values from -0.1875 to 0.1875
- w_value: bfloat16 [960, 320], P('shard'), may hold values from -0.1875 to 0.1875
- w_out: bfloat16 [960, 960], P('shard'), may hold values from -1 to 1
- norm_two: bfloat16 [960], P('shard'), may hold values from 0.099609375 to 1.8984375
- w_gate: bfloat16 [960, 2560], P('shard'), may hold values from -0.1875 to 0.1875
- w_up: bfloat16 [960, 2560], P('shard'), may hold values from -0.1875 to 0.1875
- w_down: bfloat16 [2560, 960], P('shard'), may hold values from -0.125 to 0.125
- cotangent: bfloat16 [4096, 960], P(('rep', 'shard')), may hold values from -6 to 6
Outputs:
- output: bfloat16 [4096, 960], P(('rep', 'shard'))
- input_grad: float32 [4096, 960], P(('rep', 'shard'))
- grad_norm_one: float32 [960], P('shard')
- grad_w_query: float32 [960, 960], P('shard')
- grad_w_key: float32 [960, 320], P('shard')
- grad_w_value: float32 [960, 320], P('shard')
- grad_w_out: float32 [960, 960], P('shard')
- grad_norm_two: float32 [960], P('shard')
- grad_w_gate: float32 [960, 2560], P('shard')
- grad_w_up: float32 [960, 2560], P('shard')
- grad_w_down: float32 [2560, 960], P('shard')
The draws below stay inside these ranges and needn't reach their ends.
Inputs may be any that keep to these rules, and one draw needn't show every extreme that they name: `lengths`: each row packs documents in order, each of 200 to 2000 tokens, the last one cut at the sequence's end; the slots after it hold 0, and a row sums to 1024. In one sequence, drawn from the seed, the first document instead has the largest length allowed here, which reaches from the sequence's first device to its last.
All inputs are finite; a program needn't handle non-finite values.
Results may differ from the reference program's by a relative error of at most 0.02.
Values may be sent and summed in bfloat16 or wider, within the bound.
No kernel may reach another device: no remote copies, remote signals or barrier semaphores. Data moves between devices by JAX's collectives and lax.ppermute only.
A program may use at most 128 MiB of HBM per device.

```python
import math
import jax
import jax.numpy as jnp
from jax import lax

D = 960
QH = 15
KVH = 5
HD = 64
FF = 2560
TOK_DEV = 128
MIN_DOC = 200
MAX_DOC = 2000
SEQ = 1024
DOCS = 6
TOKENS = 4096
N_REP = 4


def draw_lengths(key, part):
    key = jax.random.fold_in(key, 7)
    size_key, pick_key = jax.random.split(key)
    drawn = jax.random.randint(size_key, (N_REP, DOCS), MIN_DOC, MAX_DOC + 1)
    chosen = jax.random.randint(pick_key, (), 0, N_REP)
    longest = min(SEQ, max(MAX_DOC, SEQ - TOK_DEV // 2))
    leading = jnp.arange(DOCS)[None, :] == 0
    picked = (jnp.arange(N_REP)[:, None] == chosen) & leading
    drawn = jnp.where(picked, longest, drawn)
    starts = jnp.cumsum(drawn, axis=1) - drawn
    return jnp.clip(SEQ - starts, 0, drawn).astype(jnp.int32)


def steps_of(key, shape, cuts, smallest, top_value):
    level = 1.0
    for dim, blocks in cuts:
        steps = jax.random.uniform(jax.random.fold_in(jax.random.fold_in(key, 6), dim), (blocks,), jnp.float32, smallest / len(cuts), top_value / len(cuts))
        level = level * jnp.repeat(jnp.exp(steps), shape[dim] // blocks).reshape((-1,) + (1,) * (len(shape) - 1 - dim))
    return level


def bell_draw(stream_key, dims, scale, most, cuts=(), held_as=jnp.bfloat16):
    level = steps_of(stream_key, dims, cuts, -0.22, 0.18) if cuts else 1.0
    values = jax.random.normal(stream_key, dims, jnp.float32) * scale * level
    return jnp.minimum(jnp.maximum(values, -most), most).astype(held_as)


def setup_inputs(seed: int = 0) -> dict:
    streams_of = jax.random.split(jax.random.key(seed), 13)
    tokens = bell_draw(streams_of[0], (TOKENS, D), 1.0, 6.0, ((0, 32),))
    lengths = draw_lengths(jax.random.fold_in(streams_of[12], 71), 0)
    norm_one = jnp.clip(1.0 + 0.18 * jax.random.normal(streams_of[2], (D,), jnp.float32), 0.099609375, 1.8984375).astype(jnp.bfloat16)
    w_query = bell_draw(streams_of[3], (D, D), D ** -0.5, 0.1875, ((0, 8),))
    w_key = bell_draw(streams_of[4], (D, KVH * HD), D ** -0.5, 0.1875, ((0, 8),))
    w_value = bell_draw(streams_of[5], (D, KVH * HD), D ** -0.5, 0.1875, ((0, 8),))
    w_out = bell_draw(streams_of[6], (D, D), (max(D // 32, 1)) ** -0.5, 1.0, ((0, 8),))
    norm_two = jnp.clip(1.0 + 0.18 * jax.random.normal(streams_of[7], (D,), jnp.float32), 0.099609375, 1.8984375).astype(jnp.bfloat16)
    w_gate = bell_draw(streams_of[8], (D, FF), D ** -0.5, 0.1875, ((0, 8),))
    w_up = bell_draw(streams_of[9], (D, FF), D ** -0.5, 0.1875, ((0, 8),))
    w_down = bell_draw(streams_of[10], (FF, D), FF ** -0.5, 0.125, ((0, 8),))
    cotangent = bell_draw(streams_of[11], (TOKENS, D), 1.0, 6.0, ((0, 32),))
    return dict(tokens=tokens, lengths=lengths, norm_one=norm_one, w_query=w_query, w_key=w_key, w_value=w_value, w_out=w_out, norm_two=norm_two, w_gate=w_gate, w_up=w_up, w_down=w_down, cotangent=cotangent)


EPS = 1e-05
ROPE_BASE = 10000.0
MASKED = -1e+30
HIGHEST_PRECISION = lax.Precision.HIGHEST

@jax.custom_vjp
def low(v):
    return lax.optimization_barrier(v.astype(jnp.bfloat16)).astype(jnp.float32)

@jax.custom_vjp
def low_back(v):
    return v

def low_keep(v):
    return (low(v), None)

def low_pass(kept, grad):
    return (grad,)

def back_keep(v):
    return (v, None)

def back_low(kept, grad):
    return (low(grad),)
low.defvjp(low_keep, low_pass)
low_back.defvjp(back_keep, back_low)

def doc_layout(lengths_row, length):
    places = jnp.arange(length, dtype=jnp.int32)
    doc_ends = jnp.cumsum(lengths_row).astype(jnp.int32)
    passed = places[:, None] >= doc_ends[None, :]
    segment = lax.optimization_barrier(jnp.sum(passed.astype(jnp.int32), axis=1)).astype(jnp.int32)
    doc_start = lax.optimization_barrier(jnp.sum(jnp.where(passed, lengths_row[None, :], 0), axis=1)).astype(jnp.int32)
    return (segment, places - doc_start)

def rope_tables(position):
    half_dim = HD // 2
    fraction = jnp.arange(half_dim, dtype=jnp.float32) * (2.0 / HD)
    inverse = ROPE_BASE ** (-fraction)
    angles = position.astype(jnp.float32)[:, None] * inverse[None, :]
    return (jnp.cos(angles), jnp.sin(angles))

def rotate(values, cosines, sines):
    half_dim = values.shape[-1] // 2
    first_half = values[..., :half_dim]
    second_half = values[..., half_dim:]
    cos_wide = cosines[:, None, :]
    sin_wide = sines[:, None, :]
    return jnp.concatenate([first_half * cos_wide - second_half * sin_wide, second_half * cos_wide + first_half * sin_wide], axis=-1)

def matmul(left, right):
    return jnp.dot(left, right, precision=HIGHEST_PRECISION, preferred_element_type=jnp.float32)

def rms_norm(values, gain):
    inverse = lax.rsqrt(lax.optimization_barrier(jnp.mean(values * values, axis=-1, keepdims=True)) + EPS)
    return values * inverse * gain

def attend_sequence(queries, key_rot, values, segment):
    seq_len = queries.shape[0]
    group_size = QH // KVH
    block_rows = math.gcd(seq_len, 512)
    places = jnp.arange(seq_len, dtype=jnp.int32)
    score_scale = HD ** (-0.5)
    grouped_all = queries.reshape(seq_len, KVH, group_size, HD)

    def attend(block):
        row_begin = (block * block_rows).astype(jnp.int32)
        block_query = lax.dynamic_slice_in_dim(grouped_all, row_begin, block_rows, 0)
        row_segment = lax.dynamic_slice_in_dim(segment, row_begin, block_rows, 0)
        row_place = lax.dynamic_slice_in_dim(places, row_begin, block_rows, 0)
        logits = low_back(jnp.einsum('bkgd,skd->kgbs', block_query, key_rot, precision=HIGHEST_PRECISION) * score_scale)
        allowed = (row_segment[:, None] == segment[None, :]) & (row_place[:, None] >= places[None, :])
        logits = jnp.where(allowed[None, None], logits, MASKED)
        weights = low(jax.nn.softmax(logits, axis=-1))
        mixed_out = jnp.einsum('kgbs,skd->bkgd', weights, values, precision=HIGHEST_PRECISION)
        return mixed_out.reshape(block_rows, QH * HD)
    blocks = lax.map(jax.checkpoint(attend), jnp.arange(seq_len // block_rows, dtype=jnp.int32))
    return blocks.reshape(seq_len, QH * HD)

def layer_forward(params, inputs, cosines, sines, segment):
    norm_one, w_query, w_key, w_value, w_out, norm_two, w_gate, w_up, w_down = params
    seq_len = inputs.shape[0]
    first = low(rms_norm(inputs, norm_one))
    query_raw = low_back(matmul(first, w_query)).reshape(seq_len, QH, HD)
    key_raw = low_back(matmul(first, w_key)).reshape(seq_len, KVH, HD)
    value_all = low(low_back(matmul(first, w_value))).reshape(seq_len, KVH, HD)
    queries = low(rotate(query_raw, cosines, sines))
    key_rot = low(rotate(key_raw, cosines, sines))
    attended = low(low_back(attend_sequence(queries, key_rot, value_all, segment)))
    middle = inputs + low_back(matmul(attended, w_out))
    second = low(rms_norm(middle, norm_two))
    gate = low_back(matmul(second, w_gate))
    up_proj = low_back(matmul(second, w_up))
    hidden = low(jax.nn.silu(gate) * up_proj)
    return middle + low_back(matmul(hidden, w_down))

def reference(tokens, lengths, norm_one, w_query, w_key, w_value, w_out, norm_two, w_gate, w_up, w_down, cotangent):
    params = tuple((weight.astype(jnp.float32) for weight in (norm_one, w_query, w_key, w_value, w_out, norm_two, w_gate, w_up, w_down)))
    sequences = tokens.astype(jnp.float32).reshape(N_REP, SEQ, D)
    cot_seqs = cotangent.astype(jnp.float32).reshape(N_REP, SEQ, D)

    def one_sequence(totals, inputs_all):
        tokens_seq, cot_seq, lengths_row = inputs_all
        segment, position = doc_layout(lengths_row, SEQ)
        cosines, sines = rope_tables(position)

        def forward(weights_all, inputs):
            return layer_forward(weights_all, inputs, cosines, sines, segment)
        result, pullback = jax.vjp(forward, params, tokens_seq)
        grad_params, grad_inputs = pullback(cot_seq)
        totals = tuple((total + grad for total, grad in zip(totals, grad_params)))
        return (totals, (result, grad_inputs))
    zero_grads = tuple((jnp.zeros_like(weight) for weight in params))
    totals, (results, input_grads) = lax.scan(one_sequence, zero_grads, (sequences, cot_seqs, lengths))
    return (results.reshape(TOKENS, D).astype(jnp.bfloat16), input_grads.reshape(TOKENS, D), totals[0], totals[1], totals[2], totals[3], totals[4], totals[5], totals[6], totals[7], totals[8])
```

```python
import jax
import jax.numpy as jnp
from jax import lax
from jax.experimental import pallas as pl
from jax.experimental.pallas import tpu as pltpu
from jax.sharding import PartitionSpec as P

D = 960
QH = 15
KVH = 5
HD = 64
FF = 2560
GROUP = QH // KVH

EPS = 1e-05
ROPE_BASE = 10000.0
MASKED = -1e30
SCALE = HD ** (-0.5)
BF16 = jnp.bfloat16
F32 = jnp.float32


def doc_layout(lengths_row, length):
    places = jnp.arange(length, dtype=jnp.int32)
    doc_ends = jnp.cumsum(lengths_row)
    passed = places[:, None] >= doc_ends[None, :]
    doc_start = jnp.sum(jnp.where(passed, lengths_row[None, :], 0), axis=1)
    return (doc_start, places - doc_start)


def rope_tables(position):
    half_dim = HD // 2
    fraction = jnp.arange(half_dim, dtype=F32) * (2.0 / HD)
    inverse = ROPE_BASE ** (-fraction)
    angles = position.astype(F32)[:, None] * inverse[None, :]
    return (jnp.cos(angles), jnp.sin(angles))


def rotate(values, cosines, sines, sign):
    half_dim = HD // 2
    first_half = values[..., :half_dim]
    second_half = values[..., half_dim:]
    cos_wide = cosines[:, None, :]
    sin_wide = sign * sines[:, None, :]
    return jnp.concatenate(
        [
            first_half * cos_wide - second_half * sin_wide,
            second_half * cos_wide + first_half * sin_wide,
        ],
        axis=-1,
    )


def dot(left, right):
    return jnp.dot(left, right, preferred_element_type=F32)


def contract_rows(left, right):
    return lax.dot_general(left, right, (((0,), (0,)), ((), ())), preferred_element_type=F32)


def contract_cols(left, right):
    return lax.dot_general(left, right, (((1,), (1,)), ((), ())), preferred_element_type=F32)


def inverse_rms(values):
    return lax.rsqrt(jnp.mean(values * values, axis=-1, keepdims=True) + EPS)


def norm_backward(values, inverse, gain, grad_norm):
    scaled = grad_norm * gain
    return inverse * scaled - values * inverse**3 * jnp.mean(
        scaled * values, axis=-1, keepdims=True
    )


def swap(block, axis, count, k):
    return lax.ppermute(block, axis, [(i, i ^ k) for i in range(count)])


def at(blocks, index):
    return lax.dynamic_index_in_dim(blocks, index, 0, keepdims=False)


def gather_shard(block):
    n = lax.axis_size("shard")
    me = lax.axis_index("shard")
    parts = [block] + [swap(block, "shard", n, k) for k in range(2, n, 2)]
    total = jnp.zeros((n,) + block.shape, block.dtype)
    for j, part in enumerate(parts):
        other = swap(part, "shard", n, 1)
        total = lax.dynamic_update_index_in_dim(total, part, me ^ (2 * j), 0)
        total = lax.dynamic_update_index_in_dim(total, other, me ^ (2 * j) ^ 1, 0)
    return total


def scatter_shard(blocks):
    n = lax.axis_size("shard")
    me = lax.axis_index("shard")
    core = me % 2
    total = None
    pairs = blocks.reshape((n // 2, 2) + blocks.shape[1:])
    mine = lax.dynamic_index_in_dim(pairs, core, 1, keepdims=False)
    other = swap(lax.dynamic_index_in_dim(pairs, 1 - core, 1, keepdims=False), "shard", n, 1)
    summed = mine.astype(F32) + other.astype(F32)
    low = summed.astype(BF16)
    place = me // 2
    total = at(summed, place)
    for k in range(1, n // 2):
        total = total + swap(at(low, place ^ k), "shard", n, 2 * k).astype(F32)
    return total


def scatter_rep(blocks):
    count = lax.axis_size("rep")
    me = lax.axis_index("rep")
    total = at(blocks, me).astype(F32)
    for k in range(1, count):
        total = total + swap(at(blocks, me ^ k), "rep", count, k).astype(F32)
    return total


def gather_rep(block):
    count = lax.axis_size("rep")
    me = lax.axis_index("rep")
    total = jnp.zeros((count,) + block.shape, block.dtype)
    for k in range(count):
        part = block if k == 0 else swap(block, "rep", count, k)
        total = lax.dynamic_update_index_in_dim(total, part, me ^ k, 0)
    return total


def exchange(block, split, concat):
    return lax.all_to_all(block, "shard", split_axis=split, concat_axis=concat, tiled=True)


def masked_probs(query, key, start_ref, row, rows, cols):
    logits = contract_cols(query, key) * SCALE
    place = lax.broadcasted_iota(jnp.int32, (rows, cols), 1)
    own = lax.broadcasted_iota(jnp.int32, (rows, cols), 0) + row
    allowed = (place <= own) & (place >= start_ref[pl.ds(row, rows), :])
    logits = jnp.where(allowed, logits, MASKED)
    raised = jnp.exp(logits - jnp.max(logits, axis=-1, keepdims=True))
    return raised * (1.0 / jnp.sum(raised, axis=-1, keepdims=True))


def attend_kernel(block, q_ref, k_ref, v_ref, start_ref, out_ref):
    heads, length, _ = q_ref.shape
    for h in range(heads):
        for i in range(length // block):
            row, cols = i * block, (i + 1) * block
            probs = masked_probs(
                q_ref[h, pl.ds(row, block), :], k_ref[h, pl.ds(0, cols), :], start_ref, row, block, cols
            )
            out_ref[h, pl.ds(row, block), :] = dot(
                probs.astype(BF16), v_ref[h, pl.ds(0, cols), :]
            ).astype(BF16)


def attend_back_kernel(block, q_ref, k_ref, v_ref, g_ref, start_ref, dq_ref, dk_ref, dv_ref):
    heads, length, _ = q_ref.shape
    dk_ref[...] = jnp.zeros_like(dk_ref)
    dv_ref[...] = jnp.zeros_like(dv_ref)
    for h in range(heads):
        for i in range(length // block):
            row, cols = i * block, (i + 1) * block
            query = q_ref[h, pl.ds(row, block), :]
            key = k_ref[h, pl.ds(0, cols), :]
            grad = g_ref[h, pl.ds(row, block), :]
            probs = masked_probs(query, key, start_ref, row, block, cols)
            grad_probs = contract_cols(grad, v_ref[h, pl.ds(0, cols), :])
            delta = jnp.sum(probs * grad_probs, axis=-1, keepdims=True)
            grad_logits = (probs * (grad_probs - delta)).astype(BF16)
            dq_ref[h, pl.ds(row, block), :] = dot(grad_logits, key) * SCALE
            dv_ref[h, pl.ds(0, cols), :] += contract_rows(probs.astype(BF16), grad)
            dk_ref[h, pl.ds(0, cols), :] += contract_rows(grad_logits, query) * SCALE


def attend(query, key, value, start):
    block = min(256, query.shape[1])
    return pl.pallas_call(
        lambda *refs: attend_kernel(block, *refs),
        out_shape=jax.ShapeDtypeStruct(query.shape, BF16),
        in_specs=[pl.BlockSpec(memory_space=pltpu.VMEM)] * 4,
        out_specs=pl.BlockSpec(memory_space=pltpu.VMEM),
        compiler_params=pltpu.CompilerParams(vmem_limit_bytes=48 * 2**20),
        name="attend",
    )(query, key, value, start)


def attend_back(query, key, value, grad, start):
    block = min(256, query.shape[1])
    return pl.pallas_call(
        lambda *refs: attend_back_kernel(block, *refs),
        out_shape=[jax.ShapeDtypeStruct(query.shape, F32)] * 3,
        in_specs=[pl.BlockSpec(memory_space=pltpu.VMEM)] * 5,
        out_specs=[pl.BlockSpec(memory_space=pltpu.VMEM)] * 3,
        compiler_params=pltpu.CompilerParams(vmem_limit_bytes=48 * 2**20),
        name="attend_back",
    )(query, key, value, grad, start)


def round_up(value, step):
    return -(-value // step) * step


def per_slot(weight, slots):
    rows = weight.shape[0]
    wide = jnp.repeat(weight.reshape(rows, KVH, HD), GROUP, axis=1).reshape(rows, QH * HD)
    return jnp.pad(wide, ((0, 0), (0, (slots - QH) * HD)))


def shards(
    tokens,
    lengths,
    norm_one,
    w_query,
    w_key,
    w_value,
    w_out,
    norm_two,
    w_gate,
    w_up,
    w_down,
    cotangent,
):
    n = lax.axis_size("shard")
    reps = lax.axis_size("rep")
    row_count = tokens.shape[0]
    length = row_count * n
    own_rows = w_query.shape[0]
    hidden_own = w_down.shape[0]
    heads = -(-QH // n)
    slots = heads * n
    head_cols = heads * HD

    tokens_all = gather_shard(tokens).reshape(length, D)

    pad_rows = round_up(own_rows + 2, 8)
    attention_weights = jnp.concatenate(
        [
            jnp.pad(w_query, ((0, 0), (0, (slots - QH) * HD))).reshape(own_rows, n, head_cols),
            per_slot(w_key, slots).reshape(own_rows, n, head_cols),
            per_slot(w_value, slots).reshape(own_rows, n, head_cols),
        ],
        axis=2,
    )
    gains = jnp.pad(jnp.stack([norm_one, norm_two]), ((0, 0), (0, 3 * head_cols - own_rows)))
    message = jnp.concatenate(
        [
            attention_weights.reshape(own_rows, n * 3 * head_cols),
            jnp.tile(gains, (1, n)),
            jnp.zeros((pad_rows - own_rows - 2, n * 3 * head_cols), BF16),
        ],
        axis=0,
    )
    arrived = exchange(message, 1, 0).reshape(n, pad_rows, 3 * head_cols)
    w_qkv = arrived[:, :own_rows].reshape(D, 3 * head_cols)
    gain_one = arrived[:, own_rows, :own_rows].reshape(1, D).astype(F32)
    gain_two = arrived[:, own_rows + 1, :own_rows].reshape(1, D).astype(F32)

    w_gate_up = exchange(
        jnp.concatenate(
            [
                w_gate.reshape(own_rows, n, hidden_own),
                w_up.reshape(own_rows, n, hidden_own),
            ],
            axis=2,
        ).reshape(own_rows, n * 2 * hidden_own),
        1,
        0,
    )
    out_full = gather_shard(w_out).reshape(D, D)
    cot_all = gather_shard(cotangent).reshape(length, D)

    doc_start, position = doc_layout(lengths[0], length)
    cosines, sines = rope_tables(position)
    inputs_all = tokens_all.astype(F32)
    first_all = (inputs_all * inverse_rms(inputs_all) * gain_one).astype(BF16)
    qkv = dot(first_all, w_qkv).reshape(length, 3, heads, HD)
    query = rotate(qkv[:, 0], cosines, sines, 1.0).astype(BF16).transpose(1, 0, 2)
    key = rotate(qkv[:, 1], cosines, sines, 1.0).astype(BF16).transpose(1, 0, 2)
    value = qkv[:, 2].astype(BF16).transpose(1, 0, 2)
    start = doc_start[:, None]
    mixed = attend(query, key, value, start).transpose(1, 0, 2).reshape(length, head_cols)
    attended = exchange(mixed, 0, 1)[:, :D]

    inputs = tokens.astype(F32)
    middle = inputs + dot(attended, out_full)
    inverse_two = inverse_rms(middle)
    second = (middle * inverse_two * gain_two).astype(BF16)
    second_all = gather_shard(second).reshape(length, D)

    gate_up = dot(second_all, w_gate_up)
    gate, up_proj = gate_up[:, :hidden_own], gate_up[:, hidden_own:]
    sigmoid_gate = jax.nn.sigmoid(gate)
    silu_gate = gate * sigmoid_gate
    hidden = (silu_gate * up_proj).astype(BF16)
    grad_hidden = contract_cols(cot_all, w_down)
    grad_gate = grad_hidden * up_proj * sigmoid_gate * (1.0 + gate * (1.0 - sigmoid_gate))
    grad_up = grad_hidden * silu_gate
    grad_gate_up = jnp.concatenate([grad_gate, grad_up], axis=1).astype(BF16)
    grad_second = scatter_shard(
        contract_cols(grad_gate_up, w_gate_up).astype(BF16).reshape(n, row_count, D)
    )
    down = scatter_shard(dot(hidden, w_down).astype(BF16).reshape(n, row_count, D))
    output = (middle + down).astype(BF16)

    grad_middle = cotangent.astype(F32) + norm_backward(middle, inverse_two, gain_two, grad_second)
    grad_branch = grad_middle.astype(BF16)
    grad_attended = contract_cols(grad_branch, out_full).astype(BF16)
    grad_mixed = exchange(jnp.pad(grad_attended, ((0, 0), (0, (slots - QH) * HD))), 1, 0)

    grad_heads = grad_mixed.reshape(length, heads, HD).transpose(1, 0, 2)
    grad_query, grad_key, grad_value = attend_back(query, key, value, grad_heads, start)
    grad_qkv = jnp.concatenate(
        [
            rotate(grad_query.transpose(1, 0, 2), cosines, sines, -1.0).reshape(length, head_cols),
            rotate(grad_key.transpose(1, 0, 2), cosines, sines, -1.0).reshape(length, head_cols),
            grad_value.transpose(1, 0, 2).reshape(length, head_cols),
        ],
        axis=1,
    ).astype(BF16)
    grad_first = scatter_shard(
        contract_cols(grad_qkv, w_qkv).astype(BF16).reshape(n, row_count, D)
    )
    input_grad = grad_middle + norm_backward(inputs, inverse_rms(inputs), gain_one, grad_first)

    grad_rows = round_up(own_rows, 8 * reps)
    piece = grad_rows // reps

    def to_pieces(grad):
        blocks = grad.astype(BF16).reshape(n, own_rows, grad.shape[1])
        blocks = jnp.pad(blocks, ((0, 0), (0, grad_rows - own_rows), (0, 0)))
        return blocks.reshape(n, reps, piece, grad.shape[1]).transpose(1, 0, 2, 3)

    def columns_to_owner(grad):
        cols = grad.shape[1]
        summed = scatter_rep(to_pieces(grad)).astype(BF16).reshape(n * piece, cols)
        moved = exchange(summed, 0, 1)
        whole = gather_rep(moved).reshape(grad_rows, n * cols)[:own_rows]
        return whole.astype(F32).reshape(own_rows, n, cols)

    owned_ff = columns_to_owner(contract_rows(second_all, grad_gate_up))
    grad_w_gate = owned_ff[:, :, :hidden_own].reshape(own_rows, FF)
    grad_w_up = owned_ff[:, :, hidden_own:].reshape(own_rows, FF)

    down_rows = round_up(hidden_own, 8 * reps)
    down_grad = jnp.pad(
        contract_rows(hidden, cot_all).astype(BF16), ((0, down_rows - hidden_own), (0, 0))
    )
    grad_w_down = gather_rep(
        scatter_rep(down_grad.reshape(reps, down_rows // reps, D)).astype(BF16)
    ).reshape(down_rows, D)[:hidden_own].astype(F32)

    out_pieces = scatter_rep(to_pieces(contract_rows(attended, grad_branch))).astype(BF16)
    grad_w_out = gather_rep(scatter_shard(out_pieces).astype(BF16)).reshape(grad_rows, D)
    grad_w_out = grad_w_out[:own_rows].astype(F32)

    owned_attention = columns_to_owner(contract_rows(first_all, grad_qkv))

    def slots_of(index):
        cols = owned_attention[:, :, index * head_cols : (index + 1) * head_cols]
        return cols.reshape(own_rows, slots * HD)[:, :D]

    def key_heads(wide):
        return wide.reshape(own_rows, KVH, GROUP, HD).sum(axis=2).reshape(own_rows, KVH * HD)

    grad_w_query = slots_of(0)
    grad_w_key = key_heads(slots_of(1))
    grad_w_value = key_heads(slots_of(2))

    def gain_grad(pairs, gain):
        total = sum(jnp.sum(weight.astype(F32) * grad, axis=1) for weight, grad in pairs)
        return total / gain.astype(F32)

    grad_norm_one = gain_grad(
        [(w_query, grad_w_query), (w_key, grad_w_key), (w_value, grad_w_value)], norm_one
    )
    grad_norm_two = gain_grad([(w_gate, grad_w_gate), (w_up, grad_w_up)], norm_two)
    return (
        output,
        input_grad,
        grad_norm_one,
        grad_w_query,
        grad_w_key,
        grad_w_value,
        grad_w_out,
        grad_norm_two,
        grad_w_gate,
        grad_w_up,
        grad_w_down,
    )


def solution(mesh):
    rows = P("shard", None)
    own_tokens = P(("rep", "shard"), None)
    return jax.shard_map(
        shards,
        mesh=mesh,
        in_specs=(
            own_tokens,
            P("rep", None),
            P("shard"),
            rows,
            rows,
            rows,
            rows,
            P("shard"),
            rows,
            rows,
            rows,
            own_tokens,
        ),
        out_specs=(
            own_tokens,
            own_tokens,
            P("shard"),
            rows,
            rows,
            rows,
            rows,
            P("shard"),
            rows,
            rows,
            rows,
        ),
        check_vma=False,
    )
```

```python
import jax
import jax.numpy as jnp
from jax import lax
from jax.experimental import pallas as pl
from jax.experimental.pallas import tpu as pltpu
from jax.sharding import PartitionSpec as P

D = 960
QH = 15
KVH = 5
HD = 64
FF = 2560
GROUP = QH // KVH

EPS = 1e-05
ROPE_BASE = 10000.0
MASKED = -1e30
SCALE = HD ** (-0.5)
BF16 = jnp.bfloat16
F32 = jnp.float32


def doc_layout(lengths_row, length):
    places = jnp.arange(length, dtype=jnp.int32)
    doc_ends = jnp.cumsum(lengths_row)
    passed = places[:, None] >= doc_ends[None, :]
    doc_start = jnp.sum(jnp.where(passed, lengths_row[None, :], 0), axis=1)
    return (doc_start, places - doc_start)


def rope_tables(position):
    half_dim = HD // 2
    fraction = jnp.arange(half_dim, dtype=F32) * (2.0 / HD)
    inverse = ROPE_BASE ** (-fraction)
    angles = position.astype(F32)[:, None] * inverse[None, :]
    return (jnp.cos(angles), jnp.sin(angles))


VMEM_LIMIT = 56 * 2**20


def dot(left, right):
    return jnp.dot(left, right, preferred_element_type=F32)


def contract_rows(left, right):
    return lax.dot_general(left, right, (((0,), (0,)), ((), ())), preferred_element_type=F32)


def contract_cols(left, right):
    return lax.dot_general(left, right, (((1,), (1,)), ((), ())), preferred_element_type=F32)


def inverse_rms(values):
    return lax.rsqrt(jnp.mean(values * values, axis=-1, keepdims=True) + EPS)


def norm_backward(values, inverse, gain, grad_norm):
    scaled = grad_norm * gain
    return inverse * scaled - values * inverse**3 * jnp.mean(
        scaled * values, axis=-1, keepdims=True
    )


def round_up(value, step):
    return -(-value // step) * step


def rows_at(index, rows):
    return pl.ds(pl.multiple_of(index * rows, rows), rows)


def core_swap(block):
    n = lax.axis_size("shard")
    return lax.ppermute(block, "shard", [(i, i ^ 1) for i in range(n)])


def exchange_z(blocks):
    n = lax.axis_size("shard")
    groups = [list(range(core, n, 2)) for core in range(2)]
    return lax.all_to_all(
        blocks, "shard", split_axis=0, concat_axis=0, axis_index_groups=groups, tiled=True
    )


def exchange(block, split, concat):
    return lax.all_to_all(block, "shard", split_axis=split, concat_axis=concat, tiled=True)


def gather_tiled(tiled):
    mine = exchange_z(tiled)
    return mine, core_swap(mine)


def scatter_pairs(mine, other):
    summed = mine.astype(F32) + core_swap(other).astype(F32)
    return exchange_z(summed.astype(BF16))


def scatter_rep(pieces):
    moved = lax.all_to_all(pieces, "rep", split_axis=0, concat_axis=0, tiled=True)
    return jnp.sum(moved.astype(F32), axis=0).astype(BF16)


def gather_rep(piece):
    reps = lax.axis_size("rep")
    tiled = jnp.broadcast_to(piece[None], (reps,) + piece.shape)
    return lax.all_to_all(tiled, "rep", split_axis=0, concat_axis=0, tiled=True)


def call(kernel, name, outs, *operands, scalars=()):
    specs = [pl.BlockSpec(memory_space=pltpu.SMEM)] * len(scalars)
    specs += [pl.BlockSpec(memory_space=pltpu.VMEM)] * len(operands)
    return pl.pallas_call(
        kernel,
        out_shape=[jax.ShapeDtypeStruct(shape, dtype) for shape, dtype in outs],
        in_specs=specs,
        out_specs=[pl.BlockSpec(memory_space=pltpu.VMEM)] * len(outs),
        compiler_params=pltpu.CompilerParams(vmem_limit_bytes=VMEM_LIMIT),
        name=name,
    )(*scalars, *operands)


def turned(values):
    half = HD // 2
    parts = []
    for begin in range(0, values.shape[1], HD):
        parts.append(-values[:, begin + half : begin + HD])
        parts.append(values[:, begin : begin + half])
    return jnp.concatenate(parts, axis=1)


def head_of(values, h, heads):
    if heads == 1:
        return values
    lane = lax.broadcasted_iota(jnp.int32, values.shape, 1)
    return jnp.where(lane // HD == h, values, jnp.zeros_like(values))


def masked_probs(query, key, starts, row):
    rows, cols = query.shape[0], key.shape[0]
    logits = contract_cols(query, key) * SCALE
    place = lax.broadcasted_iota(jnp.int32, (rows, cols), 1)
    own = lax.broadcasted_iota(jnp.int32, (rows, cols), 0) + row
    logits = jnp.where((place <= own) & (place >= starts), logits, MASKED)
    raised = jnp.exp(logits - jnp.max(logits, axis=-1, keepdims=True))
    return raised * (1.0 / jnp.sum(raised, axis=-1, keepdims=True))


def attend_kernel(
    rows, core_ref, mine_ref, other_ref, w_ref, gain_ref, cos_ref, sin_ref, start_ref,
    first_ref, q_ref, k_ref, v_ref, mixed_ref,
):
    length, head_cols = q_ref.shape
    heads = head_cols // HD
    core = core_ref[0]
    for side, ref in ((core, mine_ref), (1 - core, other_ref)):
        for z in range(length // rows // 2):
            inputs = ref[pl.ds(z * rows, rows), :].astype(F32)
            normed = inputs * inverse_rms(inputs) * gain_ref[...]
            first_ref[rows_at(2 * z + side, rows), :] = normed.astype(BF16)
    block = min(256, length)
    for i in range(length // block):
        span = pl.ds(i * block, block)
        raw = dot(first_ref[span, :], w_ref[...])
        cosines, sines = cos_ref[span, :], sin_ref[span, :]
        query, key = raw[:, :head_cols], raw[:, head_cols : 2 * head_cols]
        q_ref[span, :] = (query * cosines + turned(query) * sines).astype(BF16)
        k_ref[span, :] = (key * cosines + turned(key) * sines).astype(BF16)
        v_ref[span, :] = raw[:, 2 * head_cols :].astype(BF16)
    for i in range(length // block):
        span, past = pl.ds(i * block, block), pl.ds(0, (i + 1) * block)
        total = None
        for h in range(heads):
            probs = masked_probs(
                head_of(q_ref[span, :], h, heads), k_ref[past, :], start_ref[span, :], i * block
            )
            mixed = head_of(dot(probs.astype(BF16), v_ref[past, :]), h, heads)
            total = mixed if total is None else total + mixed
        mixed_ref[span, :] = total.astype(BF16)


def attend_back_kernel(
    first_ref, q_ref, k_ref, v_ref, g_ref, cos_ref, sin_ref, start_ref, dqkv_ref, piece_ref, dk_ref, dv_ref
):
    length, head_cols = q_ref.shape
    heads = head_cols // HD
    block = min(256, length)
    dk_ref[...] = jnp.zeros_like(dk_ref)
    dv_ref[...] = jnp.zeros_like(dv_ref)
    for i in range(length // block):
        span, past = pl.ds(i * block, block), pl.ds(0, (i + 1) * block)
        total = None
        for h in range(heads):
            query = head_of(q_ref[span, :], h, heads)
            grad = head_of(g_ref[span, :], h, heads)
            key = k_ref[past, :]
            probs = masked_probs(query, key, start_ref[span, :], i * block)
            grad_probs = contract_cols(grad, v_ref[past, :])
            delta = jnp.sum(probs * grad_probs, axis=-1, keepdims=True)
            grad_logits = (probs * (grad_probs - delta)).astype(BF16)
            grad_query = head_of(dot(grad_logits, key), h, heads)
            total = grad_query if total is None else total + grad_query
            dv_ref[past, :] += contract_rows(probs.astype(BF16), grad)
            dk_ref[past, :] += contract_rows(grad_logits, query)
        total = total * SCALE
        back = total * cos_ref[span, :] - turned(total) * sin_ref[span, :]
        dqkv_ref[span, :head_cols] = back.astype(BF16)
    for i in range(length // block):
        span = pl.ds(i * block, block)
        total = dk_ref[span, :] * SCALE
        back = total * cos_ref[span, :] - turned(total) * sin_ref[span, :]
        dqkv_ref[span, head_cols : 2 * head_cols] = back.astype(BF16)
        dqkv_ref[span, 2 * head_cols :] = dv_ref[span, :].astype(BF16)
    store_pieces(piece_ref, contract_rows(first_ref[...], dqkv_ref[...]))


def store_pieces(piece_ref, grad):
    reps, n, piece, cols = piece_ref.shape
    own = grad.shape[0] // n
    for s in range(n):
        for r in range(reps):
            begin, end = r * piece, min((r + 1) * piece, own)
            if end <= begin:
                piece_ref[r, s] = jnp.zeros((piece, cols), BF16)
                continue
            rows = grad[s * own + begin : s * own + end]
            if end - begin < piece:
                rows = jnp.concatenate([rows, jnp.zeros((piece - end + begin, cols), F32)], axis=0)
            piece_ref[r, s] = rows.astype(BF16)


def first_grad_kernel(rows, core_ref, dqkv_ref, w_ref, mine_ref, other_ref, all_ref):
    length = dqkv_ref.shape[0]
    core = core_ref[0]
    block = min(256, length)
    for i in range(length // block):
        span = pl.ds(i * block, block)
        all_ref[span, :] = contract_cols(dqkv_ref[span, :], w_ref[...]).astype(BF16)
    for side, ref in ((core, mine_ref), (1 - core, other_ref)):
        for z in range(length // rows // 2):
            ref[pl.ds(z * rows, rows), :] = all_ref[rows_at(2 * z + side, rows), :]


def middle_kernel(tokens_ref, attended_ref, w_ref, gain_ref, middle_ref, tiled_ref):
    rows, width = tokens_ref.shape
    middle = tokens_ref[...].astype(F32) + dot(attended_ref[:, :width], w_ref[...])
    middle_ref[...] = middle
    second = (middle * inverse_rms(middle) * gain_ref[...]).astype(BF16)
    for z in range(tiled_ref.shape[0] // rows):
        tiled_ref[pl.ds(z * rows, rows), :] = second


def hidden_kernel(
    rows, core_ref, mine_ref, other_ref, cot_ref, w_ref, down_ref,
    grad_mine_ref, grad_other_ref, grads_ref, hidden_ref,
):
    half = mine_ref.shape[0]
    units = down_ref.shape[0]
    core = core_ref[0]
    block = min(2 * rows, half)
    each = block // rows
    for part, (side, ref, out_ref) in enumerate(
        ((core, mine_ref, grad_mine_ref), (1 - core, other_ref, grad_other_ref))
    ):
        for i in range(half // block):
            span = pl.ds(i * block, block)
            both = dot(ref[span, :], w_ref[...])
            gate, up = both[:, :units], both[:, units:]
            places = [2 * (i * each + j) + side for j in range(each)]
            cot = jnp.concatenate([cot_ref[rows_at(place, rows), :] for place in places], axis=0)
            grad_hidden = contract_cols(cot, down_ref[...])
            sigmoid = 1.0 / (1.0 + jnp.exp(-gate))
            silu = gate * sigmoid
            hidden = (silu * up).astype(BF16)
            for j, place in enumerate(places):
                hidden_ref[rows_at(place, rows), :] = hidden[j * rows : (j + 1) * rows]
            grad_gate = grad_hidden * up * sigmoid * (1.0 + gate * (1.0 - sigmoid))
            grads = jnp.concatenate([grad_gate, grad_hidden * silu], axis=1).astype(BF16)
            grads_ref[pl.ds(part * half + i * block, block), :] = grads
            out_ref[span, :] = contract_cols(grads, w_ref[...]).astype(BF16)


def hidden_weights_kernel(mine_ref, other_ref, grads_ref, hidden_ref, cot_ref, piece_ref, down_ref):
    half = mine_ref.shape[0]
    store_pieces(
        piece_ref,
        contract_rows(mine_ref[...], grads_ref[pl.ds(0, half), :])
        + contract_rows(other_ref[...], grads_ref[pl.ds(half, half), :]),
    )
    store_pieces(down_ref, contract_rows(hidden_ref[...], cot_ref[...]))


def down_kernel(hidden_ref, w_ref, out_ref):
    block = min(256, hidden_ref.shape[0])
    for i in range(hidden_ref.shape[0] // block):
        span = pl.ds(i * block, block)
        out_ref[span, :] = dot(hidden_ref[span, :], w_ref[...]).astype(BF16)


def middle_grad_kernel(
    parts_ref, cot_ref, middle_ref, gain_ref, w_ref, grad_ref, branch_ref, attended_ref
):
    rows, width = cot_ref.shape
    middle = middle_ref[...]
    grad_second = sum(
        parts_ref[pl.ds(z * rows, rows), :].astype(F32) for z in range(parts_ref.shape[0] // rows)
    )
    grad = cot_ref[...].astype(F32) + norm_backward(
        middle, inverse_rms(middle), gain_ref[...], grad_second
    )
    grad_ref[...] = grad
    branch = grad.astype(BF16)
    branch_ref[...] = branch
    attended_ref[:, :width] = contract_cols(branch, w_ref[...]).astype(BF16)
    if attended_ref.shape[1] > width:
        attended_ref[:, width:] = jnp.zeros((rows, attended_ref.shape[1] - width), BF16)


def out_weights_kernel(attended_ref, branch_ref, piece_ref):
    width = branch_ref.shape[1]
    store_pieces(piece_ref, contract_rows(attended_ref[:, :width], branch_ref[...]))


def input_grad_kernel(parts_ref, tokens_ref, gain_ref, grad_ref, out_ref):
    rows = tokens_ref.shape[0]
    inputs = tokens_ref[...].astype(F32)
    grad_first = sum(
        parts_ref[pl.ds(z * rows, rows), :].astype(F32) for z in range(parts_ref.shape[0] // rows)
    )
    out_ref[...] = grad_ref[...] + norm_backward(
        inputs, inverse_rms(inputs), gain_ref[...], grad_first
    )


def per_slot(weight, slots):
    rows = weight.shape[0]
    wide = jnp.repeat(weight.reshape(rows, KVH, HD), GROUP, axis=1).reshape(rows, QH * HD)
    return jnp.pad(wide, ((0, 0), (0, (slots - QH) * HD)))


def shards(
    tokens,
    lengths,
    norm_one,
    w_query,
    w_key,
    w_value,
    w_out,
    norm_two,
    w_gate,
    w_up,
    w_down,
    cotangent,
):
    n = lax.axis_size("shard")
    reps = lax.axis_size("rep")
    row_count = tokens.shape[0]
    length = row_count * n
    half = length // 2
    own_rows = w_query.shape[0]
    hidden_own = w_down.shape[0]
    heads = -(-QH // n)
    slots = heads * n
    head_cols = heads * HD
    core = (lax.axis_index("shard") % 2).astype(jnp.int32).reshape(1)
    my_rep = lax.axis_index("rep")
    piece = round_up(own_rows + 2, 8 * reps) // reps

    def rep_rows(block):
        padded = jnp.pad(block, ((0, piece * reps - block.shape[0]), (0, 0)))
        return lax.dynamic_slice_in_dim(padded, my_rep * piece, piece, 0)

    def to_columns(message):
        cols = message.shape[1] // n
        moved = gather_rep(exchange(message, 1, 0)).reshape(reps, n, piece, cols)
        return moved.transpose(1, 0, 2, 3).reshape(n, reps * piece, cols)

    tokens_mine, tokens_other = gather_tiled(jnp.tile(tokens, (n // 2, 1)))
    gains = jnp.pad(jnp.stack([norm_one, norm_two]), ((0, 0), (0, 3 * head_cols - own_rows)))
    attention_weights = jnp.concatenate(
        [
            jnp.pad(w_query, ((0, 0), (0, (slots - QH) * HD))).reshape(own_rows, n, head_cols),
            per_slot(w_key, slots).reshape(own_rows, n, head_cols),
            per_slot(w_value, slots).reshape(own_rows, n, head_cols),
        ],
        axis=2,
    ).reshape(own_rows, n * 3 * head_cols)
    arrived = to_columns(
        rep_rows(jnp.concatenate([attention_weights, jnp.tile(gains, (1, n))], axis=0))
    )
    w_qkv = arrived[:, :own_rows].reshape(D, 3 * head_cols)
    gain_one = arrived[:, own_rows, :own_rows].reshape(1, D).astype(F32)
    gain_two = arrived[:, own_rows + 1, :own_rows].reshape(1, D).astype(F32)

    gate_up = jnp.concatenate(
        [w_gate.reshape(own_rows, n, hidden_own), w_up.reshape(own_rows, n, hidden_own)], axis=2
    ).reshape(own_rows, n * 2 * hidden_own)
    w_gate_up = to_columns(rep_rows(gate_up))[:, :own_rows].reshape(D, 2 * hidden_own)
    out_full = lax.all_gather(w_out, "shard", axis=0, tiled=True)
    cot_all = lax.all_gather(cotangent, "shard", axis=0, tiled=True)

    doc_start, position = doc_layout(lengths[0], length)
    cosines, sines = rope_tables(position)
    cosines = jnp.tile(cosines, (1, 2 * heads))
    sines = jnp.tile(sines, (1, 2 * heads))
    start = doc_start[:, None]
    head_shape = (length, head_cols)
    first_all, query, key, value, mixed = call(
        lambda *refs: attend_kernel(row_count, *refs),
        "attend",
        [((length, D), BF16)] + [(head_shape, BF16)] * 4,
        tokens_mine,
        tokens_other,
        w_qkv,
        gain_one,
        cosines,
        sines,
        start,
        scalars=(core,),
    )
    attended = exchange(mixed, 0, 1)

    middle, second_tiled = call(
        middle_kernel,
        "middle",
        [((row_count, D), F32), ((half, D), BF16)],
        tokens,
        attended,
        out_full,
        gain_two,
    )
    second_mine, second_other = gather_tiled(second_tiled)

    grad_mine, grad_other, grads, hidden = call(
        lambda *refs: hidden_kernel(row_count, *refs),
        "hidden",
        [
            ((half, D), BF16),
            ((half, D), BF16),
            ((length, 2 * hidden_own), BF16),
            ((length, hidden_own), BF16),
        ],
        second_mine,
        second_other,
        cot_all,
        w_gate_up,
        w_down,
        scalars=(core,),
    )
    grad_second_parts = scatter_pairs(grad_mine, grad_other)
    grad_rows = round_up(own_rows, 8 * reps)
    grad_piece = grad_rows // reps
    down_piece = round_up(hidden_own, 8 * reps) // reps
    ff_pieces, down_pieces = call(
        hidden_weights_kernel,
        "hidden_weights",
        [
            ((reps, n, grad_piece, 2 * hidden_own), BF16),
            ((reps, 1, down_piece, D), BF16),
        ],
        second_mine,
        second_other,
        grads,
        hidden,
        cot_all,
    )
    (down_parts,) = call(down_kernel, "down", [((length, D), BF16)], hidden, w_down)
    down = lax.psum_scatter(down_parts, "shard", scatter_dimension=0, tiled=True)
    output = (middle + down.astype(F32)).astype(BF16)

    grad_middle, grad_branch, grad_attended = call(
        middle_grad_kernel,
        "middle_grad",
        [((row_count, D), F32), ((row_count, D), BF16), ((row_count, slots * HD), BF16)],
        grad_second_parts,
        cotangent,
        middle,
        gain_two,
        out_full,
    )
    grad_heads = exchange(grad_attended, 1, 0)
    (out_pieces,) = call(
        out_weights_kernel,
        "out_weights",
        [((reps, n, grad_piece, D), BF16)],
        attended,
        grad_branch,
    )

    grad_qkv, attention_pieces = pl.pallas_call(
        attend_back_kernel,
        out_shape=[
            jax.ShapeDtypeStruct((length, 3 * head_cols), BF16),
            jax.ShapeDtypeStruct((reps, n, grad_piece, 3 * head_cols), BF16),
        ],
        in_specs=[pl.BlockSpec(memory_space=pltpu.VMEM)] * 8,
        out_specs=[pl.BlockSpec(memory_space=pltpu.VMEM)] * 2,
        scratch_shapes=[pltpu.VMEM(head_shape, F32)] * 2,
        compiler_params=pltpu.CompilerParams(vmem_limit_bytes=VMEM_LIMIT),
        name="attend_back",
    )(first_all, query, key, value, grad_heads, cosines, sines, start)
    first_mine, first_other = pl.pallas_call(
        lambda *refs: first_grad_kernel(row_count, *refs),
        out_shape=[jax.ShapeDtypeStruct((half, D), BF16)] * 2,
        in_specs=[pl.BlockSpec(memory_space=pltpu.SMEM)]
        + [pl.BlockSpec(memory_space=pltpu.VMEM)] * 2,
        out_specs=[pl.BlockSpec(memory_space=pltpu.VMEM)] * 2,
        scratch_shapes=[pltpu.VMEM((length, D), BF16)],
        compiler_params=pltpu.CompilerParams(vmem_limit_bytes=VMEM_LIMIT),
        name="first_grad",
    )(core, grad_qkv, w_qkv)
    (input_grad,) = call(
        input_grad_kernel,
        "input_grad",
        [((row_count, D), F32)],
        scatter_pairs(first_mine, first_other),
        tokens,
        gain_one,
        grad_middle,
    )

    def columns_to_owner(pieces):
        cols = pieces.shape[3]
        summed = scatter_rep(pieces).reshape(n * grad_piece, cols)
        whole = gather_rep(exchange(summed, 0, 1)).reshape(grad_rows, n * cols)[:own_rows]
        return whole.astype(F32).reshape(own_rows, n, cols)

    owned_ff = columns_to_owner(ff_pieces)
    grad_w_gate = owned_ff[:, :, :hidden_own].reshape(own_rows, FF)
    grad_w_up = owned_ff[:, :, hidden_own:].reshape(own_rows, FF)

    grad_w_down = gather_rep(scatter_rep(down_pieces).reshape(down_piece, D))
    grad_w_down = grad_w_down.reshape(reps * down_piece, D)[:hidden_own].astype(F32)

    out_summed = exchange(scatter_rep(out_pieces).reshape(n * grad_piece, D), 0, 0)
    out_piece = jnp.sum(out_summed.reshape(n, grad_piece, D).astype(F32), axis=0).astype(BF16)
    grad_w_out = gather_rep(out_piece).reshape(grad_rows, D)[:own_rows].astype(F32)

    owned_attention = columns_to_owner(attention_pieces)

    def slots_of(index):
        cols = owned_attention[:, :, index * head_cols : (index + 1) * head_cols]
        return cols.reshape(own_rows, slots * HD)[:, :D]

    def key_heads(wide):
        return wide.reshape(own_rows, KVH, GROUP, HD).sum(axis=2).reshape(own_rows, KVH * HD)

    grad_w_query = slots_of(0)
    grad_w_key = key_heads(slots_of(1))
    grad_w_value = key_heads(slots_of(2))

    def gain_grad(pairs, gain):
        total = sum(jnp.sum(weight.astype(F32) * grad, axis=1) for weight, grad in pairs)
        return total / gain.astype(F32)

    grad_norm_one = gain_grad(
        [(w_query, grad_w_query), (w_key, grad_w_key), (w_value, grad_w_value)], norm_one
    )
    grad_norm_two = gain_grad([(w_gate, grad_w_gate), (w_up, grad_w_up)], norm_two)
    return (
        output,
        input_grad,
        grad_norm_one,
        grad_w_query,
        grad_w_key,
        grad_w_value,
        grad_w_out,
        grad_norm_two,
        grad_w_gate,
        grad_w_up,
        grad_w_down,
    )


def solution(mesh):
    rows = P("shard", None)
    own_tokens = P(("rep", "shard"), None)
    return jax.shard_map(
        shards,
        mesh=mesh,
        in_specs=(
            own_tokens,
            P("rep", None),
            P("shard"),
            rows,
            rows,
            rows,
            rows,
            P("shard"),
            rows,
            rows,
            rows,
            own_tokens,
        ),
        out_specs=(
            own_tokens,
            own_tokens,
            P("shard"),
            rows,
            rows,
            rows,
            rows,
            P("shard"),
            rows,
            rows,
            rows,
        ),
        check_vma=False,
    )
```

```python
import jax
import jax.numpy as jnp
from jax import lax
from jax.experimental import pallas as pl
from jax.experimental.pallas import tpu as pltpu
from jax.sharding import PartitionSpec as P

D = 960
QH = 15
KVH = 5
HD = 64
FF = 2560
GROUP = QH // KVH

EPS = 1e-05
ROPE_BASE = 10000.0
MASKED = -1e30
SCALE = HD ** (-0.5)
BF16 = jnp.bfloat16
F32 = jnp.float32


def doc_layout(lengths_row, length):
    places = jnp.arange(length, dtype=jnp.int32)
    doc_ends = jnp.cumsum(lengths_row)
    passed = places[:, None] >= doc_ends[None, :]
    doc_start = jnp.sum(jnp.where(passed, lengths_row[None, :], 0), axis=1)
    return (doc_start, places - doc_start)


def rope_tables(position):
    half_dim = HD // 2
    fraction = jnp.arange(half_dim, dtype=F32) * (2.0 / HD)
    inverse = ROPE_BASE ** (-fraction)
    angles = position.astype(F32)[:, None] * inverse[None, :]
    return (jnp.cos(angles), jnp.sin(angles))


VMEM_LIMIT = 56 * 2**20


def dot(left, right):
    return jnp.dot(left, right, preferred_element_type=F32)


def contract_rows(left, right):
    return lax.dot_general(left, right, (((0,), (0,)), ((), ())), preferred_element_type=F32)


def contract_cols(left, right):
    return lax.dot_general(left, right, (((1,), (1,)), ((), ())), preferred_element_type=F32)


def inverse_rms(values):
    return lax.rsqrt(jnp.sum(values * values, axis=-1, keepdims=True) * (1.0 / D) + EPS)


def norm_backward(values, inverse, gain, grad_norm):
    scaled = grad_norm * gain
    mean = jnp.sum(scaled * values, axis=-1, keepdims=True) * (1.0 / D)
    return inverse * scaled - values * inverse**3 * mean


def round_up(value, step):
    return -(-value // step) * step


def rows_at(index, rows):
    return pl.ds(pl.multiple_of(index * rows, rows), rows)


def to_blocks(values, n, width):
    rows, own = values.shape[0], values.shape[1] // n
    gap = jnp.zeros((rows, width // n - own), values.dtype)
    parts = []
    for s in range(n):
        parts += [values[:, s * own : (s + 1) * own], gap]
    return jnp.concatenate(parts, axis=1)


def from_blocks(values, n, own):
    block = values.shape[1] // n
    return jnp.concatenate([values[:, s * block : s * block + own] for s in range(n)], axis=1)


def swap(block, axis, k):
    count = lax.axis_size(axis)
    return lax.ppermute(block, axis, [(i, i ^ k) for i in range(count)])


def exchange(block):
    return lax.all_to_all(block, "shard", split_axis=0, concat_axis=0, tiled=True)


def spread(block, axis, step):
    return [block] + [swap(block, axis, k) for k in range(step, lax.axis_size(axis), step)]


def with_cores(parts):
    return parts + [swap(part, "shard", 1) for part in parts]


def deliver(blocks, axis, step):
    return [blocks[0]] + [swap(block, axis, i * step) for i, block in enumerate(blocks) if i]


def call(kernel, name, outs, *operands, scalars=(), scratch=()):
    specs = [pl.BlockSpec(memory_space=pltpu.SMEM)] * len(scalars)
    specs += [pl.BlockSpec(memory_space=pltpu.VMEM)] * len(operands)
    return pl.pallas_call(
        kernel,
        out_shape=[jax.ShapeDtypeStruct(shape, dtype) for shape, dtype in outs],
        in_specs=specs,
        out_specs=[pl.BlockSpec(memory_space=pltpu.VMEM)] * len(outs),
        scratch_shapes=[pltpu.VMEM(shape, dtype) for shape, dtype in scratch],
        compiler_params=pltpu.CompilerParams(vmem_limit_bytes=VMEM_LIMIT),
        name=name,
    )(*scalars, *operands)


def turned(values):
    half = HD // 2
    parts = []
    for begin in range(0, values.shape[1], HD):
        parts.append(-values[:, begin + half : begin + HD])
        parts.append(values[:, begin : begin + half])
    return jnp.concatenate(parts, axis=1)


def head_of(values, h, heads):
    if heads == 1:
        return values
    lane = lax.broadcasted_iota(jnp.int32, values.shape, 1)
    return jnp.where(lane // HD == h, values, jnp.zeros_like(values))


def masked_probs(query, key, starts, row):
    rows, cols = query.shape[0], key.shape[0]
    logits = contract_cols(query, key) * SCALE
    place = lax.broadcasted_iota(jnp.int32, (rows, cols), 1)
    own = lax.broadcasted_iota(jnp.int32, (rows, cols), 0) + row
    logits = jnp.where((place <= own) & (place >= starts), logits, MASKED)
    raised = jnp.exp(logits - jnp.max(logits, axis=-1, keepdims=True))
    return raised * (1.0 / jnp.sum(raised, axis=-1, keepdims=True))


def blocks_kernel(n, in_ref, out_ref):
    values = in_ref[...].astype(F32)
    out_ref[...] = to_blocks(values, n, out_ref.shape[1]).astype(BF16)


def attention_message_kernel(n, rep_ref, q_ref, k_ref, v_ref, out_ref, gain_ref, qkv_msg_ref, out_msg_ref):
    own = q_ref.shape[0]
    piece, cols = qkv_msg_ref.shape[1:]
    head_cols = cols // 3
    heads = head_cols // HD
    row = lax.broadcasted_iota(jnp.int32, (piece, own), 0) + rep_ref[0] * piece
    pick = jnp.where(row == lax.broadcasted_iota(jnp.int32, (piece, own), 1), 1.0, 0.0).astype(BF16)
    query, key, value = (dot(pick, ref[...]) for ref in (q_ref, k_ref, v_ref))
    gap = jnp.zeros((piece, HD), F32)
    wide = lax.broadcasted_iota(jnp.int32, (piece, cols), 0) + rep_ref[0] * piece
    for s in range(n):
        slots = range(s * heads, (s + 1) * heads)
        parts = [query[:, h * HD : (h + 1) * HD] if h < QH else gap for h in slots]
        for array in (key, value):
            for h in slots:
                j = h // GROUP
                parts.append(array[:, j * HD : (j + 1) * HD] if h < QH else gap)
        block = jnp.concatenate(parts, axis=1)
        for i in range(2):
            block = jnp.where(wide == own + i, gain_ref[i : i + 1, :], block)
        qkv_msg_ref[s] = block.astype(BF16)
    rows = to_blocks(dot(pick, out_ref[...]), n, out_msg_ref.shape[2]).astype(BF16)
    for s in range(n):
        out_msg_ref[s] = rows


def join_kernel(reps, rep_ref, *refs):
    for i in range(reps):
        refs[reps][:, rep_ref[0] ^ i] = refs[i][...]


def hidden_message_kernel(n, reps, block, rep_ref, core_ref, gate_ref, up_ref, down_ref, *msg_refs):
    own, units = gate_ref.shape
    held = down_ref.shape[0]
    each = held // (2 * reps)
    cols = n * each
    padded = round_up(each, 16)
    place = lax.broadcasted_iota(jnp.int32, (1, cols), 1)
    for i, msg_ref in enumerate(msg_refs):
        begin = each * (2 * rep_ref[0] + (core_ref[0] ^ i))
        unit = place + begin
        for s in range(1, n):
            unit = unit + jnp.where(place >= each * s, held - each, 0)
        pick = jnp.where(lax.broadcasted_iota(jnp.int32, (units, cols), 0) == unit, 1.0, 0.0)
        pick = pick.astype(BF16)
        both = jnp.concatenate([dot(gate_ref[...], pick), dot(up_ref[...], pick)], axis=1)
        both = jnp.concatenate([both, jnp.zeros((block - own, 2 * cols), F32)], axis=0)
        msg_ref[pl.ds(0, block), :] = both.astype(BF16)
        row = lax.broadcasted_iota(jnp.int32, (padded, held), 0)
        take = (lax.broadcasted_iota(jnp.int32, (padded, held), 1) == row + begin) & (row < each)
        down = to_blocks(dot(jnp.where(take, 1.0, 0.0).astype(BF16), down_ref[...]), n, n * block)
        for j, part in enumerate(chunks(down, 2 * cols)):
            msg_ref[pl.ds(block + j * padded, padded), :] = part.astype(BF16)


def chunks(values, cols):
    rows, width = values.shape
    parts = []
    for begin in range(0, width, cols):
        part = values[:, begin : begin + cols]
        if part.shape[1] < cols:
            part = jnp.concatenate([part, jnp.zeros((rows, cols - part.shape[1]), F32)], axis=1)
        parts.append(part)
    return parts


def hidden_weights_in_kernel(n, each, me_ref, *refs):
    parts, (w_ref, down_ref, rows_ref) = refs[:n], refs[n:]
    block, cols = w_ref.shape[1:]
    width = down_ref.shape[1]
    padded = rows_ref.shape[1]
    for i, part in enumerate(parts):
        s = me_ref[0] ^ i
        w_ref[s] = part[pl.ds(0, block), :]
        for j, begin in enumerate(range(0, width, cols)):
            size = min(cols, width - begin)
            rows = part[pl.ds(block + j * padded, padded), :].astype(F32)
            rows_ref[s, :, begin : begin + size] = rows[:, :size]
    down_ref[...] = jnp.concatenate([rows_ref[s][:each] for s in range(n)], axis=0).astype(BF16)


def attend_kernel(rows, n, me_ref, *refs):
    tokens, refs = refs[:n], refs[n:]
    w_ref, cos_ref, sin_ref, start_ref, first_ref, q_ref, k_ref, v_ref, mixed_ref, gains_ref = refs
    length, head_cols = q_ref.shape
    heads = head_cols // HD
    width = first_ref.shape[1]
    block_rows = width // n
    own = D // n
    gap = jnp.zeros((1, block_rows - own), F32)
    gains = []
    for i in range(2):
        parts = []
        for s in range(n):
            group = w_ref[pl.ds(s * block_rows + own // 16 * 16, block_rows - own // 16 * 16), :]
            row = own % 16 + i
            spread_row = group.astype(F32)[row : row + 1, :own]
            parts += [spread_row, gap]
        gains.append(jnp.concatenate(parts, axis=1))
        gains_ref[i : i + 1, :] = gains[i]
    for i, ref in enumerate(tokens):
        inputs = ref[...].astype(F32)
        normed = inputs * inverse_rms(inputs) * gains[0]
        first_ref[rows_at(me_ref[0] ^ i, rows), :] = normed.astype(BF16)
    block = min(256, length)
    for i in range(length // block):
        span = pl.ds(i * block, block)
        raw = dot(first_ref[span, :], w_ref[...])
        cosines, sines = cos_ref[span, :], sin_ref[span, :]
        query, key = raw[:, :head_cols], raw[:, head_cols : 2 * head_cols]
        q_ref[span, :] = (query * cosines + turned(query) * sines).astype(BF16)
        k_ref[span, :] = (key * cosines + turned(key) * sines).astype(BF16)
        v_ref[span, :] = raw[:, 2 * head_cols :].astype(BF16)
    for i in range(length // block):
        span, past = pl.ds(i * block, block), pl.ds(0, (i + 1) * block)
        total = None
        for h in range(heads):
            probs = masked_probs(
                head_of(q_ref[span, :], h, heads), k_ref[past, :], start_ref[span, :], i * block
            )
            mixed = head_of(dot(probs.astype(BF16), v_ref[past, :]), h, heads)
            total = mixed if total is None else total + mixed
        mixed_ref[span, :] = total.astype(BF16)


def attend_back_kernel(
    first_ref, q_ref, k_ref, v_ref, g_ref, cos_ref, sin_ref, start_ref, dqkv_ref, piece_ref, dk_ref, dv_ref
):
    length, head_cols = q_ref.shape
    heads = head_cols // HD
    block = min(256, length)
    dk_ref[...] = jnp.zeros_like(dk_ref)
    dv_ref[...] = jnp.zeros_like(dv_ref)
    for i in range(length // block):
        span, past = pl.ds(i * block, block), pl.ds(0, (i + 1) * block)
        total = None
        for h in range(heads):
            query = head_of(q_ref[span, :], h, heads)
            grad = head_of(g_ref[span, :], h, heads)
            key = k_ref[past, :]
            probs = masked_probs(query, key, start_ref[span, :], i * block)
            grad_probs = contract_cols(grad, v_ref[past, :])
            delta = jnp.sum(probs * grad_probs, axis=-1, keepdims=True)
            grad_logits = (probs * (grad_probs - delta)).astype(BF16)
            grad_query = head_of(dot(grad_logits, key), h, heads)
            total = grad_query if total is None else total + grad_query
            dv_ref[past, :] += contract_rows(probs.astype(BF16), grad)
            dk_ref[past, :] += contract_rows(grad_logits, query)
        total = total * SCALE
        back = total * cos_ref[span, :] - turned(total) * sin_ref[span, :]
        dqkv_ref[span, :head_cols] = back.astype(BF16)
    for i in range(length // block):
        span = pl.ds(i * block, block)
        total = dk_ref[span, :] * SCALE
        back = total * cos_ref[span, :] - turned(total) * sin_ref[span, :]
        dqkv_ref[span, head_cols : 2 * head_cols] = back.astype(BF16)
        dqkv_ref[span, 2 * head_cols :] = dv_ref[span, :].astype(BF16)
    store_pieces(piece_ref, contract_rows(first_ref[...], dqkv_ref[...]))


def store_pieces(piece_ref, grad):
    reps, n, piece, cols = piece_ref.shape
    for s in range(n):
        for r in range(reps):
            begin = (s * reps + r) * piece
            piece_ref[r, s] = grad[begin : begin + piece].astype(BF16)


def first_grad_kernel(rows, side, me_ref, dqkv_ref, w_ref, out_ref):
    for z in range(out_ref.shape[0]):
        part = dqkv_ref[rows_at(me_ref[0] ^ (2 * z + side), rows), :]
        out_ref[z] = contract_cols(part, w_ref[...]).astype(BF16)


def pair_sum_kernel(mine_ref, other_ref, *out_refs):
    for i, ref in enumerate(out_refs):
        ref[...] = (mine_ref[i].astype(F32) + other_ref[i].astype(F32)).astype(BF16)


def middle_kernel(n, tokens_ref, mixed_ref, w_ref, gains_ref, middle_ref, second_ref, attended_ref):
    width = tokens_ref.shape[1]
    attended = jnp.concatenate([mixed_ref[s] for s in range(n)], axis=1)[:, :D]
    attended = to_blocks(attended.astype(F32), n, width).astype(BF16)
    attended_ref[...] = attended
    middle = tokens_ref[...].astype(F32) + dot(attended, w_ref[...])
    middle_ref[...] = middle
    second_ref[...] = (middle * inverse_rms(middle) * gains_ref[1:2, :]).astype(BF16)


def stacked(refs):
    return jnp.concatenate([ref[...] for ref in refs], axis=0)


def hidden_kernel(reps, *refs):
    seconds, cots = refs[:reps], refs[reps : 2 * reps]
    w_ref, down_ref, grad_ref, grads_ref, hidden_ref = refs[2 * reps :]
    rows = seconds[0].shape[0]
    units = down_ref.shape[0]
    for i in range(0, reps, 2):
        span = pl.ds(i * rows, 2 * rows)
        both = dot(stacked(seconds[i : i + 2]), w_ref[...])
        gate, up = both[:, :units], both[:, units:]
        grad_hidden = contract_cols(stacked(cots[i : i + 2]), down_ref[...])
        sigmoid = 1.0 / (1.0 + jnp.exp(-gate))
        silu = gate * sigmoid
        hidden_ref[span, :] = (silu * up).astype(BF16)
        grad_gate = grad_hidden * up * sigmoid * (1.0 + gate * (1.0 - sigmoid))
        grads = jnp.concatenate([grad_gate, grad_hidden * silu], axis=1).astype(BF16)
        grads_ref[span, :] = grads
        grad = contract_cols(grads, w_ref[...]).astype(BF16)
        for j in range(2):
            grad_ref[i + j] = grad[j * rows : (j + 1) * rows]


def hidden_weights_kernel(reps, n, each, me_ref, *refs):
    seconds, cots = refs[: 2 * reps], refs[2 * reps : 4 * reps]
    (grads_a, grads_b, hidden_a, hidden_b), refs = refs[4 * reps : 4 * reps + 4], refs[4 * reps + 4 :]
    msg_refs, (grad_ref, rows_ref) = refs[:n], refs[n:]
    block, cols = grad_ref.shape[1:]
    padded = rows_ref.shape[1]
    grad = contract_rows(stacked(seconds[:reps]), grads_a[...])
    grad = grad + contract_rows(stacked(seconds[reps:]), grads_b[...])
    down = contract_rows(hidden_a[...], stacked(cots[:reps]))
    down = down + contract_rows(hidden_b[...], stacked(cots[reps:]))
    gap = jnp.zeros((padded - each, down.shape[1]), F32)
    for s in range(n):
        grad_ref[s] = grad[s * block : (s + 1) * block].astype(BF16)
        rows_ref[s] = jnp.concatenate([down[s * each : (s + 1) * each], gap], axis=0)
    for i, msg_ref in enumerate(msg_refs):
        s = me_ref[0] ^ i
        msg_ref[pl.ds(0, block), :] = grad_ref[s]
        for j, part in enumerate(chunks(rows_ref[s], cols)):
            msg_ref[pl.ds(block + j * padded, padded), :] = part.astype(BF16)


def core_sums_kernel(n, *refs):
    for core in range(2):
        total = sum(refs[i][...].astype(F32) for i in range(core, n, 2))
        refs[n][core] = total.astype(BF16)


def hidden_out_kernel(n, reps, each, rep_ref, core_ref, *refs):
    parts, refs = refs[:reps], refs[reps:]
    gate_w_ref, up_w_ref, gain_ref, gate_ref, up_ref, down_ref, norm_ref, hold_ref = refs
    own = gate_ref.shape[0]
    for i, part in enumerate(parts):
        for core in range(2):
            hold_ref[2 * (rep_ref[0] ^ i) + (core_ref[0] ^ core)] = part[core]
    cols = hold_ref.shape[2]
    block = round_up(own + 2, 16)
    padded = round_up(each, 16)
    total = jnp.zeros((own, 1), F32)
    for begin, w_ref, out_ref in ((0, gate_w_ref, gate_ref), (cols // 2, up_w_ref, up_ref)):
        held = [hold_ref[f, pl.ds(0, block), :].astype(F32)[:own] for f in range(2 * reps)]
        for s in range(n):
            place = begin + s * each
            rows = jnp.concatenate([part[:, place : place + each] for part in held], axis=1)
            span = slice(s * 2 * reps * each, (s + 1) * 2 * reps * each)
            out_ref[:, span] = rows
            total = total + jnp.sum(rows * w_ref[:, span].astype(F32), axis=1, keepdims=True)
    norm_ref[...] = total / gain_ref[...]
    width = n * block
    for f in range(2 * reps):
        rows = []
        for j, start in enumerate(range(0, width, cols)):
            part = hold_ref[f, pl.ds(block + j * padded, padded), :].astype(F32)[:each]
            rows.append(part[:, : min(cols, width - start)])
        rows = from_blocks(jnp.concatenate(rows, axis=1), n, own)
        down_ref[f * each : (f + 1) * each, :] = rows


def down_kernel(hidden_ref, w_ref, out_ref):
    rows = out_ref.shape[1]
    for i in range(0, out_ref.shape[0], 2):
        both = dot(hidden_ref[pl.ds(i * rows, 2 * rows), :], w_ref[...]).astype(BF16)
        for j in range(2):
            out_ref[i + j] = both[j * rows : (j + 1) * rows]


def output_kernel(n, own, middle_ref, *refs):
    total = middle_ref[...]
    for ref in refs[:-1]:
        total = total + ref[...].astype(F32)
    refs[-1][...] = from_blocks(total, n, own).astype(BF16)


def middle_grad_kernel(n, own, reps, *refs):
    parts, refs = refs[:reps], refs[reps:]
    cot_ref, middle_ref, gains_ref, w_ref, grad_ref, branch_ref, heads_ref = refs
    rows = cot_ref.shape[0]
    middle = middle_ref[...]
    grad_second = sum(ref[...].astype(F32) for ref in parts)
    grad = cot_ref[...].astype(F32) + norm_backward(
        middle, inverse_rms(middle), gains_ref[1:2, :], grad_second
    )
    grad_ref[...] = grad
    branch = grad.astype(BF16)
    branch_ref[...] = branch
    attended = from_blocks(contract_cols(branch, w_ref[...]), n, own)
    head_cols = heads_ref.shape[2]
    if n * head_cols > D:
        attended = jnp.concatenate([attended, jnp.zeros((rows, n * head_cols - D), F32)], axis=1)
    for s in range(n):
        heads_ref[s] = attended[:, s * head_cols : (s + 1) * head_cols].astype(BF16)


def out_weights_kernel(attended_ref, branch_ref, piece_ref):
    store_pieces(piece_ref, contract_rows(attended_ref[...], branch_ref[...]))


def rep_sum_kernel(reps, *refs):
    total = sum(ref[...].astype(F32) for ref in refs[:reps])
    refs[reps][...] = total.astype(BF16)


def owner_sum_kernel(in_ref, out_ref):
    out_ref[...] = jnp.sum(in_ref[...].astype(F32), axis=0).astype(BF16)


def out_out_kernel(n, reps, rep_ref, *refs):
    out_ref, hold_ref = refs[reps:]
    for i in range(reps):
        hold_ref[rep_ref[0] ^ i] = refs[i][...].astype(F32)
    own = out_ref.shape[0]
    rows = jnp.concatenate([hold_ref[r] for r in range(reps)], axis=0)[:own]
    out_ref[...] = from_blocks(rows, n, own)


def attention_out_kernel(n, reps, rep_ref, *refs):
    parts, refs = refs[:reps], refs[reps:]
    q_w_ref, k_w_ref, v_w_ref, gain_ref, q_ref, k_ref, v_ref, norm_ref, hold_ref = refs
    own = q_ref.shape[0]
    cols = parts[0].shape[2]
    head_cols = cols // 3
    heads = head_cols // HD
    for i, part in enumerate(parts):
        for s in range(n):
            hold_ref[rep_ref[0] ^ i, s] = part[s].astype(F32)
    sides = [
        jnp.concatenate([hold_ref[r, s] for r in range(reps)], axis=0)[:own] for s in range(n)
    ]

    def slot(h, kind):
        begin = kind * head_cols + h % heads * HD
        return sides[h // heads][:, begin : begin + HD]

    query = jnp.concatenate([slot(h, 0) for h in range(QH)], axis=1)
    q_ref[...] = query
    total = jnp.sum(query * q_w_ref[...].astype(F32), axis=1, keepdims=True)
    for kind, w_ref, out_ref in ((1, k_w_ref, k_ref), (2, v_w_ref, v_ref)):
        wide = jnp.concatenate(
            [sum(slot(j * GROUP + g, kind) for g in range(GROUP)) for j in range(KVH)], axis=1
        )
        out_ref[...] = wide
        total = total + jnp.sum(wide * w_ref[...].astype(F32), axis=1, keepdims=True)
    norm_ref[...] = total / gain_ref[...]


def input_grad_kernel(n, own, nz, *refs):
    parts, (tokens_ref, gains_ref, grad_ref, out_ref) = refs[:nz], refs[nz:]
    inputs = tokens_ref[...].astype(F32)
    grad_first = sum(ref[...].astype(F32) for ref in parts)
    total = grad_ref[...] + norm_backward(inputs, inverse_rms(inputs), gains_ref[0:1, :], grad_first)
    out_ref[...] = from_blocks(total, n, own)


def shards(
    tokens,
    lengths,
    norm_one,
    w_query,
    w_key,
    w_value,
    w_out,
    norm_two,
    w_gate,
    w_up,
    w_down,
    cotangent,
):
    n = lax.axis_size("shard")
    reps = lax.axis_size("rep")
    nz = n // 2
    rows = tokens.shape[0]
    length = rows * n
    own = w_query.shape[0]
    held = w_down.shape[0]
    block = round_up(own + 2, 16)
    width = n * block
    piece = block // reps
    heads = -(-QH // n)
    head_cols = heads * HD
    qkv_cols = 3 * head_cols
    each = held // (2 * reps)
    units = n * each
    padded = round_up(each, 16)
    msg_rows = block + -(-width // (2 * units)) * padded
    shard_index = lax.axis_index("shard").astype(jnp.int32)
    me = shard_index.reshape(1)
    core = (shard_index % 2).reshape(1)
    rep = lax.axis_index("rep").astype(jnp.int32).reshape(1)
    own_block = (rows, width)

    (tokens_in,) = call(lambda *r: blocks_kernel(n, *r), "tokens_blocks", [(own_block, BF16)], tokens)
    tokens_all = spread(tokens_in, "shard", 2)
    tokens_all = [part for pair in zip(tokens_all, [swap(p, "shard", 1) for p in tokens_all]) for part in pair]
    gains_own = jnp.pad(jnp.stack([norm_one, norm_two]), ((0, 0), (0, qkv_cols - own))).astype(F32)
    qkv_message, out_message = call(
        lambda *r: attention_message_kernel(n, *r),
        "attention_message",
        [((n, piece, qkv_cols), BF16), ((n, piece, width), BF16)],
        w_query,
        w_key,
        w_value,
        w_out,
        gains_own,
        scalars=(rep,),
    )

    def joined(arrived, name):
        cols = arrived.shape[2]
        parts = spread(arrived, "rep", 1)
        (whole,) = call(
            lambda *r: join_kernel(reps, *r), name, [((n, reps, piece, cols), BF16)], *parts, scalars=(rep,)
        )
        return whole.reshape(width, cols)

    w_qkv = joined(exchange(qkv_message), "join_qkv")

    (cot_in,) = call(lambda *r: blocks_kernel(n, *r), "cot_blocks", [(own_block, BF16)], cotangent)
    cots = with_cores(spread(cot_in, "rep", 1))
    messages = call(
        lambda *r: hidden_message_kernel(n, reps, block, *r),
        "hidden_message",
        [((msg_rows, 2 * units), BF16)] * 2,
        w_gate,
        w_up,
        w_down,
        scalars=(rep, core),
    )
    out_message, messages, tokens_all = lax.optimization_barrier((out_message, messages, tokens_all))
    out_full = joined(exchange(out_message), "join_out")
    arrived = [messages[0]] + [swap(messages[k % 2], "shard", k) for k in range(1, n)]
    w_hidden, w_down_in = call(
        lambda *r: hidden_weights_in_kernel(n, each, *r),
        "hidden_weights_in",
        [((n, block, 2 * units), BF16), ((units, width), BF16)],
        *arrived,
        scalars=(me,),
        scratch=[((n, padded, width), F32)],
    )
    w_hidden = w_hidden.reshape(width, 2 * units)

    doc_start, position = doc_layout(lengths[0], length)
    cosines, sines = rope_tables(position)
    cosines = jnp.tile(cosines, (1, 2 * heads))
    sines = jnp.tile(sines, (1, 2 * heads))
    start = doc_start[:, None]
    head_shape = (length, head_cols)
    first_all, query, key, value, mixed, gains = call(
        lambda *r: attend_kernel(rows, n, *r),
        "attend",
        [((length, width), BF16)] + [(head_shape, BF16)] * 4 + [((2, width), F32)],
        *tokens_all,
        w_qkv,
        cosines,
        sines,
        start,
        scalars=(me,),
    )
    mixed = exchange(mixed.reshape(n, rows, head_cols))

    middle, second, attended = call(
        lambda *r: middle_kernel(n, *r),
        "middle",
        [(own_block, F32), (own_block, BF16), (own_block, BF16)],
        tokens_in,
        mixed,
        out_full,
        gains,
    )

    seconds = with_cores(spread(second, "rep", 1))
    side_outs = [
        ((reps, rows, width), BF16),
        ((reps * rows, 2 * units), BF16),
        ((reps * rows, units), BF16),
    ]

    def hidden_side(side, name):
        span = slice(side * reps, (side + 1) * reps)
        return call(
            lambda *r: hidden_kernel(reps, *r),
            name,
            side_outs,
            *seconds[span],
            *cots[span],
            w_hidden,
            w_down_in,
        )

    def plane_sums(mine, other):
        sums = call(pair_sum_kernel, "pair_sum", [(own_block, BF16)] * reps, mine, swap(other, "shard", 1))
        return deliver(sums, "rep", 1)

    grad_other, grads_other, hidden_other = hidden_side(1, "hidden_other")
    grad_mine, grads_mine, hidden_mine = hidden_side(0, "hidden_mine")
    grad_second = plane_sums(grad_mine, grad_other)
    hidden_messages = call(
        lambda *r: hidden_weights_kernel(reps, n, each, *r),
        "hidden_weights",
        [((msg_rows, 2 * units), BF16)] * n,
        *seconds,
        *cots,
        grads_mine,
        grads_other,
        hidden_mine,
        hidden_other,
        scalars=(me,),
        scratch=[((n, block, 2 * units), BF16), ((n, padded, width), F32)],
    )
    hidden_messages = deliver(hidden_messages, "shard", 1)

    grad_middle, grad_branch, grad_heads = call(
        lambda *r: middle_grad_kernel(n, own, reps, *r),
        "middle_grad",
        [(own_block, F32), (own_block, BF16), ((n, rows, head_cols), BF16)],
        *grad_second,
        cot_in,
        middle,
        gains,
        out_full,
    )
    grad_heads = exchange(grad_heads).reshape(head_shape)
    (out_pieces,) = call(
        out_weights_kernel, "out_weights", [((reps, n, piece, width), BF16)], attended, grad_branch
    )

    grad_qkv, attention_pieces = call(
        attend_back_kernel,
        "attend_back",
        [((length, qkv_cols), BF16), ((reps, n, piece, qkv_cols), BF16)],
        first_all,
        query,
        key,
        value,
        grad_heads,
        cosines,
        sines,
        start,
        scratch=[(head_shape, F32)] * 2,
    )
    first_sides = [
        call(
            lambda *r, side=side: first_grad_kernel(rows, side, *r),
            "first_grad",
            [((nz, rows, width), BF16)],
            grad_qkv,
            w_qkv,
            scalars=(me,),
        )[0]
        for side in (1, 0)
    ]
    first_sums = call(
        pair_sum_kernel, "pair_sum", [(own_block, BF16)] * nz, first_sides[1], swap(first_sides[0], "shard", 1)
    )
    (input_grad,) = call(
        lambda *r: input_grad_kernel(n, own, nz, *r),
        "input_grad",
        [((rows, D), F32)],
        *deliver(first_sums, "shard", 2),
        tokens_in,
        gains,
        grad_middle,
    )

    def owner_pieces(pieces):
        blocks = [lax.dynamic_index_in_dim(pieces, rep[0] ^ k, 0, keepdims=False) for k in range(reps)]
        parts = deliver(blocks, "rep", 1)
        (summed,) = call(
            lambda *r: rep_sum_kernel(reps, *r), "rep_sum", [(pieces.shape[1:], BF16)], *parts
        )
        return exchange(summed)

    gain_cols = [gain.astype(F32)[:, None] for gain in (norm_one, norm_two)]
    attention_parts = spread(owner_pieces(attention_pieces), "rep", 1)
    grad_w_query, grad_w_key, grad_w_value, grad_norm_one = call(
        lambda *r: attention_out_kernel(n, reps, *r),
        "attention_out",
        [(w_query.shape, F32), (w_key.shape, F32), (w_value.shape, F32), ((own, 1), F32)],
        *attention_parts,
        w_query,
        w_key,
        w_value,
        gain_cols[0],
        scalars=(rep,),
        scratch=[((reps, n, piece, qkv_cols), F32)],
    )

    (out_piece,) = call(owner_sum_kernel, "owner_sum", [((piece, width), BF16)], owner_pieces(out_pieces))
    (grad_w_out,) = call(
        lambda *r: out_out_kernel(n, reps, *r),
        "out_out",
        [(w_out.shape, F32)],
        *spread(out_piece, "rep", 1),
        scalars=(rep,),
        scratch=[((reps, piece, width), F32)],
    )

    (core_sums,) = call(
        lambda *r: core_sums_kernel(n, *r), "core_sums", [((2, msg_rows, 2 * units), BF16)], *hidden_messages
    )
    grad_w_gate, grad_w_up, grad_w_down, grad_norm_two = call(
        lambda *r: hidden_out_kernel(n, reps, each, *r),
        "hidden_out",
        [(w_gate.shape, F32), (w_up.shape, F32), (w_down.shape, F32), ((own, 1), F32)],
        *spread(core_sums, "rep", 1),
        w_gate,
        w_up,
        gain_cols[1],
        scalars=(rep, core),
        scratch=[((2 * reps, msg_rows, 2 * units), BF16)],
    )

    down_parts = [
        call(down_kernel, "down", [((reps, rows, width), BF16)], hidden, w_down_in)[0]
        for hidden in (hidden_other, hidden_mine)
    ]
    (output,) = call(
        lambda *r: output_kernel(n, own, *r),
        "output",
        [((rows, D), BF16)],
        middle,
        *plane_sums(down_parts[1], down_parts[0]),
    )
    return (
        output,
        input_grad,
        grad_norm_one[:, 0],
        grad_w_query,
        grad_w_key,
        grad_w_value,
        grad_w_out,
        grad_norm_two[:, 0],
        grad_w_gate,
        grad_w_up,
        grad_w_down,
    )


def solution(mesh):
    rows = P("shard", None)
    own_tokens = P(("rep", "shard"), None)
    return jax.shard_map(
        shards,
        mesh=mesh,
        in_specs=(
            own_tokens,
            P("rep", None),
            P("shard"),
            rows,
            rows,
            rows,
            rows,
            P("shard"),
            rows,
            rows,
            rows,
            own_tokens,
        ),
        out_specs=(
            own_tokens,
            own_tokens,
            P("shard"),
            rows,
            rows,
            rows,
            rows,
            P("shard"),
            rows,
            rows,
            rows,
        ),
        check_vma=False,
    )
```

```python
import jax
import jax.numpy as jnp
from jax import lax
from jax.experimental import pallas as pl
from jax.experimental.pallas import tpu as pltpu
from jax.sharding import PartitionSpec as P

D = 960
QH = 15
KVH = 5
HD = 64
FF = 2560
GROUP = QH // KVH

EPS = 1e-05
ROPE_BASE = 10000.0
MASKED = -1e30
SCALE = HD ** (-0.5)
BF16 = jnp.bfloat16
F32 = jnp.float32


def doc_layout(lengths_row, length):
    places = jnp.arange(length, dtype=jnp.int32)
    doc_ends = jnp.cumsum(lengths_row)
    passed = places[:, None] >= doc_ends[None, :]
    doc_start = jnp.sum(jnp.where(passed, lengths_row[None, :], 0), axis=1)
    return (doc_start, places - doc_start)


def rope_tables(position):
    half_dim = HD // 2
    fraction = jnp.arange(half_dim, dtype=F32) * (2.0 / HD)
    inverse = ROPE_BASE ** (-fraction)
    angles = position.astype(F32)[:, None] * inverse[None, :]
    return (jnp.cos(angles), jnp.sin(angles))


VMEM_LIMIT = 56 * 2**20


def dot(left, right):
    return jnp.dot(left, right, preferred_element_type=F32)


def contract_rows(left, right):
    return lax.dot_general(left, right, (((0,), (0,)), ((), ())), preferred_element_type=F32)


def contract_cols(left, right):
    return lax.dot_general(left, right, (((1,), (1,)), ((), ())), preferred_element_type=F32)


def inverse_rms(values):
    return lax.rsqrt(jnp.sum(values * values, axis=-1, keepdims=True) * (1.0 / D) + EPS)


def norm_backward(values, inverse, gain, grad_norm):
    scaled = grad_norm * gain
    mean = jnp.sum(scaled * values, axis=-1, keepdims=True) * (1.0 / D)
    return inverse * scaled - values * inverse**3 * mean


def round_up(value, step):
    return -(-value // step) * step


def rows_at(index, rows):
    return pl.ds(pl.multiple_of(index * rows, rows), rows)


def to_blocks(values, n, width):
    rows, own = values.shape[0], values.shape[1] // n
    gap = jnp.zeros((rows, width // n - own), values.dtype)
    parts = []
    for s in range(n):
        parts += [values[:, s * own : (s + 1) * own], gap]
    return jnp.concatenate(parts, axis=1)


def from_blocks(values, n, own):
    block = values.shape[1] // n
    return jnp.concatenate([values[:, s * block : s * block + own] for s in range(n)], axis=1)


def swap(block, axis, k):
    count = lax.axis_size(axis)
    return lax.ppermute(block, axis, [(i, i ^ k) for i in range(count)])


def exchange(block):
    return lax.all_to_all(block, "shard", split_axis=0, concat_axis=0, tiled=True)


def spread(block, axis, step):
    return [block] + [swap(block, axis, k) for k in range(step, lax.axis_size(axis), step)]


def deliver(blocks, axis, step):
    return [blocks[0]] + [swap(block, axis, i * step) for i, block in enumerate(blocks) if i]


def exchange_z(blocks):
    groups = [list(range(core, lax.axis_size("shard"), 2)) for core in range(2)]
    return lax.all_to_all(
        blocks, "shard", split_axis=0, concat_axis=0, axis_index_groups=groups, tiled=True
    )


def deliver_pairs(pairs):
    parts = deliver(pairs, "shard", 2)
    return [part[0] for part in parts], swap(jnp.stack([part[1] for part in parts]), "shard", 1)


def both_cores(parts):
    stacked = jnp.stack(parts)
    return stacked, swap(stacked, "shard", 1)


def call(kernel, name, outs, *operands, scalars=(), scratch=()):
    specs = [pl.BlockSpec(memory_space=pltpu.SMEM)] * len(scalars)
    specs += [pl.BlockSpec(memory_space=pltpu.VMEM)] * len(operands)
    return pl.pallas_call(
        kernel,
        out_shape=[jax.ShapeDtypeStruct(shape, dtype) for shape, dtype in outs],
        in_specs=specs,
        out_specs=[pl.BlockSpec(memory_space=pltpu.VMEM)] * len(outs),
        scratch_shapes=[pltpu.VMEM(shape, dtype) for shape, dtype in scratch],
        compiler_params=pltpu.CompilerParams(vmem_limit_bytes=VMEM_LIMIT),
        name=name,
    )(*scalars, *operands)


def turned(values):
    half = HD // 2
    parts = []
    for begin in range(0, values.shape[1], HD):
        parts.append(-values[:, begin + half : begin + HD])
        parts.append(values[:, begin : begin + half])
    return jnp.concatenate(parts, axis=1)


def head_of(values, h, heads):
    if heads == 1:
        return values
    lane = lax.broadcasted_iota(jnp.int32, values.shape, 1)
    return jnp.where(lane // HD == h, values, jnp.zeros_like(values))


def masked_probs(query, key, starts, row):
    rows, cols = query.shape[0], key.shape[0]
    logits = contract_cols(query, key) * SCALE
    place = lax.broadcasted_iota(jnp.int32, (rows, cols), 1)
    own = lax.broadcasted_iota(jnp.int32, (rows, cols), 0) + row
    logits = jnp.where((place <= own) & (place >= starts), logits, MASKED)
    raised = jnp.exp(logits - jnp.max(logits, axis=-1, keepdims=True))
    return raised * (1.0 / jnp.sum(raised, axis=-1, keepdims=True))


def blocks_kernel(n, in_ref, out_ref):
    values = to_blocks(in_ref[...].astype(F32), n, out_ref.shape[2]).astype(BF16)
    for i in range(out_ref.shape[0]):
        out_ref[i] = values


def attention_message_kernel(n, rep_ref, me_ref, q_ref, k_ref, v_ref, out_ref, gain_ref, *refs):
    msg_refs, (out_msg_ref, hold_ref) = refs[: n // 2], refs[n // 2 :]
    own = q_ref.shape[0]
    piece, cols = hold_ref.shape[1:]
    head_cols = cols // 3
    heads = head_cols // HD
    row = lax.broadcasted_iota(jnp.int32, (piece, own), 0) + rep_ref[0] * piece
    pick = jnp.where(row == lax.broadcasted_iota(jnp.int32, (piece, own), 1), 1.0, 0.0).astype(BF16)
    query, key, value = (dot(pick, ref[...]) for ref in (q_ref, k_ref, v_ref))
    gap = jnp.zeros((piece, HD), F32)
    wide = lax.broadcasted_iota(jnp.int32, (piece, cols), 0) + rep_ref[0] * piece
    for s in range(n):
        slots = range(s * heads, (s + 1) * heads)
        parts = [query[:, h * HD : (h + 1) * HD] if h < QH else gap for h in slots]
        for array in (key, value):
            for h in slots:
                j = h // GROUP
                parts.append(array[:, j * HD : (j + 1) * HD] if h < QH else gap)
        block = jnp.concatenate(parts, axis=1)
        for i in range(2):
            block = jnp.where(wide == own + i, gain_ref[i : i + 1, :], block)
        hold_ref[s] = block.astype(BF16)
    for i in range(n):
        msg_refs[i // 2][i % 2] = hold_ref[me_ref[0] ^ i]
    out_msg_ref[...] = to_blocks(dot(pick, out_ref[...]), n, out_msg_ref.shape[1]).astype(BF16)


def join_kernel(n, reps, rep_ref, me_ref, *refs):
    for i in range(reps):
        for s in range(n):
            refs[reps][me_ref[0] ^ s, rep_ref[0] ^ i] = refs[i][s]


def join_out_kernel(nz, reps, rep_ref, me_ref, mine_ref, other_ref, out_ref):
    for core, ref in enumerate((mine_ref, other_ref)):
        for i in range(reps):
            for z in range(nz):
                out_ref[me_ref[0] ^ (2 * z + core), rep_ref[0] ^ i] = ref[i, z]


def fill_rows(values, rows):
    if values.shape[0] == rows:
        return values
    return jnp.concatenate([values, jnp.zeros((rows - values.shape[0], values.shape[1]), F32)], axis=0)


def fill_cols(values, cols):
    if values.shape[1] == cols:
        return values
    return jnp.concatenate([values, jnp.zeros((values.shape[0], cols - values.shape[1]), F32)], axis=1)


def message_plan(own, each, cols):
    top, rows = round_up(own, 8), round_up(each, 8)
    rest = D % cols
    halved = rest and 2 * rest <= cols
    first = round_up(rows // 2, 8) if halved else rows
    total = top + D // cols * rows + (first if rest else 0)
    return top, rows, rest, halved, first, total


def pack_message(both, down, cols):
    top, rows, rest, halved, first, _ = message_plan(both.shape[0], down.shape[0], cols)
    down = fill_rows(down, rows)
    parts = [fill_rows(both, top)]
    parts += [down[:, j * cols : (j + 1) * cols] for j in range(D // cols)]
    if rest:
        tail = down[:, D - rest :]
        if halved:
            tail = jnp.concatenate([tail[:first], fill_rows(tail[first:], first)], axis=1)
        parts.append(fill_cols(tail, cols))
    return jnp.concatenate(parts, axis=0)


def unpack_message(message, own, each):
    cols = message.shape[1]
    top, rows, rest, halved, first, _ = message_plan(own, each, cols)
    parts = [message[top + j * rows : top + (j + 1) * rows] for j in range(D // cols)]
    if rest:
        tail = message[top + D // cols * rows :][:first]
        if halved:
            tail = jnp.concatenate([tail[:, :rest], tail[: rows - first, rest : 2 * rest]], axis=0)
        parts.append(tail[:, :rest])
    return message[:own], jnp.concatenate(parts, axis=1)[:each]


def hidden_message_kernel(n, reps, rep_ref, core_ref, gate_ref, up_ref, down_ref, out_ref):
    own, units = gate_ref.shape
    held = down_ref.shape[0]
    each = held // (2 * reps)
    cols = n * each
    place = lax.broadcasted_iota(jnp.int32, (1, cols), 1)
    row = lax.broadcasted_iota(jnp.int32, (round_up(each, 8), held), 0)
    for i in range(2):
        begin = each * (2 * rep_ref[0] + (core_ref[0] ^ i))
        unit = place + begin
        for s in range(1, n):
            unit = unit + jnp.where(place >= each * s, held - each, 0)
        pick = jnp.where(lax.broadcasted_iota(jnp.int32, (units, cols), 0) == unit, 1.0, 0.0)
        pick = pick.astype(BF16)
        both = jnp.concatenate([dot(gate_ref[...], pick), dot(up_ref[...], pick)], axis=1)
        take = (lax.broadcasted_iota(jnp.int32, row.shape, 1) == row + begin) & (row < each)
        down = dot(jnp.where(take, 1.0, 0.0).astype(BF16), down_ref[...])
        message = pack_message(both, down[:each], 2 * cols).astype(BF16)
        for z in range(out_ref.shape[0]):
            out_ref[z, i] = message


def hidden_weights_in_kernel(n, own, each, core_ref, mine_ref, other_ref, w_ref, down_ref, rows_ref):
    block = w_ref.shape[1]
    for side in range(2):
        for z in range(n // 2):
            s = 2 * z + (core_ref[0] ^ side)
            message = other_ref[z] if side else mine_ref[z, 0]
            both, down = unpack_message(message.astype(F32), own, each)
            w_ref[s] = fill_rows(both, block).astype(BF16)
            rows_ref[s, :each, :] = down
    down = jnp.concatenate([rows_ref[s, :each, :] for s in range(n)], axis=0)
    down_ref[...] = to_blocks(down, n, down_ref.shape[1]).astype(BF16)


def attend_kernel(rows, n, me_ref, mine_ref, other_ref, *refs):
    w_ref, cos_ref, sin_ref, start_ref, first_ref, q_ref, k_ref, v_ref, gains_ref = refs[:9]
    pair_refs, mixed_ref = refs[9:-1], refs[-1]
    core = me_ref[0] % 2
    length, head_cols = q_ref.shape
    heads = head_cols // HD
    width = first_ref.shape[1]
    block_rows = width // n
    own = D // n
    gap = jnp.zeros((1, block_rows - own), F32)
    gains = []
    for i in range(2):
        parts = []
        for s in range(n):
            group = w_ref[pl.ds(s * block_rows + own // 16 * 16, block_rows - own // 16 * 16), :]
            row = own % 16 + i
            spread_row = group.astype(F32)[row : row + 1, :own]
            parts += [spread_row, gap]
        gains.append(jnp.concatenate(parts, axis=1))
        gains_ref[i : i + 1, :] = gains[i]
    for side, ref in enumerate((mine_ref, other_ref)):
        for z in range(n // 2):
            inputs = ref[z].astype(F32)
            normed = inputs * inverse_rms(inputs) * gains[0]
            first_ref[rows_at(2 * z + (core ^ side), rows), :] = normed.astype(BF16)
    block = min(256, length)
    for i in range(length // block):
        span = pl.ds(i * block, block)
        raw = dot(first_ref[span, :], w_ref[...])
        cosines, sines = cos_ref[span, :], sin_ref[span, :]
        query, key = raw[:, :head_cols], raw[:, head_cols : 2 * head_cols]
        q_ref[span, :] = (query * cosines + turned(query) * sines).astype(BF16)
        k_ref[span, :] = (key * cosines + turned(key) * sines).astype(BF16)
        v_ref[span, :] = raw[:, 2 * head_cols :].astype(BF16)
    for i in range(length // block):
        span, past = pl.ds(i * block, block), pl.ds(0, (i + 1) * block)
        total = None
        for h in range(heads):
            probs = masked_probs(
                head_of(q_ref[span, :], h, heads), k_ref[past, :], start_ref[span, :], i * block
            )
            mixed = head_of(dot(probs.astype(BF16), v_ref[past, :]), h, heads)
            total = mixed if total is None else total + mixed
        mixed_ref[span, :] = total.astype(BF16)
    for i in range(n):
        pair_refs[i // 2][i % 2] = mixed_ref[rows_at(me_ref[0] ^ i, rows), :]


def attend_back_kernel(nz, reps, rep_ref, me_ref, *refs):
    mines, refs = refs[:nz], refs[nz:]
    other_ref, first_ref, q_ref, k_ref, v_ref, cos_ref, sin_ref, start_ref, dqkv_ref = refs[:9]
    piece_refs, (g_ref, dk_ref, dv_ref, hold_ref) = refs[9 : 9 + reps], refs[9 + reps :]
    rows = other_ref.shape[1]
    for z in range(nz):
        g_ref[rows_at(me_ref[0] ^ (2 * z), rows), :] = mines[z][...]
        g_ref[rows_at(me_ref[0] ^ (2 * z + 1), rows), :] = other_ref[z]
    length, head_cols = q_ref.shape
    heads = head_cols // HD
    block = min(256, length)
    dk_ref[...] = jnp.zeros_like(dk_ref)
    dv_ref[...] = jnp.zeros_like(dv_ref)
    for i in range(length // block):
        span, past = pl.ds(i * block, block), pl.ds(0, (i + 1) * block)
        total = None
        for h in range(heads):
            query = head_of(q_ref[span, :], h, heads)
            grad = head_of(g_ref[span, :], h, heads)
            key = k_ref[past, :]
            probs = masked_probs(query, key, start_ref[span, :], i * block)
            grad_probs = contract_cols(grad, v_ref[past, :])
            delta = jnp.sum(probs * grad_probs, axis=-1, keepdims=True)
            grad_logits = (probs * (grad_probs - delta)).astype(BF16)
            grad_query = head_of(dot(grad_logits, key), h, heads)
            total = grad_query if total is None else total + grad_query
            dv_ref[past, :] += contract_rows(probs.astype(BF16), grad)
            dk_ref[past, :] += contract_rows(grad_logits, query)
        total = total * SCALE
        back = total * cos_ref[span, :] - turned(total) * sin_ref[span, :]
        dqkv_ref[span, :head_cols] = back.astype(BF16)
    for i in range(length // block):
        span = pl.ds(i * block, block)
        total = dk_ref[span, :] * SCALE
        back = total * cos_ref[span, :] - turned(total) * sin_ref[span, :]
        dqkv_ref[span, head_cols : 2 * head_cols] = back.astype(BF16)
        dqkv_ref[span, 2 * head_cols :] = dv_ref[span, :].astype(BF16)
    store_pieces(rep_ref, piece_refs, hold_ref, contract_rows(first_ref[...], dqkv_ref[...]))


def store_pieces(rep_ref, piece_refs, hold_ref, grad):
    n, reps, piece, _ = hold_ref.shape
    for s in range(n):
        for r in range(reps):
            begin = (s * reps + r) * piece
            hold_ref[s, r] = grad[begin : begin + piece].astype(BF16)
    for i, ref in enumerate(piece_refs):
        for s in range(n):
            ref[s] = hold_ref[s, rep_ref[0] ^ i]


def first_grad_kernel(rows, side, me_ref, dqkv_ref, w_ref, out_ref):
    for z in range(out_ref.shape[0]):
        part = dqkv_ref[rows_at(me_ref[0] ^ (2 * z + side), rows), :]
        out_ref[z] = contract_cols(part, w_ref[...]).astype(BF16)


def pair_sum_kernel(mine_ref, other_ref, *out_refs):
    for i, ref in enumerate(out_refs):
        ref[...] = (mine_ref[i].astype(F32) + other_ref[i].astype(F32)).astype(BF16)


def middle_kernel(n, me_ref, tokens_ref, *refs):
    mines, refs = refs[: n // 2], refs[n // 2 :]
    other_ref, w_ref, gains_ref, middle_ref, second_ref, attended_ref, hold_ref = refs
    width = tokens_ref.shape[2]
    for z in range(n // 2):
        hold_ref[me_ref[0] ^ (2 * z)] = mines[z][...]
        hold_ref[me_ref[0] ^ (2 * z + 1)] = other_ref[z]
    attended = jnp.concatenate([hold_ref[s] for s in range(n)], axis=1)[:, :D]
    attended = to_blocks(attended.astype(F32), n, width).astype(BF16)
    attended_ref[...] = attended
    middle = tokens_ref[0].astype(F32) + dot(attended, w_ref[...])
    middle_ref[...] = middle
    second_ref[...] = (middle * inverse_rms(middle) * gains_ref[1:2, :]).astype(BF16)


def stacked(ref, begin=0, count=None):
    count = ref.shape[0] if count is None else count
    return jnp.concatenate([ref[begin + i] for i in range(count)], axis=0)


def hidden_kernel(second_ref, cot_ref, w_ref, down_ref, grad_ref, grads_ref, hidden_ref):
    reps, rows, _ = second_ref.shape
    units = down_ref.shape[0]
    for i in range(0, reps, 2):
        span = pl.ds(i * rows, 2 * rows)
        both = dot(stacked(second_ref, i, 2), w_ref[...])
        gate, up = both[:, :units], both[:, units:]
        grad_hidden = contract_cols(stacked(cot_ref, i, 2), down_ref[...])
        sigmoid = 1.0 / (1.0 + jnp.exp(-gate))
        silu = gate * sigmoid
        hidden_ref[span, :] = (silu * up).astype(BF16)
        grad_gate = grad_hidden * up * sigmoid * (1.0 + gate * (1.0 - sigmoid))
        grads = jnp.concatenate([grad_gate, grad_hidden * silu], axis=1).astype(BF16)
        grads_ref[span, :] = grads
        grad = contract_cols(grads, w_ref[...]).astype(BF16)
        for j in range(2):
            grad_ref[i + j] = grad[j * rows : (j + 1) * rows]


def hidden_weights_kernel(n, own, each, core_ref, *refs):
    second_a, second_b, cot_a, cot_b, grads_a, grads_b, hidden_a, hidden_b, msg_ref, hold_ref = refs
    cols = hold_ref.shape[2]
    grad = contract_rows(stacked(second_a), grads_a[...])
    grad = grad + contract_rows(stacked(second_b), grads_b[...])
    down = contract_rows(hidden_a[...], stacked(cot_a)) + contract_rows(hidden_b[...], stacked(cot_b))
    down = from_blocks(down, n, own)
    block = grad.shape[0] // n
    for s in range(n):
        both = grad[s * block : s * block + own]
        hold_ref[s] = pack_message(both, down[s * each : (s + 1) * each], cols).astype(BF16)
    for z in range(n // 2):
        for i in range(2):
            msg_ref[z, i] = hold_ref[2 * z + (core_ref[0] ^ i)]


def core_sums_kernel(in_ref, mine_ref, other_ref):
    for core, ref in enumerate((mine_ref, other_ref)):
        ref[...] = sum(in_ref[z, core].astype(F32) for z in range(in_ref.shape[0])).astype(BF16)


def hidden_out_kernel(n, reps, each, rep_ref, core_ref, *refs):
    parts, refs = refs[:reps], refs[reps:]
    gate_w_ref, up_w_ref, gain_ref, gate_ref, up_ref, down_ref, norm_ref, hold_ref = refs
    own = gate_ref.shape[0]
    units = 2 * reps * each
    for i, part in enumerate(parts):
        for core in range(2):
            hold_ref[2 * (rep_ref[0] ^ i) + (core_ref[0] ^ core)] = part[core]
    cols = hold_ref.shape[2]
    boths = []
    for f in range(2 * reps):
        both, down = unpack_message(hold_ref[f].astype(F32), own, each)
        boths.append(both)
        down_ref[f * each : (f + 1) * each, :] = down
    total = jnp.zeros((own, 1), F32)
    for begin, w_ref, out_ref in ((0, gate_w_ref, gate_ref), (cols // 2, up_w_ref, up_ref)):
        for s in range(n):
            place = begin + s * each
            rows = jnp.concatenate([part[:, place : place + each] for part in boths], axis=1)
            span = slice(s * units, (s + 1) * units)
            out_ref[:, span] = rows
            total = total + jnp.sum(rows * w_ref[:, span].astype(F32), axis=1, keepdims=True)
    norm_ref[...] = total / gain_ref[...]


def down_kernel(hidden_ref, w_ref, out_ref):
    rows = out_ref.shape[1]
    for i in range(0, out_ref.shape[0], 2):
        both = dot(hidden_ref[pl.ds(i * rows, 2 * rows), :], w_ref[...]).astype(BF16)
        for j in range(2):
            out_ref[i + j] = both[j * rows : (j + 1) * rows]


def output_kernel(n, own, middle_ref, *refs):
    total = middle_ref[...]
    for ref in refs[:-1]:
        total = total + ref[...].astype(F32)
    refs[-1][...] = from_blocks(total, n, own).astype(BF16)


def middle_grad_kernel(n, own, reps, me_ref, *refs):
    parts, refs = refs[:reps], refs[reps:]
    cot_ref, middle_ref, gains_ref, w_ref, grad_ref, branch_ref = refs[:6]
    pair_refs, hold_ref = refs[6:-1], refs[-1]
    rows = middle_ref.shape[0]
    middle = middle_ref[...]
    grad_second = sum(ref[...].astype(F32) for ref in parts)
    grad = cot_ref[0].astype(F32) + norm_backward(
        middle, inverse_rms(middle), gains_ref[1:2, :], grad_second
    )
    grad_ref[...] = grad
    branch = grad.astype(BF16)
    branch_ref[...] = branch
    attended = from_blocks(contract_cols(branch, w_ref[...]), n, own)
    head_cols = hold_ref.shape[2]
    if n * head_cols > D:
        attended = jnp.concatenate([attended, jnp.zeros((rows, n * head_cols - D), F32)], axis=1)
    for s in range(n):
        hold_ref[s] = attended[:, s * head_cols : (s + 1) * head_cols].astype(BF16)
    for i in range(n):
        pair_refs[i // 2][i % 2] = hold_ref[me_ref[0] ^ i]


def out_weights_kernel(rep_ref, attended_ref, branch_ref, *refs):
    store_pieces(rep_ref, refs[:-1], refs[-1], contract_rows(attended_ref[...], branch_ref[...]))


def rep_sum_kernel(reps, *refs):
    total = sum(ref[...].astype(F32) for ref in refs[:reps])
    refs[reps][...] = total.astype(BF16)


def owner_sum_kernel(in_ref, out_ref):
    out_ref[...] = jnp.sum(in_ref[...].astype(F32), axis=0).astype(BF16)


def out_out_kernel(n, reps, rep_ref, *refs):
    out_ref, hold_ref = refs[reps:]
    for i in range(reps):
        hold_ref[rep_ref[0] ^ i] = refs[i][...].astype(F32)
    own = out_ref.shape[0]
    rows = jnp.concatenate([hold_ref[r] for r in range(reps)], axis=0)[:own]
    out_ref[...] = from_blocks(rows, n, own)


def attention_out_kernel(n, reps, rep_ref, *refs):
    parts, refs = refs[:reps], refs[reps:]
    q_w_ref, k_w_ref, v_w_ref, gain_ref, q_ref, k_ref, v_ref, norm_ref, hold_ref = refs
    own = q_ref.shape[0]
    cols = parts[0].shape[2]
    head_cols = cols // 3
    heads = head_cols // HD
    for i, part in enumerate(parts):
        for s in range(n):
            hold_ref[rep_ref[0] ^ i, s] = part[s].astype(F32)
    sides = [
        jnp.concatenate([hold_ref[r, s] for r in range(reps)], axis=0)[:own] for s in range(n)
    ]

    def slot(h, kind):
        begin = kind * head_cols + h % heads * HD
        return sides[h // heads][:, begin : begin + HD]

    query = jnp.concatenate([slot(h, 0) for h in range(QH)], axis=1)
    q_ref[...] = query
    total = jnp.sum(query * q_w_ref[...].astype(F32), axis=1, keepdims=True)
    for kind, w_ref, out_ref in ((1, k_w_ref, k_ref), (2, v_w_ref, v_ref)):
        wide = jnp.concatenate(
            [sum(slot(j * GROUP + g, kind) for g in range(GROUP)) for j in range(KVH)], axis=1
        )
        out_ref[...] = wide
        total = total + jnp.sum(wide * w_ref[...].astype(F32), axis=1, keepdims=True)
    norm_ref[...] = total / gain_ref[...]


def input_grad_kernel(n, own, nz, *refs):
    parts, (tokens_ref, gains_ref, grad_ref, out_ref) = refs[:nz], refs[nz:]
    inputs = tokens_ref[0].astype(F32)
    grad_first = sum(ref[...].astype(F32) for ref in parts)
    total = grad_ref[...] + norm_backward(inputs, inverse_rms(inputs), gains_ref[0:1, :], grad_first)
    out_ref[...] = from_blocks(total, n, own)


def shards(
    tokens,
    lengths,
    norm_one,
    w_query,
    w_key,
    w_value,
    w_out,
    norm_two,
    w_gate,
    w_up,
    w_down,
    cotangent,
):
    n = lax.axis_size("shard")
    reps = lax.axis_size("rep")
    nz = n // 2
    rows = tokens.shape[0]
    length = rows * n
    own = w_query.shape[0]
    held = w_down.shape[0]
    block = round_up(own + 2, 16)
    width = n * block
    piece = block // reps
    heads = -(-QH // n)
    head_cols = heads * HD
    qkv_cols = 3 * head_cols
    each = held // (2 * reps)
    units = n * each
    msg_rows = message_plan(own, each, 2 * units)[-1]
    shard_index = lax.axis_index("shard").astype(jnp.int32)
    me = shard_index.reshape(1)
    core = (shard_index % 2).reshape(1)
    rep = lax.axis_index("rep").astype(jnp.int32).reshape(1)
    own_block = (rows, width)

    (tokens_in,) = call(
        lambda *r: blocks_kernel(n, *r), "tokens_blocks", [((nz,) + own_block, BF16)], tokens
    )
    tokens_mine = exchange_z(tokens_in)
    tokens_other = swap(tokens_mine, "shard", 1)
    gains_own = jnp.pad(jnp.stack([norm_one, norm_two]), ((0, 0), (0, qkv_cols - own))).astype(F32)
    *qkv_messages, out_message = call(
        lambda *r: attention_message_kernel(n, *r),
        "attention_message",
        [((2, piece, qkv_cols), BF16)] * nz + [((piece, width), BF16)],
        w_query,
        w_key,
        w_value,
        w_out,
        gains_own,
        scalars=(rep, me),
        scratch=[((n, piece, qkv_cols), BF16)],
    )
    qkv_mine, qkv_other = deliver_pairs(qkv_messages)
    qkv_piece = jnp.stack([block for z in range(nz) for block in (qkv_mine[z], qkv_other[z])])
    (w_qkv,) = call(
        lambda *r: join_kernel(n, reps, *r),
        "join_qkv",
        [((n, reps, piece, qkv_cols), BF16)],
        *spread(qkv_piece, "rep", 1),
        scalars=(rep, me),
    )
    w_qkv = w_qkv.reshape(width, qkv_cols)

    (messages,) = call(
        lambda *r: hidden_message_kernel(n, reps, *r),
        "hidden_message",
        [((nz, 2, msg_rows, 2 * units), BF16)],
        w_gate,
        w_up,
        w_down,
        scalars=(rep, core),
    )
    out_message, messages, tokens_mine = lax.optimization_barrier((out_message, messages, tokens_mine))
    out_mine, out_other = both_cores(
        spread(jnp.stack(spread(out_message, "shard", 2)), "rep", 1)
    )
    (out_full,) = call(
        lambda *r: join_out_kernel(nz, reps, *r),
        "join_out",
        [((n, reps, piece, width), BF16)],
        out_mine,
        out_other,
        scalars=(rep, me),
    )
    out_full = out_full.reshape(width, width)
    messages = exchange_z(messages)
    w_hidden, w_down_in = call(
        lambda *r: hidden_weights_in_kernel(n, own, each, *r),
        "hidden_weights_in",
        [((n, block, 2 * units), BF16), ((units, width), BF16)],
        messages,
        swap(messages[:, 1], "shard", 1),
        scalars=(core,),
        scratch=[((n, round_up(each, 8), D), F32)],
    )
    w_hidden = w_hidden.reshape(width, 2 * units)
    (cot_in,) = call(
        lambda *r: blocks_kernel(n, *r), "cot_blocks", [((1,) + own_block, BF16)], cotangent
    )
    cot_in, w_qkv = lax.optimization_barrier((cot_in, w_qkv))
    cot_mine, cot_other = both_cores(spread(cot_in[0], "rep", 1))

    doc_start, position = doc_layout(lengths[0], length)
    cosines, sines = rope_tables(position)
    cosines = jnp.tile(cosines, (1, 2 * heads))
    sines = jnp.tile(sines, (1, 2 * heads))
    start = doc_start[:, None]
    head_shape = (length, head_cols)
    first_all, query, key, value, gains, *mixed = call(
        lambda *r: attend_kernel(rows, n, *r),
        "attend",
        [((length, width), BF16)]
        + [(head_shape, BF16)] * 3
        + [((2, width), F32)]
        + [((2, rows, head_cols), BF16)] * nz,
        tokens_mine,
        tokens_other,
        w_qkv,
        cosines,
        sines,
        start,
        scalars=(me,),
        scratch=[(head_shape, BF16)],
    )
    mixed_mine, mixed_other = deliver_pairs(mixed)

    middle, second, attended = call(
        lambda *r: middle_kernel(n, *r),
        "middle",
        [(own_block, F32), (own_block, BF16), (own_block, BF16)],
        tokens_in,
        *mixed_mine,
        mixed_other,
        out_full,
        gains,
        scalars=(me,),
        scratch=[((n, rows, head_cols), BF16)],
    )

    second_mine, second_other = both_cores(spread(second, "rep", 1))
    side_outs = [
        ((reps, rows, width), BF16),
        ((reps * rows, 2 * units), BF16),
        ((reps * rows, units), BF16),
    ]

    def hidden_side(seconds, cots, name):
        return call(hidden_kernel, name, side_outs, seconds, cots, w_hidden, w_down_in)

    def plane_sums(mine, other):
        sums = call(pair_sum_kernel, "pair_sum", [(own_block, BF16)] * reps, mine, swap(other, "shard", 1))
        return deliver(sums, "rep", 1)

    grad_mine, grads_mine, hidden_mine = hidden_side(second_mine, cot_mine, "hidden_mine")
    grad_other, grads_other, hidden_other = hidden_side(second_other, cot_other, "hidden_other")
    grad_second = plane_sums(grad_mine, grad_other)
    (hidden_messages,) = call(
        lambda *r: hidden_weights_kernel(n, own, each, *r),
        "hidden_weights",
        [((nz, 2, msg_rows, 2 * units), BF16)],
        second_mine,
        second_other,
        cot_mine,
        cot_other,
        grads_mine,
        grads_other,
        hidden_mine,
        hidden_other,
        scalars=(core,),
        scratch=[((n, msg_rows, 2 * units), BF16)],
    )
    hidden_messages = exchange_z(hidden_messages)

    grad_middle, grad_branch, *grad_heads = call(
        lambda *r: middle_grad_kernel(n, own, reps, *r),
        "middle_grad",
        [(own_block, F32), (own_block, BF16)] + [((2, rows, head_cols), BF16)] * nz,
        *grad_second,
        cot_in,
        middle,
        gains,
        out_full,
        scalars=(me,),
        scratch=[((n, rows, head_cols), BF16)],
    )
    heads_mine, heads_other = deliver_pairs(grad_heads)
    out_pieces = call(
        out_weights_kernel,
        "out_weights",
        [((n, piece, width), BF16)] * reps,
        attended,
        grad_branch,
        scalars=(rep,),
        scratch=[((n, reps, piece, width), BF16)],
    )

    grad_qkv, *attention_pieces = call(
        lambda *r: attend_back_kernel(nz, reps, *r),
        "attend_back",
        [((length, qkv_cols), BF16)] + [((n, piece, qkv_cols), BF16)] * reps,
        *heads_mine,
        heads_other,
        first_all,
        query,
        key,
        value,
        cosines,
        sines,
        start,
        scalars=(rep, me),
        scratch=[(head_shape, BF16)] + [(head_shape, F32)] * 2 + [((n, reps, piece, qkv_cols), BF16)],
    )
    first_sides = [
        call(
            lambda *r, side=side: first_grad_kernel(rows, side, *r),
            "first_grad",
            [((nz, rows, width), BF16)],
            grad_qkv,
            w_qkv,
            scalars=(me,),
        )[0]
        for side in (1, 0)
    ]
    first_sums = call(
        pair_sum_kernel, "pair_sum", [(own_block, BF16)] * nz, first_sides[1], swap(first_sides[0], "shard", 1)
    )
    (input_grad,) = call(
        lambda *r: input_grad_kernel(n, own, nz, *r),
        "input_grad",
        [((rows, D), F32)],
        *deliver(first_sums, "shard", 2),
        tokens_in,
        gains,
        grad_middle,
    )

    def owner_pieces(pieces):
        parts = deliver(pieces, "rep", 1)
        (summed,) = call(
            lambda *r: rep_sum_kernel(reps, *r), "rep_sum", [(pieces[0].shape, BF16)], *parts
        )
        return exchange(summed)

    gain_cols = [gain.astype(F32)[:, None] for gain in (norm_one, norm_two)]
    attention_parts = spread(owner_pieces(attention_pieces), "rep", 1)
    grad_w_query, grad_w_key, grad_w_value, grad_norm_one = call(
        lambda *r: attention_out_kernel(n, reps, *r),
        "attention_out",
        [(w_query.shape, F32), (w_key.shape, F32), (w_value.shape, F32), ((own, 1), F32)],
        *attention_parts,
        w_query,
        w_key,
        w_value,
        gain_cols[0],
        scalars=(rep,),
        scratch=[((reps, n, piece, qkv_cols), F32)],
    )

    (out_piece,) = call(owner_sum_kernel, "owner_sum", [((piece, width), BF16)], owner_pieces(out_pieces))
    (grad_w_out,) = call(
        lambda *r: out_out_kernel(n, reps, *r),
        "out_out",
        [(w_out.shape, F32)],
        *spread(out_piece, "rep", 1),
        scalars=(rep,),
        scratch=[((reps, piece, width), F32)],
    )

    sum_mine, sum_other = call(
        core_sums_kernel, "core_sums", [((msg_rows, 2 * units), BF16)] * 2, hidden_messages
    )
    core_sums = jnp.stack([sum_mine, swap(sum_other, "shard", 1)])
    grad_w_gate, grad_w_up, grad_w_down, grad_norm_two = call(
        lambda *r: hidden_out_kernel(n, reps, each, *r),
        "hidden_out",
        [(w_gate.shape, F32), (w_up.shape, F32), (w_down.shape, F32), ((own, 1), F32)],
        *spread(core_sums, "rep", 1),
        w_gate,
        w_up,
        gain_cols[1],
        scalars=(rep, core),
        scratch=[((2 * reps, msg_rows, 2 * units), BF16)],
    )

    down_parts = [
        call(down_kernel, "down", [((reps, rows, width), BF16)], hidden, w_down_in)[0]
        for hidden in (hidden_other, hidden_mine)
    ]
    (output,) = call(
        lambda *r: output_kernel(n, own, *r),
        "output",
        [((rows, D), BF16)],
        middle,
        *plane_sums(down_parts[1], down_parts[0]),
    )
    return (
        output,
        input_grad,
        grad_norm_one[:, 0],
        grad_w_query,
        grad_w_key,
        grad_w_value,
        grad_w_out,
        grad_norm_two[:, 0],
        grad_w_gate,
        grad_w_up,
        grad_w_down,
    )


def solution(mesh):
    rows = P("shard", None)
    own_tokens = P(("rep", "shard"), None)
    return jax.shard_map(
        shards,
        mesh=mesh,
        in_specs=(
            own_tokens,
            P("rep", None),
            P("shard"),
            rows,
            rows,
            rows,
            rows,
            P("shard"),
            rows,
            rows,
            rows,
            own_tokens,
        ),
        out_specs=(
            own_tokens,
            own_tokens,
            P("shard"),
            rows,
            rows,
            rows,
            rows,
            P("shard"),
            rows,
            rows,
            rows,
        ),
        check_vma=False,
    )
```

```python
import jax
import jax.numpy as jnp
from jax import lax
from jax.experimental import pallas as pl
from jax.experimental.pallas import tpu as pltpu
from jax.sharding import PartitionSpec as P

D = 960
QH = 15
KVH = 5
HD = 64
FF = 2560
GROUP = QH // KVH

EPS = 1e-05
ROPE_BASE = 10000.0
MASKED = -1e30
SCALE = HD ** (-0.5)
BF16 = jnp.bfloat16
F32 = jnp.float32


def doc_layout(lengths_row, length):
    places = jnp.arange(length, dtype=jnp.int32)
    doc_ends = jnp.cumsum(lengths_row)
    passed = places[:, None] >= doc_ends[None, :]
    doc_start = jnp.sum(jnp.where(passed, lengths_row[None, :], 0), axis=1)
    return (doc_start, places - doc_start)


def rope_tables(position):
    half_dim = HD // 2
    fraction = jnp.arange(half_dim, dtype=F32) * (2.0 / HD)
    inverse = ROPE_BASE ** (-fraction)
    angles = position.astype(F32)[:, None] * inverse[None, :]
    return (jnp.cos(angles), jnp.sin(angles))


VMEM_LIMIT = 56 * 2**20


def dot(left, right):
    return jnp.dot(left, right, preferred_element_type=F32)


def contract_rows(left, right):
    return lax.dot_general(left, right, (((0,), (0,)), ((), ())), preferred_element_type=F32)


def contract_cols(left, right):
    return lax.dot_general(left, right, (((1,), (1,)), ((), ())), preferred_element_type=F32)


def inverse_rms(values):
    return lax.rsqrt(jnp.sum(values * values, axis=-1, keepdims=True) * (1.0 / D) + EPS)


def norm_backward(values, inverse, gain, grad_norm):
    scaled = grad_norm * gain
    mean = jnp.sum(scaled * values, axis=-1, keepdims=True) * (1.0 / D)
    return inverse * scaled - values * inverse**3 * mean


def round_up(value, step):
    return -(-value // step) * step


def rows_at(index, rows):
    return pl.ds(pl.multiple_of(index * rows, rows), rows)


def to_blocks(values, n, width):
    rows, own = values.shape[0], values.shape[1] // n
    gap = jnp.zeros((rows, width // n - own), values.dtype)
    parts = []
    for s in range(n):
        parts += [values[:, s * own : (s + 1) * own], gap]
    return jnp.concatenate(parts, axis=1)


def from_blocks(values, n, own):
    block = values.shape[1] // n
    return jnp.concatenate([values[:, s * block : s * block + own] for s in range(n)], axis=1)


def swap(block, axis, k):
    count = lax.axis_size(axis)
    return lax.ppermute(block, axis, [(i, i ^ k) for i in range(count)])


def exchange(block):
    return lax.all_to_all(block, "shard", split_axis=0, concat_axis=0, tiled=True)


def spread(block, axis, step):
    return [block] + [swap(block, axis, k) for k in range(step, lax.axis_size(axis), step)]


def deliver(blocks, axis, step):
    return [blocks[0]] + [swap(block, axis, i * step) for i, block in enumerate(blocks) if i]


def after(value, *earlier):
    return lax.optimization_barrier((value,) + earlier)[0]


def both_cores(parts):
    stacked = jnp.stack(parts)
    return stacked, swap(stacked, "shard", 1)


def call(kernel, name, outs, *operands, scalars=(), scratch=()):
    specs = [pl.BlockSpec(memory_space=pltpu.SMEM)] * len(scalars)
    specs += [pl.BlockSpec(memory_space=pltpu.VMEM)] * len(operands)
    return pl.pallas_call(
        kernel,
        out_shape=[jax.ShapeDtypeStruct(shape, dtype) for shape, dtype in outs],
        in_specs=specs,
        out_specs=[pl.BlockSpec(memory_space=pltpu.VMEM)] * len(outs),
        scratch_shapes=[pltpu.VMEM(shape, dtype) for shape, dtype in scratch],
        compiler_params=pltpu.CompilerParams(vmem_limit_bytes=VMEM_LIMIT),
        name=name,
    )(*scalars, *operands)


def turned(values):
    half = HD // 2
    parts = []
    for begin in range(0, values.shape[1], HD):
        parts.append(-values[:, begin + half : begin + HD])
        parts.append(values[:, begin : begin + half])
    return jnp.concatenate(parts, axis=1)


def head_of(values, h, heads):
    if heads == 1:
        return values
    lane = lax.broadcasted_iota(jnp.int32, values.shape, 1)
    return jnp.where(lane // HD == h, values, jnp.zeros_like(values))


def masked_probs(query, key, starts, row):
    rows, cols = query.shape[0], key.shape[0]
    logits = contract_cols(query, key) * SCALE
    place = lax.broadcasted_iota(jnp.int32, (rows, cols), 1)
    own = lax.broadcasted_iota(jnp.int32, (rows, cols), 0) + row
    logits = jnp.where((place <= own) & (place >= starts), logits, MASKED)
    raised = jnp.exp(logits - jnp.max(logits, axis=-1, keepdims=True))
    return raised * (1.0 / jnp.sum(raised, axis=-1, keepdims=True))


def blocks_kernel(n, in_ref, *out_refs):
    values = to_blocks(in_ref[...].astype(F32), n, out_refs[0].shape[1]).astype(BF16)
    out_refs[0][...] = values
    for ref in out_refs[1:]:
        for i in range(ref.shape[0]):
            ref[i] = values


def attention_message_kernel(n, rep_ref, q_ref, k_ref, v_ref, out_ref, gain_ref, msg_ref):
    own = q_ref.shape[0]
    piece = msg_ref.shape[1]
    cols = gain_ref.shape[1]
    half = msg_ref.shape[2] - cols
    head_cols = cols // 3
    heads = head_cols // HD
    row = lax.broadcasted_iota(jnp.int32, (piece, own), 0) + rep_ref[0] * piece
    pick = jnp.where(row == lax.broadcasted_iota(jnp.int32, (piece, own), 1), 1.0, 0.0).astype(BF16)
    query, key, value = (dot(pick, ref[...]) for ref in (q_ref, k_ref, v_ref))
    gap = jnp.zeros((piece, HD), F32)
    wide = lax.broadcasted_iota(jnp.int32, (piece, cols), 0) + rep_ref[0] * piece
    for s in range(n):
        slots = range(s * heads, (s + 1) * heads)
        parts = [query[:, h * HD : (h + 1) * HD] if h < QH else gap for h in slots]
        for array in (key, value):
            for h in slots:
                j = h // GROUP
                parts.append(array[:, j * HD : (j + 1) * HD] if h < QH else gap)
        block = jnp.concatenate(parts, axis=1)
        for i in range(2):
            block = jnp.where(wide == own + i, gain_ref[i : i + 1, :], block)
        msg_ref[s, :, :cols] = block.astype(BF16)
    rows = to_blocks(dot(pick, out_ref[...]), n, 2 * half).astype(BF16)
    for s in range(n):
        msg_ref[s, :, cols:] = rows[:, s % 2 * half : (s % 2 + 1) * half]


def join_kernel(reps, rep_ref, *refs):
    for i in range(reps):
        refs[reps][:, rep_ref[0] ^ i] = refs[i][...]


def join_out_kernel(reps, rep_ref, core_ref, mine_ref, other_ref, out_ref):
    first = core_ref[0] == 0
    half = mine_ref.shape[3]
    for i in range(reps):
        mine, other = mine_ref[i], other_ref[i]
        out_ref[:, rep_ref[0] ^ i, :, :half] = jnp.where(first, mine, other)
        out_ref[:, rep_ref[0] ^ i, :, half:] = jnp.where(first, other, mine)


def fill_rows(values, rows):
    if values.shape[0] == rows:
        return values
    return jnp.concatenate([values, jnp.zeros((rows - values.shape[0], values.shape[1]), F32)], axis=0)


def fill_cols(values, cols):
    if values.shape[1] == cols:
        return values
    return jnp.concatenate([values, jnp.zeros((values.shape[0], cols - values.shape[1]), F32)], axis=1)


def message_plan(own, each, cols):
    top, rows = round_up(own, 8), round_up(each, 8)
    rest = D % cols
    halved = rest and 2 * rest <= cols
    first = round_up(rows // 2, 8) if halved else rows
    total = top + D // cols * rows + (first if rest else 0)
    return top, rows, rest, halved, first, total


def pack_message(both, down, cols):
    top, rows, rest, halved, first, _ = message_plan(both.shape[0], down.shape[0], cols)
    down = fill_rows(down, rows)
    parts = [fill_rows(both, top)]
    parts += [down[:, j * cols : (j + 1) * cols] for j in range(D // cols)]
    if rest:
        tail = down[:, D - rest :]
        if halved:
            tail = jnp.concatenate([tail[:first], fill_rows(tail[first:], first)], axis=1)
        parts.append(fill_cols(tail, cols))
    return jnp.concatenate(parts, axis=0)


def unpack_message(message, own, each):
    cols = message.shape[1]
    top, rows, rest, halved, first, _ = message_plan(own, each, cols)
    parts = [message[top + j * rows : top + (j + 1) * rows] for j in range(D // cols)]
    if rest:
        tail = message[top + D // cols * rows :][:first]
        if halved:
            tail = jnp.concatenate([tail[:, :rest], tail[: rows - first, rest : 2 * rest]], axis=0)
        parts.append(tail[:, :rest])
    return message[:own], jnp.concatenate(parts, axis=1)[:each]


def hidden_message_kernel(n, reps, rep_ref, gate_ref, up_ref, down_ref, *out_refs):
    own, units = gate_ref.shape
    held = down_ref.shape[0]
    each = held // (2 * reps)
    cols = n * each
    place = lax.broadcasted_iota(jnp.int32, (1, cols), 1)
    row = lax.broadcasted_iota(jnp.int32, (round_up(each, 8), held), 0)
    for i in range(2):
        begin = each * (2 * rep_ref[0] + i)
        unit = place + begin
        for s in range(1, n):
            unit = unit + jnp.where(place >= each * s, held - each, 0)
        pick = jnp.where(lax.broadcasted_iota(jnp.int32, (units, cols), 0) == unit, 1.0, 0.0)
        pick = pick.astype(BF16)
        both = jnp.concatenate([dot(gate_ref[...], pick), dot(up_ref[...], pick)], axis=1)
        take = (lax.broadcasted_iota(jnp.int32, row.shape, 1) == row + begin) & (row < each)
        down = dot(jnp.where(take, 1.0, 0.0).astype(BF16), down_ref[...])
        message = pack_message(both, down[:each], 2 * cols).astype(BF16)
        for z in range(n // 2):
            split_rows([ref.at[2 * z + i] for ref in out_refs], message)


def split_rows(refs, values):
    begin = 0
    for ref in refs:
        rows = ref.shape[0]
        ref[...] = values[begin : begin + rows]
        begin += rows


def hidden_weights_in_kernel(n, own, each, *refs):
    parts, (w_ref, down_ref) = refs[:-2], refs[-2:]
    block = w_ref.shape[1]
    downs = []
    for s in range(n):
        message = jnp.concatenate([part[s].astype(F32) for part in parts], axis=0)
        both, down = unpack_message(message, own, each)
        w_ref[s] = fill_rows(both, block).astype(BF16)
        downs.append(down)
    down_ref[...] = to_blocks(jnp.concatenate(downs, axis=0), n, down_ref.shape[1]).astype(BF16)


def attend_kernel(rows, n, me_ref, mine_ref, other_ref, *refs):
    w_ref, cos_ref, sin_ref, start_ref, first_ref, q_ref, k_ref, v_ref, gains_ref = refs[:9]
    part_refs, mixed_ref = refs[9:-1], refs[-1]
    length, head_cols = q_ref.shape
    heads = head_cols // HD
    width = first_ref.shape[1]
    block_rows = width // n
    own = D // n
    gap = jnp.zeros((1, block_rows - own), F32)
    gains = []
    for i in range(2):
        parts = []
        for s in range(n):
            group = w_ref[pl.ds(s * block_rows + own // 16 * 16, block_rows - own // 16 * 16), :]
            row = own % 16 + i
            spread_row = group.astype(F32)[row : row + 1, :own]
            parts += [spread_row, gap]
        gains.append(jnp.concatenate(parts, axis=1))
        gains_ref[i : i + 1, :] = gains[i]
    for side, ref in enumerate((mine_ref, other_ref)):
        for z in range(n // 2):
            inputs = ref[z].astype(F32)
            normed = inputs * inverse_rms(inputs) * gains[0]
            first_ref[rows_at(me_ref[0] ^ (2 * z + side), rows), :] = normed.astype(BF16)
    block = min(256, length)
    for i in range(length // block):
        span = pl.ds(i * block, block)
        raw = dot(first_ref[span, :], w_ref[...])
        cosines, sines = cos_ref[span, :], sin_ref[span, :]
        query, key = raw[:, :head_cols], raw[:, head_cols : 2 * head_cols]
        q_ref[span, :] = (query * cosines + turned(query) * sines).astype(BF16)
        k_ref[span, :] = (key * cosines + turned(key) * sines).astype(BF16)
        v_ref[span, :] = raw[:, 2 * head_cols :].astype(BF16)
    for i in range(length // block):
        span, past = pl.ds(i * block, block), pl.ds(0, (i + 1) * block)
        total = None
        for h in range(heads):
            probs = masked_probs(
                head_of(q_ref[span, :], h, heads), k_ref[past, :], start_ref[span, :], i * block
            )
            mixed = head_of(dot(probs.astype(BF16), v_ref[past, :]), h, heads)
            total = mixed if total is None else total + mixed
        mixed_ref[span, :] = total.astype(BF16)
    for i, ref in enumerate(part_refs):
        ref[...] = mixed_ref[rows_at(me_ref[0] ^ i, rows), :]


def attend_back_kernel(n, reps, rep_ref, me_ref, *refs):
    parts, refs = refs[:n], refs[n:]
    first_ref, q_ref, k_ref, v_ref, cos_ref, sin_ref, start_ref, dqkv_ref = refs[:8]
    piece_refs, (g_ref, dk_ref, dv_ref, hold_ref) = refs[8 : 8 + reps], refs[8 + reps :]
    for i, ref in enumerate(parts):
        g_ref[rows_at(me_ref[0] ^ i, ref.shape[0]), :] = ref[...]
    length, head_cols = q_ref.shape
    heads = head_cols // HD
    block = min(256, length)
    dk_ref[...] = jnp.zeros_like(dk_ref)
    dv_ref[...] = jnp.zeros_like(dv_ref)
    for i in range(length // block):
        span, past = pl.ds(i * block, block), pl.ds(0, (i + 1) * block)
        total = None
        for h in range(heads):
            query = head_of(q_ref[span, :], h, heads)
            grad = head_of(g_ref[span, :], h, heads)
            key = k_ref[past, :]
            probs = masked_probs(query, key, start_ref[span, :], i * block)
            grad_probs = contract_cols(grad, v_ref[past, :])
            delta = jnp.sum(probs * grad_probs, axis=-1, keepdims=True)
            grad_logits = (probs * (grad_probs - delta)).astype(BF16)
            grad_query = head_of(dot(grad_logits, key), h, heads)
            total = grad_query if total is None else total + grad_query
            dv_ref[past, :] += contract_rows(probs.astype(BF16), grad)
            dk_ref[past, :] += contract_rows(grad_logits, query)
        total = total * SCALE
        back = total * cos_ref[span, :] - turned(total) * sin_ref[span, :]
        dqkv_ref[span, :head_cols] = back.astype(BF16)
    for i in range(length // block):
        span = pl.ds(i * block, block)
        total = dk_ref[span, :] * SCALE
        back = total * cos_ref[span, :] - turned(total) * sin_ref[span, :]
        dqkv_ref[span, head_cols : 2 * head_cols] = back.astype(BF16)
        dqkv_ref[span, 2 * head_cols :] = dv_ref[span, :].astype(BF16)
    store_pieces(rep_ref, piece_refs, hold_ref, contract_rows(first_ref[...], dqkv_ref[...]))


def store_pieces(rep_ref, piece_refs, hold_ref, grad):
    n, reps, piece, _ = hold_ref.shape
    for s in range(n):
        for r in range(reps):
            begin = (s * reps + r) * piece
            hold_ref[s, r] = grad[begin : begin + piece].astype(BF16)
    for i, ref in enumerate(piece_refs):
        for s in range(n):
            ref[s] = hold_ref[s, rep_ref[0] ^ i]


def first_grad_kernel(rows, side, me_ref, dqkv_ref, w_ref, out_ref):
    for z in range(out_ref.shape[0]):
        part = dqkv_ref[rows_at(me_ref[0] ^ (2 * z + side), rows), :]
        out_ref[z] = contract_cols(part, w_ref[...]).astype(BF16)


def pair_sum_kernel(mine_ref, other_ref, *out_refs):
    for i, ref in enumerate(out_refs):
        ref[...] = (mine_ref[i].astype(F32) + other_ref[i].astype(F32)).astype(BF16)


def middle_kernel(n, me_ref, tokens_ref, *refs):
    parts, refs = refs[:n], refs[n:]
    w_ref, gains_ref, middle_ref, second_ref, attended_ref, hold_ref = refs
    width = tokens_ref.shape[1]
    for i, ref in enumerate(parts):
        hold_ref[me_ref[0] ^ i] = ref[...]
    attended = jnp.concatenate([hold_ref[s] for s in range(n)], axis=1)[:, :D]
    attended = to_blocks(attended.astype(F32), n, width).astype(BF16)
    attended_ref[...] = attended
    middle = tokens_ref[...].astype(F32) + dot(attended, w_ref[...])
    middle_ref[...] = middle
    second_ref[...] = (middle * inverse_rms(middle) * gains_ref[1:2, :]).astype(BF16)


def stacked(ref, begin=0, count=None):
    count = ref.shape[0] if count is None else count
    return jnp.concatenate([ref[begin + i] for i in range(count)], axis=0)


def hidden_kernel(rep_ref, second_ref, cot_ref, w_ref, down_ref, grad_ref, grads_ref, hidden_ref):
    reps, rows, _ = second_ref.shape
    units = down_ref.shape[0]
    for i in range(0, reps, 2):
        span = pl.ds(i * rows, 2 * rows)
        both = dot(stacked(second_ref, i, 2), w_ref[...])
        gate, up = both[:, :units], both[:, units:]
        cots = jnp.concatenate([cot_ref[rep_ref[0] ^ (i + j)] for j in range(2)], axis=0)
        grad_hidden = contract_cols(cots, down_ref[...])
        sigmoid = 1.0 / (1.0 + jnp.exp(-gate))
        silu = gate * sigmoid
        hidden_ref[span, :] = (silu * up).astype(BF16)
        grad_gate = grad_hidden * up * sigmoid * (1.0 + gate * (1.0 - sigmoid))
        grads = jnp.concatenate([grad_gate, grad_hidden * silu], axis=1).astype(BF16)
        grads_ref[span, :] = grads
        grad = contract_cols(grads, w_ref[...]).astype(BF16)
        for j in range(2):
            grad_ref[i + j] = grad[j * rows : (j + 1) * rows]


def hidden_weights_kernel(n, own, each, rep_ref, *refs):
    second_a, second_b, cot_a, cot_b, grads_a, grads_b, hidden_a, hidden_b, *msg_refs = refs
    cols = msg_refs[0].shape[2]
    grad = contract_rows(stacked(second_a), grads_a[...])
    grad = grad + contract_rows(stacked(second_b), grads_b[...])
    cots = [
        jnp.concatenate([ref[rep_ref[0] ^ i] for i in range(ref.shape[0])], axis=0) for ref in (cot_a, cot_b)
    ]
    down = contract_rows(hidden_a[...], cots[0]) + contract_rows(hidden_b[...], cots[1])
    down = from_blocks(down, n, own)
    block = grad.shape[0] // n
    for s in range(n):
        both = grad[s * block : s * block + own]
        message = pack_message(both, down[s * each : (s + 1) * each], cols).astype(BF16)
        split_rows([ref.at[s] for ref in msg_refs], message)


def core_sums_kernel(*refs):
    out_ref = refs[-1]
    for core in range(2):
        sums = [
            sum(part[s].astype(F32) for s in range(core, part.shape[0], 2)) for part in refs[:-1]
        ]
        out_ref[core] = jnp.concatenate(sums, axis=0).astype(BF16)


def hidden_out_kernel(n, reps, each, rep_ref, *refs):
    parts, refs = refs[:reps], refs[reps:]
    gate_w_ref, up_w_ref, gain_ref, gate_ref, up_ref, down_ref, norm_ref, hold_ref = refs
    own = gate_ref.shape[0]
    units = 2 * reps * each
    for i, part in enumerate(parts):
        for core in range(2):
            hold_ref[2 * (rep_ref[0] ^ i) + core] = part[core]
    cols = hold_ref.shape[2]
    boths = []
    for f in range(2 * reps):
        both, down = unpack_message(hold_ref[f].astype(F32), own, each)
        boths.append(both)
        down_ref[f * each : (f + 1) * each, :] = down
    total = jnp.zeros((own, 1), F32)
    for begin, w_ref, out_ref in ((0, gate_w_ref, gate_ref), (cols // 2, up_w_ref, up_ref)):
        for s in range(n):
            place = begin + s * each
            rows = jnp.concatenate([part[:, place : place + each] for part in boths], axis=1)
            span = slice(s * units, (s + 1) * units)
            out_ref[:, span] = rows
            total = total + jnp.sum(rows * w_ref[:, span].astype(F32), axis=1, keepdims=True)
    norm_ref[...] = total / gain_ref[...]


def down_kernel(hidden_ref, w_ref, out_ref):
    rows = out_ref.shape[1]
    for i in range(0, out_ref.shape[0], 2):
        both = dot(hidden_ref[pl.ds(i * rows, 2 * rows), :], w_ref[...]).astype(BF16)
        for j in range(2):
            out_ref[i + j] = both[j * rows : (j + 1) * rows]


def output_kernel(n, own, middle_ref, *refs):
    total = middle_ref[...]
    for ref in refs[:-1]:
        total = total + ref[...].astype(F32)
    refs[-1][...] = from_blocks(total, n, own).astype(BF16)


def middle_grad_kernel(n, own, reps, me_ref, *refs):
    parts, refs = refs[:reps], refs[reps:]
    cot_ref, middle_ref, gains_ref, w_ref, grad_ref, branch_ref = refs[:6]
    part_refs, hold_ref = refs[6:-1], refs[-1]
    rows = middle_ref.shape[0]
    middle = middle_ref[...]
    grad_second = sum(ref[...].astype(F32) for ref in parts)
    grad = cot_ref[...].astype(F32) + norm_backward(
        middle, inverse_rms(middle), gains_ref[1:2, :], grad_second
    )
    grad_ref[...] = grad
    branch = grad.astype(BF16)
    branch_ref[...] = branch
    attended = from_blocks(contract_cols(branch, w_ref[...]), n, own)
    head_cols = hold_ref.shape[2]
    if n * head_cols > D:
        attended = jnp.concatenate([attended, jnp.zeros((rows, n * head_cols - D), F32)], axis=1)
    for s in range(n):
        hold_ref[s] = attended[:, s * head_cols : (s + 1) * head_cols].astype(BF16)
    for i, ref in enumerate(part_refs):
        ref[...] = hold_ref[me_ref[0] ^ i]


def out_weights_kernel(rep_ref, attended_ref, branch_ref, *refs):
    store_pieces(rep_ref, refs[:-1], refs[-1], contract_rows(attended_ref[...], branch_ref[...]))


def rep_sum_kernel(reps, *refs):
    total = sum(ref[...].astype(F32) for ref in refs[:reps])
    refs[reps][...] = total.astype(BF16)


def owner_sum_kernel(in_ref, out_ref):
    out_ref[...] = jnp.sum(in_ref[...].astype(F32), axis=0).astype(BF16)


def out_out_kernel(n, reps, rep_ref, *refs):
    out_ref, hold_ref = refs[reps:]
    for i in range(reps):
        hold_ref[rep_ref[0] ^ i] = refs[i][...].astype(F32)
    own = out_ref.shape[0]
    rows = jnp.concatenate([hold_ref[r] for r in range(reps)], axis=0)[:own]
    out_ref[...] = from_blocks(rows, n, own)


def attention_out_kernel(n, reps, rep_ref, *refs):
    parts, refs = refs[:reps], refs[reps:]
    q_w_ref, k_w_ref, v_w_ref, gain_ref, q_ref, k_ref, v_ref, norm_ref, hold_ref = refs
    own = q_ref.shape[0]
    cols = parts[0].shape[2]
    head_cols = cols // 3
    heads = head_cols // HD
    for i, part in enumerate(parts):
        for s in range(n):
            hold_ref[rep_ref[0] ^ i, s] = part[s].astype(F32)
    sides = [
        jnp.concatenate([hold_ref[r, s] for r in range(reps)], axis=0)[:own] for s in range(n)
    ]

    def slot(h, kind):
        begin = kind * head_cols + h % heads * HD
        return sides[h // heads][:, begin : begin + HD]

    query = jnp.concatenate([slot(h, 0) for h in range(QH)], axis=1)
    q_ref[...] = query
    total = jnp.sum(query * q_w_ref[...].astype(F32), axis=1, keepdims=True)
    for kind, w_ref, out_ref in ((1, k_w_ref, k_ref), (2, v_w_ref, v_ref)):
        wide = jnp.concatenate(
            [sum(slot(j * GROUP + g, kind) for g in range(GROUP)) for j in range(KVH)], axis=1
        )
        out_ref[...] = wide
        total = total + jnp.sum(wide * w_ref[...].astype(F32), axis=1, keepdims=True)
    norm_ref[...] = total / gain_ref[...]


def input_grad_kernel(n, own, nz, *refs):
    parts, (tokens_ref, gains_ref, grad_ref, out_ref) = refs[:nz], refs[nz:]
    inputs = tokens_ref[...].astype(F32)
    grad_first = sum(ref[...].astype(F32) for ref in parts)
    total = grad_ref[...] + norm_backward(inputs, inverse_rms(inputs), gains_ref[0:1, :], grad_first)
    out_ref[...] = from_blocks(total, n, own)


def shards(
    tokens,
    lengths,
    norm_one,
    w_query,
    w_key,
    w_value,
    w_out,
    norm_two,
    w_gate,
    w_up,
    w_down,
    cotangent,
):
    n = lax.axis_size("shard")
    reps = lax.axis_size("rep")
    nz = n // 2
    rows = tokens.shape[0]
    length = rows * n
    own = w_query.shape[0]
    held = w_down.shape[0]
    block = round_up(own + 2, 16)
    width = n * block
    piece = block // reps
    heads = -(-QH // n)
    head_cols = heads * HD
    qkv_cols = 3 * head_cols
    each = held // (2 * reps)
    units = n * each
    msg_rows = message_plan(own, each, 2 * units)[-1]
    shard_index = lax.axis_index("shard").astype(jnp.int32)
    me = shard_index.reshape(1)
    core = (shard_index % 2).reshape(1)
    rep = lax.axis_index("rep").astype(jnp.int32).reshape(1)
    own_block = (rows, width)

    (tokens_in,) = call(lambda *r: blocks_kernel(n, *r), "tokens_blocks", [(own_block, BF16)], tokens)
    tokens_mine, tokens_other = both_cores(spread(tokens_in, "shard", 2))
    gains_own = jnp.pad(jnp.stack([norm_one, norm_two]), ((0, 0), (0, qkv_cols - own))).astype(F32)
    (message,) = call(
        lambda *r: attention_message_kernel(n, *r),
        "attention_message",
        [((n, piece, qkv_cols + width // 2), BF16)],
        after(w_query, tokens_in),
        w_key,
        w_value,
        w_out,
        gains_own,
        scalars=(rep,),
    )
    arrived = exchange(message)
    (w_qkv,) = call(
        lambda *r: join_kernel(reps, *r),
        "join_qkv",
        [((n, reps, piece, qkv_cols), BF16)],
        *spread(arrived[:, :, :qkv_cols], "rep", 1),
        scalars=(rep,),
    )
    w_qkv = w_qkv.reshape(width, qkv_cols)
    cot_in, cot_tiled = call(
        lambda *r: blocks_kernel(n, *r),
        "cot_blocks",
        [(own_block, BF16), ((reps,) + own_block, BF16)],
        after(cotangent, message),
    )
    cot_mine = lax.all_to_all(after(cot_tiled, arrived), "rep", split_axis=0, concat_axis=0, tiled=True)

    split = msg_rows // 2 // 16 * 16 + 16
    part_rows = (split, msg_rows - split) if split < msg_rows else (msg_rows,)
    messages = call(
        lambda *r: hidden_message_kernel(n, reps, *r),
        "hidden_message",
        [((n, part, 2 * units), BF16) for part in part_rows],
        after(w_gate, cot_in),
        w_up,
        w_down,
        scalars=(rep,),
    )
    hidden_first = exchange(after(messages[0], tokens_mine, cot_mine))

    out_mine, out_other = both_cores(spread(after(arrived, w_qkv)[:, :, qkv_cols:], "rep", 1))

    doc_start, position = doc_layout(lengths[0], length)
    cosines, sines = rope_tables(position)
    cosines = jnp.tile(cosines, (1, 2 * heads))
    sines = jnp.tile(sines, (1, 2 * heads))
    start = doc_start[:, None]
    head_shape = (length, head_cols)
    first_all, query, key, value, gains, *mixed = call(
        lambda *r: attend_kernel(rows, n, *r),
        "attend",
        [((length, width), BF16)]
        + [(head_shape, BF16)] * 3
        + [((2, width), F32)]
        + [((rows, head_cols), BF16)] * n,
        tokens_mine,
        tokens_other,
        w_qkv,
        cosines,
        sines,
        start,
        scalars=(me,),
        scratch=[(head_shape, BF16)],
    )
    mixed = deliver([after(mixed[0], hidden_first)] + mixed[1:], "shard", 1)
    hidden_rest = [exchange(after(message, *mixed)) for message in messages[1:]]
    (out_full,) = call(
        lambda *r: join_out_kernel(reps, *r),
        "join_out",
        [((n, reps, piece, width), BF16)],
        after(out_mine, gains),
        out_other,
        scalars=(rep, core),
    )
    out_full = out_full.reshape(width, width)

    middle, second, attended = call(
        lambda *r: middle_kernel(n, *r),
        "middle",
        [(own_block, F32), (own_block, BF16), (own_block, BF16)],
        tokens_in,
        *mixed,
        out_full,
        gains,
        scalars=(me,),
        scratch=[((n, rows, head_cols), BF16)],
    )
    w_hidden, w_down_in = call(
        lambda *r: hidden_weights_in_kernel(n, own, each, *r),
        "hidden_weights_in",
        [((n, block, 2 * units), BF16), ((units, width), BF16)],
        after(hidden_first, second),
        *hidden_rest,
    )
    w_hidden = w_hidden.reshape(width, 2 * units)
    cot_other = swap(cot_mine, "shard", 1)

    second_mine, second_other = both_cores(spread(second, "rep", 1))
    side_outs = [
        ((reps, rows, width), BF16),
        ((reps * rows, 2 * units), BF16),
        ((reps * rows, units), BF16),
    ]

    def hidden_side(seconds, cots, name):
        return call(hidden_kernel, name, side_outs, seconds, cots, w_hidden, w_down_in, scalars=(rep,))

    def plane_sums(mine, other):
        sums = call(pair_sum_kernel, "pair_sum", [(own_block, BF16)] * reps, mine, swap(other, "shard", 1))
        return sums, deliver(sums, "rep", 1)

    grad_other, grads_other, hidden_other = hidden_side(second_other, cot_other, "hidden_other")
    grad_mine, grads_mine, hidden_mine = hidden_side(
        after(second_mine, grad_other), cot_mine, "hidden_mine"
    )
    sums, grad_second = plane_sums(grad_mine, grad_other)
    hidden_messages = call(
        lambda *r: hidden_weights_kernel(n, own, each, *r),
        "hidden_weights",
        [((n, part, 2 * units), BF16) for part in part_rows],
        second_mine,
        second_other,
        cot_mine,
        cot_other,
        grads_mine,
        grads_other,
        after(hidden_mine, sums[0]),
        hidden_other,
        scalars=(rep,),
    )
    hidden_sums = [exchange(hidden_messages[0])]

    grad_middle, grad_branch, *grad_heads = call(
        lambda *r: middle_grad_kernel(n, own, reps, *r),
        "middle_grad",
        [(own_block, F32), (own_block, BF16)] + [((rows, head_cols), BF16)] * n,
        *grad_second,
        cot_in,
        after(middle, hidden_messages[0]),
        gains,
        out_full,
        scalars=(me,),
        scratch=[((n, rows, head_cols), BF16)],
    )
    grad_heads = deliver(grad_heads, "shard", 1)
    hidden_sums += [exchange(after(message, *grad_heads)) for message in hidden_messages[1:]]
    out_pieces = call(
        out_weights_kernel,
        "out_weights",
        [((n, piece, width), BF16)] * reps,
        attended,
        grad_branch,
        scalars=(rep,),
        scratch=[((n, reps, piece, width), BF16)],
    )
    down_other, down_mine = [
        call(down_kernel, "down", [((reps, rows, width), BF16)], after(hidden, out_pieces[0]), w_down_in)[0]
        for hidden in (hidden_other, hidden_mine)
    ]

    grad_qkv, *attention_pieces = call(
        lambda *r: attend_back_kernel(n, reps, *r),
        "attend_back",
        [((length, qkv_cols), BF16)] + [((n, piece, qkv_cols), BF16)] * reps,
        *grad_heads,
        first_all,
        query,
        key,
        value,
        cosines,
        sines,
        after(start, down_mine, down_other),
        scalars=(rep, me),
        scratch=[(head_shape, BF16)] + [(head_shape, F32)] * 2 + [((n, reps, piece, qkv_cols), BF16)],
    )

    def first_side(grads, side):
        return call(
            lambda *r: first_grad_kernel(rows, side, *r),
            "first_grad",
            [((nz, rows, width), BF16)],
            grads,
            w_qkv,
            scalars=(me,),
        )[0]

    first_other = first_side(grad_qkv, 1)
    first_mine = first_side(after(grad_qkv, first_other), 0)
    first_sums = call(
        pair_sum_kernel, "pair_sum", [(own_block, BF16)] * nz, first_mine, swap(first_other, "shard", 1)
    )
    first_parts = deliver(first_sums, "shard", 2)
    (input_grad,) = call(
        lambda *r: input_grad_kernel(n, own, nz, *r),
        "input_grad",
        [((rows, D), F32)],
        *first_parts,
        tokens_in,
        gains,
        grad_middle,
    )

    def owner_pieces(pieces, *earlier):
        parts = deliver(pieces, "rep", 1)
        parts[0] = after(parts[0], *earlier)
        (summed,) = call(
            lambda *r: rep_sum_kernel(reps, *r), "rep_sum", [(pieces[0].shape, BF16)], *parts
        )
        return exchange(summed)

    gain_cols = [gain.astype(F32)[:, None] for gain in (norm_one, norm_two)]
    attention_parts = spread(owner_pieces(attention_pieces, first_sums[0]), "rep", 1)
    grad_w_query, grad_w_key, grad_w_value, grad_norm_one = call(
        lambda *r: attention_out_kernel(n, reps, *r),
        "attention_out",
        [(w_query.shape, F32), (w_key.shape, F32), (w_value.shape, F32), ((own, 1), F32)],
        *attention_parts,
        w_query,
        w_key,
        w_value,
        gain_cols[0],
        scalars=(rep,),
        scratch=[((reps, n, piece, qkv_cols), F32)],
    )

    (out_piece,) = call(owner_sum_kernel, "owner_sum", [((piece, width), BF16)], owner_pieces(out_pieces, first_sums[0]))
    (grad_w_out,) = call(
        lambda *r: out_out_kernel(n, reps, *r),
        "out_out",
        [(w_out.shape, F32)],
        *spread(out_piece, "rep", 1),
        scalars=(rep,),
        scratch=[((reps, piece, width), F32)],
    )

    (core_sums,) = call(core_sums_kernel, "core_sums", [((2, msg_rows, 2 * units), BF16)], *hidden_sums)
    grad_w_gate, grad_w_up, grad_w_down, grad_norm_two = call(
        lambda *r: hidden_out_kernel(n, reps, each, *r),
        "hidden_out",
        [(w_gate.shape, F32), (w_up.shape, F32), (w_down.shape, F32), ((own, 1), F32)],
        *spread(core_sums, "rep", 1),
        w_gate,
        w_up,
        gain_cols[1],
        scalars=(rep,),
        scratch=[((2 * reps, msg_rows, 2 * units), BF16)],
    )

    (output,) = call(
        lambda *r: output_kernel(n, own, *r),
        "output",
        [((rows, D), BF16)],
        middle,
        *plane_sums(after(down_mine, first_sums[0]), down_other)[1],
    )
    return (
        output,
        input_grad,
        grad_norm_one[:, 0],
        grad_w_query,
        grad_w_key,
        grad_w_value,
        grad_w_out,
        grad_norm_two[:, 0],
        grad_w_gate,
        grad_w_up,
        grad_w_down,
    )


def solution(mesh):
    rows = P("shard", None)
    own_tokens = P(("rep", "shard"), None)
    return jax.shard_map(
        shards,
        mesh=mesh,
        in_specs=(
            own_tokens,
            P("rep", None),
            P("shard"),
            rows,
            rows,
            rows,
            rows,
            P("shard"),
            rows,
            rows,
            rows,
            own_tokens,
        ),
        out_specs=(
            own_tokens,
            own_tokens,
            P("shard"),
            rows,
            rows,
            rows,
            rows,
            P("shard"),
            rows,
            rows,
            rows,
        ),
        check_vma=False,
    )
```

```python
import jax
import jax.numpy as jnp
from jax import lax
from jax.experimental import pallas as pl
from jax.experimental.pallas import tpu as pltpu
from jax.sharding import PartitionSpec as P

D = 960
QH = 15
KVH = 5
HD = 64
FF = 2560
GROUP = QH // KVH

EPS = 1e-05
ROPE_BASE = 10000.0
MASKED = -1e30
SCALE = HD ** (-0.5)
BF16 = jnp.bfloat16
F32 = jnp.float32


def doc_layout(lengths_row, length):
    places = jnp.arange(length, dtype=jnp.int32)
    doc_ends = jnp.cumsum(lengths_row)
    passed = places[:, None] >= doc_ends[None, :]
    doc_start = jnp.sum(jnp.where(passed, lengths_row[None, :], 0), axis=1)
    return (doc_start, places - doc_start)


def rope_tables(position):
    half_dim = HD // 2
    fraction = jnp.arange(half_dim, dtype=F32) * (2.0 / HD)
    inverse = ROPE_BASE ** (-fraction)
    angles = position.astype(F32)[:, None] * inverse[None, :]
    return (jnp.cos(angles), jnp.sin(angles))


VMEM_LIMIT = 56 * 2**20


def dot(left, right):
    return jnp.dot(left, right, preferred_element_type=F32)


def contract_rows(left, right):
    return lax.dot_general(left, right, (((0,), (0,)), ((), ())), preferred_element_type=F32)


def contract_cols(left, right):
    return lax.dot_general(left, right, (((1,), (1,)), ((), ())), preferred_element_type=F32)


def inverse_rms(values):
    return lax.rsqrt(jnp.sum(values * values, axis=-1, keepdims=True) * (1.0 / D) + EPS)


def norm_backward(values, inverse, gain, grad_norm):
    scaled = grad_norm * gain
    mean = jnp.sum(scaled * values, axis=-1, keepdims=True) * (1.0 / D)
    return inverse * scaled - values * inverse**3 * mean


def round_up(value, step):
    return -(-value // step) * step


def rows_at(index, rows):
    return pl.ds(pl.multiple_of(index * rows, rows), rows)


def to_blocks(values, n, width):
    rows, own = values.shape[0], values.shape[1] // n
    gap = jnp.zeros((rows, width // n - own), values.dtype)
    parts = []
    for s in range(n):
        parts += [values[:, s * own : (s + 1) * own], gap]
    return jnp.concatenate(parts, axis=1)


def from_blocks(values, n, own):
    block = values.shape[1] // n
    return jnp.concatenate([values[:, s * block : s * block + own] for s in range(n)], axis=1)


def swap(block, axis, k):
    count = lax.axis_size(axis)
    return lax.ppermute(block, axis, [(i, i ^ k) for i in range(count)])


def exchange(block):
    return lax.all_to_all(block, "shard", split_axis=0, concat_axis=0, tiled=True)


def spread(block, axis, step):
    return [block] + [swap(block, axis, k) for k in range(step, lax.axis_size(axis), step)]


def deliver(blocks, axis, step):
    return [blocks[0]] + [swap(block, axis, i * step) for i, block in enumerate(blocks) if i]


def exchange_z(blocks):
    groups = [list(range(core, lax.axis_size("shard"), 2)) for core in range(2)]
    return lax.all_to_all(
        blocks, "shard", split_axis=0, concat_axis=0, axis_index_groups=groups, tiled=True
    )


def after(value, *earlier):
    return lax.optimization_barrier((value,) + earlier)[0]


def later(values, *earlier):
    values = tuple(values)
    return list(lax.optimization_barrier(values + earlier)[: len(values)])


def both_cores(parts):
    stacked = jnp.stack(parts)
    return stacked, swap(stacked, "shard", 1)


def call(kernel, name, outs, *operands, scalars=(), scratch=()):
    specs = [pl.BlockSpec(memory_space=pltpu.SMEM)] * len(scalars)
    specs += [pl.BlockSpec(memory_space=pltpu.VMEM)] * len(operands)
    return pl.pallas_call(
        kernel,
        out_shape=[jax.ShapeDtypeStruct(shape, dtype) for shape, dtype in outs],
        in_specs=specs,
        out_specs=[pl.BlockSpec(memory_space=pltpu.VMEM)] * len(outs),
        scratch_shapes=[pltpu.VMEM(shape, dtype) for shape, dtype in scratch],
        compiler_params=pltpu.CompilerParams(vmem_limit_bytes=VMEM_LIMIT),
        name=name,
    )(*scalars, *operands)


def turned(values):
    half = HD // 2
    parts = []
    for begin in range(0, values.shape[1], HD):
        parts.append(-values[:, begin + half : begin + HD])
        parts.append(values[:, begin : begin + half])
    return jnp.concatenate(parts, axis=1)


def widened(values, times):
    return jnp.concatenate([values] * times, axis=1)


def head_of(values, h, heads):
    if heads == 1:
        return values
    lane = lax.broadcasted_iota(jnp.int32, values.shape, 1)
    return jnp.where(lane // HD == h, values, jnp.zeros_like(values))


def masked_probs(query, key, starts, row):
    rows, cols = query.shape[0], key.shape[0]
    logits = contract_cols(query, key) * SCALE
    place = lax.broadcasted_iota(jnp.int32, (rows, cols), 1)
    own = lax.broadcasted_iota(jnp.int32, (rows, cols), 0) + row
    logits = jnp.where((place <= own) & (place >= starts), logits, MASKED)
    raised = jnp.exp(logits - jnp.max(logits, axis=-1, keepdims=True))
    return raised * (1.0 / jnp.sum(raised, axis=-1, keepdims=True))


def blocks_kernel(n, in_ref, *out_refs):
    values = to_blocks(in_ref[...].astype(F32).T, n, out_refs[0].shape[1]).astype(BF16)
    out_refs[0][...] = values
    for ref in out_refs[1:]:
        for i in range(ref.shape[0]):
            ref[i] = values


def attention_message_kernel(n, rep_ref, q_ref, k_ref, v_ref, out_ref, gain_ref, msg_ref):
    own = q_ref.shape[0]
    piece = msg_ref.shape[1]
    cols = gain_ref.shape[1]
    half = msg_ref.shape[2] - cols
    head_cols = cols // 3
    heads = head_cols // HD
    row = lax.broadcasted_iota(jnp.int32, (piece, own), 0) + rep_ref[0] * piece
    pick = jnp.where(row == lax.broadcasted_iota(jnp.int32, (piece, own), 1), 1.0, 0.0).astype(BF16)
    query, key, value = dot(pick, q_ref[...]), contract_cols(pick, k_ref[...]), contract_cols(pick, v_ref[...])
    gap = jnp.zeros((piece, HD), F32)
    wide = lax.broadcasted_iota(jnp.int32, (piece, cols), 0) + rep_ref[0] * piece
    for s in range(n):
        slots = range(s * heads, (s + 1) * heads)
        parts = [query[:, h * HD : (h + 1) * HD] if h < QH else gap for h in slots]
        for array in (key, value):
            for h in slots:
                j = h // GROUP
                parts.append(array[:, j * HD : (j + 1) * HD] if h < QH else gap)
        block = jnp.concatenate(parts, axis=1)
        for i in range(2):
            block = jnp.where(wide == own + i, gain_ref[i : i + 1, :], block)
        msg_ref[s, :, :cols] = block.astype(BF16)
    rows = to_blocks(dot(pick, out_ref[...]), n, 2 * half).astype(BF16)
    for s in range(n):
        msg_ref[s, :, cols:] = rows[:, s % 2 * half : (s % 2 + 1) * half]


def as_row(column):
    return jnp.broadcast_to(column, (column.shape[0], 128)).T[0:1, :]


def join_kernel(reps, rep_ref, *refs):
    for i in range(reps):
        refs[reps][:, rep_ref[0] ^ i] = refs[i][...]


def join_out_kernel(reps, rep_ref, core_ref, mine_ref, other_ref, out_ref):
    first = core_ref[0] == 0
    half = mine_ref.shape[3]
    for i in range(reps):
        mine, other = mine_ref[i], other_ref[i]
        out_ref[:, rep_ref[0] ^ i, :, :half] = jnp.where(first, mine, other)
        out_ref[:, rep_ref[0] ^ i, :, half:] = jnp.where(first, other, mine)


def fill_rows(values, rows):
    if values.shape[0] == rows:
        return values
    return jnp.concatenate([values, jnp.zeros((rows - values.shape[0], values.shape[1]), F32)], axis=0)


def fill_cols(values, cols):
    if values.shape[1] == cols:
        return values
    return jnp.concatenate([values, jnp.zeros((values.shape[0], cols - values.shape[1]), F32)], axis=1)


def message_plan(own, each, cols):
    top, rows = round_up(own, 8), round_up(each, 8)
    rest = D % cols
    halved = rest and 2 * rest <= cols
    first = round_up(rows // 2, 8) if halved else rows
    total = top + D // cols * rows + (first if rest else 0)
    return top, rows, rest, halved, first, total


def pack_message(both, down, cols):
    top, rows, rest, halved, first, _ = message_plan(both.shape[0], down.shape[0], cols)
    down = fill_rows(down, rows)
    parts = [fill_rows(both, top)]
    parts += [down[:, j * cols : (j + 1) * cols] for j in range(D // cols)]
    if rest:
        tail = down[:, D - rest :]
        if halved:
            tail = jnp.concatenate([tail[:first], fill_rows(tail[first:], first)], axis=1)
        parts.append(fill_cols(tail, cols))
    return jnp.concatenate(parts, axis=0)


def unpack_message(message, own, each):
    cols = message.shape[1]
    top, rows, rest, halved, first, _ = message_plan(own, each, cols)
    parts = [message[top + j * rows : top + (j + 1) * rows] for j in range(D // cols)]
    if rest:
        tail = message[top + D // cols * rows :][:first]
        if halved:
            tail = jnp.concatenate([tail[:, :rest], tail[: rows - first, rest : 2 * rest]], axis=0)
        parts.append(tail[:, :rest])
    return message[:own], jnp.concatenate(parts, axis=1)[:each]


def hidden_message_kernel(n, reps, rep_ref, gate_ref, up_ref, down_ref, *out_refs):
    own, units = gate_ref.shape
    held = down_ref.shape[0]
    each = held // (2 * reps)
    cols = n * each
    place = lax.broadcasted_iota(jnp.int32, (1, cols), 1)
    row = lax.broadcasted_iota(jnp.int32, (round_up(each, 8), held), 0)
    for i in range(2):
        begin = each * (2 * rep_ref[0] + i)
        unit = place + begin
        for s in range(1, n):
            unit = unit + jnp.where(place >= each * s, held - each, 0)
        pick = jnp.where(lax.broadcasted_iota(jnp.int32, (units, cols), 0) == unit, 1.0, 0.0)
        pick = pick.astype(BF16)
        both = jnp.concatenate([dot(gate_ref[...], pick), dot(up_ref[...], pick)], axis=1)
        take = (lax.broadcasted_iota(jnp.int32, row.shape, 1) == row + begin) & (row < each)
        down = dot(jnp.where(take, 1.0, 0.0).astype(BF16), down_ref[...])
        message = pack_message(both, down[:each], 2 * cols).astype(BF16)
        for z in range(n // 2):
            split_rows([ref.at[2 * z + i] for ref in out_refs], message)


def split_rows(refs, values):
    begin = 0
    for ref in refs:
        rows = ref.shape[0]
        ref[...] = values[begin : begin + rows]
        begin += rows


def hidden_weights_in_kernel(n, own, each, *refs):
    parts, (w_ref, down_ref) = refs[:-2], refs[-2:]
    block = w_ref.shape[1]
    downs = []
    for s in range(n):
        message = jnp.concatenate([part[s].astype(F32) for part in parts], axis=0)
        both, down = unpack_message(message, own, each)
        w_ref[s] = fill_rows(both, block).astype(BF16)
        downs.append(down)
    down_ref[...] = to_blocks(jnp.concatenate(downs, axis=0), n, down_ref.shape[1]).astype(BF16)


def attend_kernel(rows, n, me_ref, mine_ref, other_ref, *refs):
    w_ref, cos_ref, sin_ref, start_ref, first_ref, q_ref, k_ref, v_ref, gains_ref = refs[:9]
    part_refs, mixed_ref = refs[9:-1], refs[-1]
    core = me_ref[0] % 2
    length, head_cols = q_ref.shape
    heads = head_cols // HD
    width = first_ref.shape[1]
    block_rows = width // n
    own = D // n
    gap = jnp.zeros((1, block_rows - own), F32)
    gains = []
    for i in range(2):
        parts = []
        for s in range(n):
            group = w_ref[pl.ds(s * block_rows + own // 16 * 16, block_rows - own // 16 * 16), :]
            row = own % 16 + i
            spread_row = group.astype(F32)[row : row + 1, :own]
            parts += [spread_row, gap]
        gains.append(jnp.concatenate(parts, axis=1))
        gains_ref[i : i + 1, :] = gains[i]
    for side, ref in enumerate((mine_ref, other_ref)):
        for z in range(n // 2):
            inputs = ref[z].astype(F32)
            normed = inputs * inverse_rms(inputs) * gains[0]
            first_ref[rows_at(2 * z + (core ^ side), rows), :] = normed.astype(BF16)
    block = min(256, length)
    for i in range(length // block):
        span = pl.ds(i * block, block)
        raw = dot(first_ref[span, :], w_ref[...])
        cosines, sines = widened(cos_ref[span, :], 2 * heads), widened(sin_ref[span, :], 2 * heads)
        query, key = raw[:, :head_cols], raw[:, head_cols : 2 * head_cols]
        q_ref[span, :] = (query * cosines + turned(query) * sines).astype(BF16)
        k_ref[span, :] = (key * cosines + turned(key) * sines).astype(BF16)
        v_ref[span, :] = raw[:, 2 * head_cols :].astype(BF16)
    for i in range(length // block):
        span, past = pl.ds(i * block, block), pl.ds(0, (i + 1) * block)
        total = None
        for h in range(heads):
            probs = masked_probs(
                head_of(q_ref[span, :], h, heads), k_ref[past, :], start_ref[span, :], i * block
            )
            mixed = head_of(dot(probs.astype(BF16), v_ref[past, :]), h, heads)
            total = mixed if total is None else total + mixed
        mixed_ref[span, :] = total.astype(BF16)
    for i, ref in enumerate(part_refs):
        ref[...] = mixed_ref[rows_at(me_ref[0] ^ i, rows), :]


def attend_back_kernel(n, reps, rep_ref, me_ref, *refs):
    parts, refs = refs[:n], refs[n:]
    first_ref, q_ref, k_ref, v_ref, cos_ref, sin_ref, start_ref, dqkv_ref = refs[:8]
    piece_refs, (g_ref, dk_ref, dv_ref, hold_ref) = refs[8 : 8 + reps], refs[8 + reps :]
    for i, ref in enumerate(parts):
        g_ref[rows_at(me_ref[0] ^ i, ref.shape[0]), :] = ref[...]
    length, head_cols = q_ref.shape
    heads = head_cols // HD
    block = min(256, length)
    dk_ref[...] = jnp.zeros_like(dk_ref)
    dv_ref[...] = jnp.zeros_like(dv_ref)
    for i in range(length // block):
        span, past = pl.ds(i * block, block), pl.ds(0, (i + 1) * block)
        total = None
        for h in range(heads):
            query = head_of(q_ref[span, :], h, heads)
            grad = head_of(g_ref[span, :], h, heads)
            key = k_ref[past, :]
            probs = masked_probs(query, key, start_ref[span, :], i * block)
            grad_probs = contract_cols(grad, v_ref[past, :])
            delta = jnp.sum(probs * grad_probs, axis=-1, keepdims=True)
            grad_logits = (probs * (grad_probs - delta)).astype(BF16)
            grad_query = head_of(dot(grad_logits, key), h, heads)
            total = grad_query if total is None else total + grad_query
            dv_ref[past, :] += contract_rows(probs.astype(BF16), grad)
            dk_ref[past, :] += contract_rows(grad_logits, query)
        total = total * SCALE
        cosines, sines = widened(cos_ref[span, :], 2 * heads), widened(sin_ref[span, :], 2 * heads)
        back = total * cosines - turned(total) * sines
        dqkv_ref[span, :head_cols] = back.astype(BF16)
    for i in range(length // block):
        span = pl.ds(i * block, block)
        total = dk_ref[span, :] * SCALE
        cosines, sines = widened(cos_ref[span, :], 2 * heads), widened(sin_ref[span, :], 2 * heads)
        back = total * cosines - turned(total) * sines
        dqkv_ref[span, head_cols : 2 * head_cols] = back.astype(BF16)
        dqkv_ref[span, 2 * head_cols :] = dv_ref[span, :].astype(BF16)
    store_pieces(rep_ref, piece_refs, hold_ref, contract_rows(first_ref[...], dqkv_ref[...]))


def store_pieces(rep_ref, piece_refs, hold_ref, grad):
    n, reps, piece, _ = hold_ref.shape
    for s in range(n):
        for r in range(reps):
            begin = (s * reps + r) * piece
            hold_ref[s, r] = grad[begin : begin + piece].astype(BF16)
    for i, ref in enumerate(piece_refs):
        for s in range(n):
            ref[s] = hold_ref[s, rep_ref[0] ^ i]


def first_grad_kernel(rows, side, me_ref, dqkv_ref, w_ref, out_ref):
    for z in range(out_ref.shape[0]):
        part = dqkv_ref[rows_at(me_ref[0] ^ (2 * z + side), rows), :]
        out_ref[z] = contract_cols(part, w_ref[...]).astype(BF16)


def pair_sum_kernel(mine_ref, other_ref, *out_refs):
    for i, ref in enumerate(out_refs):
        ref[...] = (mine_ref[i].astype(F32) + other_ref[i].astype(F32)).astype(BF16)


def middle_kernel(n, me_ref, tokens_ref, *refs):
    parts, refs = refs[:n], refs[n:]
    w_ref, gains_ref, middle_ref, second_ref, attended_ref, hold_ref = refs
    width = tokens_ref.shape[1]
    for i, ref in enumerate(parts):
        hold_ref[me_ref[0] ^ i] = ref[...]
    attended = jnp.concatenate([hold_ref[s] for s in range(n)], axis=1)[:, :D]
    attended = to_blocks(attended.astype(F32), n, width).astype(BF16)
    attended_ref[...] = attended
    middle = tokens_ref[...].astype(F32) + dot(attended, w_ref[...])
    middle_ref[...] = middle
    second_ref[...] = (middle * inverse_rms(middle) * gains_ref[1:2, :]).astype(BF16)


def stacked(ref, begin=0, count=None):
    count = ref.shape[0] if count is None else count
    return jnp.concatenate([ref[begin + i] for i in range(count)], axis=0)


def hidden_kernel(second_ref, cot_ref, w_ref, down_ref, grad_ref, grads_ref, hidden_ref):
    reps, rows, _ = second_ref.shape
    units = down_ref.shape[0]
    for i in range(0, reps, 2):
        span = pl.ds(i * rows, 2 * rows)
        both = dot(stacked(second_ref, i, 2), w_ref[...])
        gate, up = both[:, :units], both[:, units:]
        grad_hidden = contract_cols(stacked(cot_ref, i, 2), down_ref[...])
        sigmoid = 1.0 / (1.0 + jnp.exp(-gate))
        silu = gate * sigmoid
        hidden_ref[span, :] = (silu * up).astype(BF16)
        grad_gate = grad_hidden * up * sigmoid * (1.0 + gate * (1.0 - sigmoid))
        grads = jnp.concatenate([grad_gate, grad_hidden * silu], axis=1).astype(BF16)
        grads_ref[span, :] = grads
        grad = contract_cols(grads, w_ref[...]).astype(BF16)
        for j in range(2):
            grad_ref[i + j] = grad[j * rows : (j + 1) * rows]


def hidden_weights_kernel(n, own, each, *refs):
    second_a, second_b, cot_a, cot_b, grads_a, grads_b, hidden_a, hidden_b, *msg_refs = refs
    cols = msg_refs[0].shape[2]
    grad = contract_rows(stacked(second_a), grads_a[...])
    grad = grad + contract_rows(stacked(second_b), grads_b[...])
    down = contract_rows(hidden_a[...], stacked(cot_a)) + contract_rows(hidden_b[...], stacked(cot_b))
    down = from_blocks(down, n, own)
    block = grad.shape[0] // n
    for s in range(n):
        both = grad[s * block : s * block + own]
        message = pack_message(both, down[s * each : (s + 1) * each], cols).astype(BF16)
        split_rows([ref.at[s] for ref in msg_refs], message)


def core_sums_kernel(*refs):
    out_ref = refs[-1]
    for core in range(2):
        sums = [
            sum(part[s].astype(F32) for s in range(core, part.shape[0], 2)) for part in refs[:-1]
        ]
        out_ref[core] = jnp.concatenate(sums, axis=0).astype(BF16)


def hidden_out_kernel(n, reps, each, rep_ref, *refs):
    parts, refs = refs[:reps], refs[reps:]
    gate_w_ref, up_w_ref, gain_ref, gate_ref, up_ref, down_ref, norm_ref, hold_ref = refs
    own = gate_ref.shape[0]
    units = 2 * reps * each
    for i, part in enumerate(parts):
        hold_ref[rep_ref[0] ^ i] = part[...]
    cols = hold_ref.shape[3]
    boths = []
    for f in range(2 * reps):
        both, down = unpack_message(hold_ref[f // 2, f % 2].astype(F32), own, each)
        boths.append(both)
        down_ref[f * each : (f + 1) * each, :] = down
    total = jnp.zeros((own, 1), F32)
    for begin, w_ref, out_ref in ((0, gate_w_ref, gate_ref), (cols // 2, up_w_ref, up_ref)):
        for s in range(n):
            place = begin + s * each
            rows = jnp.concatenate([part[:, place : place + each] for part in boths], axis=1)
            span = slice(s * units, (s + 1) * units)
            out_ref[:, span] = rows
            total = total + jnp.sum(rows * w_ref[:, span].astype(F32), axis=1, keepdims=True)
    norm_ref[...] = as_row(total) / gain_ref[...]


def down_kernel(hidden_ref, w_ref, out_ref):
    rows = out_ref.shape[1]
    for i in range(0, out_ref.shape[0], 2):
        both = dot(hidden_ref[pl.ds(i * rows, 2 * rows), :], w_ref[...]).astype(BF16)
        for j in range(2):
            out_ref[i + j] = both[j * rows : (j + 1) * rows]


def output_kernel(n, own, middle_ref, *refs):
    total = middle_ref[...]
    for ref in refs[:-1]:
        total = total + ref[...].astype(F32)
    refs[-1][...] = from_blocks(total, n, own).T.astype(BF16)


def middle_grad_kernel(n, own, reps, me_ref, *refs):
    parts, refs = refs[:reps], refs[reps:]
    cot_ref, middle_ref, gains_ref, w_ref, grad_ref, branch_ref = refs[:6]
    part_refs, hold_ref = refs[6:-1], refs[-1]
    rows = middle_ref.shape[0]
    middle = middle_ref[...]
    grad_second = sum(ref[...].astype(F32) for ref in parts)
    grad = cot_ref[...].astype(F32) + norm_backward(
        middle, inverse_rms(middle), gains_ref[1:2, :], grad_second
    )
    grad_ref[...] = grad
    branch = grad.astype(BF16)
    branch_ref[...] = branch
    attended = from_blocks(contract_cols(branch, w_ref[...]), n, own)
    head_cols = hold_ref.shape[2]
    if n * head_cols > D:
        attended = jnp.concatenate([attended, jnp.zeros((rows, n * head_cols - D), F32)], axis=1)
    for s in range(n):
        hold_ref[s] = attended[:, s * head_cols : (s + 1) * head_cols].astype(BF16)
    for i, ref in enumerate(part_refs):
        ref[...] = hold_ref[me_ref[0] ^ i]


def out_weights_kernel(rep_ref, attended_ref, branch_ref, *refs):
    store_pieces(rep_ref, refs[:-1], refs[-1], contract_rows(attended_ref[...], branch_ref[...]))


def rep_sum_kernel(reps, *refs):
    total = sum(ref[...].astype(F32) for ref in refs[:reps])
    refs[reps][...] = total.astype(BF16)


def owner_sum_kernel(in_ref, out_ref):
    out_ref[...] = jnp.sum(in_ref[...].astype(F32), axis=0).astype(BF16)


def out_out_kernel(n, reps, rep_ref, *refs):
    out_ref, hold_ref = refs[reps:]
    for i in range(reps):
        hold_ref[rep_ref[0] ^ i] = refs[i][...].astype(F32)
    own = out_ref.shape[0]
    rows = jnp.concatenate([hold_ref[r] for r in range(reps)], axis=0)[:own]
    out_ref[...] = from_blocks(rows, n, own)


def attention_out_kernel(n, reps, rep_ref, *refs):
    parts, refs = refs[:reps], refs[reps:]
    q_w_ref, k_w_ref, v_w_ref, gain_ref, q_ref, k_ref, v_ref, norm_ref, hold_ref = refs
    own = q_ref.shape[0]
    cols = parts[0].shape[2]
    head_cols = cols // 3
    heads = head_cols // HD
    for i, part in enumerate(parts):
        for s in range(n):
            hold_ref[rep_ref[0] ^ i, s] = part[s].astype(F32)
    sides = [
        jnp.concatenate([hold_ref[r, s] for r in range(reps)], axis=0)[:own] for s in range(n)
    ]

    def slot(h, kind):
        begin = kind * head_cols + h % heads * HD
        return sides[h // heads][:, begin : begin + HD]

    query = jnp.concatenate([slot(h, 0) for h in range(QH)], axis=1)
    q_ref[...] = query
    total = jnp.sum(query * q_w_ref[...].astype(F32), axis=1, keepdims=True)
    total = as_row(total)
    for kind, w_ref, out_ref in ((1, k_w_ref, k_ref), (2, v_w_ref, v_ref)):
        wide = jnp.concatenate(
            [sum(slot(j * GROUP + g, kind) for g in range(GROUP)) for j in range(KVH)], axis=1
        ).T
        out_ref[...] = wide
        total = total + jnp.sum(wide * w_ref[...].astype(F32), axis=0, keepdims=True)
    norm_ref[...] = total / gain_ref[...]


def input_grad_kernel(n, own, nz, *refs):
    parts, (tokens_ref, gains_ref, grad_ref, out_ref) = refs[:nz], refs[nz:]
    inputs = tokens_ref[...].astype(F32)
    grad_first = sum(ref[...].astype(F32) for ref in parts)
    total = grad_ref[...] + norm_backward(inputs, inverse_rms(inputs), gains_ref[0:1, :], grad_first)
    out_ref[...] = from_blocks(total, n, own).T


def shards(
    tokens,
    lengths,
    norm_one,
    w_query,
    w_key,
    w_value,
    w_out,
    norm_two,
    w_gate,
    w_up,
    w_down,
    cotangent,
):
    n = lax.axis_size("shard")
    reps = lax.axis_size("rep")
    nz = n // 2
    rows = tokens.shape[0]
    length = rows * n
    own = w_query.shape[0]
    held = w_down.shape[0]
    block = round_up(own + 2, 16)
    width = n * block
    piece = block // reps
    heads = -(-QH // n)
    head_cols = heads * HD
    qkv_cols = 3 * head_cols
    each = held // (2 * reps)
    units = n * each
    msg_rows = message_plan(own, each, 2 * units)[-1]
    shard_index = lax.axis_index("shard").astype(jnp.int32)
    me = shard_index.reshape(1)
    core = (shard_index % 2).reshape(1)
    rep = lax.axis_index("rep").astype(jnp.int32).reshape(1)
    own_block = (rows, width)

    tokens_in, tokens_tiled = call(
        lambda *r: blocks_kernel(n, *r),
        "tokens_blocks",
        [(own_block, BF16), ((nz,) + own_block, BF16)],
        tokens.T,
    )
    gains_own = jnp.pad(jnp.stack([norm_one, norm_two]), ((0, 0), (0, qkv_cols - own))).astype(F32)
    (message,) = call(
        lambda *r: attention_message_kernel(n, *r),
        "attention_message",
        [((n, piece, qkv_cols + width // 2), BF16)],
        after(w_query, tokens_in),
        w_key.T,
        w_value.T,
        w_out,
        gains_own,
        scalars=(rep,),
    )
    arrived = exchange(message)
    (w_qkv,) = call(
        lambda *r: join_kernel(reps, *r),
        "join_qkv",
        [((n, reps, piece, qkv_cols), BF16)],
        *spread(arrived[:, :, :qkv_cols], "rep", 1),
        scalars=(rep,),
    )
    w_qkv = w_qkv.reshape(width, qkv_cols)
    tokens_mine = exchange_z(after(tokens_tiled, arrived))
    tokens_other = swap(tokens_mine, "shard", 1)
    (cot_in,) = call(
        lambda *r: blocks_kernel(n, *r), "cot_blocks", [(own_block, BF16)], after(cotangent.T, message)
    )
    cot_parts = spread(after(cot_in, w_qkv), "rep", 1)
    doc_start, position = doc_layout(after(lengths, cot_in)[0], length)
    cosines, sines = rope_tables(position)
    start = doc_start[:, None]

    split = msg_rows // 2 // 16 * 16 + 16
    part_rows = (split, msg_rows - split) if split < msg_rows else (msg_rows,)
    messages = call(
        lambda *r: hidden_message_kernel(n, reps, *r),
        "hidden_message",
        [((n, part, 2 * units), BF16) for part in part_rows],
        after(w_gate, cosines, sines, start),
        w_up,
        w_down,
        scalars=(rep,),
    )
    hidden_first = exchange(after(messages[0], tokens_mine))

    out_parts = spread(after(arrived, w_qkv)[:, :, qkv_cols:], "rep", 1)

    head_shape = (length, head_cols)
    first_all, query, key, value, gains, *mixed = call(
        lambda *r: attend_kernel(rows, n, *r),
        "attend",
        [((length, width), BF16)]
        + [(head_shape, BF16)] * 3
        + [((2, width), F32)]
        + [((rows, head_cols), BF16)] * n,
        tokens_mine,
        tokens_other,
        w_qkv,
        cosines,
        sines,
        after(start, messages[0]),
        scalars=(me,),
        scratch=[(head_shape, BF16)],
    )
    mixed = deliver(later(mixed, hidden_first), "shard", 1)
    hidden_rest = [exchange(after(message, *mixed)) for message in messages[1:]]
    (out_full,) = call(
        lambda *r: join_out_kernel(reps, *r),
        "join_out",
        [((n, reps, piece, width), BF16)],
        *both_cores([after(out_parts[0], gains)] + out_parts[1:]),
        scalars=(rep, core),
    )
    out_full = out_full.reshape(width, width)

    middle, second, attended = call(
        lambda *r: middle_kernel(n, *r),
        "middle",
        [(own_block, F32), (own_block, BF16), (own_block, BF16)],
        tokens_in,
        *mixed,
        out_full,
        gains,
        scalars=(me,),
        scratch=[((n, rows, head_cols), BF16)],
    )
    w_hidden, w_down_in = call(
        lambda *r: hidden_weights_in_kernel(n, own, each, *r),
        "hidden_weights_in",
        [((n, block, 2 * units), BF16), ((units, width), BF16)],
        after(hidden_first, second),
        *hidden_rest,
    )
    w_hidden = w_hidden.reshape(width, 2 * units)
    cot_mine, cot_other = both_cores([after(cot_parts[0], out_full)] + cot_parts[1:])

    second_mine, second_other = both_cores(spread(second, "rep", 1))
    side_outs = [
        ((reps, rows, width), BF16),
        ((reps * rows, 2 * units), BF16),
        ((reps * rows, units), BF16),
    ]

    def hidden_side(seconds, cots, name):
        return call(hidden_kernel, name, side_outs, seconds, cots, w_hidden, w_down_in)

    def plane_sums(mine, other):
        sums = call(pair_sum_kernel, "pair_sum", [(own_block, BF16)] * reps, mine, swap(other, "shard", 1))
        return sums, deliver(sums, "rep", 1)

    grad_other, grads_other, hidden_other = hidden_side(second_other, cot_other, "hidden_other")
    grad_mine, grads_mine, hidden_mine = hidden_side(
        after(second_mine, grad_other), cot_mine, "hidden_mine"
    )
    sums, grad_second = plane_sums(grad_mine, grad_other)
    hidden_messages = call(
        lambda *r: hidden_weights_kernel(n, own, each, *r),
        "hidden_weights",
        [((n, part, 2 * units), BF16) for part in part_rows],
        second_mine,
        second_other,
        cot_mine,
        cot_other,
        grads_mine,
        grads_other,
        after(hidden_mine, sums[0]),
        hidden_other,
    )
    hidden_sums = [exchange(hidden_messages[0])]
    down_other, down_mine = [
        call(
            down_kernel,
            "down",
            [((reps, rows, width), BF16)],
            after(hidden, hidden_messages[0]),
            w_down_in,
        )[0]
        for hidden in (hidden_other, hidden_mine)
    ]

    grad_middle, grad_branch, *grad_heads = call(
        lambda *r: middle_grad_kernel(n, own, reps, *r),
        "middle_grad",
        [(own_block, F32), (own_block, BF16)] + [((rows, head_cols), BF16)] * n,
        *grad_second,
        cot_in,
        after(middle, down_other, down_mine),
        gains,
        out_full,
        scalars=(me,),
        scratch=[((n, rows, head_cols), BF16)],
    )
    grad_heads = deliver(grad_heads, "shard", 1)
    down_sums, down_parts = plane_sums(after(down_mine, grad_branch), down_other)
    hidden_sums += [exchange(after(message, *grad_heads)) for message in hidden_messages[1:]]
    out_pieces = call(
        out_weights_kernel,
        "out_weights",
        [((n, piece, width), BF16)] * reps,
        attended,
        after(grad_branch, down_sums[0]),
        scalars=(rep,),
        scratch=[((n, reps, piece, width), BF16)],
    )
    grad_qkv, *attention_pieces = call(
        lambda *r: attend_back_kernel(n, reps, *r),
        "attend_back",
        [((length, qkv_cols), BF16)] + [((n, piece, qkv_cols), BF16)] * reps,
        *grad_heads,
        first_all,
        query,
        key,
        value,
        cosines,
        sines,
        after(start, out_pieces[0], hidden_sums[0]),
        scalars=(rep, me),
        scratch=[(head_shape, BF16)] + [(head_shape, F32)] * 2 + [((n, reps, piece, qkv_cols), BF16)],
    )

    def rep_sum(parts, *earlier):
        return call(
            lambda *r: rep_sum_kernel(reps, *r),
            "rep_sum",
            [(parts[0].shape, BF16)],
            after(parts[0], *earlier),
            *parts[1:],
        )[0]

    def first_side(grads, side):
        return call(
            lambda *r: first_grad_kernel(rows, side, *r),
            "first_grad",
            [((nz, rows, width), BF16)],
            grads,
            w_qkv,
            scalars=(me,),
        )[0]

    first_other = first_side(grad_qkv, 1)
    first_mine = first_side(after(grad_qkv, first_other), 0)
    (output,) = call(
        lambda *r: output_kernel(n, own, *r),
        "output",
        [((D, rows), BF16)],
        after(middle, first_mine),
        *down_parts,
    )
    out_summed = rep_sum(deliver(out_pieces, "rep", 1), output)
    attention_summed = rep_sum(deliver(attention_pieces, "rep", 1), out_summed)
    first_sums = call(
        pair_sum_kernel,
        "pair_sum",
        [(own_block, BF16)] * nz,
        after(first_mine, attention_summed, *hidden_sums),
        swap(first_other, "shard", 1),
    )
    first_parts = deliver(first_sums, "shard", 2)
    attention_moved = exchange(after(attention_summed, *hidden_sums))
    (core_sums,) = call(
        core_sums_kernel,
        "core_sums",
        [((2, msg_rows, 2 * units), BF16)],
        after(hidden_sums[0], first_sums[0]),
        *hidden_sums[1:],
    )
    out_moved = exchange(after(out_summed, attention_moved))

    gain_rows = [gain.astype(F32)[None] for gain in (norm_one, norm_two)]
    (input_grad,) = call(
        lambda *r: input_grad_kernel(n, own, nz, *r),
        "input_grad",
        [((D, rows), F32)],
        *first_parts,
        tokens_in,
        gains,
        grad_middle,
    )

    grad_w_gate, grad_w_up, grad_w_down, grad_norm_two = call(
        lambda *r: hidden_out_kernel(n, reps, each, *r),
        "hidden_out",
        [(w_gate.shape, F32), (w_up.shape, F32), (w_down.shape, F32), ((1, own), F32)],
        *spread(core_sums, "rep", 1),
        w_gate,
        w_up,
        after(gain_rows[1], input_grad),
        scalars=(rep,),
        scratch=[((reps, 2, msg_rows, 2 * units), BF16)],
    )

    attention_parts = spread(attention_moved, "rep", 1)
    grad_w_query, grad_w_key, grad_w_value, grad_norm_one = call(
        lambda *r: attention_out_kernel(n, reps, *r),
        "attention_out",
        [(w_query.shape, F32), (w_key.shape[::-1], F32), (w_value.shape[::-1], F32), ((1, own), F32)],
        *attention_parts,
        after(w_query, grad_norm_two),
        w_key.T,
        w_value.T,
        gain_rows[0],
        scalars=(rep,),
        scratch=[((reps, n, piece, qkv_cols), F32)],
    )

    (out_piece,) = call(owner_sum_kernel, "owner_sum", [((piece, width), BF16)], after(out_moved, input_grad))
    (grad_w_out,) = call(
        lambda *r: out_out_kernel(n, reps, *r),
        "out_out",
        [(w_out.shape, F32)],
        *spread(out_piece, "rep", 1),
        scalars=(rep,),
        scratch=[((reps, piece, width), F32)],
    )

    return (
        output.T,
        input_grad.T,
        grad_norm_one[0],
        grad_w_query,
        grad_w_key.T,
        grad_w_value.T,
        grad_w_out,
        grad_norm_two[0],
        grad_w_gate,
        grad_w_up,
        grad_w_down,
    )


def solution(mesh):
    rows = P("shard", None)
    own_tokens = P(("rep", "shard"), None)
    return jax.shard_map(
        shards,
        mesh=mesh,
        in_specs=(
            own_tokens,
            P("rep", None),
            P("shard"),
            rows,
            rows,
            rows,
            rows,
            P("shard"),
            rows,
            rows,
            rows,
            own_tokens,
        ),
        out_specs=(
            own_tokens,
            own_tokens,
            P("shard"),
            rows,
            rows,
            rows,
            rows,
            P("shard"),
            rows,
            rows,
            rows,
        ),
        check_vma=False,
    )
```

```python
import jax
import jax.numpy as jnp
from jax import lax
from jax.experimental import pallas as pl
from jax.experimental.pallas import tpu as pltpu
from jax.sharding import PartitionSpec as P

D = 960
QH = 15
KVH = 5
HD = 64
FF = 2560
GROUP = QH // KVH

EPS = 1e-05
ROPE_BASE = 10000.0
MASKED = -1e30
SCALE = HD ** (-0.5)
BF16 = jnp.bfloat16
F32 = jnp.float32


def doc_layout(lengths_row, length):
    places = jnp.arange(length, dtype=jnp.int32)
    doc_ends = jnp.cumsum(lengths_row)
    passed = places[:, None] >= doc_ends[None, :]
    doc_start = jnp.sum(jnp.where(passed, lengths_row[None, :], 0), axis=1)
    return (doc_start, places - doc_start)


def rope_tables(position):
    half_dim = HD // 2
    fraction = jnp.arange(half_dim, dtype=F32) * (2.0 / HD)
    inverse = ROPE_BASE ** (-fraction)
    angles = position.astype(F32)[:, None] * inverse[None, :]
    return (jnp.cos(angles), jnp.sin(angles))


VMEM_LIMIT = 56 * 2**20


def dot(left, right):
    return jnp.dot(left, right, preferred_element_type=F32)


def contract_rows(left, right):
    return lax.dot_general(left, right, (((0,), (0,)), ((), ())), preferred_element_type=F32)


def contract_cols(left, right):
    return lax.dot_general(left, right, (((1,), (1,)), ((), ())), preferred_element_type=F32)


def inverse_rms(values):
    return lax.rsqrt(jnp.sum(values * values, axis=-1, keepdims=True) * (1.0 / D) + EPS)


def norm_backward(values, inverse, gain, grad_norm):
    scaled = grad_norm * gain
    mean = jnp.sum(scaled * values, axis=-1, keepdims=True) * (1.0 / D)
    return inverse * scaled - values * inverse**3 * mean


def round_up(value, step):
    return -(-value // step) * step


def rows_at(index, rows):
    return pl.ds(pl.multiple_of(index * rows, rows), rows)


def to_blocks(values, n, width):
    rows, own = values.shape[0], values.shape[1] // n
    gap = jnp.zeros((rows, width // n - own), values.dtype)
    parts = []
    for s in range(n):
        parts += [values[:, s * own : (s + 1) * own], gap]
    return jnp.concatenate(parts, axis=1)


def from_blocks(values, n, own):
    block = values.shape[1] // n
    return jnp.concatenate([values[:, s * block : s * block + own] for s in range(n)], axis=1)


def swap(block, axis, k):
    count = lax.axis_size(axis)
    return lax.ppermute(block, axis, [(i, i ^ k) for i in range(count)])


def exchange(block):
    return lax.all_to_all(block, "shard", split_axis=0, concat_axis=0, tiled=True)


def spread(block, axis, step):
    return [block] + [swap(block, axis, k) for k in range(step, lax.axis_size(axis), step)]


def deliver(blocks, axis, step):
    return [blocks[0]] + [swap(block, axis, i * step) for i, block in enumerate(blocks) if i]


def exchange_z(blocks):
    groups = [list(range(core, lax.axis_size("shard"), 2)) for core in range(2)]
    return lax.all_to_all(
        blocks, "shard", split_axis=0, concat_axis=0, axis_index_groups=groups, tiled=True
    )


def after(value, *earlier):
    return lax.optimization_barrier((value,) + earlier)[0]


def later(values, *earlier):
    values = tuple(values)
    return list(lax.optimization_barrier(values + earlier)[: len(values)])


def both_cores(parts):
    stacked = jnp.stack(parts)
    return stacked, swap(stacked, "shard", 1)


def call(kernel, name, outs, *operands, scalars=(), scratch=()):
    specs = [pl.BlockSpec(memory_space=pltpu.SMEM)] * len(scalars)
    specs += [pl.BlockSpec(memory_space=pltpu.VMEM)] * len(operands)
    return pl.pallas_call(
        kernel,
        out_shape=[jax.ShapeDtypeStruct(shape, dtype) for shape, dtype in outs],
        in_specs=specs,
        out_specs=[pl.BlockSpec(memory_space=pltpu.VMEM)] * len(outs),
        scratch_shapes=[pltpu.VMEM(shape, dtype) for shape, dtype in scratch],
        compiler_params=pltpu.CompilerParams(vmem_limit_bytes=VMEM_LIMIT),
        name=name,
    )(*scalars, *operands)


def turned(values):
    half = HD // 2
    parts = []
    for begin in range(0, values.shape[1], HD):
        parts.append(-values[:, begin + half : begin + HD])
        parts.append(values[:, begin : begin + half])
    return jnp.concatenate(parts, axis=1)


def widened(values, times):
    return jnp.concatenate([values] * times, axis=1)


def head_of(values, h, heads):
    if heads == 1:
        return values
    lane = lax.broadcasted_iota(jnp.int32, values.shape, 1)
    return jnp.where(lane // HD == h, values, jnp.zeros_like(values))


def masked_probs(query, key, starts, row):
    rows, cols = query.shape[0], key.shape[0]
    logits = contract_cols(query, key) * SCALE
    place = lax.broadcasted_iota(jnp.int32, (rows, cols), 1)
    own = lax.broadcasted_iota(jnp.int32, (rows, cols), 0) + row
    logits = jnp.where((place <= own) & (place >= starts), logits, MASKED)
    raised = jnp.exp(logits - jnp.max(logits, axis=-1, keepdims=True))
    return raised * (1.0 / jnp.sum(raised, axis=-1, keepdims=True))


def blocks_kernel(n, in_ref, *out_refs):
    values = to_blocks(in_ref[...].astype(F32).T, n, out_refs[0].shape[1]).astype(BF16)
    out_refs[0][...] = values
    for ref in out_refs[1:]:
        for i in range(ref.shape[0]):
            ref[i] = values


def attention_message_kernel(n, rep_ref, q_ref, k_ref, v_ref, out_ref, gain_ref, msg_ref):
    own = q_ref.shape[0]
    piece = msg_ref.shape[1]
    cols = gain_ref.shape[1]
    half = msg_ref.shape[2] - cols
    head_cols = cols // 3
    heads = head_cols // HD
    row = lax.broadcasted_iota(jnp.int32, (piece, own), 0) + rep_ref[0] * piece
    pick = jnp.where(row == lax.broadcasted_iota(jnp.int32, (piece, own), 1), 1.0, 0.0).astype(BF16)
    query, key, value = dot(pick, q_ref[...]), contract_cols(pick, k_ref[...]), contract_cols(pick, v_ref[...])
    gap = jnp.zeros((piece, HD), F32)
    wide = lax.broadcasted_iota(jnp.int32, (piece, cols), 0) + rep_ref[0] * piece
    for s in range(n):
        slots = range(s * heads, (s + 1) * heads)
        parts = [query[:, h * HD : (h + 1) * HD] if h < QH else gap for h in slots]
        for array in (key, value):
            for h in slots:
                j = h // GROUP
                parts.append(array[:, j * HD : (j + 1) * HD] if h < QH else gap)
        block = jnp.concatenate(parts, axis=1)
        for i in range(2):
            block = jnp.where(wide == own + i, gain_ref[i : i + 1, :], block)
        msg_ref[s, :, :cols] = block.astype(BF16)
    rows = to_blocks(dot(pick, out_ref[...]), n, 2 * half).astype(BF16)
    for s in range(n):
        msg_ref[s, :, cols:] = rows[:, s % 2 * half : (s % 2 + 1) * half]


def as_row(column):
    return jnp.broadcast_to(column, (column.shape[0], 128)).T[0:1, :]


def join_kernel(reps, rep_ref, *refs):
    for i in range(reps):
        refs[reps][:, rep_ref[0] ^ i] = refs[i][...]


def join_out_kernel(reps, rep_ref, core_ref, mine_ref, other_ref, out_ref):
    first = core_ref[0] == 0
    half = mine_ref.shape[3]
    for i in range(reps):
        mine, other = mine_ref[i], other_ref[i]
        out_ref[:, rep_ref[0] ^ i, :, :half] = jnp.where(first, mine, other)
        out_ref[:, rep_ref[0] ^ i, :, half:] = jnp.where(first, other, mine)


def fill_rows(values, rows):
    if values.shape[0] == rows:
        return values
    return jnp.concatenate([values, jnp.zeros((rows - values.shape[0], values.shape[1]), F32)], axis=0)


def fill_cols(values, cols):
    if values.shape[1] == cols:
        return values
    return jnp.concatenate([values, jnp.zeros((values.shape[0], cols - values.shape[1]), F32)], axis=1)


def message_plan(own, each, cols):
    top, rows = round_up(own, 8), round_up(each, 8)
    rest = D % cols
    halved = rest and 2 * rest <= cols
    first = round_up(rows // 2, 8) if halved else rows
    total = top + D // cols * rows + (first if rest else 0)
    return top, rows, rest, halved, first, total


def pack_message(both, down, cols):
    top, rows, rest, halved, first, _ = message_plan(both.shape[0], down.shape[0], cols)
    down = fill_rows(down, rows)
    parts = [fill_rows(both, top)]
    parts += [down[:, j * cols : (j + 1) * cols] for j in range(D // cols)]
    if rest:
        tail = down[:, D - rest :]
        if halved:
            tail = jnp.concatenate([tail[:first], fill_rows(tail[first:], first)], axis=1)
        parts.append(fill_cols(tail, cols))
    return jnp.concatenate(parts, axis=0)


def unpack_message(message, own, each):
    cols = message.shape[1]
    top, rows, rest, halved, first, _ = message_plan(own, each, cols)
    parts = [message[top + j * rows : top + (j + 1) * rows] for j in range(D // cols)]
    if rest:
        tail = message[top + D // cols * rows :][:first]
        if halved:
            tail = jnp.concatenate([tail[:, :rest], tail[: rows - first, rest : 2 * rest]], axis=0)
        parts.append(tail[:, :rest])
    return message[:own], jnp.concatenate(parts, axis=1)[:each]


def hidden_message_kernel(n, reps, rep_ref, gate_ref, up_ref, down_ref, *out_refs):
    own, units = gate_ref.shape
    held = down_ref.shape[0]
    each = held // (2 * reps)
    cols = n * each
    place = lax.broadcasted_iota(jnp.int32, (1, cols), 1)
    row = lax.broadcasted_iota(jnp.int32, (round_up(each, 8), held), 0)
    for i in range(2):
        begin = each * (2 * rep_ref[0] + i)
        unit = place + begin
        for s in range(1, n):
            unit = unit + jnp.where(place >= each * s, held - each, 0)
        pick = jnp.where(lax.broadcasted_iota(jnp.int32, (units, cols), 0) == unit, 1.0, 0.0)
        pick = pick.astype(BF16)
        both = jnp.concatenate([dot(gate_ref[...], pick), dot(up_ref[...], pick)], axis=1)
        take = (lax.broadcasted_iota(jnp.int32, row.shape, 1) == row + begin) & (row < each)
        down = dot(jnp.where(take, 1.0, 0.0).astype(BF16), down_ref[...])
        message = pack_message(both, down[:each], 2 * cols).astype(BF16)
        for z in range(n // 2):
            split_rows([ref.at[2 * z + i] for ref in out_refs], message)


def split_rows(refs, values):
    begin = 0
    for ref in refs:
        rows = ref.shape[0]
        ref[...] = values[begin : begin + rows]
        begin += rows


def hidden_weights_in_kernel(n, own, each, *refs):
    parts, (w_ref, down_ref) = refs[:-2], refs[-2:]
    block = w_ref.shape[1]
    downs = []
    for s in range(n):
        message = jnp.concatenate([part[s].astype(F32) for part in parts], axis=0)
        both, down = unpack_message(message, own, each)
        w_ref[s] = fill_rows(both, block).astype(BF16)
        downs.append(down)
    down_ref[...] = to_blocks(jnp.concatenate(downs, axis=0), n, down_ref.shape[1]).astype(BF16)


def attend_kernel(rows, n, me_ref, mine_ref, other_ref, *refs):
    w_ref, cos_ref, sin_ref, start_ref, first_ref, q_ref, k_ref, v_ref, gains_ref = refs[:9]
    mixed_ref = refs[9]
    core = me_ref[0] % 2
    length, head_cols = q_ref.shape
    heads = head_cols // HD
    width = first_ref.shape[1]
    block_rows = width // n
    own = D // n
    gap = jnp.zeros((1, block_rows - own), F32)
    gains = []
    for i in range(2):
        parts = []
        for s in range(n):
            group = w_ref[pl.ds(s * block_rows + own // 16 * 16, block_rows - own // 16 * 16), :]
            row = own % 16 + i
            spread_row = group.astype(F32)[row : row + 1, :own]
            parts += [spread_row, gap]
        gains.append(jnp.concatenate(parts, axis=1))
        gains_ref[i : i + 1, :] = gains[i]
    for side, ref in enumerate((mine_ref, other_ref)):
        for z in range(n // 2):
            inputs = ref[z].astype(F32)
            normed = inputs * inverse_rms(inputs) * gains[0]
            first_ref[rows_at(2 * z + (core ^ side), rows), :] = normed.astype(BF16)
    block = min(256, length)
    for i in range(length // block):
        span = pl.ds(i * block, block)
        raw = dot(first_ref[span, :], w_ref[...])
        cosines, sines = widened(cos_ref[span, :], 2 * heads), widened(sin_ref[span, :], 2 * heads)
        query, key = raw[:, :head_cols], raw[:, head_cols : 2 * head_cols]
        q_ref[span, :] = (query * cosines + turned(query) * sines).astype(BF16)
        k_ref[span, :] = (key * cosines + turned(key) * sines).astype(BF16)
        v_ref[span, :] = raw[:, 2 * head_cols :].astype(BF16)
    for i in range(length // block):
        span, past = pl.ds(i * block, block), pl.ds(0, (i + 1) * block)
        total = None
        for h in range(heads):
            probs = masked_probs(
                head_of(q_ref[span, :], h, heads), k_ref[past, :], start_ref[span, :], i * block
            )
            mixed = head_of(dot(probs.astype(BF16), v_ref[past, :]), h, heads)
            total = mixed if total is None else total + mixed
        mixed_ref[span, :] = total.astype(BF16)


def attend_back_kernel(reps, rep_ref, *refs):
    g_ref, first_ref, q_ref, k_ref, v_ref, cos_ref, sin_ref, start_ref, dqkv_ref = refs[:9]
    piece_refs, (dk_ref, dv_ref, hold_ref) = refs[9 : 9 + reps], refs[9 + reps :]
    length, head_cols = q_ref.shape
    heads = head_cols // HD
    block = min(256, length)
    dk_ref[...] = jnp.zeros_like(dk_ref)
    dv_ref[...] = jnp.zeros_like(dv_ref)
    for i in range(length // block):
        span, past = pl.ds(i * block, block), pl.ds(0, (i + 1) * block)
        total = None
        for h in range(heads):
            query = head_of(q_ref[span, :], h, heads)
            grad = head_of(g_ref[span, :], h, heads)
            key = k_ref[past, :]
            probs = masked_probs(query, key, start_ref[span, :], i * block)
            grad_probs = contract_cols(grad, v_ref[past, :])
            delta = jnp.sum(probs * grad_probs, axis=-1, keepdims=True)
            grad_logits = (probs * (grad_probs - delta)).astype(BF16)
            grad_query = head_of(dot(grad_logits, key), h, heads)
            total = grad_query if total is None else total + grad_query
            dv_ref[past, :] += contract_rows(probs.astype(BF16), grad)
            dk_ref[past, :] += contract_rows(grad_logits, query)
        total = total * SCALE
        cosines, sines = widened(cos_ref[span, :], 2 * heads), widened(sin_ref[span, :], 2 * heads)
        back = total * cosines - turned(total) * sines
        dqkv_ref[span, :head_cols] = back.astype(BF16)
    for i in range(length // block):
        span = pl.ds(i * block, block)
        total = dk_ref[span, :] * SCALE
        cosines, sines = widened(cos_ref[span, :], 2 * heads), widened(sin_ref[span, :], 2 * heads)
        back = total * cosines - turned(total) * sines
        dqkv_ref[span, head_cols : 2 * head_cols] = back.astype(BF16)
        dqkv_ref[span, 2 * head_cols :] = dv_ref[span, :].astype(BF16)
    store_pieces(rep_ref, piece_refs, hold_ref, contract_rows(first_ref[...], dqkv_ref[...]))


def store_pieces(rep_ref, piece_refs, hold_ref, grad):
    n, reps, piece, _ = hold_ref.shape
    for s in range(n):
        for r in range(reps):
            begin = (s * reps + r) * piece
            hold_ref[s, r] = grad[begin : begin + piece].astype(BF16)
    for i, ref in enumerate(piece_refs):
        for s in range(n):
            ref[s] = hold_ref[s, rep_ref[0] ^ i]


def first_grad_kernel(rows, side, me_ref, dqkv_ref, w_ref, out_ref):
    for z in range(out_ref.shape[0]):
        part = dqkv_ref[rows_at(me_ref[0] ^ (2 * z + side), rows), :]
        out_ref[z] = contract_cols(part, w_ref[...]).astype(BF16)


def pair_sum_kernel(mine_ref, other_ref, *out_refs):
    for i, ref in enumerate(out_refs):
        ref[...] = (mine_ref[i].astype(F32) + other_ref[i].astype(F32)).astype(BF16)


def middle_kernel(n, tokens_ref, mixed_ref, w_ref, gains_ref, middle_ref, second_ref, attended_ref):
    width = tokens_ref.shape[1]
    attended = jnp.concatenate([mixed_ref[s] for s in range(n)], axis=1)[:, :D]
    attended = to_blocks(attended.astype(F32), n, width).astype(BF16)
    attended_ref[...] = attended
    middle = tokens_ref[...].astype(F32) + dot(attended, w_ref[...])
    middle_ref[...] = middle
    second_ref[...] = (middle * inverse_rms(middle) * gains_ref[1:2, :]).astype(BF16)


def stacked(ref, begin=0, count=None):
    count = ref.shape[0] if count is None else count
    return jnp.concatenate([ref[begin + i] for i in range(count)], axis=0)


def hidden_kernel(second_ref, cot_ref, w_ref, down_ref, grad_ref, grads_ref, hidden_ref):
    reps, rows, _ = second_ref.shape
    units = down_ref.shape[0]
    for i in range(0, reps, 2):
        span = pl.ds(i * rows, 2 * rows)
        both = dot(stacked(second_ref, i, 2), w_ref[...])
        gate, up = both[:, :units], both[:, units:]
        grad_hidden = contract_cols(stacked(cot_ref, i, 2), down_ref[...])
        sigmoid = 1.0 / (1.0 + jnp.exp(-gate))
        silu = gate * sigmoid
        hidden_ref[span, :] = (silu * up).astype(BF16)
        grad_gate = grad_hidden * up * sigmoid * (1.0 + gate * (1.0 - sigmoid))
        grads = jnp.concatenate([grad_gate, grad_hidden * silu], axis=1).astype(BF16)
        grads_ref[span, :] = grads
        grad = contract_cols(grads, w_ref[...]).astype(BF16)
        for j in range(2):
            grad_ref[i + j] = grad[j * rows : (j + 1) * rows]


def hidden_weights_kernel(n, own, each, *refs):
    second_a, second_b, cot_a, cot_b, grads_a, grads_b, hidden_a, hidden_b, *msg_refs = refs
    cols = msg_refs[0].shape[2]
    grad = contract_rows(stacked(second_a), grads_a[...])
    grad = grad + contract_rows(stacked(second_b), grads_b[...])
    down = contract_rows(hidden_a[...], stacked(cot_a)) + contract_rows(hidden_b[...], stacked(cot_b))
    down = from_blocks(down, n, own)
    block = grad.shape[0] // n
    for s in range(n):
        both = grad[s * block : s * block + own]
        message = pack_message(both, down[s * each : (s + 1) * each], cols).astype(BF16)
        split_rows([ref.at[s] for ref in msg_refs], message)


def core_sums_kernel(*refs):
    out_ref = refs[-1]
    for core in range(2):
        sums = [
            sum(part[s].astype(F32) for s in range(core, part.shape[0], 2)) for part in refs[:-1]
        ]
        total = jnp.concatenate(sums, axis=0).astype(BF16)
        for r in range(out_ref.shape[0]):
            out_ref[r, core] = total


def hidden_out_kernel(
    n, each, in_ref, gate_w_ref, up_w_ref, gain_ref, gate_ref, up_ref, down_ref, norm_ref
):
    reps = in_ref.shape[0]
    own = gate_ref.shape[0]
    units = 2 * reps * each
    cols = in_ref.shape[3]
    boths = []
    for f in range(2 * reps):
        both, down = unpack_message(in_ref[f // 2, f % 2].astype(F32), own, each)
        boths.append(both)
        down_ref[f * each : (f + 1) * each, :] = down
    total = jnp.zeros((own, 1), F32)
    for begin, w_ref, out_ref in ((0, gate_w_ref, gate_ref), (cols // 2, up_w_ref, up_ref)):
        for s in range(n):
            place = begin + s * each
            rows = jnp.concatenate([part[:, place : place + each] for part in boths], axis=1)
            span = slice(s * units, (s + 1) * units)
            out_ref[:, span] = rows
            total = total + jnp.sum(rows * w_ref[:, span].astype(F32), axis=1, keepdims=True)
    norm_ref[...] = as_row(total) / gain_ref[...]


def down_kernel(hidden_ref, w_ref, out_ref):
    rows = out_ref.shape[1]
    for i in range(0, out_ref.shape[0], 2):
        both = dot(hidden_ref[pl.ds(i * rows, 2 * rows), :], w_ref[...]).astype(BF16)
        for j in range(2):
            out_ref[i + j] = both[j * rows : (j + 1) * rows]


def output_kernel(n, own, middle_ref, *refs):
    total = middle_ref[...]
    for ref in refs[:-1]:
        total = total + ref[...].astype(F32)
    refs[-1][...] = from_blocks(total, n, own).T.astype(BF16)


def middle_grad_kernel(n, own, reps, *refs):
    parts, refs = refs[:reps], refs[reps:]
    cot_ref, middle_ref, gains_ref, w_ref, grad_ref, branch_ref, heads_ref = refs
    rows = middle_ref.shape[0]
    middle = middle_ref[...]
    grad_second = sum(ref[...].astype(F32) for ref in parts)
    grad = cot_ref[...].astype(F32) + norm_backward(
        middle, inverse_rms(middle), gains_ref[1:2, :], grad_second
    )
    grad_ref[...] = grad
    branch = grad.astype(BF16)
    branch_ref[...] = branch
    attended = from_blocks(contract_cols(branch, w_ref[...]), n, own)
    head_cols = heads_ref.shape[2]
    if n * head_cols > D:
        attended = jnp.concatenate([attended, jnp.zeros((rows, n * head_cols - D), F32)], axis=1)
    for s in range(n):
        heads_ref[s] = attended[:, s * head_cols : (s + 1) * head_cols].astype(BF16)


def out_weights_kernel(rep_ref, core_ref, attended_ref, branch_ref, mine_ref, other_ref, hold_ref):
    store_pieces(rep_ref, (), hold_ref, contract_rows(attended_ref[...], branch_ref[...]))
    for side, ref in enumerate((mine_ref, other_ref)):
        for i in range(ref.shape[0]):
            for z in range(ref.shape[1]):
                ref[i, z] = hold_ref[2 * z + (core_ref[0] ^ side), rep_ref[0] ^ i]


def rep_sum_kernel(reps, *refs):
    total = sum(ref[...].astype(F32) for ref in refs[:reps])
    refs[reps][...] = total.astype(BF16)


def owner_sum_kernel(in_ref, out_ref):
    out_ref[...] = jnp.sum(in_ref[...].astype(F32), axis=0).astype(BF16)


def out_out_kernel(n, reps, rep_ref, *refs):
    out_ref, hold_ref = refs[reps:]
    for i in range(reps):
        hold_ref[rep_ref[0] ^ i] = refs[i][...].astype(F32)
    own = out_ref.shape[0]
    rows = jnp.concatenate([hold_ref[r] for r in range(reps)], axis=0)[:own]
    out_ref[...] = from_blocks(rows, n, own)


def attention_out_kernel(n, reps, rep_ref, *refs):
    parts, refs = refs[:reps], refs[reps:]
    q_w_ref, k_w_ref, v_w_ref, gain_ref, q_ref, k_ref, v_ref, norm_ref, hold_ref = refs
    own = q_ref.shape[0]
    cols = parts[0].shape[2]
    head_cols = cols // 3
    heads = head_cols // HD
    for i, part in enumerate(parts):
        for s in range(n):
            hold_ref[rep_ref[0] ^ i, s] = part[s].astype(F32)
    sides = [
        jnp.concatenate([hold_ref[r, s] for r in range(reps)], axis=0)[:own] for s in range(n)
    ]

    def slot(h, kind):
        begin = kind * head_cols + h % heads * HD
        return sides[h // heads][:, begin : begin + HD]

    query = jnp.concatenate([slot(h, 0) for h in range(QH)], axis=1)
    q_ref[...] = query
    total = jnp.sum(query * q_w_ref[...].astype(F32), axis=1, keepdims=True)
    total = as_row(total)
    for kind, w_ref, out_ref in ((1, k_w_ref, k_ref), (2, v_w_ref, v_ref)):
        wide = jnp.concatenate(
            [sum(slot(j * GROUP + g, kind) for g in range(GROUP)) for j in range(KVH)], axis=1
        ).T
        out_ref[...] = wide
        total = total + jnp.sum(wide * w_ref[...].astype(F32), axis=0, keepdims=True)
    norm_ref[...] = total / gain_ref[...]


def input_grad_kernel(n, own, nz, *refs):
    parts, (tokens_ref, gains_ref, grad_ref, out_ref) = refs[:nz], refs[nz:]
    inputs = tokens_ref[...].astype(F32)
    grad_first = sum(ref[...].astype(F32) for ref in parts)
    total = grad_ref[...] + norm_backward(inputs, inverse_rms(inputs), gains_ref[0:1, :], grad_first)
    out_ref[...] = from_blocks(total, n, own).T


def shards(
    tokens,
    lengths,
    norm_one,
    w_query,
    w_key,
    w_value,
    w_out,
    norm_two,
    w_gate,
    w_up,
    w_down,
    cotangent,
):
    n = lax.axis_size("shard")
    reps = lax.axis_size("rep")
    nz = n // 2
    rows = tokens.shape[0]
    length = rows * n
    own = w_query.shape[0]
    held = w_down.shape[0]
    block = round_up(own + 2, 16)
    width = n * block
    piece = block // reps
    heads = -(-QH // n)
    head_cols = heads * HD
    qkv_cols = 3 * head_cols
    each = held // (2 * reps)
    units = n * each
    msg_rows = message_plan(own, each, 2 * units)[-1]
    shard_index = lax.axis_index("shard").astype(jnp.int32)
    me = shard_index.reshape(1)
    core = (shard_index % 2).reshape(1)
    rep = lax.axis_index("rep").astype(jnp.int32).reshape(1)
    own_block = (rows, width)

    tokens_in, tokens_tiled = call(
        lambda *r: blocks_kernel(n, *r),
        "tokens_blocks",
        [(own_block, BF16), ((nz,) + own_block, BF16)],
        tokens.T,
    )
    gains_own = jnp.pad(jnp.stack([norm_one, norm_two]), ((0, 0), (0, qkv_cols - own))).astype(F32)
    (message,) = call(
        lambda *r: attention_message_kernel(n, *r),
        "attention_message",
        [((n, piece, qkv_cols + width // 2), BF16)],
        after(w_query, tokens_in),
        w_key.T,
        w_value.T,
        w_out,
        gains_own,
        scalars=(rep,),
    )
    arrived = exchange(message)
    (w_qkv,) = call(
        lambda *r: join_kernel(reps, *r),
        "join_qkv",
        [((n, reps, piece, qkv_cols), BF16)],
        *spread(arrived[:, :, :qkv_cols], "rep", 1),
        scalars=(rep,),
    )
    w_qkv = w_qkv.reshape(width, qkv_cols)
    tokens_mine = exchange_z(after(tokens_tiled, arrived))
    (cot_in,) = call(
        lambda *r: blocks_kernel(n, *r), "cot_blocks", [(own_block, BF16)], after(cotangent.T, message)
    )
    cot_parts = spread(after(cot_in, w_qkv), "rep", 1)
    doc_start, position = doc_layout(after(lengths, cot_in)[0], length)
    cosines, sines = rope_tables(position)
    start = doc_start[:, None]

    split = msg_rows // 2 // 16 * 16 + 16
    part_rows = (split, msg_rows - split) if split < msg_rows else (msg_rows,)
    messages = call(
        lambda *r: hidden_message_kernel(n, reps, *r),
        "hidden_message",
        [((n, part, 2 * units), BF16) for part in part_rows],
        after(w_gate, cosines, sines, start),
        w_up,
        w_down,
        scalars=(rep,),
    )
    tokens_mine = after(tokens_mine, w_qkv, *messages)
    tokens_other = swap(tokens_mine, "shard", 1)
    hidden_first = exchange(after(messages[0], tokens_mine))

    out_parts = spread(after(arrived, w_qkv)[:, :, qkv_cols:], "rep", 1)

    head_shape = (length, head_cols)
    first_all, query, key, value, gains, mixed = call(
        lambda *r: attend_kernel(rows, n, *r),
        "attend",
        [((length, width), BF16)]
        + [(head_shape, BF16)] * 3
        + [((2, width), F32)]
        + [(head_shape, BF16)],
        tokens_mine,
        tokens_other,
        w_qkv,
        cosines,
        sines,
        start,
        scalars=(me,),
    )
    mixed = exchange(after(mixed, hidden_first).reshape(n, rows, head_cols))
    hidden_rest = [exchange(after(message, mixed)) for message in messages[1:]]
    (out_full,) = call(
        lambda *r: join_out_kernel(reps, *r),
        "join_out",
        [((n, reps, piece, width), BF16)],
        *both_cores([after(out_parts[0], gains)] + out_parts[1:]),
        scalars=(rep, core),
    )
    out_full = out_full.reshape(width, width)

    middle, second, attended = call(
        lambda *r: middle_kernel(n, *r),
        "middle",
        [(own_block, F32), (own_block, BF16), (own_block, BF16)],
        tokens_in,
        mixed,
        out_full,
        gains,
    )
    w_hidden, w_down_in = call(
        lambda *r: hidden_weights_in_kernel(n, own, each, *r),
        "hidden_weights_in",
        [((n, block, 2 * units), BF16), ((units, width), BF16)],
        after(hidden_first, second),
        *hidden_rest,
    )
    w_hidden = w_hidden.reshape(width, 2 * units)
    cot_mine, cot_other = both_cores([after(cot_parts[0], out_full)] + cot_parts[1:])

    second_mine, second_other = both_cores(spread(second, "rep", 1))
    side_outs = [
        ((reps, rows, width), BF16),
        ((reps * rows, 2 * units), BF16),
        ((reps * rows, units), BF16),
    ]

    def hidden_side(seconds, cots, name):
        return call(hidden_kernel, name, side_outs, seconds, cots, w_hidden, w_down_in)

    def plane_sums(mine, other):
        sums = call(pair_sum_kernel, "pair_sum", [(own_block, BF16)] * reps, mine, swap(other, "shard", 1))
        return sums, deliver(sums, "rep", 1)

    grad_other, grads_other, hidden_other = hidden_side(second_other, cot_other, "hidden_other")
    grad_mine, grads_mine, hidden_mine = hidden_side(
        after(second_mine, grad_other), cot_mine, "hidden_mine"
    )
    hidden_messages = call(
        lambda *r: hidden_weights_kernel(n, own, each, *r),
        "hidden_weights",
        [((n, part, 2 * units), BF16) for part in part_rows],
        second_mine,
        second_other,
        cot_mine,
        cot_other,
        grads_mine,
        grads_other,
        hidden_mine,
        hidden_other,
    )
    hidden_sums = [exchange(hidden_messages[0])]
    sums, grad_second = plane_sums(after(grad_mine, hidden_messages[0]), grad_other)
    down_other, down_mine = [
        call(
            down_kernel,
            "down",
            [((reps, rows, width), BF16)],
            after(hidden, grad_second[1]),
            w_down_in,
        )[0]
        for hidden in (hidden_other, hidden_mine)
    ]

    grad_middle, grad_branch, grad_heads = call(
        lambda *r: middle_grad_kernel(n, own, reps, *r),
        "middle_grad",
        [(own_block, F32), (own_block, BF16), ((n, rows, head_cols), BF16)],
        *grad_second,
        cot_in,
        after(middle, down_other, down_mine),
        gains,
        out_full,
    )
    grad_heads = exchange(after(grad_heads, *hidden_sums))
    out_pieces = call(
        out_weights_kernel,
        "out_weights",
        [((reps, nz, piece, width), BF16)] * 2,
        attended,
        grad_branch,
        scalars=(rep, core),
        scratch=[((n, reps, piece, width), BF16)],
    )
    down_sums, down_parts = plane_sums(after(down_mine, out_pieces[0]), down_other)
    out_sums = call(
        pair_sum_kernel,
        "pair_sum",
        [((nz, piece, width), BF16)] * reps,
        after(out_pieces[0], down_sums[0]),
        swap(out_pieces[1], "shard", 1),
    )
    hidden_sums += [exchange(after(message, grad_heads)) for message in hidden_messages[1:]]
    grad_heads = grad_heads.reshape(head_shape)
    grad_qkv, *attention_pieces = call(
        lambda *r: attend_back_kernel(reps, *r),
        "attend_back",
        [((length, qkv_cols), BF16)] + [((n, piece, qkv_cols), BF16)] * reps,
        grad_heads,
        first_all,
        query,
        key,
        value,
        cosines,
        sines,
        after(start, out_sums[0], down_sums[0]),
        scalars=(rep,),
        scratch=[(head_shape, F32)] * 2 + [((n, reps, piece, qkv_cols), BF16)],
    )

    def rep_sum(parts, *earlier):
        return call(
            lambda *r: rep_sum_kernel(reps, *r),
            "rep_sum",
            [(parts[0].shape, BF16)],
            after(parts[0], *earlier),
            *parts[1:],
        )[0]

    def first_side(grads, side):
        return call(
            lambda *r: first_grad_kernel(rows, side, *r),
            "first_grad",
            [((nz, rows, width), BF16)],
            grads,
            w_qkv,
            scalars=(me,),
        )[0]

    first_other = first_side(grad_qkv, 1)
    first_mine = first_side(after(grad_qkv, first_other), 0)
    (output,) = call(
        lambda *r: output_kernel(n, own, *r),
        "output",
        [((D, rows), BF16)],
        after(middle, first_mine),
        *down_parts,
    )
    out_summed = rep_sum(deliver(out_sums, "rep", 1), output)
    attention_summed = rep_sum(deliver(attention_pieces, "rep", 1), out_summed)
    first_sums = call(
        pair_sum_kernel,
        "pair_sum",
        [(own_block, BF16)] * nz,
        after(first_mine, attention_summed, *hidden_sums),
        swap(first_other, "shard", 1),
    )
    first_parts = deliver(first_sums, "shard", 2)
    attention_moved = exchange(after(attention_summed, *hidden_sums))
    (core_sums,) = call(
        core_sums_kernel,
        "core_sums",
        [((reps, 2, msg_rows, 2 * units), BF16)],
        after(hidden_sums[0], first_sums[0]),
        *hidden_sums[1:],
    )
    hidden_moved = lax.all_to_all(
        after(core_sums, attention_moved), "rep", split_axis=0, concat_axis=0, tiled=True
    )
    out_moved = exchange_z(after(out_summed, hidden_moved))

    gain_rows = [gain.astype(F32)[None] for gain in (norm_one, norm_two)]
    (input_grad,) = call(
        lambda *r: input_grad_kernel(n, own, nz, *r),
        "input_grad",
        [((D, rows), F32)],
        *first_parts,
        tokens_in,
        gains,
        grad_middle,
    )

    attention_parts = spread(attention_moved, "rep", 1)
    grad_w_query, grad_w_key, grad_w_value, grad_norm_one = call(
        lambda *r: attention_out_kernel(n, reps, *r),
        "attention_out",
        [(w_query.shape, F32), (w_key.shape[::-1], F32), (w_value.shape[::-1], F32), ((1, own), F32)],
        *attention_parts,
        after(w_query, input_grad),
        w_key.T,
        w_value.T,
        gain_rows[0],
        scalars=(rep,),
        scratch=[((reps, n, piece, qkv_cols), F32)],
    )

    grad_w_gate, grad_w_up, grad_w_down, grad_norm_two = call(
        lambda *r: hidden_out_kernel(n, each, *r),
        "hidden_out",
        [(w_gate.shape, F32), (w_up.shape, F32), (w_down.shape, F32), ((1, own), F32)],
        hidden_moved,
        w_gate,
        w_up,
        after(gain_rows[1], grad_norm_one),
    )

    (out_piece,) = call(owner_sum_kernel, "owner_sum", [((piece, width), BF16)], after(out_moved, input_grad))
    (grad_w_out,) = call(
        lambda *r: out_out_kernel(n, reps, *r),
        "out_out",
        [(w_out.shape, F32)],
        *spread(out_piece, "rep", 1),
        scalars=(rep,),
        scratch=[((reps, piece, width), F32)],
    )

    return (
        output.T,
        input_grad.T,
        grad_norm_one[0],
        grad_w_query,
        grad_w_key.T,
        grad_w_value.T,
        grad_w_out,
        grad_norm_two[0],
        grad_w_gate,
        grad_w_up,
        grad_w_down,
    )


def solution(mesh):
    rows = P("shard", None)
    own_tokens = P(("rep", "shard"), None)
    return jax.shard_map(
        shards,
        mesh=mesh,
        in_specs=(
            own_tokens,
            P("rep", None),
            P("shard"),
            rows,
            rows,
            rows,
            rows,
            P("shard"),
            rows,
            rows,
            rows,
            own_tokens,
        ),
        out_specs=(
            own_tokens,
            own_tokens,
            P("shard"),
            rows,
            rows,
            rows,
            rows,
            P("shard"),
            rows,
            rows,
            rows,
        ),
        check_vma=False,
    )
```

```python
import jax
import jax.numpy as jnp
from jax import lax
from jax.experimental import pallas as pl
from jax.experimental.pallas import tpu as pltpu
from jax.sharding import PartitionSpec as P

D = 960
QH = 15
KVH = 5
HD = 64
FF = 2560
GROUP = QH // KVH

EPS = 1e-05
ROPE_BASE = 10000.0
MASKED = -1e30
SCALE = HD ** (-0.5)
BF16 = jnp.bfloat16
F32 = jnp.float32


def doc_layout(lengths_row, length):
    places = jnp.arange(length, dtype=jnp.int32)
    doc_ends = jnp.cumsum(lengths_row)
    passed = places[:, None] >= doc_ends[None, :]
    doc_start = jnp.sum(jnp.where(passed, lengths_row[None, :], 0), axis=1)
    return (doc_start, places - doc_start)


def rope_tables(position):
    half_dim = HD // 2
    fraction = jnp.arange(half_dim, dtype=F32) * (2.0 / HD)
    inverse = ROPE_BASE ** (-fraction)
    angles = position.astype(F32)[:, None] * inverse[None, :]
    return (jnp.cos(angles), jnp.sin(angles))


VMEM_LIMIT = 56 * 2**20


def dot(left, right):
    return jnp.dot(left, right, preferred_element_type=F32)


def contract_rows(left, right):
    return lax.dot_general(left, right, (((0,), (0,)), ((), ())), preferred_element_type=F32)


def contract_cols(left, right):
    return lax.dot_general(left, right, (((1,), (1,)), ((), ())), preferred_element_type=F32)


def inverse_rms(values):
    return lax.rsqrt(jnp.sum(values * values, axis=-1, keepdims=True) * (1.0 / D) + EPS)


def norm_backward(values, inverse, gain, grad_norm):
    scaled = grad_norm * gain
    mean = jnp.sum(scaled * values, axis=-1, keepdims=True) * (1.0 / D)
    return inverse * scaled - values * inverse**3 * mean


def round_up(value, step):
    return -(-value // step) * step


def rows_at(index, rows):
    return pl.ds(pl.multiple_of(index * rows, rows), rows)


def to_blocks(values, n, width):
    rows, own = values.shape[0], values.shape[1] // n
    gap = jnp.zeros((rows, width // n - own), values.dtype)
    parts = []
    for s in range(n):
        parts += [values[:, s * own : (s + 1) * own], gap]
    return jnp.concatenate(parts, axis=1)


def from_blocks(values, n, own):
    block = values.shape[1] // n
    return jnp.concatenate([values[:, s * block : s * block + own] for s in range(n)], axis=1)


def swap(block, axis, k):
    count = lax.axis_size(axis)
    return lax.ppermute(block, axis, [(i, i ^ k) for i in range(count)])


def exchange(block):
    return lax.all_to_all(block, "shard", split_axis=0, concat_axis=0, tiled=True)


def spread(block, axis, step):
    return [block] + [swap(block, axis, k) for k in range(step, lax.axis_size(axis), step)]


def deliver(blocks, axis, step):
    return [blocks[0]] + [swap(block, axis, i * step) for i, block in enumerate(blocks) if i]


def exchange_z(blocks):
    groups = [list(range(core, lax.axis_size("shard"), 2)) for core in range(2)]
    return lax.all_to_all(
        blocks, "shard", split_axis=0, concat_axis=0, axis_index_groups=groups, tiled=True
    )


def after(value, *earlier):
    return lax.optimization_barrier((value,) + earlier)[0]


def later(values, *earlier):
    values = tuple(values)
    return list(lax.optimization_barrier(values + earlier)[: len(values)])


def both_cores(parts):
    stacked = jnp.stack(parts)
    return stacked, swap(stacked, "shard", 1)


def call(kernel, name, outs, *operands, scalars=(), scratch=()):
    specs = [pl.BlockSpec(memory_space=pltpu.SMEM)] * len(scalars)
    specs += [pl.BlockSpec(memory_space=pltpu.VMEM)] * len(operands)
    return pl.pallas_call(
        kernel,
        out_shape=[jax.ShapeDtypeStruct(shape, dtype) for shape, dtype in outs],
        in_specs=specs,
        out_specs=[pl.BlockSpec(memory_space=pltpu.VMEM)] * len(outs),
        scratch_shapes=[pltpu.VMEM(shape, dtype) for shape, dtype in scratch],
        compiler_params=pltpu.CompilerParams(vmem_limit_bytes=VMEM_LIMIT),
        name=name,
    )(*scalars, *operands)


def turned(values):
    half = HD // 2
    parts = []
    for begin in range(0, values.shape[1], HD):
        parts.append(-values[:, begin + half : begin + HD])
        parts.append(values[:, begin : begin + half])
    return jnp.concatenate(parts, axis=1)


def widened(values, times):
    return jnp.concatenate([values] * times, axis=1)


def head_of(values, h, heads):
    if heads == 1:
        return values
    lane = lax.broadcasted_iota(jnp.int32, values.shape, 1)
    return jnp.where(lane // HD == h, values, jnp.zeros_like(values))


def masked_probs(query, key, starts, row):
    rows, cols = query.shape[0], key.shape[0]
    logits = contract_cols(query, key) * SCALE
    place = lax.broadcasted_iota(jnp.int32, (rows, cols), 1)
    own = lax.broadcasted_iota(jnp.int32, (rows, cols), 0) + row
    logits = jnp.where((place <= own) & (place >= starts), logits, MASKED)
    raised = jnp.exp(logits - jnp.max(logits, axis=-1, keepdims=True))
    return raised * (1.0 / jnp.sum(raised, axis=-1, keepdims=True))


def blocks_kernel(n, in_ref, *out_refs):
    values = to_blocks(in_ref[...].astype(F32).T, n, out_refs[0].shape[1]).astype(BF16)
    out_refs[0][...] = values
    for ref in out_refs[1:]:
        for i in range(ref.shape[0]):
            ref[i] = values


def attention_message_kernel(n, rep_ref, q_ref, k_ref, v_ref, out_ref, gain_ref, msg_ref):
    own = q_ref.shape[0]
    piece = msg_ref.shape[1]
    cols = gain_ref.shape[1]
    half = msg_ref.shape[2] - cols
    head_cols = cols // 3
    heads = head_cols // HD
    row = lax.broadcasted_iota(jnp.int32, (piece, own), 0) + rep_ref[0] * piece
    pick = jnp.where(row == lax.broadcasted_iota(jnp.int32, (piece, own), 1), 1.0, 0.0).astype(BF16)
    query, key, value = dot(pick, q_ref[...]), contract_cols(pick, k_ref[...]), contract_cols(pick, v_ref[...])
    gap = jnp.zeros((piece, HD), F32)
    wide = lax.broadcasted_iota(jnp.int32, (piece, cols), 0) + rep_ref[0] * piece
    for s in range(n):
        slots = range(s * heads, (s + 1) * heads)
        parts = [query[:, h * HD : (h + 1) * HD] if h < QH else gap for h in slots]
        for array in (key, value):
            for h in slots:
                j = h // GROUP
                parts.append(array[:, j * HD : (j + 1) * HD] if h < QH else gap)
        block = jnp.concatenate(parts, axis=1)
        for i in range(2):
            block = jnp.where(wide == own + i, gain_ref[i : i + 1, :], block)
        msg_ref[s, :, :cols] = block.astype(BF16)
    rows = to_blocks(dot(pick, out_ref[...]), n, 2 * half).astype(BF16)
    for s in range(n):
        msg_ref[s, :, cols:] = rows[:, s % 2 * half : (s % 2 + 1) * half]


def as_row(column):
    return jnp.broadcast_to(column, (column.shape[0], 128)).T[0:1, :]


def join_kernel(in_ref, out_ref):
    for r in range(in_ref.shape[0]):
        out_ref[:, r] = in_ref[r]


def join_out_kernel(reps, rep_ref, core_ref, mine_ref, other_ref, out_ref):
    first = core_ref[0] == 0
    half = mine_ref.shape[3]
    for i in range(reps):
        mine, other = mine_ref[i], other_ref[i]
        out_ref[:, rep_ref[0] ^ i, :, :half] = jnp.where(first, mine, other)
        out_ref[:, rep_ref[0] ^ i, :, half:] = jnp.where(first, other, mine)


def fill_rows(values, rows):
    if values.shape[0] == rows:
        return values
    return jnp.concatenate([values, jnp.zeros((rows - values.shape[0], values.shape[1]), F32)], axis=0)


def fill_cols(values, cols):
    if values.shape[1] == cols:
        return values
    return jnp.concatenate([values, jnp.zeros((values.shape[0], cols - values.shape[1]), F32)], axis=1)


def message_plan(own, each, cols):
    top, rows = round_up(own, 8), round_up(each, 8)
    rest = D % cols
    halved = rest and 2 * rest <= cols
    first = round_up(rows // 2, 8) if halved else rows
    total = top + D // cols * rows + (first if rest else 0)
    return top, rows, rest, halved, first, total


def pack_message(both, down, cols):
    top, rows, rest, halved, first, _ = message_plan(both.shape[0], down.shape[0], cols)
    down = fill_rows(down, rows)
    parts = [fill_rows(both, top)]
    parts += [down[:, j * cols : (j + 1) * cols] for j in range(D // cols)]
    if rest:
        tail = down[:, D - rest :]
        if halved:
            tail = jnp.concatenate([tail[:first], fill_rows(tail[first:], first)], axis=1)
        parts.append(fill_cols(tail, cols))
    return jnp.concatenate(parts, axis=0)


def unpack_message(message, own, each):
    cols = message.shape[1]
    top, rows, rest, halved, first, _ = message_plan(own, each, cols)
    parts = [message[top + j * rows : top + (j + 1) * rows] for j in range(D // cols)]
    if rest:
        tail = message[top + D // cols * rows :][:first]
        if halved:
            tail = jnp.concatenate([tail[:, :rest], tail[: rows - first, rest : 2 * rest]], axis=0)
        parts.append(tail[:, :rest])
    return message[:own], jnp.concatenate(parts, axis=1)[:each]


def hidden_message_kernel(n, reps, rep_ref, gate_ref, up_ref, down_ref, *out_refs):
    own, units = gate_ref.shape
    held = down_ref.shape[0]
    each = held // (2 * reps)
    cols = n * each
    place = lax.broadcasted_iota(jnp.int32, (1, cols), 1)
    row = lax.broadcasted_iota(jnp.int32, (round_up(each, 8), held), 0)
    for i in range(2):
        begin = each * (2 * rep_ref[0] + i)
        unit = place + begin
        for s in range(1, n):
            unit = unit + jnp.where(place >= each * s, held - each, 0)
        pick = jnp.where(lax.broadcasted_iota(jnp.int32, (units, cols), 0) == unit, 1.0, 0.0)
        pick = pick.astype(BF16)
        both = jnp.concatenate([dot(gate_ref[...], pick), dot(up_ref[...], pick)], axis=1)
        take = (lax.broadcasted_iota(jnp.int32, row.shape, 1) == row + begin) & (row < each)
        down = dot(jnp.where(take, 1.0, 0.0).astype(BF16), down_ref[...])
        message = pack_message(both, down[:each], 2 * cols).astype(BF16)
        for z in range(n // 2):
            split_rows([ref.at[2 * z + i] for ref in out_refs], message)


def split_rows(refs, values):
    begin = 0
    for ref in refs:
        rows = ref.shape[0]
        ref[...] = values[begin : begin + rows]
        begin += rows


def hidden_weights_in_kernel(n, own, each, *refs):
    parts, (w_ref, down_ref) = refs[:-2], refs[-2:]
    block = w_ref.shape[1]
    downs = []
    for s in range(n):
        message = jnp.concatenate([part[s].astype(F32) for part in parts], axis=0)
        both, down = unpack_message(message, own, each)
        w_ref[s] = fill_rows(both, block).astype(BF16)
        downs.append(down)
    down_ref[...] = to_blocks(jnp.concatenate(downs, axis=0), n, down_ref.shape[1]).astype(BF16)


def attend_kernel(rows, n, me_ref, mine_ref, other_ref, *refs):
    w_ref, cos_ref, sin_ref, start_ref, first_ref, q_ref, k_ref, v_ref, gains_ref = refs[:9]
    mixed_ref = refs[9]
    length, head_cols = q_ref.shape
    heads = head_cols // HD
    width = first_ref.shape[1]
    block_rows = width // n
    own = D // n
    gap = jnp.zeros((1, block_rows - own), F32)
    gains = []
    for i in range(2):
        parts = []
        for s in range(n):
            group = w_ref[pl.ds(s * block_rows + own // 16 * 16, block_rows - own // 16 * 16), :]
            row = own % 16 + i
            spread_row = group.astype(F32)[row : row + 1, :own]
            parts += [spread_row, gap]
        gains.append(jnp.concatenate(parts, axis=1))
        gains_ref[i : i + 1, :] = gains[i]
    for side, ref in enumerate((mine_ref, other_ref)):
        for z in range(n // 2):
            inputs = ref[z].astype(F32)
            normed = inputs * inverse_rms(inputs) * gains[0]
            first_ref[rows_at(me_ref[0] ^ (2 * z + side), rows), :] = normed.astype(BF16)
    block = min(256, length)
    for i in range(length // block):
        span = pl.ds(i * block, block)
        raw = dot(first_ref[span, :], w_ref[...])
        cosines, sines = widened(cos_ref[span, :], 2 * heads), widened(sin_ref[span, :], 2 * heads)
        query, key = raw[:, :head_cols], raw[:, head_cols : 2 * head_cols]
        q_ref[span, :] = (query * cosines + turned(query) * sines).astype(BF16)
        k_ref[span, :] = (key * cosines + turned(key) * sines).astype(BF16)
        v_ref[span, :] = raw[:, 2 * head_cols :].astype(BF16)
    for i in range(length // block):
        span, past = pl.ds(i * block, block), pl.ds(0, (i + 1) * block)
        total = None
        for h in range(heads):
            probs = masked_probs(
                head_of(q_ref[span, :], h, heads), k_ref[past, :], start_ref[span, :], i * block
            )
            mixed = head_of(dot(probs.astype(BF16), v_ref[past, :]), h, heads)
            total = mixed if total is None else total + mixed
        mixed_ref[span, :] = total.astype(BF16)


def attend_back_kernel(reps, rep_ref, *refs):
    g_ref, first_ref, q_ref, k_ref, v_ref, cos_ref, sin_ref, start_ref, dqkv_ref = refs[:9]
    piece_refs, (dk_ref, dv_ref, hold_ref) = refs[9 : 9 + reps], refs[9 + reps :]
    length, head_cols = q_ref.shape
    heads = head_cols // HD
    block = min(256, length)
    dk_ref[...] = jnp.zeros_like(dk_ref)
    dv_ref[...] = jnp.zeros_like(dv_ref)
    for i in range(length // block):
        span, past = pl.ds(i * block, block), pl.ds(0, (i + 1) * block)
        total = None
        for h in range(heads):
            query = head_of(q_ref[span, :], h, heads)
            grad = head_of(g_ref[span, :], h, heads)
            key = k_ref[past, :]
            probs = masked_probs(query, key, start_ref[span, :], i * block)
            grad_probs = contract_cols(grad, v_ref[past, :])
            delta = jnp.sum(probs * grad_probs, axis=-1, keepdims=True)
            grad_logits = (probs * (grad_probs - delta)).astype(BF16)
            grad_query = head_of(dot(grad_logits, key), h, heads)
            total = grad_query if total is None else total + grad_query
            dv_ref[past, :] += contract_rows(probs.astype(BF16), grad)
            dk_ref[past, :] += contract_rows(grad_logits, query)
        total = total * SCALE
        cosines, sines = widened(cos_ref[span, :], 2 * heads), widened(sin_ref[span, :], 2 * heads)
        back = total * cosines - turned(total) * sines
        dqkv_ref[span, :head_cols] = back.astype(BF16)
    for i in range(length // block):
        span = pl.ds(i * block, block)
        total = dk_ref[span, :] * SCALE
        cosines, sines = widened(cos_ref[span, :], 2 * heads), widened(sin_ref[span, :], 2 * heads)
        back = total * cosines - turned(total) * sines
        dqkv_ref[span, head_cols : 2 * head_cols] = back.astype(BF16)
        dqkv_ref[span, 2 * head_cols :] = dv_ref[span, :].astype(BF16)
    store_pieces(rep_ref, piece_refs, hold_ref, contract_rows(first_ref[...], dqkv_ref[...]))


def store_pieces(rep_ref, piece_refs, hold_ref, grad):
    n, reps, piece, _ = hold_ref.shape
    for s in range(n):
        for r in range(reps):
            begin = (s * reps + r) * piece
            hold_ref[s, r] = grad[begin : begin + piece].astype(BF16)
    for i, ref in enumerate(piece_refs):
        for s in range(n):
            ref[s] = hold_ref[s, rep_ref[0] ^ i]


def first_grad_kernel(rows, side, core_ref, dqkv_ref, w_ref, out_ref):
    chips = out_ref.shape[0]
    parts = [dqkv_ref[rows_at(2 * z + (core_ref[0] ^ side), rows), :] for z in range(chips)]
    grad = contract_cols(jnp.concatenate(parts, axis=0), w_ref[...]).astype(BF16)
    for z in range(chips):
        out_ref[z] = grad[z * rows : (z + 1) * rows]


def pair_sum_kernel(mine_ref, other_ref, *out_refs):
    for i, ref in enumerate(out_refs):
        ref[...] = (mine_ref[i].astype(F32) + other_ref[i].astype(F32)).astype(BF16)


def pair_sum_whole_kernel(mine_ref, other_ref, out_ref):
    out_ref[...] = (mine_ref[...].astype(F32) + other_ref[...].astype(F32)).astype(BF16)


def middle_kernel(n, tokens_ref, mixed_ref, w_ref, gains_ref, middle_ref, second_ref, attended_ref):
    width = tokens_ref.shape[1]
    attended = jnp.concatenate([mixed_ref[s] for s in range(n)], axis=1)[:, :D]
    attended = to_blocks(attended.astype(F32), n, width).astype(BF16)
    attended_ref[...] = attended
    middle = tokens_ref[...].astype(F32) + dot(attended, w_ref[...])
    middle_ref[...] = middle
    second_ref[...] = (middle * inverse_rms(middle) * gains_ref[1:2, :]).astype(BF16)


def stacked(ref, begin=0, count=None):
    count = ref.shape[0] if count is None else count
    return jnp.concatenate([ref[begin + i] for i in range(count)], axis=0)


def hidden_kernel(second_ref, cot_ref, w_ref, down_ref, grad_ref, grads_ref, hidden_ref):
    reps, rows, _ = second_ref.shape
    units = down_ref.shape[0]
    for i in range(0, reps, 2):
        span = pl.ds(i * rows, 2 * rows)
        both = dot(stacked(second_ref, i, 2), w_ref[...])
        gate, up = both[:, :units], both[:, units:]
        grad_hidden = contract_cols(stacked(cot_ref, i, 2), down_ref[...])
        sigmoid = 1.0 / (1.0 + jnp.exp(-gate))
        silu = gate * sigmoid
        hidden_ref[span, :] = (silu * up).astype(BF16)
        grad_gate = grad_hidden * up * sigmoid * (1.0 + gate * (1.0 - sigmoid))
        grads = jnp.concatenate([grad_gate, grad_hidden * silu], axis=1).astype(BF16)
        grads_ref[span, :] = grads
        grad = contract_cols(grads, w_ref[...]).astype(BF16)
        for j in range(2):
            grad_ref[i + j] = grad[j * rows : (j + 1) * rows]


def hidden_weights_kernel(n, own, each, *refs):
    second_a, second_b, cot_a, cot_b, grads_a, grads_b, hidden_a, hidden_b, *msg_refs = refs
    cols = msg_refs[0].shape[2]
    grad = contract_rows(stacked(second_a), grads_a[...])
    grad = grad + contract_rows(stacked(second_b), grads_b[...])
    down = contract_rows(hidden_a[...], stacked(cot_a)) + contract_rows(hidden_b[...], stacked(cot_b))
    down = from_blocks(down, n, own)
    block = grad.shape[0] // n
    for s in range(n):
        both = grad[s * block : s * block + own]
        message = pack_message(both, down[s * each : (s + 1) * each], cols).astype(BF16)
        split_rows([ref.at[s] for ref in msg_refs], message)


def core_sums_kernel(*refs):
    out_ref = refs[-1]
    for core in range(2):
        sums = [
            sum(part[s].astype(F32) for s in range(core, part.shape[0], 2)) for part in refs[:-1]
        ]
        out_ref[core] = jnp.concatenate(sums, axis=0).astype(BF16)


def hidden_out_kernel(n, reps, each, rep_ref, *refs):
    parts, refs = refs[:reps], refs[reps:]
    gate_w_ref, up_w_ref, gain_ref, gate_ref, up_ref, down_ref, norm_ref, hold_ref = refs
    own = gate_ref.shape[0]
    units = 2 * reps * each
    for i, part in enumerate(parts):
        hold_ref[rep_ref[0] ^ i] = part[...]
    cols = hold_ref.shape[3]
    boths = []
    for f in range(2 * reps):
        both, down = unpack_message(hold_ref[f // 2, f % 2].astype(F32), own, each)
        boths.append(both)
        down_ref[f * each : (f + 1) * each, :] = down
    total = jnp.zeros((own, 1), F32)
    for begin, w_ref, out_ref in ((0, gate_w_ref, gate_ref), (cols // 2, up_w_ref, up_ref)):
        for s in range(n):
            place = begin + s * each
            rows = jnp.concatenate([part[:, place : place + each] for part in boths], axis=1)
            span = slice(s * units, (s + 1) * units)
            out_ref[:, span] = rows
            total = total + jnp.sum(rows * w_ref[:, span].astype(F32), axis=1, keepdims=True)
    norm_ref[...] = as_row(total) / gain_ref[...]


def down_kernel(hidden_ref, w_ref, out_ref):
    rows = out_ref.shape[1]
    for i in range(0, out_ref.shape[0], 2):
        both = dot(hidden_ref[pl.ds(i * rows, 2 * rows), :], w_ref[...]).astype(BF16)
        for j in range(2):
            out_ref[i + j] = both[j * rows : (j + 1) * rows]


def output_kernel(n, own, middle_ref, *refs):
    total = middle_ref[...]
    for ref in refs[:-1]:
        total = total + ref[...].astype(F32)
    refs[-1][...] = from_blocks(total, n, own).T.astype(BF16)


def middle_grad_kernel(n, own, reps, *refs):
    parts, refs = refs[:reps], refs[reps:]
    cot_ref, middle_ref, gains_ref, w_ref, grad_ref, branch_ref, heads_ref = refs
    rows = middle_ref.shape[0]
    middle = middle_ref[...]
    grad_second = sum(ref[...].astype(F32) for ref in parts)
    grad = cot_ref[...].astype(F32) + norm_backward(
        middle, inverse_rms(middle), gains_ref[1:2, :], grad_second
    )
    grad_ref[...] = grad
    branch = grad.astype(BF16)
    branch_ref[...] = branch
    attended = from_blocks(contract_cols(branch, w_ref[...]), n, own)
    head_cols = heads_ref.shape[2]
    if n * head_cols > D:
        attended = jnp.concatenate([attended, jnp.zeros((rows, n * head_cols - D), F32)], axis=1)
    for s in range(n):
        heads_ref[s] = attended[:, s * head_cols : (s + 1) * head_cols].astype(BF16)


def out_weights_kernel(rep_ref, core_ref, attended_ref, branch_ref, mine_ref, other_ref, hold_ref):
    store_pieces(rep_ref, (), hold_ref, contract_rows(attended_ref[...], branch_ref[...]))
    for side, ref in enumerate((mine_ref, other_ref)):
        for i in range(ref.shape[0]):
            for z in range(ref.shape[1]):
                ref[i, z] = hold_ref[2 * z + (core_ref[0] ^ side), rep_ref[0] ^ i]


def rep_sum_kernel(reps, *refs):
    total = sum(ref[...].astype(F32) for ref in refs[:reps])
    refs[reps][...] = total.astype(BF16)


def owner_sum_kernel(in_ref, out_ref):
    out_ref[...] = jnp.sum(in_ref[...].astype(F32), axis=0).astype(BF16)


def out_out_kernel(n, reps, rep_ref, *refs):
    out_ref, hold_ref = refs[reps:]
    for i in range(reps):
        hold_ref[rep_ref[0] ^ i] = refs[i][...].astype(F32)
    own = out_ref.shape[0]
    rows = jnp.concatenate([hold_ref[r] for r in range(reps)], axis=0)[:own]
    out_ref[...] = from_blocks(rows, n, own)


def attention_out_kernel(n, reps, rep_ref, *refs):
    parts, refs = refs[:reps], refs[reps:]
    q_w_ref, k_w_ref, v_w_ref, gain_ref, q_ref, k_ref, v_ref, norm_ref, hold_ref = refs
    own = q_ref.shape[0]
    cols = parts[0].shape[2]
    head_cols = cols // 3
    heads = head_cols // HD
    for i, part in enumerate(parts):
        for s in range(n):
            hold_ref[rep_ref[0] ^ i, s] = part[s].astype(F32)
    sides = [
        jnp.concatenate([hold_ref[r, s] for r in range(reps)], axis=0)[:own] for s in range(n)
    ]

    def slot(h, kind):
        begin = kind * head_cols + h % heads * HD
        return sides[h // heads][:, begin : begin + HD]

    query = jnp.concatenate([slot(h, 0) for h in range(QH)], axis=1)
    q_ref[...] = query
    total = jnp.sum(query * q_w_ref[...].astype(F32), axis=1, keepdims=True)
    total = as_row(total)
    for kind, w_ref, out_ref in ((1, k_w_ref, k_ref), (2, v_w_ref, v_ref)):
        wide = jnp.concatenate(
            [sum(slot(j * GROUP + g, kind) for g in range(GROUP)) for j in range(KVH)], axis=1
        ).T
        out_ref[...] = wide
        total = total + jnp.sum(wide * w_ref[...].astype(F32), axis=0, keepdims=True)
    norm_ref[...] = total / gain_ref[...]


def input_grad_kernel(n, own, parts_ref, tokens_ref, gains_ref, grad_ref, out_ref):
    inputs = tokens_ref[...].astype(F32)
    grad_first = sum(parts_ref[z].astype(F32) for z in range(parts_ref.shape[0]))
    total = grad_ref[...] + norm_backward(inputs, inverse_rms(inputs), gains_ref[0:1, :], grad_first)
    out_ref[...] = from_blocks(total, n, own).T


def shards(
    tokens,
    lengths,
    norm_one,
    w_query,
    w_key,
    w_value,
    w_out,
    norm_two,
    w_gate,
    w_up,
    w_down,
    cotangent,
):
    n = lax.axis_size("shard")
    reps = lax.axis_size("rep")
    nz = n // 2
    rows = tokens.shape[0]
    length = rows * n
    own = w_query.shape[0]
    held = w_down.shape[0]
    block = round_up(own + 2, 16)
    width = n * block
    piece = block // reps
    heads = -(-QH // n)
    head_cols = heads * HD
    qkv_cols = 3 * head_cols
    each = held // (2 * reps)
    units = n * each
    msg_rows = message_plan(own, each, 2 * units)[-1]
    shard_index = lax.axis_index("shard").astype(jnp.int32)
    me = shard_index.reshape(1)
    core = (shard_index % 2).reshape(1)
    rep = lax.axis_index("rep").astype(jnp.int32).reshape(1)
    own_block = (rows, width)

    (tokens_in,) = call(lambda *r: blocks_kernel(n, *r), "tokens_blocks", [(own_block, BF16)], tokens.T)
    tokens_parts = spread(tokens_in, "shard", 2)
    gains_own = jnp.pad(jnp.stack([norm_one, norm_two]), ((0, 0), (0, qkv_cols - own))).astype(F32)
    (message,) = call(
        lambda *r: attention_message_kernel(n, *r),
        "attention_message",
        [((n, piece, qkv_cols + width // 2), BF16)],
        after(w_query, tokens_in),
        w_key.T,
        w_value.T,
        w_out,
        gains_own,
        scalars=(rep,),
    )
    arrived = exchange(message)
    qkv_piece = arrived[:, :, :qkv_cols]
    qkv_tiled = jnp.broadcast_to(qkv_piece[None], (reps,) + qkv_piece.shape)
    (w_qkv,) = call(
        join_kernel,
        "join_qkv",
        [((n, reps, piece, qkv_cols), BF16)],
        lax.all_to_all(qkv_tiled, "rep", split_axis=0, concat_axis=0, tiled=True),
    )
    w_qkv = w_qkv.reshape(width, qkv_cols)
    doc_start, position = doc_layout(after(lengths, message)[0], length)
    cosines, sines = rope_tables(position)
    start = doc_start[:, None]

    split = msg_rows // 2 // 16 * 16 + 16
    part_rows = (split, msg_rows - split) if split < msg_rows else (msg_rows,)
    messages = call(
        lambda *r: hidden_message_kernel(n, reps, *r),
        "hidden_message",
        [((n, part, 2 * units), BF16) for part in part_rows],
        after(w_gate, cosines, sines, start),
        w_up,
        w_down,
        scalars=(rep,),
    )
    (cot_in,) = call(
        lambda *r: blocks_kernel(n, *r),
        "cot_blocks",
        [(own_block, BF16)],
        after(cotangent.T, messages[0], arrived, *tokens_parts[1:]),
    )
    cot_parts = spread(after(cot_in, w_qkv), "rep", 1)
    tokens_mine, tokens_other = both_cores([after(tokens_parts[0], cot_in)] + tokens_parts[1:])
    hidden_first = exchange(after(messages[0], tokens_mine))

    out_parts = spread(after(arrived, w_qkv)[:, :, qkv_cols:], "rep", 1)

    head_shape = (length, head_cols)
    first_all, query, key, value, gains, mixed = call(
        lambda *r: attend_kernel(rows, n, *r),
        "attend",
        [((length, width), BF16)]
        + [(head_shape, BF16)] * 3
        + [((2, width), F32)]
        + [(head_shape, BF16)],
        tokens_mine,
        tokens_other,
        w_qkv,
        cosines,
        sines,
        start,
        scalars=(me,),
    )
    mixed = exchange(after(mixed, hidden_first).reshape(n, rows, head_cols))
    hidden_rest = [exchange(after(message, mixed)) for message in messages[1:]]
    (out_full,) = call(
        lambda *r: join_out_kernel(reps, *r),
        "join_out",
        [((n, reps, piece, width), BF16)],
        *both_cores([after(out_parts[0], gains)] + out_parts[1:]),
        scalars=(rep, core),
    )
    out_full = out_full.reshape(width, width)

    middle, second, attended = call(
        lambda *r: middle_kernel(n, *r),
        "middle",
        [(own_block, F32), (own_block, BF16), (own_block, BF16)],
        tokens_in,
        mixed,
        out_full,
        gains,
    )
    w_hidden, w_down_in = call(
        lambda *r: hidden_weights_in_kernel(n, own, each, *r),
        "hidden_weights_in",
        [((n, block, 2 * units), BF16), ((units, width), BF16)],
        after(hidden_first, second),
        *hidden_rest,
    )
    w_hidden = w_hidden.reshape(width, 2 * units)
    cot_mine, cot_other = both_cores([after(cot_parts[0], out_full)] + cot_parts[1:])

    second_mine, second_other = both_cores(spread(second, "rep", 1))
    side_outs = [
        ((reps, rows, width), BF16),
        ((reps * rows, 2 * units), BF16),
        ((reps * rows, units), BF16),
    ]

    def hidden_side(seconds, cots, name):
        return call(hidden_kernel, name, side_outs, seconds, cots, w_hidden, w_down_in)

    def plane_sums(mine, other):
        sums = call(pair_sum_kernel, "pair_sum", [(own_block, BF16)] * reps, mine, swap(other, "shard", 1))
        return sums, deliver(sums, "rep", 1)

    grad_other, grads_other, hidden_other = hidden_side(second_other, cot_other, "hidden_other")
    grad_mine, grads_mine, hidden_mine = hidden_side(
        after(second_mine, grad_other), cot_mine, "hidden_mine"
    )
    hidden_messages = call(
        lambda *r: hidden_weights_kernel(n, own, each, *r),
        "hidden_weights",
        [((n, part, 2 * units), BF16) for part in part_rows],
        second_mine,
        second_other,
        cot_mine,
        cot_other,
        grads_mine,
        grads_other,
        hidden_mine,
        hidden_other,
    )
    hidden_sums = [exchange(hidden_messages[0])]
    sums, grad_second = plane_sums(after(grad_mine, hidden_messages[0]), grad_other)
    down_other, down_mine = [
        call(
            down_kernel,
            "down",
            [((reps, rows, width), BF16)],
            after(hidden, grad_second[1]),
            w_down_in,
        )[0]
        for hidden in (hidden_other, hidden_mine)
    ]

    grad_middle, grad_branch, grad_heads = call(
        lambda *r: middle_grad_kernel(n, own, reps, *r),
        "middle_grad",
        [(own_block, F32), (own_block, BF16), ((n, rows, head_cols), BF16)],
        *grad_second,
        cot_in,
        after(middle, down_other, down_mine),
        gains,
        out_full,
    )
    grad_heads = exchange(after(grad_heads, *hidden_sums))
    out_pieces = call(
        out_weights_kernel,
        "out_weights",
        [((reps, nz, piece, width), BF16)] * 2,
        attended,
        grad_branch,
        scalars=(rep, core),
        scratch=[((n, reps, piece, width), BF16)],
    )
    out_sums = call(
        pair_sum_kernel,
        "pair_sum",
        [((nz, piece, width), BF16)] * reps,
        out_pieces[0],
        swap(out_pieces[1], "shard", 1),
    )
    out_parts = deliver(out_sums, "rep", 1)
    hidden_sums += [exchange(after(message, grad_heads)) for message in hidden_messages[1:]]
    grad_heads = grad_heads.reshape(head_shape)
    grad_qkv, *attention_pieces = call(
        lambda *r: attend_back_kernel(reps, *r),
        "attend_back",
        [((length, qkv_cols), BF16)] + [((n, piece, qkv_cols), BF16)] * reps,
        grad_heads,
        first_all,
        query,
        key,
        value,
        cosines,
        sines,
        after(start, out_sums[0]),
        scalars=(rep,),
        scratch=[(head_shape, F32)] * 2 + [((n, reps, piece, qkv_cols), BF16)],
    )

    def rep_sum(parts, *earlier):
        return call(
            lambda *r: rep_sum_kernel(reps, *r),
            "rep_sum",
            [(parts[0].shape, BF16)],
            after(parts[0], *earlier),
            *parts[1:],
        )[0]

    def first_side(grads, side):
        return call(
            lambda *r: first_grad_kernel(rows, side, *r),
            "first_grad",
            [((nz, rows, width), BF16)],
            grads,
            w_qkv,
            scalars=(core,),
        )[0]

    out_summed = rep_sum(out_parts, grad_qkv)
    out_moved = exchange_z(after(out_summed, *hidden_sums))
    first_other = first_side(after(grad_qkv, out_summed), 1)
    first_mine = first_side(after(grad_qkv, first_other), 0)
    attention_summed = rep_sum(deliver(attention_pieces, "rep", 1), first_mine)
    attention_moved = exchange(after(attention_summed, out_moved))
    (first_sums,) = call(
        pair_sum_whole_kernel,
        "first_sum",
        [((nz, rows, width), BF16)],
        after(first_mine, attention_summed),
        swap(first_other, "shard", 1),
    )
    first_parts = exchange_z(after(first_sums, attention_moved))
    (core_sums,) = call(
        core_sums_kernel,
        "core_sums",
        [((2, msg_rows, 2 * units), BF16)],
        after(hidden_sums[0], first_sums),
        *hidden_sums[1:],
    )
    hidden_parts = spread(core_sums, "rep", 1)
    (out_piece,) = call(
        owner_sum_kernel, "owner_sum", [((piece, width), BF16)], after(out_moved, core_sums)
    )
    down_sums, down_parts = plane_sums(after(down_mine, out_piece), down_other)

    gain_rows = [gain.astype(F32)[None] for gain in (norm_one, norm_two)]
    attention_parts = spread(attention_moved, "rep", 1)
    grad_w_query, grad_w_key, grad_w_value, grad_norm_one = call(
        lambda *r: attention_out_kernel(n, reps, *r),
        "attention_out",
        [(w_query.shape, F32), (w_key.shape[::-1], F32), (w_value.shape[::-1], F32), ((1, own), F32)],
        *attention_parts,
        after(w_query, down_sums[0]),
        w_key.T,
        w_value.T,
        gain_rows[0],
        scalars=(rep,),
        scratch=[((reps, n, piece, qkv_cols), F32)],
    )

    grad_w_gate, grad_w_up, grad_w_down, grad_norm_two = call(
        lambda *r: hidden_out_kernel(n, reps, each, *r),
        "hidden_out",
        [(w_gate.shape, F32), (w_up.shape, F32), (w_down.shape, F32), ((1, own), F32)],
        *hidden_parts,
        w_gate,
        w_up,
        after(gain_rows[1], grad_norm_one),
        scalars=(rep,),
        scratch=[((reps, 2, msg_rows, 2 * units), BF16)],
    )

    (grad_w_out,) = call(
        lambda *r: out_out_kernel(n, reps, *r),
        "out_out",
        [(w_out.shape, F32)],
        *spread(out_piece, "rep", 1),
        scalars=(rep,),
        scratch=[((reps, piece, width), F32)],
    )

    (output,) = call(
        lambda *r: output_kernel(n, own, *r),
        "output",
        [((D, rows), BF16)],
        after(middle, grad_norm_two),
        *down_parts,
    )
    (input_grad,) = call(
        lambda *r: input_grad_kernel(n, own, *r),
        "input_grad",
        [((D, rows), F32)],
        first_parts,
        after(tokens_in, output, grad_w_out),
        gains,
        grad_middle,
    )

    return (
        output.T,
        input_grad.T,
        grad_norm_one[0],
        grad_w_query,
        grad_w_key.T,
        grad_w_value.T,
        grad_w_out,
        grad_norm_two[0],
        grad_w_gate,
        grad_w_up,
        grad_w_down,
    )


def solution(mesh):
    rows = P("shard", None)
    own_tokens = P(("rep", "shard"), None)
    return jax.shard_map(
        shards,
        mesh=mesh,
        in_specs=(
            own_tokens,
            P("rep", None),
            P("shard"),
            rows,
            rows,
            rows,
            rows,
            P("shard"),
            rows,
            rows,
            rows,
            own_tokens,
        ),
        out_specs=(
            own_tokens,
            own_tokens,
            P("shard"),
            rows,
            rows,
            rows,
            rows,
            P("shard"),
            rows,
            rows,
            rows,
        ),
        check_vma=False,
    )
```

```python
import jax
import jax.numpy as jnp
from jax import lax
from jax.experimental import pallas as pl
from jax.experimental.pallas import tpu as pltpu
from jax.sharding import PartitionSpec as P

D = 960
QH = 15
KVH = 5
HD = 64
FF = 2560
GROUP = QH // KVH

EPS = 1e-05
ROPE_BASE = 10000.0
MASKED = -1e30
SCALE = HD ** (-0.5)
BF16 = jnp.bfloat16
F32 = jnp.float32


def doc_layout(lengths_row, length):
    places = jnp.arange(length, dtype=jnp.int32)
    doc_ends = jnp.cumsum(lengths_row)
    passed = places[:, None] >= doc_ends[None, :]
    doc_start = jnp.sum(jnp.where(passed, lengths_row[None, :], 0), axis=1)
    return places - doc_start


def rope_tables(position):
    half_dim = HD // 2
    fraction = jnp.arange(half_dim, dtype=F32) * (2.0 / HD)
    inverse = ROPE_BASE ** (-fraction)
    angles = position.astype(F32)[:, None] * inverse[None, :]
    return (jnp.cos(angles), jnp.sin(angles))


VMEM_LIMIT = 56 * 2**20


def dot(left, right):
    return jnp.dot(left, right, preferred_element_type=F32)


def contract_rows(left, right):
    return lax.dot_general(left, right, (((0,), (0,)), ((), ())), preferred_element_type=F32)


def contract_cols(left, right):
    return lax.dot_general(left, right, (((1,), (1,)), ((), ())), preferred_element_type=F32)


def inverse_rms(values):
    return lax.rsqrt(jnp.sum(values * values, axis=-1, keepdims=True) * (1.0 / D) + EPS)


def norm_backward(values, inverse, gain, grad_norm):
    scaled = grad_norm * gain
    mean = jnp.sum(scaled * values, axis=-1, keepdims=True) * (1.0 / D)
    return inverse * scaled - values * inverse**3 * mean


def round_up(value, step):
    return -(-value // step) * step


def rows_at(index, rows):
    return pl.ds(pl.multiple_of(index * rows, rows), rows)


def to_blocks(values, n, width):
    rows, own = values.shape[0], values.shape[1] // n
    gap = jnp.zeros((rows, width // n - own), values.dtype)
    parts = []
    for s in range(n):
        parts += [values[:, s * own : (s + 1) * own], gap]
    return jnp.concatenate(parts, axis=1)


def from_blocks(values, n, own):
    block = values.shape[1] // n
    return jnp.concatenate([values[:, s * block : s * block + own] for s in range(n)], axis=1)


def swap(block, axis, k):
    count = lax.axis_size(axis)
    return lax.ppermute(block, axis, [(i, i ^ k) for i in range(count)])


def exchange(block):
    return lax.all_to_all(block, "shard", split_axis=0, concat_axis=0, tiled=True)


def spread(block, axis, step):
    return [block] + [swap(block, axis, k) for k in range(step, lax.axis_size(axis), step)]


def deliver(blocks, axis, step):
    return [blocks[0]] + [swap(block, axis, i * step) for i, block in enumerate(blocks) if i]


def exchange_z(blocks):
    groups = [list(range(core, lax.axis_size("shard"), 2)) for core in range(2)]
    return lax.all_to_all(
        blocks, "shard", split_axis=0, concat_axis=0, axis_index_groups=groups, tiled=True
    )


def after(value, *earlier):
    return lax.optimization_barrier((value,) + earlier)[0]


def later(values, *earlier):
    values = tuple(values)
    return list(lax.optimization_barrier(values + earlier)[: len(values)])


def both_cores(parts):
    stacked = jnp.stack(parts)
    return stacked, swap(stacked, "shard", 1)


def call(kernel, name, outs, *operands, scalars=(), scratch=()):
    specs = [pl.BlockSpec(memory_space=pltpu.SMEM)] * len(scalars)
    specs += [pl.BlockSpec(memory_space=pltpu.VMEM)] * len(operands)
    return pl.pallas_call(
        kernel,
        out_shape=[jax.ShapeDtypeStruct(shape, dtype) for shape, dtype in outs],
        in_specs=specs,
        out_specs=[pl.BlockSpec(memory_space=pltpu.VMEM)] * len(outs),
        scratch_shapes=[pltpu.VMEM(shape, dtype) for shape, dtype in scratch],
        compiler_params=pltpu.CompilerParams(vmem_limit_bytes=VMEM_LIMIT),
        name=name,
    )(*scalars, *operands)


def turned(values):
    half = HD // 2
    parts = []
    for begin in range(0, values.shape[1], HD):
        parts.append(-values[:, begin + half : begin + HD])
        parts.append(values[:, begin : begin + half])
    return jnp.concatenate(parts, axis=1)


def widened(values, times):
    return jnp.concatenate([values] * times, axis=1)


def head_of(values, h, heads):
    if heads == 1:
        return values
    lane = lax.broadcasted_iota(jnp.int32, values.shape, 1)
    return jnp.where(lane // HD == h, values, jnp.zeros_like(values))


def doc_starts(lengths_ref, row, rows):
    place = lax.broadcasted_iota(jnp.int32, (rows, 1), 0) + row
    end = lengths_ref[0, 0]
    starts = jnp.where(place >= end, end, 0)
    for slot in range(1, lengths_ref.shape[1]):
        end = end + lengths_ref[0, slot]
        starts = jnp.where(place >= end, end, starts)
    return starts


def masked_probs(query, key, starts, row):
    rows, cols = query.shape[0], key.shape[0]
    logits = contract_cols(query, key) * SCALE
    place = lax.broadcasted_iota(jnp.int32, (rows, cols), 1)
    own = lax.broadcasted_iota(jnp.int32, (rows, cols), 0) + row
    logits = jnp.where((place <= own) & (place >= starts), logits, MASKED)
    raised = jnp.exp(logits - jnp.max(logits, axis=-1, keepdims=True))
    return raised * (1.0 / jnp.sum(raised, axis=-1, keepdims=True))


def blocks_kernel(n, in_ref, *out_refs):
    values = to_blocks(in_ref[...].astype(F32).T, n, out_refs[0].shape[1]).astype(BF16)
    out_refs[0][...] = values
    for ref in out_refs[1:]:
        for i in range(ref.shape[0]):
            ref[i] = values


def attention_message_kernel(n, rep_ref, q_ref, k_ref, v_ref, out_ref, gain_ref, msg_ref):
    own = q_ref.shape[0]
    piece = msg_ref.shape[1]
    cols = gain_ref.shape[1]
    half = msg_ref.shape[2] - cols
    head_cols = cols // 3
    heads = head_cols // HD
    row = lax.broadcasted_iota(jnp.int32, (piece, own), 0) + rep_ref[0] * piece
    pick = jnp.where(row == lax.broadcasted_iota(jnp.int32, (piece, own), 1), 1.0, 0.0).astype(BF16)
    query, key, value = dot(pick, q_ref[...]), contract_cols(pick, k_ref[...]), contract_cols(pick, v_ref[...])
    gap = jnp.zeros((piece, HD), F32)
    wide = lax.broadcasted_iota(jnp.int32, (piece, cols), 0) + rep_ref[0] * piece
    for s in range(n):
        slots = range(s * heads, (s + 1) * heads)
        parts = [query[:, h * HD : (h + 1) * HD] if h < QH else gap for h in slots]
        for array in (key, value):
            for h in slots:
                j = h // GROUP
                parts.append(array[:, j * HD : (j + 1) * HD] if h < QH else gap)
        block = jnp.concatenate(parts, axis=1)
        for i in range(2):
            block = jnp.where(wide == own + i, gain_ref[i : i + 1, :], block)
        msg_ref[s, :, :cols] = block.astype(BF16)
    rows = to_blocks(dot(pick, out_ref[...]), n, 2 * half).astype(BF16)
    for s in range(n):
        msg_ref[s, :, cols:] = rows[:, s % 2 * half : (s % 2 + 1) * half]


def as_row(column):
    return jnp.broadcast_to(column, (column.shape[0], 128)).T[0:1, :]


def join_kernel(in_ref, out_ref):
    for r in range(in_ref.shape[0]):
        out_ref[:, r] = in_ref[r]


def join_out_kernel(reps, rep_ref, core_ref, mine_ref, other_ref, out_ref):
    first = core_ref[0] == 0
    half = mine_ref.shape[3]
    for i in range(reps):
        mine, other = mine_ref[i], other_ref[i]
        out_ref[:, rep_ref[0] ^ i, :, :half] = jnp.where(first, mine, other)
        out_ref[:, rep_ref[0] ^ i, :, half:] = jnp.where(first, other, mine)


def fill_rows(values, rows):
    if values.shape[0] == rows:
        return values
    return jnp.concatenate([values, jnp.zeros((rows - values.shape[0], values.shape[1]), F32)], axis=0)


def fill_cols(values, cols):
    if values.shape[1] == cols:
        return values
    return jnp.concatenate([values, jnp.zeros((values.shape[0], cols - values.shape[1]), F32)], axis=1)


def message_plan(own, each, cols):
    top, rows = round_up(own, 8), round_up(each, 8)
    rest = D % cols
    halved = rest and 2 * rest <= cols
    first = round_up(rows // 2, 8) if halved else rows
    total = top + D // cols * rows + (first if rest else 0)
    return top, rows, rest, halved, first, total


def pack_message(both, down, cols):
    top, rows, rest, halved, first, _ = message_plan(both.shape[0], down.shape[0], cols)
    down = fill_rows(down, rows)
    parts = [fill_rows(both, top)]
    parts += [down[:, j * cols : (j + 1) * cols] for j in range(D // cols)]
    if rest:
        tail = down[:, D - rest :]
        if halved:
            tail = jnp.concatenate([tail[:first], fill_rows(tail[first:], first)], axis=1)
        parts.append(fill_cols(tail, cols))
    return jnp.concatenate(parts, axis=0)


def unpack_message(message, own, each):
    cols = message.shape[1]
    top, rows, rest, halved, first, _ = message_plan(own, each, cols)
    parts = [message[top + j * rows : top + (j + 1) * rows] for j in range(D // cols)]
    if rest:
        tail = message[top + D // cols * rows :][:first]
        if halved:
            tail = jnp.concatenate([tail[:, :rest], tail[: rows - first, rest : 2 * rest]], axis=0)
        parts.append(tail[:, :rest])
    return message[:own], jnp.concatenate(parts, axis=1)[:each]


def hidden_message_kernel(n, reps, rep_ref, gate_ref, up_ref, down_ref, *out_refs):
    own, units = gate_ref.shape
    held = down_ref.shape[0]
    each = held // (2 * reps)
    cols = n * each
    place = lax.broadcasted_iota(jnp.int32, (1, cols), 1)
    row = lax.broadcasted_iota(jnp.int32, (round_up(each, 8), held), 0)
    for i in range(2):
        begin = each * (2 * rep_ref[0] + i)
        unit = place + begin
        for s in range(1, n):
            unit = unit + jnp.where(place >= each * s, held - each, 0)
        pick = jnp.where(lax.broadcasted_iota(jnp.int32, (units, cols), 0) == unit, 1.0, 0.0)
        pick = pick.astype(BF16)
        both = jnp.concatenate([dot(gate_ref[...], pick), dot(up_ref[...], pick)], axis=1)
        take = (lax.broadcasted_iota(jnp.int32, row.shape, 1) == row + begin) & (row < each)
        down = dot(jnp.where(take, 1.0, 0.0).astype(BF16), down_ref[...])
        message = pack_message(both, down[:each], 2 * cols).astype(BF16)
        for z in range(n // 2):
            split_rows([ref.at[2 * z + i] for ref in out_refs], message)


def split_rows(refs, values):
    begin = 0
    for ref in refs:
        rows = ref.shape[0]
        ref[...] = values[begin : begin + rows]
        begin += rows


def hidden_weights_in_kernel(n, own, each, *refs):
    parts, (w_ref, down_ref) = refs[:-2], refs[-2:]
    block = w_ref.shape[1]
    downs = []
    for s in range(n):
        message = jnp.concatenate([part[s].astype(F32) for part in parts], axis=0)
        both, down = unpack_message(message, own, each)
        w_ref[s] = fill_rows(both, block).astype(BF16)
        downs.append(down)
    down_ref[...] = to_blocks(jnp.concatenate(downs, axis=0), n, down_ref.shape[1]).astype(BF16)


def attend_kernel(rows, n, me_ref, lengths_ref, mine_ref, other_ref, *refs):
    w_ref, cos_ref, sin_ref, first_ref, q_ref, k_ref, v_ref, gains_ref, mixed_ref = refs
    length, head_cols = q_ref.shape
    heads = head_cols // HD
    width = first_ref.shape[1]
    block_rows = width // n
    own = D // n
    gap = jnp.zeros((1, block_rows - own), F32)
    gains = []
    for i in range(2):
        parts = []
        for s in range(n):
            group = w_ref[pl.ds(s * block_rows + own // 16 * 16, block_rows - own // 16 * 16), :]
            row = own % 16 + i
            spread_row = group.astype(F32)[row : row + 1, :own]
            parts += [spread_row, gap]
        gains.append(jnp.concatenate(parts, axis=1))
        gains_ref[i : i + 1, :] = gains[i]
    for side, ref in enumerate((mine_ref, other_ref)):
        for z in range(n // 2):
            inputs = ref[z].astype(F32)
            normed = inputs * inverse_rms(inputs) * gains[0]
            first_ref[rows_at(me_ref[0] ^ (2 * z + side), rows), :] = normed.astype(BF16)
    block = min(256, length)
    for i in range(length // block):
        span = pl.ds(i * block, block)
        raw = dot(first_ref[span, :], w_ref[...])
        cosines, sines = widened(cos_ref[span, :], 2 * heads), widened(sin_ref[span, :], 2 * heads)
        query, key = raw[:, :head_cols], raw[:, head_cols : 2 * head_cols]
        q_ref[span, :] = (query * cosines + turned(query) * sines).astype(BF16)
        k_ref[span, :] = (key * cosines + turned(key) * sines).astype(BF16)
        v_ref[span, :] = raw[:, 2 * head_cols :].astype(BF16)
    for i in range(length // block):
        span, past = pl.ds(i * block, block), pl.ds(0, (i + 1) * block)
        total, starts = None, doc_starts(lengths_ref, i * block, block)
        for h in range(heads):
            probs = masked_probs(head_of(q_ref[span, :], h, heads), k_ref[past, :], starts, i * block)
            mixed = head_of(dot(probs.astype(BF16), v_ref[past, :]), h, heads)
            total = mixed if total is None else total + mixed
        mixed_ref[span, :] = total.astype(BF16)


def attend_back_kernel(lengths_ref, *refs):
    g_ref, first_ref, q_ref, k_ref, v_ref, cos_ref, sin_ref, dqkv_ref, piece_ref, dk_ref, dv_ref = refs
    length, head_cols = q_ref.shape
    heads = head_cols // HD
    block = min(256, length)
    dk_ref[...] = jnp.zeros_like(dk_ref)
    dv_ref[...] = jnp.zeros_like(dv_ref)
    for i in range(length // block):
        span, past = pl.ds(i * block, block), pl.ds(0, (i + 1) * block)
        total, starts = None, doc_starts(lengths_ref, i * block, block)
        for h in range(heads):
            query = head_of(q_ref[span, :], h, heads)
            grad = head_of(g_ref[span, :], h, heads)
            key = k_ref[past, :]
            probs = masked_probs(query, key, starts, i * block)
            grad_probs = contract_cols(grad, v_ref[past, :])
            delta = jnp.sum(probs * grad_probs, axis=-1, keepdims=True)
            grad_logits = (probs * (grad_probs - delta)).astype(BF16)
            grad_query = head_of(dot(grad_logits, key), h, heads)
            total = grad_query if total is None else total + grad_query
            dv_ref[past, :] += contract_rows(probs.astype(BF16), grad)
            dk_ref[past, :] += contract_rows(grad_logits, query)
        total = total * SCALE
        cosines, sines = widened(cos_ref[span, :], 2 * heads), widened(sin_ref[span, :], 2 * heads)
        back = total * cosines - turned(total) * sines
        dqkv_ref[span, :head_cols] = back.astype(BF16)
    for i in range(length // block):
        span = pl.ds(i * block, block)
        total = dk_ref[span, :] * SCALE
        cosines, sines = widened(cos_ref[span, :], 2 * heads), widened(sin_ref[span, :], 2 * heads)
        back = total * cosines - turned(total) * sines
        dqkv_ref[span, head_cols : 2 * head_cols] = back.astype(BF16)
        dqkv_ref[span, 2 * head_cols :] = dv_ref[span, :].astype(BF16)
    store_pieces(piece_ref, contract_rows(first_ref[...], dqkv_ref[...]))


def store_pieces(piece_ref, grad):
    reps, n, piece, _ = piece_ref.shape
    for s in range(n):
        for r in range(reps):
            begin = (s * reps + r) * piece
            piece_ref[r, s] = grad[begin : begin + piece].astype(BF16)


def first_grad_kernel(rows, side, core_ref, dqkv_ref, w_ref, out_ref):
    chips = out_ref.shape[0]
    parts = [dqkv_ref[rows_at(2 * z + (core_ref[0] ^ side), rows), :] for z in range(chips)]
    grad = contract_cols(jnp.concatenate(parts, axis=0), w_ref[...]).astype(BF16)
    for z in range(chips):
        out_ref[z] = grad[z * rows : (z + 1) * rows]


def pair_sum_kernel(mine_ref, other_ref, *out_refs):
    for i, ref in enumerate(out_refs):
        ref[...] = (mine_ref[i].astype(F32) + other_ref[i].astype(F32)).astype(BF16)


def pair_sum_whole_kernel(mine_ref, other_ref, out_ref):
    out_ref[...] = (mine_ref[...].astype(F32) + other_ref[...].astype(F32)).astype(BF16)


def middle_kernel(n, tokens_ref, mixed_ref, w_ref, gains_ref, middle_ref, second_ref, attended_ref):
    width = tokens_ref.shape[1]
    attended = jnp.concatenate([mixed_ref[s] for s in range(n)], axis=1)[:, :D]
    attended = to_blocks(attended.astype(F32), n, width).astype(BF16)
    attended_ref[...] = attended
    middle = tokens_ref[...].astype(F32) + dot(attended, w_ref[...])
    middle_ref[...] = middle
    second_ref[...] = (middle * inverse_rms(middle) * gains_ref[1:2, :]).astype(BF16)


def stacked(ref, begin=0, count=None):
    count = ref.shape[0] if count is None else count
    return jnp.concatenate([ref[begin + i] for i in range(count)], axis=0)


def hidden_kernel(second_ref, cot_ref, w_ref, down_ref, grad_ref, grads_ref, hidden_ref):
    reps, rows, _ = second_ref.shape
    units = down_ref.shape[0]
    for i in range(0, reps, 2):
        span = pl.ds(i * rows, 2 * rows)
        both = dot(stacked(second_ref, i, 2), w_ref[...])
        gate, up = both[:, :units], both[:, units:]
        grad_hidden = contract_cols(stacked(cot_ref, i, 2), down_ref[...])
        sigmoid = 1.0 / (1.0 + jnp.exp(-gate))
        silu = gate * sigmoid
        hidden_ref[span, :] = (silu * up).astype(BF16)
        grad_gate = grad_hidden * up * sigmoid * (1.0 + gate * (1.0 - sigmoid))
        grads = jnp.concatenate([grad_gate, grad_hidden * silu], axis=1).astype(BF16)
        grads_ref[span, :] = grads
        grad = contract_cols(grads, w_ref[...]).astype(BF16)
        for j in range(2):
            grad_ref[i + j] = grad[j * rows : (j + 1) * rows]


def hidden_weights_kernel(n, own, each, *refs):
    second_a, second_b, cot_a, cot_b, grads_a, grads_b, hidden_a, hidden_b, *msg_refs = refs
    cols = msg_refs[0].shape[2]
    grad = contract_rows(stacked(second_a), grads_a[...])
    grad = grad + contract_rows(stacked(second_b), grads_b[...])
    down = contract_rows(hidden_a[...], stacked(cot_a)) + contract_rows(hidden_b[...], stacked(cot_b))
    down = from_blocks(down, n, own)
    block = grad.shape[0] // n
    for s in range(n):
        both = grad[s * block : s * block + own]
        message = pack_message(both, down[s * each : (s + 1) * each], cols).astype(BF16)
        split_rows([ref.at[s] for ref in msg_refs], message)


def core_sums_kernel(*refs):
    out_ref = refs[-1]
    for core in range(2):
        sums = [
            sum(part[s].astype(F32) for s in range(core, part.shape[0], 2)) for part in refs[:-1]
        ]
        out_ref[core] = jnp.concatenate(sums, axis=0).astype(BF16)


def hidden_out_kernel(n, reps, each, rep_ref, *refs):
    parts, refs = refs[:reps], refs[reps:]
    gate_w_ref, up_w_ref, gain_ref, gate_ref, up_ref, down_ref, norm_ref, hold_ref = refs
    own = gate_ref.shape[0]
    units = 2 * reps * each
    for i, part in enumerate(parts):
        hold_ref[rep_ref[0] ^ i] = part[...]
    cols = hold_ref.shape[3]
    boths = []
    for f in range(2 * reps):
        both, down = unpack_message(hold_ref[f // 2, f % 2].astype(F32), own, each)
        boths.append(both)
        down_ref[f * each : (f + 1) * each, :] = down
    total = jnp.zeros((own, 1), F32)
    for begin, w_ref, out_ref in ((0, gate_w_ref, gate_ref), (cols // 2, up_w_ref, up_ref)):
        for s in range(n):
            place = begin + s * each
            rows = jnp.concatenate([part[:, place : place + each] for part in boths], axis=1)
            span = slice(s * units, (s + 1) * units)
            out_ref[:, span] = rows
            total = total + jnp.sum(rows * w_ref[:, span].astype(F32), axis=1, keepdims=True)
    norm_ref[...] = as_row(total) / gain_ref[...]


def down_kernel(hidden_ref, w_ref, out_ref):
    rows = out_ref.shape[1]
    for i in range(0, out_ref.shape[0], 2):
        both = dot(hidden_ref[pl.ds(i * rows, 2 * rows), :], w_ref[...]).astype(BF16)
        for j in range(2):
            out_ref[i + j] = both[j * rows : (j + 1) * rows]


def output_kernel(n, own, middle_ref, *refs):
    total = middle_ref[...]
    for ref in refs[:-1]:
        total = total + ref[...].astype(F32)
    refs[-1][...] = from_blocks(total, n, own).T.astype(BF16)


def middle_grad_kernel(n, own, reps, *refs):
    parts, refs = refs[:reps], refs[reps:]
    cot_ref, middle_ref, gains_ref, w_ref, grad_ref, branch_ref, heads_ref = refs
    rows = middle_ref.shape[0]
    middle = middle_ref[...]
    grad_second = sum(ref[...].astype(F32) for ref in parts)
    grad = cot_ref[...].astype(F32) + norm_backward(
        middle, inverse_rms(middle), gains_ref[1:2, :], grad_second
    )
    grad_ref[...] = grad
    branch = grad.astype(BF16)
    branch_ref[...] = branch
    attended = from_blocks(contract_cols(branch, w_ref[...]), n, own)
    head_cols = heads_ref.shape[2]
    if n * head_cols > D:
        attended = jnp.concatenate([attended, jnp.zeros((rows, n * head_cols - D), F32)], axis=1)
    for s in range(n):
        heads_ref[s] = attended[:, s * head_cols : (s + 1) * head_cols].astype(BF16)


def out_weights_kernel(rep_ref, me_ref, attended_ref, branch_ref, mine_ref, other_ref, hold_ref):
    store_pieces(hold_ref, contract_rows(attended_ref[...], branch_ref[...]))
    for side, ref in enumerate((mine_ref, other_ref)):
        for i in range(ref.shape[0]):
            for z in range(ref.shape[1]):
                ref[i, z] = hold_ref[rep_ref[0] ^ i, me_ref[0] ^ (2 * z + side)]


def rep_sum_kernel(in_ref, out_ref):
    out_ref[...] = sum(in_ref[r].astype(F32) for r in range(in_ref.shape[0])).astype(BF16)


def chip_sums_kernel(reps, *refs):
    for z, out_ref in enumerate(refs[reps:]):
        out_ref[...] = sum(ref[z].astype(F32) for ref in refs[:reps]).astype(BF16)


def owner_sum_kernel(*refs):
    refs[-1][...] = sum(ref[...].astype(F32) for ref in refs[:-1]).astype(BF16)


def out_out_kernel(n, reps, rep_ref, *refs):
    out_ref, hold_ref = refs[reps:]
    for i in range(reps):
        hold_ref[rep_ref[0] ^ i] = refs[i][...].astype(F32)
    own = out_ref.shape[0]
    rows = jnp.concatenate([hold_ref[r] for r in range(reps)], axis=0)[:own]
    out_ref[...] = from_blocks(rows, n, own)


def attention_out_kernel(n, reps, rep_ref, *refs):
    parts, refs = refs[:reps], refs[reps:]
    q_w_ref, k_w_ref, v_w_ref, gain_ref, q_ref, k_ref, v_ref, norm_ref, hold_ref = refs
    own = q_ref.shape[0]
    cols = parts[0].shape[2]
    head_cols = cols // 3
    heads = head_cols // HD
    for i, part in enumerate(parts):
        for s in range(n):
            hold_ref[rep_ref[0] ^ i, s] = part[s].astype(F32)
    sides = [
        jnp.concatenate([hold_ref[r, s] for r in range(reps)], axis=0)[:own] for s in range(n)
    ]

    def slot(h, kind):
        begin = kind * head_cols + h % heads * HD
        return sides[h // heads][:, begin : begin + HD]

    query = jnp.concatenate([slot(h, 0) for h in range(QH)], axis=1)
    q_ref[...] = query
    total = jnp.sum(query * q_w_ref[...].astype(F32), axis=1, keepdims=True)
    total = as_row(total)
    for kind, w_ref, out_ref in ((1, k_w_ref, k_ref), (2, v_w_ref, v_ref)):
        wide = jnp.concatenate(
            [sum(slot(j * GROUP + g, kind) for g in range(GROUP)) for j in range(KVH)], axis=1
        ).T
        out_ref[...] = wide
        total = total + jnp.sum(wide * w_ref[...].astype(F32), axis=0, keepdims=True)
    norm_ref[...] = total / gain_ref[...]


def input_grad_kernel(n, own, parts_ref, tokens_ref, gains_ref, grad_ref, out_ref):
    inputs = tokens_ref[...].astype(F32)
    grad_first = sum(parts_ref[z].astype(F32) for z in range(parts_ref.shape[0]))
    total = grad_ref[...] + norm_backward(inputs, inverse_rms(inputs), gains_ref[0:1, :], grad_first)
    out_ref[...] = from_blocks(total, n, own).T


def shards(
    tokens,
    lengths,
    norm_one,
    w_query,
    w_key,
    w_value,
    w_out,
    norm_two,
    w_gate,
    w_up,
    w_down,
    cotangent,
):
    n = lax.axis_size("shard")
    reps = lax.axis_size("rep")
    nz = n // 2
    rows = tokens.shape[0]
    length = rows * n
    own = w_query.shape[0]
    held = w_down.shape[0]
    block = round_up(own + 2, 16)
    width = n * block
    piece = block // reps
    heads = -(-QH // n)
    head_cols = heads * HD
    qkv_cols = 3 * head_cols
    each = held // (2 * reps)
    units = n * each
    msg_rows = message_plan(own, each, 2 * units)[-1]
    shard_index = lax.axis_index("shard").astype(jnp.int32)
    me = shard_index.reshape(1)
    core = (shard_index % 2).reshape(1)
    rep = lax.axis_index("rep").astype(jnp.int32).reshape(1)
    own_block = (rows, width)

    (tokens_in,) = call(lambda *r: blocks_kernel(n, *r), "tokens_blocks", [(own_block, BF16)], tokens.T)
    tokens_parts = spread(tokens_in, "shard", 2)
    gains_own = jnp.pad(jnp.stack([norm_one, norm_two]), ((0, 0), (0, qkv_cols - own))).astype(F32)
    (message,) = call(
        lambda *r: attention_message_kernel(n, *r),
        "attention_message",
        [((n, piece, qkv_cols + width // 2), BF16)],
        after(w_query, tokens_in),
        w_key.T,
        w_value.T,
        w_out,
        gains_own,
        scalars=(rep,),
    )
    arrived = exchange(message)
    qkv_piece = arrived[:, :, :qkv_cols]
    qkv_tiled = jnp.broadcast_to(qkv_piece[None], (reps,) + qkv_piece.shape)
    (w_qkv,) = call(
        join_kernel,
        "join_qkv",
        [((n, reps, piece, qkv_cols), BF16)],
        lax.all_to_all(qkv_tiled, "rep", split_axis=0, concat_axis=0, tiled=True),
    )
    w_qkv = w_qkv.reshape(width, qkv_cols)
    position = doc_layout(after(lengths, message)[0], length)
    cosines, sines = rope_tables(position)

    split = round_up(msg_rows // 3, 16)
    part_rows = (split, msg_rows - split) if split < msg_rows else (msg_rows,)
    messages = call(
        lambda *r: hidden_message_kernel(n, reps, *r),
        "hidden_message",
        [((n, part, 2 * units), BF16) for part in part_rows],
        after(w_gate, cosines, sines),
        w_up,
        w_down,
        scalars=(rep,),
    )
    (cot_in,) = call(
        lambda *r: blocks_kernel(n, *r),
        "cot_blocks",
        [(own_block, BF16)],
        after(cotangent.T, messages[0], arrived, *tokens_parts[1:]),
    )
    cot_parts = spread(after(cot_in, w_qkv), "rep", 1)
    tokens_mine, tokens_other = both_cores([after(tokens_parts[0], cot_in)] + tokens_parts[1:])
    hidden_first = exchange(after(messages[0], tokens_mine))

    out_parts = spread(after(arrived, w_qkv)[:, :, qkv_cols:], "rep", 1)

    head_shape = (length, head_cols)
    first_all, query, key, value, gains, mixed = call(
        lambda *r: attend_kernel(rows, n, *r),
        "attend",
        [((length, width), BF16)]
        + [(head_shape, BF16)] * 3
        + [((2, width), F32)]
        + [(head_shape, BF16)],
        tokens_mine,
        tokens_other,
        w_qkv,
        cosines,
        sines,
        scalars=(me, lengths),
    )
    mixed = exchange(after(mixed, hidden_first).reshape(n, rows, head_cols))
    hidden_rest = [exchange(after(message, mixed)) for message in messages[1:]]
    (out_full,) = call(
        lambda *r: join_out_kernel(reps, *r),
        "join_out",
        [((n, reps, piece, width), BF16)],
        *both_cores([after(out_parts[0], gains)] + out_parts[1:]),
        scalars=(rep, core),
    )
    out_full = out_full.reshape(width, width)

    middle, second, attended = call(
        lambda *r: middle_kernel(n, *r),
        "middle",
        [(own_block, F32), (own_block, BF16), (own_block, BF16)],
        tokens_in,
        mixed,
        out_full,
        gains,
    )
    w_hidden, w_down_in = call(
        lambda *r: hidden_weights_in_kernel(n, own, each, *r),
        "hidden_weights_in",
        [((n, block, 2 * units), BF16), ((units, width), BF16)],
        after(hidden_first, second),
        *hidden_rest,
    )
    w_hidden = w_hidden.reshape(width, 2 * units)
    cot_mine, cot_other = both_cores([after(cot_parts[0], out_full)] + cot_parts[1:])

    second_mine, second_other = both_cores(spread(second, "rep", 1))
    side_outs = [
        ((reps, rows, width), BF16),
        ((reps * rows, 2 * units), BF16),
        ((reps * rows, units), BF16),
    ]

    def hidden_side(seconds, cots, name):
        return call(hidden_kernel, name, side_outs, seconds, cots, w_hidden, w_down_in)

    def plane_sums(mine, other):
        sums = call(pair_sum_kernel, "pair_sum", [(own_block, BF16)] * reps, mine, swap(other, "shard", 1))
        return sums, deliver(sums, "rep", 1)

    grad_other, grads_other, hidden_other = hidden_side(second_other, cot_other, "hidden_other")
    grad_mine, grads_mine, hidden_mine = hidden_side(
        after(second_mine, grad_other), cot_mine, "hidden_mine"
    )
    hidden_messages = call(
        lambda *r: hidden_weights_kernel(n, own, each, *r),
        "hidden_weights",
        [((n, part, 2 * units), BF16) for part in part_rows],
        second_mine,
        second_other,
        cot_mine,
        cot_other,
        grads_mine,
        grads_other,
        hidden_mine,
        hidden_other,
    )
    hidden_sums = [exchange(hidden_messages[0])]
    sums, grad_second = plane_sums(after(grad_mine, hidden_messages[0]), grad_other)
    down_other, down_mine = [
        call(
            down_kernel,
            "down",
            [((reps, rows, width), BF16)],
            after(hidden, grad_second[1]),
            w_down_in,
        )[0]
        for hidden in (hidden_other, hidden_mine)
    ]

    grad_middle, grad_branch, grad_heads = call(
        lambda *r: middle_grad_kernel(n, own, reps, *r),
        "middle_grad",
        [(own_block, F32), (own_block, BF16), ((n, rows, head_cols), BF16)],
        *grad_second,
        cot_in,
        after(middle, down_other, down_mine),
        gains,
        out_full,
    )
    grad_heads = exchange(after(grad_heads, *hidden_sums))
    out_pieces = call(
        out_weights_kernel,
        "out_weights",
        [((reps, nz, piece, width), BF16)] * 2,
        attended,
        grad_branch,
        scalars=(rep, me),
        scratch=[((reps, n, piece, width), BF16)],
    )
    out_sums = call(
        pair_sum_kernel,
        "pair_sum",
        [((nz, piece, width), BF16)] * reps,
        out_pieces[0],
        swap(out_pieces[1], "shard", 1),
    )
    out_parts = deliver(out_sums, "rep", 1)
    hidden_sums += [exchange(after(message, grad_heads)) for message in hidden_messages[1:]]
    grad_heads = grad_heads.reshape(head_shape)
    grad_qkv, attention_pieces = call(
        attend_back_kernel,
        "attend_back",
        [((length, qkv_cols), BF16), ((reps, n, piece, qkv_cols), BF16)],
        grad_heads,
        first_all,
        query,
        key,
        value,
        cosines,
        after(sines, out_sums[0]),
        scalars=(lengths,),
        scratch=[(head_shape, F32)] * 2,
    )

    def first_side(grads, side):
        return call(
            lambda *r: first_grad_kernel(rows, side, *r),
            "first_grad",
            [((nz, rows, width), BF16)],
            grads,
            w_qkv,
            scalars=(core,),
        )[0]

    attention_arrived = lax.all_to_all(
        after(attention_pieces, *hidden_sums), "rep", split_axis=0, concat_axis=0, tiled=True
    )
    out_summed = call(
        lambda *r: chip_sums_kernel(reps, *r),
        "chip_sums",
        [((piece, width), BF16)] * nz,
        after(out_parts[0], grad_qkv),
        *out_parts[1:],
    )
    out_moved = deliver(out_summed, "shard", 2)
    first_other = first_side(after(grad_qkv, out_summed[0]), 1)
    first_mine = first_side(after(grad_qkv, first_other), 0)
    (attention_summed,) = call(
        rep_sum_kernel,
        "rep_sum",
        [((n, piece, qkv_cols), BF16)],
        after(attention_arrived, first_mine, *out_moved[1:]),
    )
    attention_moved = exchange(attention_summed)
    (first_sums,) = call(
        pair_sum_whole_kernel,
        "first_sum",
        [((nz, rows, width), BF16)],
        after(first_mine, attention_summed),
        swap(first_other, "shard", 1),
    )
    (core_sums,) = call(
        core_sums_kernel,
        "core_sums",
        [((2, msg_rows, 2 * units), BF16)],
        after(hidden_sums[0], first_sums),
        *hidden_sums[1:],
    )
    hidden_parts = spread(core_sums, "rep", 1)
    first_parts = exchange_z(after(first_sums, attention_moved, core_sums))

    gain_rows = [gain.astype(F32)[None] for gain in (norm_one, norm_two)]
    attention_parts = spread(attention_moved, "rep", 1)
    grad_w_query, grad_w_key, grad_w_value, grad_norm_one = call(
        lambda *r: attention_out_kernel(n, reps, *r),
        "attention_out",
        [(w_query.shape, F32), (w_key.shape[::-1], F32), (w_value.shape[::-1], F32), ((1, own), F32)],
        *attention_parts,
        after(w_query, core_sums),
        w_key.T,
        w_value.T,
        gain_rows[0],
        scalars=(rep,),
        scratch=[((reps, n, piece, qkv_cols), F32)],
    )

    grad_w_gate, grad_w_up, grad_w_down, grad_norm_two = call(
        lambda *r: hidden_out_kernel(n, reps, each, *r),
        "hidden_out",
        [(w_gate.shape, F32), (w_up.shape, F32), (w_down.shape, F32), ((1, own), F32)],
        *hidden_parts,
        w_gate,
        w_up,
        after(gain_rows[1], grad_norm_one),
        scalars=(rep,),
        scratch=[((reps, 2, msg_rows, 2 * units), BF16)],
    )

    (out_piece,) = call(
        owner_sum_kernel,
        "owner_sum",
        [((piece, width), BF16)],
        after(out_moved[0], grad_norm_two),
        *out_moved[1:],
    )
    _, down_parts = plane_sums(after(down_mine, out_piece), after(down_other, grad_norm_one))
    (output,) = call(
        lambda *r: output_kernel(n, own, *r),
        "output",
        [((D, rows), BF16)],
        after(middle, out_piece),
        *down_parts,
    )
    (grad_w_out,) = call(
        lambda *r: out_out_kernel(n, reps, *r),
        "out_out",
        [(w_out.shape, F32)],
        *spread(out_piece, "rep", 1),
        scalars=(rep,),
        scratch=[((reps, piece, width), F32)],
    )

    (input_grad,) = call(
        lambda *r: input_grad_kernel(n, own, *r),
        "input_grad",
        [((D, rows), F32)],
        first_parts,
        after(tokens_in, output, grad_w_out),
        gains,
        grad_middle,
    )

    return (
        output.T,
        input_grad.T,
        grad_norm_one[0],
        grad_w_query,
        grad_w_key.T,
        grad_w_value.T,
        grad_w_out,
        grad_norm_two[0],
        grad_w_gate,
        grad_w_up,
        grad_w_down,
    )


def solution(mesh):
    rows = P("shard", None)
    own_tokens = P(("rep", "shard"), None)
    return jax.shard_map(
        shards,
        mesh=mesh,
        in_specs=(
            own_tokens,
            P("rep", None),
            P("shard"),
            rows,
            rows,
            rows,
            rows,
            P("shard"),
            rows,
            rows,
            rows,
            own_tokens,
        ),
        out_specs=(
            own_tokens,
            own_tokens,
            P("shard"),
            rows,
            rows,
            rows,
            rows,
            P("shard"),
            rows,
            rows,
            rows,
        ),
        check_vma=False,
    )
```

```python
import jax
import jax.numpy as jnp
from jax import lax
from jax.experimental import pallas as pl
from jax.experimental.pallas import tpu as pltpu
from jax.sharding import PartitionSpec as P

D = 960
QH = 15
KVH = 5
HD = 64
FF = 2560
GROUP = QH // KVH

EPS = 1e-05
ROPE_BASE = 10000.0
MASKED = -1e30
SCALE = HD ** (-0.5)
BF16 = jnp.bfloat16
F32 = jnp.float32


def doc_layout(lengths_row, length):
    places = jnp.arange(length, dtype=jnp.int32)
    doc_ends = jnp.cumsum(lengths_row)
    passed = places[:, None] >= doc_ends[None, :]
    doc_start = jnp.sum(jnp.where(passed, lengths_row[None, :], 0), axis=1)
    return places - doc_start


def rope_tables(position):
    half_dim = HD // 2
    fraction = jnp.arange(half_dim, dtype=F32) * (2.0 / HD)
    inverse = ROPE_BASE ** (-fraction)
    angles = position.astype(F32)[:, None] * inverse[None, :]
    return (jnp.cos(angles), jnp.sin(angles))


VMEM_LIMIT = 56 * 2**20


def dot(left, right):
    return jnp.dot(left, right, preferred_element_type=F32)


def contract_rows(left, right):
    return lax.dot_general(left, right, (((0,), (0,)), ((), ())), preferred_element_type=F32)


def contract_cols(left, right):
    return lax.dot_general(left, right, (((1,), (1,)), ((), ())), preferred_element_type=F32)


def inverse_rms(values):
    return lax.rsqrt(jnp.sum(values * values, axis=-1, keepdims=True) * (1.0 / D) + EPS)


def norm_backward(values, inverse, gain, grad_norm):
    scaled = grad_norm * gain
    mean = jnp.sum(scaled * values, axis=-1, keepdims=True) * (1.0 / D)
    return inverse * scaled - values * inverse**3 * mean


def round_up(value, step):
    return -(-value // step) * step


def rows_at(index, rows):
    return pl.ds(pl.multiple_of(index * rows, rows), rows)


def to_blocks(values, n, width):
    rows, own = values.shape[0], values.shape[1] // n
    gap = jnp.zeros((rows, width // n - own), values.dtype)
    parts = []
    for s in range(n):
        parts += [values[:, s * own : (s + 1) * own], gap]
    return jnp.concatenate(parts, axis=1)


def from_blocks(values, n, own):
    block = values.shape[1] // n
    return jnp.concatenate([values[:, s * block : s * block + own] for s in range(n)], axis=1)


def swap(block, axis, k):
    count = lax.axis_size(axis)
    return lax.ppermute(block, axis, [(i, i ^ k) for i in range(count)])


def exchange(block):
    return lax.all_to_all(block, "shard", split_axis=0, concat_axis=0, tiled=True)


def spread(block, axis, step):
    return [block] + [swap(block, axis, k) for k in range(step, lax.axis_size(axis), step)]


def deliver(blocks, axis, step):
    return [blocks[0]] + [swap(block, axis, i * step) for i, block in enumerate(blocks) if i]


def exchange_z(blocks):
    groups = [list(range(core, lax.axis_size("shard"), 2)) for core in range(2)]
    return lax.all_to_all(
        blocks, "shard", split_axis=0, concat_axis=0, axis_index_groups=groups, tiled=True
    )


def after(value, *earlier):
    return lax.optimization_barrier((value,) + earlier)[0]


def later(values, *earlier):
    values = tuple(values)
    return list(lax.optimization_barrier(values + earlier)[: len(values)])


def both_cores(parts):
    stacked = jnp.stack(parts)
    return stacked, swap(stacked, "shard", 1)


def call(kernel, name, outs, *operands, scalars=(), scratch=()):
    specs = [pl.BlockSpec(memory_space=pltpu.SMEM)] * len(scalars)
    specs += [pl.BlockSpec(memory_space=pltpu.VMEM)] * len(operands)
    return pl.pallas_call(
        kernel,
        out_shape=[jax.ShapeDtypeStruct(shape, dtype) for shape, dtype in outs],
        in_specs=specs,
        out_specs=[pl.BlockSpec(memory_space=pltpu.VMEM)] * len(outs),
        scratch_shapes=[pltpu.VMEM(shape, dtype) for shape, dtype in scratch],
        compiler_params=pltpu.CompilerParams(vmem_limit_bytes=VMEM_LIMIT),
        name=name,
    )(*scalars, *operands)


def turned(values):
    half = HD // 2
    parts = []
    for begin in range(0, values.shape[1], HD):
        parts.append(-values[:, begin + half : begin + HD])
        parts.append(values[:, begin : begin + half])
    return jnp.concatenate(parts, axis=1)


def widened(values, times):
    return jnp.concatenate([values] * times, axis=1)


def head_of(values, h, heads):
    if heads == 1:
        return values
    lane = lax.broadcasted_iota(jnp.int32, values.shape, 1)
    return jnp.where(lane // HD == h, values, jnp.zeros_like(values))


def doc_starts(lengths_ref, row, rows):
    place = lax.broadcasted_iota(jnp.int32, (rows, 1), 0) + row
    end = lengths_ref[0, 0]
    starts = jnp.where(place >= end, end, 0)
    for slot in range(1, lengths_ref.shape[1]):
        end = end + lengths_ref[0, slot]
        starts = jnp.where(place >= end, end, starts)
    return starts


def masked_probs(query, key, starts, row):
    rows, cols = query.shape[0], key.shape[0]
    logits = contract_cols(query, key) * SCALE
    place = lax.broadcasted_iota(jnp.int32, (rows, cols), 1)
    own = lax.broadcasted_iota(jnp.int32, (rows, cols), 0) + row
    logits = jnp.where((place <= own) & (place >= starts), logits, MASKED)
    raised = jnp.exp(logits - jnp.max(logits, axis=-1, keepdims=True))
    return raised * (1.0 / jnp.sum(raised, axis=-1, keepdims=True))


def blocks_kernel(n, in_ref, *out_refs):
    values = to_blocks(in_ref[...].astype(F32).T, n, out_refs[0].shape[1]).astype(BF16)
    out_refs[0][...] = values
    for ref in out_refs[1:]:
        for i in range(ref.shape[0]):
            ref[i] = values


def attention_message_kernel(n, rep_ref, q_ref, k_ref, v_ref, out_ref, gain_ref, msg_ref):
    own = q_ref.shape[0]
    piece = msg_ref.shape[1]
    cols = gain_ref.shape[1]
    half = msg_ref.shape[2] - cols
    head_cols = cols // 3
    heads = head_cols // HD
    row = lax.broadcasted_iota(jnp.int32, (piece, own), 0) + rep_ref[0] * piece
    pick = jnp.where(row == lax.broadcasted_iota(jnp.int32, (piece, own), 1), 1.0, 0.0).astype(BF16)
    query, key, value = dot(pick, q_ref[...]), contract_cols(pick, k_ref[...]), contract_cols(pick, v_ref[...])
    gap = jnp.zeros((piece, HD), F32)
    wide = lax.broadcasted_iota(jnp.int32, (piece, cols), 0) + rep_ref[0] * piece
    for s in range(n):
        slots = range(s * heads, (s + 1) * heads)
        parts = [query[:, h * HD : (h + 1) * HD] if h < QH else gap for h in slots]
        for array in (key, value):
            for h in slots:
                j = h // GROUP
                parts.append(array[:, j * HD : (j + 1) * HD] if h < QH else gap)
        block = jnp.concatenate(parts, axis=1)
        for i in range(2):
            block = jnp.where(wide == own + i, gain_ref[i : i + 1, :], block)
        msg_ref[s, :, :cols] = block.astype(BF16)
    rows = to_blocks(dot(pick, out_ref[...]), n, 2 * half).astype(BF16)
    for s in range(n):
        msg_ref[s, :, cols:] = rows[:, s % 2 * half : (s % 2 + 1) * half]


def as_row(column):
    return jnp.broadcast_to(column, (column.shape[0], 128)).T[0:1, :]


def join_kernel(in_ref, out_ref):
    for r in range(in_ref.shape[0]):
        out_ref[:, r] = in_ref[r]


def join_out_kernel(reps, rep_ref, core_ref, mine_ref, other_ref, out_ref):
    first = core_ref[0] == 0
    half = mine_ref.shape[3]
    for i in range(reps):
        mine, other = mine_ref[i], other_ref[i]
        out_ref[:, rep_ref[0] ^ i, :, :half] = jnp.where(first, mine, other)
        out_ref[:, rep_ref[0] ^ i, :, half:] = jnp.where(first, other, mine)


def fill_rows(values, rows):
    if values.shape[0] == rows:
        return values
    return jnp.concatenate([values, jnp.zeros((rows - values.shape[0], values.shape[1]), F32)], axis=0)


def fill_cols(values, cols):
    if values.shape[1] == cols:
        return values
    return jnp.concatenate([values, jnp.zeros((values.shape[0], cols - values.shape[1]), F32)], axis=1)


def message_plan(own, each, cols):
    top, rows = round_up(own, 8), round_up(each, 8)
    rest = D % cols
    halved = rest and 2 * rest <= cols
    first = round_up(rows // 2, 8) if halved else rows
    total = top + D // cols * rows + (first if rest else 0)
    return top, rows, rest, halved, first, total


def pack_message(both, down, cols):
    top, rows, rest, halved, first, _ = message_plan(both.shape[0], down.shape[0], cols)
    down = fill_rows(down, rows)
    parts = [fill_rows(both, top)]
    parts += [down[:, j * cols : (j + 1) * cols] for j in range(D // cols)]
    if rest:
        tail = down[:, D - rest :]
        if halved:
            tail = jnp.concatenate([tail[:first], fill_rows(tail[first:], first)], axis=1)
        parts.append(fill_cols(tail, cols))
    return jnp.concatenate(parts, axis=0)


def unpack_message(message, own, each):
    cols = message.shape[1]
    top, rows, rest, halved, first, _ = message_plan(own, each, cols)
    parts = [message[top + j * rows : top + (j + 1) * rows] for j in range(D // cols)]
    if rest:
        tail = message[top + D // cols * rows :][:first]
        if halved:
            tail = jnp.concatenate([tail[:, :rest], tail[: rows - first, rest : 2 * rest]], axis=0)
        parts.append(tail[:, :rest])
    return message[:own], jnp.concatenate(parts, axis=1)[:each]


def hidden_message_kernel(n, reps, rep_ref, gate_ref, up_ref, down_ref, *out_refs):
    own, units = gate_ref.shape
    held = down_ref.shape[0]
    each = held // (2 * reps)
    cols = n * each
    place = lax.broadcasted_iota(jnp.int32, (1, cols), 1)
    row = lax.broadcasted_iota(jnp.int32, (round_up(each, 8), held), 0)
    for i in range(2):
        begin = each * (2 * rep_ref[0] + i)
        unit = place + begin
        for s in range(1, n):
            unit = unit + jnp.where(place >= each * s, held - each, 0)
        pick = jnp.where(lax.broadcasted_iota(jnp.int32, (units, cols), 0) == unit, 1.0, 0.0)
        pick = pick.astype(BF16)
        both = jnp.concatenate([dot(gate_ref[...], pick), dot(up_ref[...], pick)], axis=1)
        take = (lax.broadcasted_iota(jnp.int32, row.shape, 1) == row + begin) & (row < each)
        down = dot(jnp.where(take, 1.0, 0.0).astype(BF16), down_ref[...])
        message = pack_message(both, down[:each], 2 * cols).astype(BF16)
        for z in range(n // 2):
            split_rows([ref.at[2 * z + i] for ref in out_refs], message)


def split_rows(refs, values):
    begin = 0
    for ref in refs:
        rows = ref.shape[0]
        ref[...] = values[begin : begin + rows]
        begin += rows


def hidden_weights_in_kernel(n, own, each, *refs):
    parts, (w_ref, down_ref) = refs[:-2], refs[-2:]
    block = w_ref.shape[1]
    downs = []
    for s in range(n):
        message = jnp.concatenate([part[s].astype(F32) for part in parts], axis=0)
        both, down = unpack_message(message, own, each)
        w_ref[s] = fill_rows(both, block).astype(BF16)
        downs.append(down)
    down_ref[...] = to_blocks(jnp.concatenate(downs, axis=0), n, down_ref.shape[1]).astype(BF16)


def attend_kernel(rows, n, me_ref, lengths_ref, mine_ref, other_ref, *refs):
    w_ref, cos_ref, sin_ref, first_ref, q_ref, k_ref, v_ref, gains_ref, mixed_ref = refs
    length, head_cols = q_ref.shape
    heads = head_cols // HD
    width = first_ref.shape[1]
    block_rows = width // n
    own = D // n
    gap = jnp.zeros((1, block_rows - own), F32)
    gains = []
    for i in range(2):
        parts = []
        for s in range(n):
            group = w_ref[pl.ds(s * block_rows + own // 16 * 16, block_rows - own // 16 * 16), :]
            row = own % 16 + i
            spread_row = group.astype(F32)[row : row + 1, :own]
            parts += [spread_row, gap]
        gains.append(jnp.concatenate(parts, axis=1))
        gains_ref[i : i + 1, :] = gains[i]
    for side, ref in enumerate((mine_ref, other_ref)):
        for z in range(n // 2):
            inputs = ref[z].astype(F32)
            normed = inputs * inverse_rms(inputs) * gains[0]
            first_ref[rows_at(me_ref[0] ^ (2 * z + side), rows), :] = normed.astype(BF16)
    block = min(256, length)
    for i in range(length // block):
        span = pl.ds(i * block, block)
        raw = dot(first_ref[span, :], w_ref[...])
        cosines, sines = widened(cos_ref[span, :], 2 * heads), widened(sin_ref[span, :], 2 * heads)
        query, key = raw[:, :head_cols], raw[:, head_cols : 2 * head_cols]
        q_ref[span, :] = (query * cosines + turned(query) * sines).astype(BF16)
        k_ref[span, :] = (key * cosines + turned(key) * sines).astype(BF16)
        v_ref[span, :] = raw[:, 2 * head_cols :].astype(BF16)
    for i in range(length // block):
        span, past = pl.ds(i * block, block), pl.ds(0, (i + 1) * block)
        total, starts = None, doc_starts(lengths_ref, i * block, block)
        for h in range(heads):
            probs = masked_probs(head_of(q_ref[span, :], h, heads), k_ref[past, :], starts, i * block)
            mixed = head_of(dot(probs.astype(BF16), v_ref[past, :]), h, heads)
            total = mixed if total is None else total + mixed
        mixed_ref[span, :] = total.astype(BF16)


def attend_back_kernel(lengths_ref, *refs):
    g_ref, first_ref, q_ref, k_ref, v_ref, cos_ref, sin_ref, dqkv_ref, piece_ref, dk_ref, dv_ref = refs
    length, head_cols = q_ref.shape
    heads = head_cols // HD
    block = min(256, length)
    dk_ref[...] = jnp.zeros_like(dk_ref)
    dv_ref[...] = jnp.zeros_like(dv_ref)
    for i in range(length // block):
        span, past = pl.ds(i * block, block), pl.ds(0, (i + 1) * block)
        total, starts = None, doc_starts(lengths_ref, i * block, block)
        for h in range(heads):
            query = head_of(q_ref[span, :], h, heads)
            grad = head_of(g_ref[span, :], h, heads)
            key = k_ref[past, :]
            probs = masked_probs(query, key, starts, i * block)
            grad_probs = contract_cols(grad, v_ref[past, :])
            delta = jnp.sum(probs * grad_probs, axis=-1, keepdims=True)
            grad_logits = (probs * (grad_probs - delta)).astype(BF16)
            grad_query = head_of(dot(grad_logits, key), h, heads)
            total = grad_query if total is None else total + grad_query
            dv_ref[past, :] += contract_rows(probs.astype(BF16), grad)
            dk_ref[past, :] += contract_rows(grad_logits, query)
        total = total * SCALE
        cosines, sines = widened(cos_ref[span, :], 2 * heads), widened(sin_ref[span, :], 2 * heads)
        back = total * cosines - turned(total) * sines
        dqkv_ref[span, :head_cols] = back.astype(BF16)
    for i in range(length // block):
        span = pl.ds(i * block, block)
        total = dk_ref[span, :] * SCALE
        cosines, sines = widened(cos_ref[span, :], 2 * heads), widened(sin_ref[span, :], 2 * heads)
        back = total * cosines - turned(total) * sines
        dqkv_ref[span, head_cols : 2 * head_cols] = back.astype(BF16)
        dqkv_ref[span, 2 * head_cols :] = dv_ref[span, :].astype(BF16)
    store_pieces(piece_ref, contract_rows(first_ref[...], dqkv_ref[...]))


def store_pieces(piece_ref, grad):
    reps, n, piece, _ = piece_ref.shape
    for s in range(n):
        for r in range(reps):
            begin = (s * reps + r) * piece
            piece_ref[r, s] = grad[begin : begin + piece].astype(BF16)


def first_grad_kernel(rows, side, core_ref, dqkv_ref, w_ref, out_ref):
    chips = out_ref.shape[0]
    parts = [dqkv_ref[rows_at(2 * z + (core_ref[0] ^ side), rows), :] for z in range(chips)]
    grad = contract_cols(jnp.concatenate(parts, axis=0), w_ref[...]).astype(BF16)
    for z in range(chips):
        out_ref[z] = grad[z * rows : (z + 1) * rows]


def pair_sum_kernel(mine_ref, other_ref, *out_refs):
    for i, ref in enumerate(out_refs):
        ref[...] = (mine_ref[i].astype(F32) + other_ref[i].astype(F32)).astype(BF16)


def pair_sum_whole_kernel(mine_ref, other_ref, out_ref):
    out_ref[...] = (mine_ref[...].astype(F32) + other_ref[...].astype(F32)).astype(BF16)


def middle_kernel(n, tokens_ref, mixed_ref, w_ref, gains_ref, middle_ref, second_ref, attended_ref):
    width = tokens_ref.shape[1]
    attended = jnp.concatenate([mixed_ref[s] for s in range(n)], axis=1)[:, :D]
    attended = to_blocks(attended.astype(F32), n, width).astype(BF16)
    attended_ref[...] = attended
    middle = tokens_ref[...].astype(F32) + dot(attended, w_ref[...])
    middle_ref[...] = middle
    second_ref[...] = (middle * inverse_rms(middle) * gains_ref[1:2, :]).astype(BF16)


def stacked(ref, begin=0, count=None):
    count = ref.shape[0] if count is None else count
    return jnp.concatenate([ref[begin + i] for i in range(count)], axis=0)


def hidden_kernel(second_ref, cot_ref, w_ref, down_ref, grad_ref, grads_ref, hidden_ref):
    reps, rows, _ = second_ref.shape
    units = down_ref.shape[0]
    for i in range(0, reps, 2):
        span = pl.ds(i * rows, 2 * rows)
        both = dot(stacked(second_ref, i, 2), w_ref[...])
        gate, up = both[:, :units], both[:, units:]
        grad_hidden = contract_cols(stacked(cot_ref, i, 2), down_ref[...])
        sigmoid = 1.0 / (1.0 + jnp.exp(-gate))
        silu = gate * sigmoid
        hidden_ref[span, :] = (silu * up).astype(BF16)
        grad_gate = grad_hidden * up * sigmoid * (1.0 + gate * (1.0 - sigmoid))
        grads = jnp.concatenate([grad_gate, grad_hidden * silu], axis=1).astype(BF16)
        grads_ref[span, :] = grads
        grad = contract_cols(grads, w_ref[...]).astype(BF16)
        for j in range(2):
            grad_ref[i + j] = grad[j * rows : (j + 1) * rows]


def hidden_weights_kernel(n, own, each, *refs):
    second_a, second_b, cot_a, cot_b, grads_a, grads_b, hidden_a, hidden_b, *msg_refs = refs
    cols = msg_refs[0].shape[2]
    grad = contract_rows(stacked(second_a), grads_a[...])
    grad = grad + contract_rows(stacked(second_b), grads_b[...])
    down = contract_rows(hidden_a[...], stacked(cot_a)) + contract_rows(hidden_b[...], stacked(cot_b))
    down = from_blocks(down, n, own)
    block = grad.shape[0] // n
    for s in range(n):
        both = grad[s * block : s * block + own]
        message = pack_message(both, down[s * each : (s + 1) * each], cols).astype(BF16)
        split_rows([ref.at[s] for ref in msg_refs], message)


def core_sums_kernel(*refs):
    out_ref = refs[-1]
    for core in range(2):
        sums = [
            sum(part[s].astype(F32) for s in range(core, part.shape[0], 2)) for part in refs[:-1]
        ]
        out_ref[core] = jnp.concatenate(sums, axis=0).astype(BF16)


def hidden_out_kernel(n, reps, each, rep_ref, *refs):
    parts, refs = refs[:reps], refs[reps:]
    gate_w_ref, up_w_ref, gain_ref, gate_ref, up_ref, down_ref, norm_ref, hold_ref = refs
    own = gate_ref.shape[0]
    units = 2 * reps * each
    for i, part in enumerate(parts):
        hold_ref[rep_ref[0] ^ i] = part[...]
    cols = hold_ref.shape[3]
    boths = []
    for f in range(2 * reps):
        both, down = unpack_message(hold_ref[f // 2, f % 2].astype(F32), own, each)
        boths.append(both)
        down_ref[f * each : (f + 1) * each, :] = down
    total = jnp.zeros((own, 1), F32)
    for begin, w_ref, out_ref in ((0, gate_w_ref, gate_ref), (cols // 2, up_w_ref, up_ref)):
        for s in range(n):
            place = begin + s * each
            rows = jnp.concatenate([part[:, place : place + each] for part in boths], axis=1)
            span = slice(s * units, (s + 1) * units)
            out_ref[:, span] = rows
            total = total + jnp.sum(rows * w_ref[:, span].astype(F32), axis=1, keepdims=True)
    norm_ref[...] = as_row(total) / gain_ref[...]


def down_kernel(hidden_ref, w_ref, out_ref):
    rows = out_ref.shape[1]
    for i in range(0, out_ref.shape[0], 2):
        both = dot(hidden_ref[pl.ds(i * rows, 2 * rows), :], w_ref[...]).astype(BF16)
        for j in range(2):
            out_ref[i + j] = both[j * rows : (j + 1) * rows]


def output_kernel(n, own, middle_ref, *refs):
    total = middle_ref[...]
    for ref in refs[:-1]:
        total = total + ref[...].astype(F32)
    refs[-1][...] = from_blocks(total, n, own).T.astype(BF16)


def middle_grad_kernel(n, own, reps, *refs):
    parts, refs = refs[:reps], refs[reps:]
    cot_ref, middle_ref, gains_ref, w_ref, grad_ref, branch_ref, heads_ref = refs
    rows = middle_ref.shape[0]
    middle = middle_ref[...]
    grad_second = sum(ref[...].astype(F32) for ref in parts)
    grad = cot_ref[...].astype(F32) + norm_backward(
        middle, inverse_rms(middle), gains_ref[1:2, :], grad_second
    )
    grad_ref[...] = grad
    branch = grad.astype(BF16)
    branch_ref[...] = branch
    attended = from_blocks(contract_cols(branch, w_ref[...]), n, own)
    head_cols = heads_ref.shape[2]
    if n * head_cols > D:
        attended = jnp.concatenate([attended, jnp.zeros((rows, n * head_cols - D), F32)], axis=1)
    for s in range(n):
        heads_ref[s] = attended[:, s * head_cols : (s + 1) * head_cols].astype(BF16)


def out_weights_kernel(rep_ref, me_ref, attended_ref, branch_ref, mine_ref, other_ref, hold_ref):
    store_pieces(hold_ref, contract_rows(attended_ref[...], branch_ref[...]))
    for side, ref in enumerate((mine_ref, other_ref)):
        for i in range(ref.shape[0]):
            for z in range(ref.shape[1]):
                ref[i, z] = hold_ref[rep_ref[0] ^ i, me_ref[0] ^ (2 * z + side)]


def rep_sum_kernel(in_ref, out_ref):
    out_ref[...] = sum(in_ref[r].astype(F32) for r in range(in_ref.shape[0])).astype(BF16)


def chip_sums_kernel(reps, *refs):
    for z, out_ref in enumerate(refs[reps:]):
        out_ref[...] = sum(ref[z].astype(F32) for ref in refs[:reps]).astype(BF16)


def owner_sum_kernel(*refs):
    refs[-1][...] = sum(ref[...].astype(F32) for ref in refs[:-1]).astype(BF16)


def out_out_kernel(n, reps, rep_ref, *refs):
    out_ref, hold_ref = refs[reps:]
    for i in range(reps):
        hold_ref[rep_ref[0] ^ i] = refs[i][...].astype(F32)
    own = out_ref.shape[0]
    rows = jnp.concatenate([hold_ref[r] for r in range(reps)], axis=0)[:own]
    out_ref[...] = from_blocks(rows, n, own)


def attention_out_kernel(n, reps, rep_ref, *refs):
    parts, refs = refs[:reps], refs[reps:]
    q_w_ref, k_w_ref, v_w_ref, gain_ref, q_ref, k_ref, v_ref, norm_ref, hold_ref = refs
    own = q_ref.shape[0]
    cols = parts[0].shape[2]
    head_cols = cols // 3
    heads = head_cols // HD
    for i, part in enumerate(parts):
        for s in range(n):
            hold_ref[rep_ref[0] ^ i, s] = part[s].astype(F32)
    sides = [
        jnp.concatenate([hold_ref[r, s] for r in range(reps)], axis=0)[:own] for s in range(n)
    ]

    def slot(h, kind):
        begin = kind * head_cols + h % heads * HD
        return sides[h // heads][:, begin : begin + HD]

    query = jnp.concatenate([slot(h, 0) for h in range(QH)], axis=1)
    q_ref[...] = query
    total = jnp.sum(query * q_w_ref[...].astype(F32), axis=1, keepdims=True)
    total = as_row(total)
    for kind, w_ref, out_ref in ((1, k_w_ref, k_ref), (2, v_w_ref, v_ref)):
        wide = jnp.concatenate(
            [sum(slot(j * GROUP + g, kind) for g in range(GROUP)) for j in range(KVH)], axis=1
        ).T
        out_ref[...] = wide
        total = total + jnp.sum(wide * w_ref[...].astype(F32), axis=0, keepdims=True)
    norm_ref[...] = total / gain_ref[...]


def input_grad_kernel(n, own, parts_ref, tokens_ref, gains_ref, grad_ref, out_ref):
    inputs = tokens_ref[...].astype(F32)
    grad_first = sum(parts_ref[z].astype(F32) for z in range(parts_ref.shape[0]))
    total = grad_ref[...] + norm_backward(inputs, inverse_rms(inputs), gains_ref[0:1, :], grad_first)
    out_ref[...] = from_blocks(total, n, own).T


def shards(
    tokens,
    lengths,
    norm_one,
    w_query,
    w_key,
    w_value,
    w_out,
    norm_two,
    w_gate,
    w_up,
    w_down,
    cotangent,
):
    n = lax.axis_size("shard")
    reps = lax.axis_size("rep")
    nz = n // 2
    rows = tokens.shape[0]
    length = rows * n
    own = w_query.shape[0]
    held = w_down.shape[0]
    block = round_up(own + 2, 16)
    width = n * block
    piece = block // reps
    heads = -(-QH // n)
    head_cols = heads * HD
    qkv_cols = 3 * head_cols
    each = held // (2 * reps)
    units = n * each
    msg_rows = message_plan(own, each, 2 * units)[-1]
    shard_index = lax.axis_index("shard").astype(jnp.int32)
    me = shard_index.reshape(1)
    core = (shard_index % 2).reshape(1)
    rep = lax.axis_index("rep").astype(jnp.int32).reshape(1)
    own_block = (rows, width)

    (tokens_in,) = call(lambda *r: blocks_kernel(n, *r), "tokens_blocks", [(own_block, BF16)], tokens.T)
    tokens_parts = spread(tokens_in, "shard", 2)
    gains_own = jnp.pad(jnp.stack([norm_one, norm_two]), ((0, 0), (0, qkv_cols - own))).astype(F32)
    (message,) = call(
        lambda *r: attention_message_kernel(n, *r),
        "attention_message",
        [((n, piece, qkv_cols + width // 2), BF16)],
        after(w_query, tokens_in),
        w_key.T,
        w_value.T,
        w_out,
        gains_own,
        scalars=(rep,),
    )
    arrived = exchange(message)
    qkv_piece = arrived[:, :, :qkv_cols]
    qkv_tiled = jnp.broadcast_to(qkv_piece[None], (reps,) + qkv_piece.shape)
    (w_qkv,) = call(
        join_kernel,
        "join_qkv",
        [((n, reps, piece, qkv_cols), BF16)],
        lax.all_to_all(qkv_tiled, "rep", split_axis=0, concat_axis=0, tiled=True),
    )
    w_qkv = w_qkv.reshape(width, qkv_cols)
    position = doc_layout(after(lengths, message)[0], length)
    cosines, sines = rope_tables(position)

    split = round_up(msg_rows // 2, 16)
    part_rows = (split, msg_rows - split) if split < msg_rows else (msg_rows,)
    messages = call(
        lambda *r: hidden_message_kernel(n, reps, *r),
        "hidden_message",
        [((n, part, 2 * units), BF16) for part in part_rows],
        after(w_gate, cosines, sines),
        w_up,
        w_down,
        scalars=(rep,),
    )
    (cot_in,) = call(
        lambda *r: blocks_kernel(n, *r),
        "cot_blocks",
        [(own_block, BF16)],
        after(cotangent.T, messages[0], arrived, *tokens_parts[1:]),
    )
    cot_parts = spread(after(cot_in, w_qkv), "rep", 1)
    tokens_mine, tokens_other = both_cores([after(tokens_parts[0], cot_in)] + tokens_parts[1:])
    hidden_first = exchange(after(messages[0], tokens_mine))

    out_parts = spread(after(arrived, w_qkv)[:, :, qkv_cols:], "rep", 1)

    head_shape = (length, head_cols)
    first_all, query, key, value, gains, mixed = call(
        lambda *r: attend_kernel(rows, n, *r),
        "attend",
        [((length, width), BF16)]
        + [(head_shape, BF16)] * 3
        + [((2, width), F32)]
        + [(head_shape, BF16)],
        tokens_mine,
        tokens_other,
        w_qkv,
        cosines,
        sines,
        scalars=(me, lengths),
    )
    mixed = exchange(after(mixed, hidden_first).reshape(n, rows, head_cols))
    hidden_rest = [exchange(after(message, mixed)) for message in messages[1:]]
    (out_full,) = call(
        lambda *r: join_out_kernel(reps, *r),
        "join_out",
        [((n, reps, piece, width), BF16)],
        *both_cores([after(out_parts[0], gains)] + out_parts[1:]),
        scalars=(rep, core),
    )
    out_full = out_full.reshape(width, width)

    middle, second, attended = call(
        lambda *r: middle_kernel(n, *r),
        "middle",
        [(own_block, F32), (own_block, BF16), (own_block, BF16)],
        tokens_in,
        mixed,
        out_full,
        gains,
    )
    w_hidden, w_down_in = call(
        lambda *r: hidden_weights_in_kernel(n, own, each, *r),
        "hidden_weights_in",
        [((n, block, 2 * units), BF16), ((units, width), BF16)],
        after(hidden_first, second),
        *hidden_rest,
    )
    w_hidden = w_hidden.reshape(width, 2 * units)
    cot_mine, cot_other = both_cores([after(cot_parts[0], out_full)] + cot_parts[1:])

    second_mine, second_other = both_cores(spread(second, "rep", 1))
    side_outs = [
        ((reps, rows, width), BF16),
        ((reps * rows, 2 * units), BF16),
        ((reps * rows, units), BF16),
    ]

    def hidden_side(seconds, cots, name):
        return call(hidden_kernel, name, side_outs, seconds, cots, w_hidden, w_down_in)

    def plane_sums(mine, other):
        sums = call(pair_sum_kernel, "pair_sum", [(own_block, BF16)] * reps, mine, swap(other, "shard", 1))
        return sums, deliver(sums, "rep", 1)

    grad_other, grads_other, hidden_other = hidden_side(second_other, cot_other, "hidden_other")
    grad_mine, grads_mine, hidden_mine = hidden_side(
        after(second_mine, grad_other), cot_mine, "hidden_mine"
    )
    hidden_messages = call(
        lambda *r: hidden_weights_kernel(n, own, each, *r),
        "hidden_weights",
        [((n, part, 2 * units), BF16) for part in part_rows],
        second_mine,
        second_other,
        cot_mine,
        cot_other,
        grads_mine,
        grads_other,
        hidden_mine,
        hidden_other,
    )
    hidden_sums = [exchange(hidden_messages[0])]
    sums, grad_second = plane_sums(after(grad_mine, hidden_messages[0]), grad_other)
    down_other, down_mine = [
        call(
            down_kernel,
            "down",
            [((reps, rows, width), BF16)],
            after(hidden, grad_second[1]),
            w_down_in,
        )[0]
        for hidden in (hidden_other, hidden_mine)
    ]

    grad_middle, grad_branch, grad_heads = call(
        lambda *r: middle_grad_kernel(n, own, reps, *r),
        "middle_grad",
        [(own_block, F32), (own_block, BF16), ((n, rows, head_cols), BF16)],
        *grad_second,
        cot_in,
        after(middle, down_other, down_mine),
        gains,
        out_full,
    )
    grad_heads = exchange(after(grad_heads, *hidden_sums))
    out_pieces = call(
        out_weights_kernel,
        "out_weights",
        [((reps, nz, piece, width), BF16)] * 2,
        attended,
        grad_branch,
        scalars=(rep, me),
        scratch=[((reps, n, piece, width), BF16)],
    )
    out_sums = call(
        pair_sum_kernel,
        "pair_sum",
        [((nz, piece, width), BF16)] * reps,
        out_pieces[0],
        swap(out_pieces[1], "shard", 1),
    )
    out_parts = deliver(out_sums, "rep", 1)
    hidden_sums += [exchange(after(message, grad_heads, out_pieces[0])) for message in hidden_messages[1:]]
    grad_heads = grad_heads.reshape(head_shape)
    grad_qkv, attention_pieces = call(
        attend_back_kernel,
        "attend_back",
        [((length, qkv_cols), BF16), ((reps, n, piece, qkv_cols), BF16)],
        grad_heads,
        first_all,
        query,
        key,
        value,
        cosines,
        after(sines, out_sums[0]),
        scalars=(lengths,),
        scratch=[(head_shape, F32)] * 2,
    )

    def first_side(grads, side):
        return call(
            lambda *r: first_grad_kernel(rows, side, *r),
            "first_grad",
            [((nz, rows, width), BF16)],
            grads,
            w_qkv,
            scalars=(core,),
        )[0]

    attention_arrived = lax.all_to_all(
        after(attention_pieces, *hidden_sums), "rep", split_axis=0, concat_axis=0, tiled=True
    )
    (core_sums,) = call(
        core_sums_kernel,
        "core_sums",
        [((2, msg_rows, 2 * units), BF16)],
        after(hidden_sums[0], grad_qkv, *out_parts[1:]),
        *hidden_sums[1:],
    )
    hidden_parts = spread(core_sums, "rep", 1)
    first_other = first_side(after(grad_qkv, core_sums), 1)
    first_mine = first_side(after(grad_qkv, first_other), 0)
    out_summed = call(
        lambda *r: chip_sums_kernel(reps, *r),
        "chip_sums",
        [((piece, width), BF16)] * nz,
        after(out_parts[0], first_mine),
        *out_parts[1:],
    )
    out_moved = deliver(out_summed, "shard", 2)
    (attention_summed,) = call(
        rep_sum_kernel,
        "rep_sum",
        [((n, piece, qkv_cols), BF16)],
        after(attention_arrived, out_summed[0]),
    )
    attention_moved = exchange(attention_summed)
    (first_sums,) = call(
        pair_sum_whole_kernel,
        "first_sum",
        [((nz, rows, width), BF16)],
        after(first_mine, attention_summed, *hidden_parts[1:3]),
        swap(first_other, "shard", 1),
    )
    first_parts = exchange_z(after(first_sums, attention_moved))
    attention_parts = spread(attention_moved, "rep", 1)
    (out_piece,) = call(
        owner_sum_kernel,
        "owner_sum",
        [((piece, width), BF16)],
        after(out_moved[0], first_sums),
        *out_moved[1:],
    )
    down_sums, down_parts = plane_sums(
        after(down_mine, out_piece, attention_parts[1]), after(down_other, first_sums)
    )

    gain_rows = [gain.astype(F32)[None] for gain in (norm_one, norm_two)]
    grad_w_gate, grad_w_up, grad_w_down, grad_norm_two = call(
        lambda *r: hidden_out_kernel(n, reps, each, *r),
        "hidden_out",
        [(w_gate.shape, F32), (w_up.shape, F32), (w_down.shape, F32), ((1, own), F32)],
        *hidden_parts,
        w_gate,
        w_up,
        after(gain_rows[1], down_sums[0]),
        scalars=(rep,),
        scratch=[((reps, 2, msg_rows, 2 * units), BF16)],
    )

    grad_w_query, grad_w_key, grad_w_value, grad_norm_one = call(
        lambda *r: attention_out_kernel(n, reps, *r),
        "attention_out",
        [(w_query.shape, F32), (w_key.shape[::-1], F32), (w_value.shape[::-1], F32), ((1, own), F32)],
        *attention_parts,
        after(w_query, grad_norm_two),
        w_key.T,
        w_value.T,
        gain_rows[0],
        scalars=(rep,),
        scratch=[((reps, n, piece, qkv_cols), F32)],
    )

    (grad_w_out,) = call(
        lambda *r: out_out_kernel(n, reps, *r),
        "out_out",
        [(w_out.shape, F32)],
        *later(spread(out_piece, "rep", 1), grad_norm_one),
        scalars=(rep,),
        scratch=[((reps, piece, width), F32)],
    )

    (input_grad,) = call(
        lambda *r: input_grad_kernel(n, own, *r),
        "input_grad",
        [((D, rows), F32)],
        first_parts,
        after(tokens_in, grad_w_out),
        gains,
        grad_middle,
    )

    (output,) = call(
        lambda *r: output_kernel(n, own, *r),
        "output",
        [((D, rows), BF16)],
        after(middle, input_grad),
        *down_parts,
    )
    return (
        output.T,
        input_grad.T,
        grad_norm_one[0],
        grad_w_query,
        grad_w_key.T,
        grad_w_value.T,
        grad_w_out,
        grad_norm_two[0],
        grad_w_gate,
        grad_w_up,
        grad_w_down,
    )


def solution(mesh):
    rows = P("shard", None)
    own_tokens = P(("rep", "shard"), None)
    return jax.shard_map(
        shards,
        mesh=mesh,
        in_specs=(
            own_tokens,
            P("rep", None),
            P("shard"),
            rows,
            rows,
            rows,
            rows,
            P("shard"),
            rows,
            rows,
            rows,
            own_tokens,
        ),
        out_specs=(
            own_tokens,
            own_tokens,
            P("shard"),
            rows,
            rows,
            rows,
            rows,
            P("shard"),
            rows,
            rows,
            rows,
        ),
        check_vma=False,
    )
```

```python
import jax
import jax.numpy as jnp
from jax import lax
from jax.experimental import pallas as pl
from jax.experimental.pallas import tpu as pltpu
from jax.sharding import PartitionSpec as P

D = 960
QH = 15
KVH = 5
HD = 64
FF = 2560
GROUP = QH // KVH

EPS = 1e-05
ROPE_BASE = 10000.0
MASKED = -1e30
SCALE = HD ** (-0.5)
BF16 = jnp.bfloat16
F32 = jnp.float32


def doc_layout(lengths_row, length):
    places = jnp.arange(length, dtype=jnp.int32)
    doc_ends = jnp.cumsum(lengths_row)
    passed = places[:, None] >= doc_ends[None, :]
    doc_start = jnp.sum(jnp.where(passed, lengths_row[None, :], 0), axis=1)
    return places - doc_start


def rope_tables(position):
    half_dim = HD // 2
    fraction = jnp.arange(half_dim, dtype=F32) * (2.0 / HD)
    inverse = ROPE_BASE ** (-fraction)
    angles = position.astype(F32)[:, None] * inverse[None, :]
    return (jnp.cos(angles), jnp.sin(angles))


VMEM_LIMIT = 56 * 2**20


def dot(left, right):
    return jnp.dot(left, right, preferred_element_type=F32)


def contract_rows(left, right):
    return lax.dot_general(left, right, (((0,), (0,)), ((), ())), preferred_element_type=F32)


def contract_cols(left, right):
    return lax.dot_general(left, right, (((1,), (1,)), ((), ())), preferred_element_type=F32)


def inverse_rms(values):
    return lax.rsqrt(jnp.sum(values * values, axis=-1, keepdims=True) * (1.0 / D) + EPS)


def norm_backward(values, inverse, gain, grad_norm):
    scaled = grad_norm * gain
    mean = jnp.sum(scaled * values, axis=-1, keepdims=True) * (1.0 / D)
    return inverse * scaled - values * inverse**3 * mean


def round_up(value, step):
    return -(-value // step) * step


def rows_at(index, rows):
    return pl.ds(pl.multiple_of(index * rows, rows), rows)


def to_blocks(values, n, width):
    rows, own = values.shape[0], values.shape[1] // n
    gap = jnp.zeros((rows, width // n - own), values.dtype)
    parts = []
    for s in range(n):
        parts += [values[:, s * own : (s + 1) * own], gap]
    return jnp.concatenate(parts, axis=1)


def from_blocks(values, n, own):
    block = values.shape[1] // n
    return jnp.concatenate([values[:, s * block : s * block + own] for s in range(n)], axis=1)


def swap(block, axis, k):
    count = lax.axis_size(axis)
    return lax.ppermute(block, axis, [(i, i ^ k) for i in range(count)])


def exchange(block):
    return lax.all_to_all(block, "shard", split_axis=0, concat_axis=0, tiled=True)


def spread(block, axis, step):
    return [block] + [swap(block, axis, k) for k in range(step, lax.axis_size(axis), step)]


def deliver(blocks, axis, step):
    return [blocks[0]] + [swap(block, axis, i * step) for i, block in enumerate(blocks) if i]


def exchange_z(blocks):
    groups = [list(range(core, lax.axis_size("shard"), 2)) for core in range(2)]
    return lax.all_to_all(
        blocks, "shard", split_axis=0, concat_axis=0, axis_index_groups=groups, tiled=True
    )


def after(value, *earlier):
    return lax.optimization_barrier((value,) + earlier)[0]


def later(values, *earlier):
    values = tuple(values)
    return list(lax.optimization_barrier(values + earlier)[: len(values)])


def both_cores(parts):
    stacked = jnp.stack(parts)
    return stacked, swap(stacked, "shard", 1)


def call(kernel, name, outs, *operands, scalars=(), scratch=()):
    specs = [pl.BlockSpec(memory_space=pltpu.SMEM)] * len(scalars)
    specs += [pl.BlockSpec(memory_space=pltpu.VMEM)] * len(operands)
    return pl.pallas_call(
        kernel,
        out_shape=[jax.ShapeDtypeStruct(shape, dtype) for shape, dtype in outs],
        in_specs=specs,
        out_specs=[pl.BlockSpec(memory_space=pltpu.VMEM)] * len(outs),
        scratch_shapes=[pltpu.VMEM(shape, dtype) for shape, dtype in scratch],
        compiler_params=pltpu.CompilerParams(vmem_limit_bytes=VMEM_LIMIT),
        name=name,
    )(*scalars, *operands)


def turned(values):
    half = HD // 2
    parts = []
    for begin in range(0, values.shape[1], HD):
        parts.append(-values[:, begin + half : begin + HD])
        parts.append(values[:, begin : begin + half])
    return jnp.concatenate(parts, axis=1)


def widened(values, times):
    return jnp.concatenate([values] * times, axis=1)


def head_of(values, h, heads):
    if heads == 1:
        return values
    lane = lax.broadcasted_iota(jnp.int32, values.shape, 1)
    return jnp.where(lane // HD == h, values, jnp.zeros_like(values))


def doc_starts(lengths_ref, row, rows):
    place = lax.broadcasted_iota(jnp.int32, (rows, 1), 0) + row
    end = lengths_ref[0, 0]
    starts = jnp.where(place >= end, end, 0)
    for slot in range(1, lengths_ref.shape[1]):
        end = end + lengths_ref[0, slot]
        starts = jnp.where(place >= end, end, starts)
    return starts


def masked_probs(query, key, starts, row):
    rows, cols = query.shape[0], key.shape[0]
    logits = contract_cols(query, key) * SCALE
    place = lax.broadcasted_iota(jnp.int32, (rows, cols), 1)
    own = lax.broadcasted_iota(jnp.int32, (rows, cols), 0) + row
    logits = jnp.where((place <= own) & (place >= starts), logits, MASKED)
    raised = jnp.exp(logits - jnp.max(logits, axis=-1, keepdims=True))
    return raised * (1.0 / jnp.sum(raised, axis=-1, keepdims=True))


def blocks_kernel(n, in_ref, *out_refs):
    values = to_blocks(in_ref[...].astype(F32).T, n, out_refs[0].shape[1]).astype(BF16)
    out_refs[0][...] = values
    for ref in out_refs[1:]:
        for i in range(ref.shape[0]):
            ref[i] = values


def attention_message_kernel(n, rep_ref, q_ref, k_ref, v_ref, out_ref, gain_ref, msg_ref):
    own = q_ref.shape[0]
    piece = msg_ref.shape[1]
    cols = gain_ref.shape[1]
    half = msg_ref.shape[2] - cols
    head_cols = cols // 3
    heads = head_cols // HD
    row = lax.broadcasted_iota(jnp.int32, (piece, own), 0) + rep_ref[0] * piece
    pick = jnp.where(row == lax.broadcasted_iota(jnp.int32, (piece, own), 1), 1.0, 0.0).astype(BF16)
    query, key, value = dot(pick, q_ref[...]), contract_cols(pick, k_ref[...]), contract_cols(pick, v_ref[...])
    gap = jnp.zeros((piece, HD), F32)
    wide = lax.broadcasted_iota(jnp.int32, (piece, cols), 0) + rep_ref[0] * piece
    for s in range(n):
        slots = range(s * heads, (s + 1) * heads)
        parts = [query[:, h * HD : (h + 1) * HD] if h < QH else gap for h in slots]
        for array in (key, value):
            for h in slots:
                j = h // GROUP
                parts.append(array[:, j * HD : (j + 1) * HD] if h < QH else gap)
        block = jnp.concatenate(parts, axis=1)
        for i in range(2):
            block = jnp.where(wide == own + i, gain_ref[i : i + 1, :], block)
        msg_ref[s, :, :cols] = block.astype(BF16)
    rows = to_blocks(dot(pick, out_ref[...]), n, 2 * half).astype(BF16)
    for s in range(n):
        msg_ref[s, :, cols:] = rows[:, s % 2 * half : (s % 2 + 1) * half]


def as_row(column):
    return jnp.broadcast_to(column, (column.shape[0], 128)).T[0:1, :]


def join_kernel(in_ref, out_ref):
    for r in range(in_ref.shape[0]):
        out_ref[:, r] = in_ref[r]


def join_out_kernel(reps, rep_ref, core_ref, mine_ref, other_ref, out_ref):
    first = core_ref[0] == 0
    half = mine_ref.shape[3]
    for i in range(reps):
        mine, other = mine_ref[i], other_ref[i]
        out_ref[:, rep_ref[0] ^ i, :, :half] = jnp.where(first, mine, other)
        out_ref[:, rep_ref[0] ^ i, :, half:] = jnp.where(first, other, mine)


def fill_rows(values, rows):
    if values.shape[0] == rows:
        return values
    return jnp.concatenate([values, jnp.zeros((rows - values.shape[0], values.shape[1]), F32)], axis=0)


def fill_cols(values, cols):
    if values.shape[1] == cols:
        return values
    return jnp.concatenate([values, jnp.zeros((values.shape[0], cols - values.shape[1]), F32)], axis=1)


def message_plan(own, each, cols):
    top, rows = round_up(own, 8), round_up(each, 8)
    rest = D % cols
    halved = rest and 2 * rest <= cols
    first = round_up(rows // 2, 8) if halved else rows
    total = top + D // cols * rows + (first if rest else 0)
    return top, rows, rest, halved, first, total


def pack_message(both, down, cols):
    top, rows, rest, halved, first, _ = message_plan(both.shape[0], down.shape[0], cols)
    down = fill_rows(down, rows)
    parts = [fill_rows(both, top)]
    parts += [down[:, j * cols : (j + 1) * cols] for j in range(D // cols)]
    if rest:
        tail = down[:, D - rest :]
        if halved:
            tail = jnp.concatenate([tail[:first], fill_rows(tail[first:], first)], axis=1)
        parts.append(fill_cols(tail, cols))
    return jnp.concatenate(parts, axis=0)


def unpack_message(message, own, each):
    cols = message.shape[1]
    top, rows, rest, halved, first, _ = message_plan(own, each, cols)
    parts = [message[top + j * rows : top + (j + 1) * rows] for j in range(D // cols)]
    if rest:
        tail = message[top + D // cols * rows :][:first]
        if halved:
            tail = jnp.concatenate([tail[:, :rest], tail[: rows - first, rest : 2 * rest]], axis=0)
        parts.append(tail[:, :rest])
    return message[:own], jnp.concatenate(parts, axis=1)[:each]


def hidden_message_kernel(n, reps, rep_ref, gate_ref, up_ref, down_ref, *out_refs):
    own, units = gate_ref.shape
    held = down_ref.shape[0]
    each = held // (2 * reps)
    cols = n * each
    place = lax.broadcasted_iota(jnp.int32, (1, cols), 1)
    row = lax.broadcasted_iota(jnp.int32, (round_up(each, 8), held), 0)
    for i in range(2):
        begin = each * (2 * rep_ref[0] + i)
        unit = place + begin
        for s in range(1, n):
            unit = unit + jnp.where(place >= each * s, held - each, 0)
        pick = jnp.where(lax.broadcasted_iota(jnp.int32, (units, cols), 0) == unit, 1.0, 0.0)
        pick = pick.astype(BF16)
        both = jnp.concatenate([dot(gate_ref[...], pick), dot(up_ref[...], pick)], axis=1)
        take = (lax.broadcasted_iota(jnp.int32, row.shape, 1) == row + begin) & (row < each)
        down = dot(jnp.where(take, 1.0, 0.0).astype(BF16), down_ref[...])
        message = pack_message(both, down[:each], 2 * cols).astype(BF16)
        for z in range(n // 2):
            split_rows([ref.at[2 * z + i] for ref in out_refs], message)


def split_rows(refs, values):
    begin = 0
    for ref in refs:
        rows = ref.shape[0]
        ref[...] = values[begin : begin + rows]
        begin += rows


def hidden_weights_in_kernel(n, own, each, *refs):
    parts, (w_ref, down_ref) = refs[:-2], refs[-2:]
    block = w_ref.shape[1]
    downs = []
    for s in range(n):
        message = jnp.concatenate([part[s].astype(F32) for part in parts], axis=0)
        both, down = unpack_message(message, own, each)
        w_ref[s] = fill_rows(both, block).astype(BF16)
        downs.append(down)
    down_ref[...] = to_blocks(jnp.concatenate(downs, axis=0), n, down_ref.shape[1]).astype(BF16)


def attend_kernel(rows, n, me_ref, lengths_ref, mine_ref, other_ref, *refs):
    w_ref, cos_ref, sin_ref, first_ref, q_ref, k_ref, v_ref, gains_ref, mixed_ref = refs
    length, head_cols = q_ref.shape
    heads = head_cols // HD
    width = first_ref.shape[1]
    block_rows = width // n
    own = D // n
    gap = jnp.zeros((1, block_rows - own), F32)
    gains = []
    for i in range(2):
        parts = []
        for s in range(n):
            group = w_ref[pl.ds(s * block_rows + own // 16 * 16, block_rows - own // 16 * 16), :]
            row = own % 16 + i
            spread_row = group.astype(F32)[row : row + 1, :own]
            parts += [spread_row, gap]
        gains.append(jnp.concatenate(parts, axis=1))
        gains_ref[i : i + 1, :] = gains[i]
    for side, ref in enumerate((mine_ref, other_ref)):
        for z in range(n // 2):
            inputs = ref[z].astype(F32)
            normed = inputs * inverse_rms(inputs) * gains[0]
            first_ref[rows_at(me_ref[0] ^ (2 * z + side), rows), :] = normed.astype(BF16)
    block = min(256, length)
    for i in range(length // block):
        span = pl.ds(i * block, block)
        raw = dot(first_ref[span, :], w_ref[...])
        cosines, sines = widened(cos_ref[span, :], 2 * heads), widened(sin_ref[span, :], 2 * heads)
        query, key = raw[:, :head_cols], raw[:, head_cols : 2 * head_cols]
        q_ref[span, :] = (query * cosines + turned(query) * sines).astype(BF16)
        k_ref[span, :] = (key * cosines + turned(key) * sines).astype(BF16)
        v_ref[span, :] = raw[:, 2 * head_cols :].astype(BF16)
    for i in range(length // block):
        span, past = pl.ds(i * block, block), pl.ds(0, (i + 1) * block)
        total, starts = None, doc_starts(lengths_ref, i * block, block)
        for h in range(heads):
            probs = masked_probs(head_of(q_ref[span, :], h, heads), k_ref[past, :], starts, i * block)
            mixed = head_of(dot(probs.astype(BF16), v_ref[past, :]), h, heads)
            total = mixed if total is None else total + mixed
        mixed_ref[span, :] = total.astype(BF16)


def attend_back_kernel(lengths_ref, *refs):
    g_ref, first_ref, q_ref, k_ref, v_ref, cos_ref, sin_ref, dqkv_ref, piece_ref, dk_ref, dv_ref = refs
    length, head_cols = q_ref.shape
    heads = head_cols // HD
    block = min(256, length)
    dk_ref[...] = jnp.zeros_like(dk_ref)
    dv_ref[...] = jnp.zeros_like(dv_ref)
    for i in range(length // block):
        span, past = pl.ds(i * block, block), pl.ds(0, (i + 1) * block)
        total, starts = None, doc_starts(lengths_ref, i * block, block)
        for h in range(heads):
            query = head_of(q_ref[span, :], h, heads)
            grad = head_of(g_ref[span, :], h, heads)
            key = k_ref[past, :]
            probs = masked_probs(query, key, starts, i * block)
            grad_probs = contract_cols(grad, v_ref[past, :])
            delta = jnp.sum(probs * grad_probs, axis=-1, keepdims=True)
            grad_logits = (probs * (grad_probs - delta)).astype(BF16)
            grad_query = head_of(dot(grad_logits, key), h, heads)
            total = grad_query if total is None else total + grad_query
            dv_ref[past, :] += contract_rows(probs.astype(BF16), grad)
            dk_ref[past, :] += contract_rows(grad_logits, query)
        total = total * SCALE
        cosines, sines = widened(cos_ref[span, :], 2 * heads), widened(sin_ref[span, :], 2 * heads)
        back = total * cosines - turned(total) * sines
        dqkv_ref[span, :head_cols] = back.astype(BF16)
    for i in range(length // block):
        span = pl.ds(i * block, block)
        total = dk_ref[span, :] * SCALE
        cosines, sines = widened(cos_ref[span, :], 2 * heads), widened(sin_ref[span, :], 2 * heads)
        back = total * cosines - turned(total) * sines
        dqkv_ref[span, head_cols : 2 * head_cols] = back.astype(BF16)
        dqkv_ref[span, 2 * head_cols :] = dv_ref[span, :].astype(BF16)
    store_pieces(piece_ref, contract_rows(first_ref[...], dqkv_ref[...]))


def store_pieces(piece_ref, grad):
    reps, n, piece, _ = piece_ref.shape
    for s in range(n):
        for r in range(reps):
            begin = (s * reps + r) * piece
            piece_ref[r, s] = grad[begin : begin + piece].astype(BF16)


def first_grad_kernel(rows, side, core_ref, dqkv_ref, w_ref, out_ref):
    chips = out_ref.shape[0]
    parts = [dqkv_ref[rows_at(2 * z + (core_ref[0] ^ side), rows), :] for z in range(chips)]
    grad = contract_cols(jnp.concatenate(parts, axis=0), w_ref[...]).astype(BF16)
    for z in range(chips):
        out_ref[z] = grad[z * rows : (z + 1) * rows]


def pair_sum_kernel(mine_ref, other_ref, *out_refs):
    for i, ref in enumerate(out_refs):
        ref[...] = (mine_ref[i].astype(F32) + other_ref[i].astype(F32)).astype(BF16)


def pair_sum_whole_kernel(mine_ref, other_ref, out_ref):
    out_ref[...] = (mine_ref[...].astype(F32) + other_ref[...].astype(F32)).astype(BF16)


def middle_kernel(n, tokens_ref, mixed_ref, w_ref, gains_ref, middle_ref, second_ref, attended_ref):
    width = tokens_ref.shape[1]
    attended = jnp.concatenate([mixed_ref[s] for s in range(n)], axis=1)[:, :D]
    attended = to_blocks(attended.astype(F32), n, width).astype(BF16)
    attended_ref[...] = attended
    middle = tokens_ref[...].astype(F32) + dot(attended, w_ref[...])
    middle_ref[...] = middle
    second_ref[...] = (middle * inverse_rms(middle) * gains_ref[1:2, :]).astype(BF16)


def stacked(ref, begin=0, count=None):
    count = ref.shape[0] if count is None else count
    return jnp.concatenate([ref[begin + i] for i in range(count)], axis=0)


def hidden_kernel(second_ref, cot_ref, w_ref, down_ref, grad_ref, grads_ref, hidden_ref):
    reps, rows, _ = second_ref.shape
    units = down_ref.shape[0]
    for i in range(0, reps, 2):
        span = pl.ds(i * rows, 2 * rows)
        both = dot(stacked(second_ref, i, 2), w_ref[...])
        gate, up = both[:, :units], both[:, units:]
        grad_hidden = contract_cols(stacked(cot_ref, i, 2), down_ref[...])
        sigmoid = 1.0 / (1.0 + jnp.exp(-gate))
        silu = gate * sigmoid
        hidden_ref[span, :] = (silu * up).astype(BF16)
        grad_gate = grad_hidden * up * sigmoid * (1.0 + gate * (1.0 - sigmoid))
        grads = jnp.concatenate([grad_gate, grad_hidden * silu], axis=1).astype(BF16)
        grads_ref[span, :] = grads
        grad = contract_cols(grads, w_ref[...]).astype(BF16)
        for j in range(2):
            grad_ref[i + j] = grad[j * rows : (j + 1) * rows]


def hidden_weights_kernel(n, own, each, *refs):
    second_a, second_b, cot_a, cot_b, grads_a, grads_b, hidden_a, hidden_b, *msg_refs = refs
    cols = msg_refs[0].shape[2]
    grad = contract_rows(stacked(second_a), grads_a[...])
    grad = grad + contract_rows(stacked(second_b), grads_b[...])
    down = contract_rows(hidden_a[...], stacked(cot_a)) + contract_rows(hidden_b[...], stacked(cot_b))
    down = from_blocks(down, n, own)
    block = grad.shape[0] // n
    for s in range(n):
        both = grad[s * block : s * block + own]
        message = pack_message(both, down[s * each : (s + 1) * each], cols).astype(BF16)
        split_rows([ref.at[s] for ref in msg_refs], message)


def core_sums_kernel(*refs):
    out_ref = refs[-1]
    for core in range(2):
        sums = [
            sum(part[s].astype(F32) for s in range(core, part.shape[0], 2)) for part in refs[:-1]
        ]
        out_ref[core] = jnp.concatenate(sums, axis=0).astype(BF16)


def hidden_out_kernel(n, reps, each, rep_ref, *refs):
    parts, refs = refs[:reps], refs[reps:]
    gate_w_ref, up_w_ref, gain_ref, gate_ref, up_ref, down_ref, norm_ref, hold_ref = refs
    own = gate_ref.shape[0]
    units = 2 * reps * each
    for i, part in enumerate(parts):
        hold_ref[rep_ref[0] ^ i] = part[...]
    cols = hold_ref.shape[3]
    boths = []
    for f in range(2 * reps):
        _, down = unpack_message(hold_ref[f // 2, f % 2].astype(F32), own, each)
        boths.append(hold_ref[f // 2, f % 2, pl.ds(0, round_up(own, 16)), :])
        down_ref[f * each : (f + 1) * each, :] = down
    total = jnp.zeros((own, 1), F32)
    for begin, w_ref, out_ref in ((0, gate_w_ref, gate_ref), (cols // 2, up_w_ref, up_ref)):
        for s in range(n):
            place = begin + s * each
            rows = jnp.concatenate([part[:, place : place + each] for part in boths], axis=1)
            rows = rows.astype(F32)[:own]
            span = slice(s * units, (s + 1) * units)
            out_ref[:, span] = rows
            total = total + jnp.sum(rows * w_ref[:, span].astype(F32), axis=1, keepdims=True)
    norm_ref[...] = as_row(total) / gain_ref[...]


def down_kernel(hidden_ref, w_ref, out_ref):
    rows = out_ref.shape[1]
    for i in range(0, out_ref.shape[0], 2):
        both = dot(hidden_ref[pl.ds(i * rows, 2 * rows), :], w_ref[...]).astype(BF16)
        for j in range(2):
            out_ref[i + j] = both[j * rows : (j + 1) * rows]


def output_kernel(n, own, middle_ref, *refs):
    total = middle_ref[...]
    for ref in refs[:-1]:
        total = total + ref[...].astype(F32)
    refs[-1][...] = from_blocks(total, n, own).T.astype(BF16)


def middle_grad_kernel(n, own, reps, *refs):
    parts, refs = refs[:reps], refs[reps:]
    cot_ref, middle_ref, gains_ref, w_ref, grad_ref, branch_ref, heads_ref = refs
    rows = middle_ref.shape[0]
    middle = middle_ref[...]
    grad_second = sum(ref[...].astype(F32) for ref in parts)
    grad = cot_ref[...].astype(F32) + norm_backward(
        middle, inverse_rms(middle), gains_ref[1:2, :], grad_second
    )
    grad_ref[...] = grad
    branch = grad.astype(BF16)
    branch_ref[...] = branch
    attended = from_blocks(contract_cols(branch, w_ref[...]), n, own)
    head_cols = heads_ref.shape[2]
    if n * head_cols > D:
        attended = jnp.concatenate([attended, jnp.zeros((rows, n * head_cols - D), F32)], axis=1)
    for s in range(n):
        heads_ref[s] = attended[:, s * head_cols : (s + 1) * head_cols].astype(BF16)


def out_weights_kernel(rep_ref, me_ref, attended_ref, branch_ref, mine_ref, other_ref, hold_ref):
    store_pieces(hold_ref, contract_rows(attended_ref[...], branch_ref[...]))
    for side, ref in enumerate((mine_ref, other_ref)):
        for i in range(ref.shape[0]):
            for z in range(ref.shape[1]):
                ref[i, z] = hold_ref[rep_ref[0] ^ i, me_ref[0] ^ (2 * z + side)]


def rep_sum_kernel(in_ref, out_ref):
    out_ref[...] = sum(in_ref[r].astype(F32) for r in range(in_ref.shape[0])).astype(BF16)


def chip_sums_kernel(reps, *refs):
    for z, out_ref in enumerate(refs[reps:]):
        out_ref[...] = sum(ref[z].astype(F32) for ref in refs[:reps]).astype(BF16)


def owner_sum_kernel(*refs):
    refs[-1][...] = sum(ref[...].astype(F32) for ref in refs[:-1]).astype(BF16)


def out_out_kernel(n, reps, rep_ref, *refs):
    out_ref, hold_ref = refs[reps:]
    for i in range(reps):
        hold_ref[rep_ref[0] ^ i] = refs[i][...].astype(F32)
    own = out_ref.shape[0]
    rows = jnp.concatenate([hold_ref[r] for r in range(reps)], axis=0)[:own]
    out_ref[...] = from_blocks(rows, n, own)


def attention_out_kernel(n, reps, rep_ref, *refs):
    parts, refs = refs[:reps], refs[reps:]
    q_w_ref, k_w_ref, v_w_ref, gain_ref, q_ref, k_ref, v_ref, norm_ref, hold_ref = refs
    own = q_ref.shape[0]
    cols = parts[0].shape[2]
    head_cols = cols // 3
    heads = head_cols // HD
    for i, part in enumerate(parts):
        for s in range(n):
            hold_ref[rep_ref[0] ^ i, s] = part[s].astype(F32)
    sides = [
        jnp.concatenate([hold_ref[r, s] for r in range(reps)], axis=0)[:own] for s in range(n)
    ]

    def slot(h, kind):
        begin = kind * head_cols + h % heads * HD
        return sides[h // heads][:, begin : begin + HD]

    query = jnp.concatenate([slot(h, 0) for h in range(QH)], axis=1)
    q_ref[...] = query
    total = jnp.sum(query * q_w_ref[...].astype(F32), axis=1, keepdims=True)
    total = as_row(total)
    for kind, w_ref, out_ref in ((1, k_w_ref, k_ref), (2, v_w_ref, v_ref)):
        wide = jnp.concatenate(
            [sum(slot(j * GROUP + g, kind) for g in range(GROUP)) for j in range(KVH)], axis=1
        ).T
        out_ref[...] = wide
        total = total + jnp.sum(wide * w_ref[...].astype(F32), axis=0, keepdims=True)
    norm_ref[...] = total / gain_ref[...]


def input_grad_kernel(n, own, parts_ref, tokens_ref, gains_ref, grad_ref, out_ref):
    inputs = tokens_ref[...].astype(F32)
    grad_first = sum(parts_ref[z].astype(F32) for z in range(parts_ref.shape[0]))
    total = grad_ref[...] + norm_backward(inputs, inverse_rms(inputs), gains_ref[0:1, :], grad_first)
    out_ref[...] = from_blocks(total, n, own).T


def shards(
    tokens,
    lengths,
    norm_one,
    w_query,
    w_key,
    w_value,
    w_out,
    norm_two,
    w_gate,
    w_up,
    w_down,
    cotangent,
):
    n = lax.axis_size("shard")
    reps = lax.axis_size("rep")
    nz = n // 2
    rows = tokens.shape[0]
    length = rows * n
    own = w_query.shape[0]
    held = w_down.shape[0]
    block = round_up(own + 2, 16)
    width = n * block
    piece = block // reps
    heads = -(-QH // n)
    head_cols = heads * HD
    qkv_cols = 3 * head_cols
    each = held // (2 * reps)
    units = n * each
    msg_rows = message_plan(own, each, 2 * units)[-1]
    shard_index = lax.axis_index("shard").astype(jnp.int32)
    me = shard_index.reshape(1)
    core = (shard_index % 2).reshape(1)
    rep = lax.axis_index("rep").astype(jnp.int32).reshape(1)
    own_block = (rows, width)

    (tokens_in,) = call(lambda *r: blocks_kernel(n, *r), "tokens_blocks", [(own_block, BF16)], tokens.T)
    tokens_parts = spread(tokens_in, "shard", 2)
    gains_own = jnp.pad(jnp.stack([norm_one, norm_two]), ((0, 0), (0, qkv_cols - own))).astype(F32)
    (message,) = call(
        lambda *r: attention_message_kernel(n, *r),
        "attention_message",
        [((n, piece, qkv_cols + width // 2), BF16)],
        after(w_query, tokens_in),
        w_key.T,
        w_value.T,
        w_out,
        gains_own,
        scalars=(rep,),
    )
    arrived = exchange(message)
    qkv_piece = arrived[:, :, :qkv_cols]
    qkv_tiled = jnp.broadcast_to(qkv_piece[None], (reps,) + qkv_piece.shape)
    (w_qkv,) = call(
        join_kernel,
        "join_qkv",
        [((n, reps, piece, qkv_cols), BF16)],
        lax.all_to_all(qkv_tiled, "rep", split_axis=0, concat_axis=0, tiled=True),
    )
    w_qkv = w_qkv.reshape(width, qkv_cols)
    position = doc_layout(after(lengths, message)[0], length)
    cosines, sines = rope_tables(position)

    split = round_up(msg_rows // 2, 16)
    part_rows = (split, msg_rows - split) if split < msg_rows else (msg_rows,)
    messages = call(
        lambda *r: hidden_message_kernel(n, reps, *r),
        "hidden_message",
        [((n, part, 2 * units), BF16) for part in part_rows],
        after(w_gate, cosines, sines),
        w_up,
        w_down,
        scalars=(rep,),
    )
    (cot_in,) = call(
        lambda *r: blocks_kernel(n, *r),
        "cot_blocks",
        [(own_block, BF16)],
        after(cotangent.T, messages[0], arrived, *tokens_parts[1:]),
    )
    cot_parts = spread(after(cot_in, w_qkv), "rep", 1)
    tokens_mine, tokens_other = both_cores([after(tokens_parts[0], cot_in)] + tokens_parts[1:])
    hidden_first = exchange(after(messages[0], tokens_mine))

    out_parts = spread(after(arrived, w_qkv)[:, :, qkv_cols:], "rep", 1)

    head_shape = (length, head_cols)
    first_all, query, key, value, gains, mixed = call(
        lambda *r: attend_kernel(rows, n, *r),
        "attend",
        [((length, width), BF16)]
        + [(head_shape, BF16)] * 3
        + [((2, width), F32)]
        + [(head_shape, BF16)],
        tokens_mine,
        tokens_other,
        w_qkv,
        cosines,
        sines,
        scalars=(me, lengths),
    )
    mixed = exchange(after(mixed, hidden_first).reshape(n, rows, head_cols))
    hidden_rest = [exchange(after(message, mixed)) for message in messages[1:]]
    (out_full,) = call(
        lambda *r: join_out_kernel(reps, *r),
        "join_out",
        [((n, reps, piece, width), BF16)],
        *both_cores([after(out_parts[0], gains)] + out_parts[1:]),
        scalars=(rep, core),
    )
    out_full = out_full.reshape(width, width)

    middle, second, attended = call(
        lambda *r: middle_kernel(n, *r),
        "middle",
        [(own_block, F32), (own_block, BF16), (own_block, BF16)],
        tokens_in,
        mixed,
        out_full,
        gains,
    )
    w_hidden, w_down_in = call(
        lambda *r: hidden_weights_in_kernel(n, own, each, *r),
        "hidden_weights_in",
        [((n, block, 2 * units), BF16), ((units, width), BF16)],
        after(hidden_first, second),
        *hidden_rest,
    )
    w_hidden = w_hidden.reshape(width, 2 * units)
    cot_mine, cot_other = both_cores([after(cot_parts[0], out_full)] + cot_parts[1:])

    second_mine, second_other = both_cores(spread(second, "rep", 1))
    side_outs = [
        ((reps, rows, width), BF16),
        ((reps * rows, 2 * units), BF16),
        ((reps * rows, units), BF16),
    ]

    def hidden_side(seconds, cots, name):
        return call(hidden_kernel, name, side_outs, seconds, cots, w_hidden, w_down_in)

    def plane_sums(mine, other):
        sums = call(pair_sum_kernel, "pair_sum", [(own_block, BF16)] * reps, mine, swap(other, "shard", 1))
        return sums, deliver(sums, "rep", 1)

    grad_other, grads_other, hidden_other = hidden_side(second_other, cot_other, "hidden_other")
    grad_mine, grads_mine, hidden_mine = hidden_side(
        after(second_mine, grad_other), cot_mine, "hidden_mine"
    )
    hidden_messages = call(
        lambda *r: hidden_weights_kernel(n, own, each, *r),
        "hidden_weights",
        [((n, part, 2 * units), BF16) for part in part_rows],
        second_mine,
        second_other,
        cot_mine,
        cot_other,
        grads_mine,
        grads_other,
        hidden_mine,
        hidden_other,
    )
    hidden_sums = [exchange(hidden_messages[0])]
    sums, grad_second = plane_sums(after(grad_mine, hidden_messages[0]), grad_other)
    down_other, down_mine = [
        call(
            down_kernel,
            "down",
            [((reps, rows, width), BF16)],
            after(hidden, grad_second[1]),
            w_down_in,
        )[0]
        for hidden in (hidden_other, hidden_mine)
    ]

    grad_middle, grad_branch, grad_heads = call(
        lambda *r: middle_grad_kernel(n, own, reps, *r),
        "middle_grad",
        [(own_block, F32), (own_block, BF16), ((n, rows, head_cols), BF16)],
        *grad_second,
        cot_in,
        after(middle, down_other, down_mine),
        gains,
        out_full,
    )
    grad_heads = exchange(after(grad_heads, *hidden_sums))
    out_pieces = call(
        out_weights_kernel,
        "out_weights",
        [((reps, nz, piece, width), BF16)] * 2,
        attended,
        grad_branch,
        scalars=(rep, me),
        scratch=[((reps, n, piece, width), BF16)],
    )
    out_sums = call(
        pair_sum_kernel,
        "pair_sum",
        [((nz, piece, width), BF16)] * reps,
        out_pieces[0],
        swap(out_pieces[1], "shard", 1),
    )
    out_parts = deliver(out_sums, "rep", 1)
    hidden_sums += [exchange(after(message, grad_heads, out_pieces[0])) for message in hidden_messages[1:]]
    grad_heads = grad_heads.reshape(head_shape)
    grad_qkv, attention_pieces = call(
        attend_back_kernel,
        "attend_back",
        [((length, qkv_cols), BF16), ((reps, n, piece, qkv_cols), BF16)],
        grad_heads,
        first_all,
        query,
        key,
        value,
        cosines,
        after(sines, out_sums[0]),
        scalars=(lengths,),
        scratch=[(head_shape, F32)] * 2,
    )

    def first_side(grads, side):
        return call(
            lambda *r: first_grad_kernel(rows, side, *r),
            "first_grad",
            [((nz, rows, width), BF16)],
            grads,
            w_qkv,
            scalars=(core,),
        )[0]

    attention_arrived = lax.all_to_all(
        after(attention_pieces, *hidden_sums), "rep", split_axis=0, concat_axis=0, tiled=True
    )
    (core_sums,) = call(
        core_sums_kernel,
        "core_sums",
        [((2, msg_rows, 2 * units), BF16)],
        after(hidden_sums[0], grad_qkv, *out_parts[1:]),
        *hidden_sums[1:],
    )
    hidden_parts = spread(core_sums, "rep", 1)
    first_other = first_side(after(grad_qkv, core_sums), 1)
    (attention_summed,) = call(
        rep_sum_kernel,
        "rep_sum",
        [((n, piece, qkv_cols), BF16)],
        after(attention_arrived, first_other),
    )
    attention_moved = exchange(attention_summed)
    out_summed = call(
        lambda *r: chip_sums_kernel(reps, *r),
        "chip_sums",
        [((piece, width), BF16)] * nz,
        after(out_parts[0], attention_summed),
        *out_parts[1:],
    )
    out_moved = deliver(out_summed, "shard", 2)
    first_mine = first_side(after(grad_qkv, out_summed[0]), 0)
    (first_sums,) = call(
        pair_sum_whole_kernel,
        "first_sum",
        [((nz, rows, width), BF16)],
        after(first_mine, *out_moved[1:], *hidden_parts[1:3]),
        swap(first_other, "shard", 1),
    )
    first_parts = exchange_z(after(first_sums, attention_moved))
    attention_parts = spread(attention_moved, "rep", 1)
    (out_piece,) = call(
        owner_sum_kernel,
        "owner_sum",
        [((piece, width), BF16)],
        after(out_moved[0], first_sums),
        *out_moved[1:],
    )
    down_sums, down_parts = plane_sums(
        after(down_mine, out_piece, attention_parts[1]), after(down_other, first_sums)
    )

    gain_rows = [gain.astype(F32)[None] for gain in (norm_one, norm_two)]
    grad_w_gate, grad_w_up, grad_w_down, grad_norm_two = call(
        lambda *r: hidden_out_kernel(n, reps, each, *r),
        "hidden_out",
        [(w_gate.shape, F32), (w_up.shape, F32), (w_down.shape, F32), ((1, own), F32)],
        *hidden_parts,
        w_gate,
        w_up,
        after(gain_rows[1], down_sums[0]),
        scalars=(rep,),
        scratch=[((reps, 2, msg_rows, 2 * units), BF16)],
    )

    grad_w_query, grad_w_key, grad_w_value, grad_norm_one = call(
        lambda *r: attention_out_kernel(n, reps, *r),
        "attention_out",
        [(w_query.shape, F32), (w_key.shape[::-1], F32), (w_value.shape[::-1], F32), ((1, own), F32)],
        *attention_parts,
        after(w_query, grad_norm_two),
        w_key.T,
        w_value.T,
        gain_rows[0],
        scalars=(rep,),
        scratch=[((reps, n, piece, qkv_cols), F32)],
    )

    (grad_w_out,) = call(
        lambda *r: out_out_kernel(n, reps, *r),
        "out_out",
        [(w_out.shape, F32)],
        *later(spread(out_piece, "rep", 1), grad_norm_one),
        scalars=(rep,),
        scratch=[((reps, piece, width), F32)],
    )

    (input_grad,) = call(
        lambda *r: input_grad_kernel(n, own, *r),
        "input_grad",
        [((D, rows), F32)],
        first_parts,
        after(tokens_in, grad_w_out),
        gains,
        grad_middle,
    )

    (output,) = call(
        lambda *r: output_kernel(n, own, *r),
        "output",
        [((D, rows), BF16)],
        after(middle, input_grad),
        *down_parts,
    )
    return (
        output.T,
        input_grad.T,
        grad_norm_one[0],
        grad_w_query,
        grad_w_key.T,
        grad_w_value.T,
        grad_w_out,
        grad_norm_two[0],
        grad_w_gate,
        grad_w_up,
        grad_w_down,
    )


def solution(mesh):
    rows = P("shard", None)
    own_tokens = P(("rep", "shard"), None)
    return jax.shard_map(
        shards,
        mesh=mesh,
        in_specs=(
            own_tokens,
            P("rep", None),
            P("shard"),
            rows,
            rows,
            rows,
            rows,
            P("shard"),
            rows,
            rows,
            rows,
            own_tokens,
        ),
        out_specs=(
            own_tokens,
            own_tokens,
            P("shard"),
            rows,
            rows,
            rows,
            rows,
            P("shard"),
            rows,
            rows,
            rows,
        ),
        check_vma=False,
    )
```

```python
import jax
import jax.numpy as jnp
from jax import lax
from jax.experimental import pallas as pl
from jax.experimental.pallas import tpu as pltpu
from jax.sharding import PartitionSpec as P

D = 960
QH = 15
KVH = 5
HD = 64
FF = 2560
GROUP = QH // KVH

EPS = 1e-05
ROPE_BASE = 10000.0
MASKED = -1e30
SCALE = HD ** (-0.5)
BF16 = jnp.bfloat16
F32 = jnp.float32


def doc_layout(lengths_row, length):
    places = jnp.arange(length, dtype=jnp.int32)
    doc_ends = jnp.cumsum(lengths_row)
    passed = places[:, None] >= doc_ends[None, :]
    doc_start = jnp.sum(jnp.where(passed, lengths_row[None, :], 0), axis=1)
    return places - doc_start


def rope_tables(position):
    half_dim = HD // 2
    fraction = jnp.arange(half_dim, dtype=F32) * (2.0 / HD)
    inverse = ROPE_BASE ** (-fraction)
    angles = position.astype(F32)[:, None] * inverse[None, :]
    return (jnp.cos(angles), jnp.sin(angles))


VMEM_LIMIT = 56 * 2**20


def dot(left, right):
    return jnp.dot(left, right, preferred_element_type=F32)


def contract_rows(left, right):
    return lax.dot_general(left, right, (((0,), (0,)), ((), ())), preferred_element_type=F32)


def contract_cols(left, right):
    return lax.dot_general(left, right, (((1,), (1,)), ((), ())), preferred_element_type=F32)


def inverse_rms(values):
    return lax.rsqrt(jnp.sum(values * values, axis=-1, keepdims=True) * (1.0 / D) + EPS)


def norm_backward(values, inverse, gain, grad_norm):
    scaled = grad_norm * gain
    mean = jnp.sum(scaled * values, axis=-1, keepdims=True) * (1.0 / D)
    return inverse * scaled - values * inverse**3 * mean


def round_up(value, step):
    return -(-value // step) * step


def rows_at(index, rows):
    return pl.ds(pl.multiple_of(index * rows, rows), rows)


def to_blocks(values, n, width):
    rows, own = values.shape[0], values.shape[1] // n
    gap = jnp.zeros((rows, width // n - own), values.dtype)
    parts = []
    for s in range(n):
        parts += [values[:, s * own : (s + 1) * own], gap]
    return jnp.concatenate(parts, axis=1)


def from_blocks(values, n, own):
    block = values.shape[1] // n
    return jnp.concatenate([values[:, s * block : s * block + own] for s in range(n)], axis=1)


def swap(block, axis, k):
    count = lax.axis_size(axis)
    return lax.ppermute(block, axis, [(i, i ^ k) for i in range(count)])


def exchange(block):
    return lax.all_to_all(block, "shard", split_axis=0, concat_axis=0, tiled=True)


def spread(block, axis, step):
    return [block] + [swap(block, axis, k) for k in range(step, lax.axis_size(axis), step)]


def deliver(blocks, axis, step):
    return [blocks[0]] + [swap(block, axis, i * step) for i, block in enumerate(blocks) if i]


def exchange_z(blocks):
    groups = [list(range(core, lax.axis_size("shard"), 2)) for core in range(2)]
    return lax.all_to_all(
        blocks, "shard", split_axis=0, concat_axis=0, axis_index_groups=groups, tiled=True
    )


def after(value, *earlier):
    return lax.optimization_barrier((value,) + earlier)[0]


def later(values, *earlier):
    values = tuple(values)
    return list(lax.optimization_barrier(values + earlier)[: len(values)])


def both_cores(parts):
    stacked = jnp.stack(parts)
    return stacked, swap(stacked, "shard", 1)


def call(kernel, name, outs, *operands, scalars=(), scratch=()):
    specs = [pl.BlockSpec(memory_space=pltpu.SMEM)] * len(scalars)
    specs += [pl.BlockSpec(memory_space=pltpu.VMEM)] * len(operands)
    return pl.pallas_call(
        kernel,
        out_shape=[jax.ShapeDtypeStruct(shape, dtype) for shape, dtype in outs],
        in_specs=specs,
        out_specs=[pl.BlockSpec(memory_space=pltpu.VMEM)] * len(outs),
        scratch_shapes=[pltpu.VMEM(shape, dtype) for shape, dtype in scratch],
        compiler_params=pltpu.CompilerParams(vmem_limit_bytes=VMEM_LIMIT),
        name=name,
    )(*scalars, *operands)


def turned(values):
    half = HD // 2
    parts = []
    for begin in range(0, values.shape[1], HD):
        parts.append(-values[:, begin + half : begin + HD])
        parts.append(values[:, begin : begin + half])
    return jnp.concatenate(parts, axis=1)


def widened(values, times):
    return jnp.concatenate([values] * times, axis=1)


def head_of(values, h, heads):
    if heads == 1:
        return values
    lane = lax.broadcasted_iota(jnp.int32, values.shape, 1)
    return jnp.where(lane // HD == h, values, jnp.zeros_like(values))


def doc_starts(lengths_ref, row, rows):
    place = lax.broadcasted_iota(jnp.int32, (rows, 1), 0) + row
    end = lengths_ref[0, 0]
    starts = jnp.where(place >= end, end, 0)
    for slot in range(1, lengths_ref.shape[1]):
        end = end + lengths_ref[0, slot]
        starts = jnp.where(place >= end, end, starts)
    return starts


def masked_probs(query, key, starts, row):
    rows, cols = query.shape[0], key.shape[0]
    logits = contract_cols(query, key) * SCALE
    place = lax.broadcasted_iota(jnp.int32, (rows, cols), 1)
    own = lax.broadcasted_iota(jnp.int32, (rows, cols), 0) + row
    logits = jnp.where((place <= own) & (place >= starts), logits, MASKED)
    raised = jnp.exp(logits - jnp.max(logits, axis=-1, keepdims=True))
    return raised * (1.0 / jnp.sum(raised, axis=-1, keepdims=True))


def blocks_kernel(n, in_ref, *out_refs):
    values = to_blocks(in_ref[...].astype(F32).T, n, out_refs[0].shape[1]).astype(BF16)
    out_refs[0][...] = values
    for ref in out_refs[1:]:
        for i in range(ref.shape[0]):
            ref[i] = values


def attention_message_kernel(n, rep_ref, q_ref, k_ref, v_ref, out_ref, gain_ref, msg_ref):
    own = q_ref.shape[0]
    piece = msg_ref.shape[1]
    cols = gain_ref.shape[1]
    half = msg_ref.shape[2] - cols
    head_cols = cols // 3
    heads = head_cols // HD
    row = lax.broadcasted_iota(jnp.int32, (piece, own), 0) + rep_ref[0] * piece
    pick = jnp.where(row == lax.broadcasted_iota(jnp.int32, (piece, own), 1), 1.0, 0.0).astype(BF16)
    query, key, value = dot(pick, q_ref[...]), contract_cols(pick, k_ref[...]), contract_cols(pick, v_ref[...])
    gap = jnp.zeros((piece, HD), F32)
    wide = lax.broadcasted_iota(jnp.int32, (piece, cols), 0) + rep_ref[0] * piece
    for s in range(n):
        slots = range(s * heads, (s + 1) * heads)
        parts = [query[:, h * HD : (h + 1) * HD] if h < QH else gap for h in slots]
        for array in (key, value):
            for h in slots:
                j = h // GROUP
                parts.append(array[:, j * HD : (j + 1) * HD] if h < QH else gap)
        block = jnp.concatenate(parts, axis=1)
        for i in range(2):
            block = jnp.where(wide == own + i, gain_ref[i : i + 1, :], block)
        msg_ref[s, :, :cols] = block.astype(BF16)
    rows = to_blocks(dot(pick, out_ref[...]), n, 2 * half).astype(BF16)
    for s in range(n):
        msg_ref[s, :, cols:] = rows[:, s % 2 * half : (s % 2 + 1) * half]


def as_row(column):
    return jnp.broadcast_to(column, (column.shape[0], 128)).T[0:1, :]


def join_kernel(in_ref, out_ref):
    for r in range(in_ref.shape[0]):
        out_ref[:, r] = in_ref[r]


def join_out_kernel(reps, rep_ref, core_ref, mine_ref, other_ref, out_ref):
    first = core_ref[0] == 0
    half = mine_ref.shape[3]
    for i in range(reps):
        mine, other = mine_ref[i], other_ref[i]
        out_ref[:, rep_ref[0] ^ i, :, :half] = jnp.where(first, mine, other)
        out_ref[:, rep_ref[0] ^ i, :, half:] = jnp.where(first, other, mine)


def fill_rows(values, rows):
    if values.shape[0] == rows:
        return values
    return jnp.concatenate([values, jnp.zeros((rows - values.shape[0], values.shape[1]), F32)], axis=0)


def fill_cols(values, cols):
    if values.shape[1] == cols:
        return values
    return jnp.concatenate([values, jnp.zeros((values.shape[0], cols - values.shape[1]), F32)], axis=1)


def message_plan(own, each, cols):
    top, rows = round_up(own, 8), round_up(each, 8)
    rest = D % cols
    halved = rest and 2 * rest <= cols
    first = round_up(rows // 2, 8) if halved else rows
    total = top + D // cols * rows + (first if rest else 0)
    return top, rows, rest, halved, first, total


def pack_message(both, down, cols):
    top, rows, rest, halved, first, _ = message_plan(both.shape[0], down.shape[0], cols)
    down = fill_rows(down, rows)
    parts = [fill_rows(both, top)]
    parts += [down[:, j * cols : (j + 1) * cols] for j in range(D // cols)]
    if rest:
        tail = down[:, D - rest :]
        if halved:
            tail = jnp.concatenate([tail[:first], fill_rows(tail[first:], first)], axis=1)
        parts.append(fill_cols(tail, cols))
    return jnp.concatenate(parts, axis=0)


def unpack_message(message, own, each):
    cols = message.shape[1]
    top, rows, rest, halved, first, _ = message_plan(own, each, cols)
    parts = [message[top + j * rows : top + (j + 1) * rows] for j in range(D // cols)]
    if rest:
        tail = message[top + D // cols * rows :][:first]
        if halved:
            tail = jnp.concatenate([tail[:, :rest], tail[: rows - first, rest : 2 * rest]], axis=0)
        parts.append(tail[:, :rest])
    return message[:own], jnp.concatenate(parts, axis=1)[:each]


def hidden_message_kernel(n, reps, rep_ref, gate_ref, up_ref, down_ref, *out_refs):
    own, units = gate_ref.shape
    held = down_ref.shape[0]
    each = held // (2 * reps)
    cols = n * each
    place = lax.broadcasted_iota(jnp.int32, (1, cols), 1)
    row = lax.broadcasted_iota(jnp.int32, (round_up(each, 8), held), 0)
    for i in range(2):
        begin = each * (2 * rep_ref[0] + i)
        unit = place + begin
        for s in range(1, n):
            unit = unit + jnp.where(place >= each * s, held - each, 0)
        pick = jnp.where(lax.broadcasted_iota(jnp.int32, (units, cols), 0) == unit, 1.0, 0.0)
        pick = pick.astype(BF16)
        both = jnp.concatenate([dot(gate_ref[...], pick), dot(up_ref[...], pick)], axis=1)
        take = (lax.broadcasted_iota(jnp.int32, row.shape, 1) == row + begin) & (row < each)
        down = dot(jnp.where(take, 1.0, 0.0).astype(BF16), down_ref[...])
        message = pack_message(both, down[:each], 2 * cols).astype(BF16)
        for z in range(n // 2):
            split_rows([ref.at[2 * z + i] for ref in out_refs], message)


def split_rows(refs, values):
    begin = 0
    for ref in refs:
        rows = ref.shape[0]
        ref[...] = values[begin : begin + rows]
        begin += rows


def hidden_weights_in_kernel(n, own, each, *refs):
    parts, (w_ref, down_ref) = refs[:-2], refs[-2:]
    block = w_ref.shape[1]
    downs = []
    for s in range(n):
        message = jnp.concatenate([part[s].astype(F32) for part in parts], axis=0)
        both, down = unpack_message(message, own, each)
        w_ref[s] = fill_rows(both, block).astype(BF16)
        downs.append(down)
    down_ref[...] = to_blocks(jnp.concatenate(downs, axis=0), n, down_ref.shape[1]).astype(BF16)


def attend_kernel(rows, n, me_ref, lengths_ref, mine_ref, other_ref, *refs):
    w_ref, cos_ref, sin_ref, first_ref, q_ref, k_ref, v_ref, gains_ref, mixed_ref = refs
    length, head_cols = q_ref.shape
    heads = head_cols // HD
    width = first_ref.shape[1]
    block_rows = width // n
    own = D // n
    gap = jnp.zeros((1, block_rows - own), F32)
    gains = []
    for i in range(2):
        parts = []
        for s in range(n):
            group = w_ref[pl.ds(s * block_rows + own // 16 * 16, block_rows - own // 16 * 16), :]
            row = own % 16 + i
            spread_row = group.astype(F32)[row : row + 1, :own]
            parts += [spread_row, gap]
        gains.append(jnp.concatenate(parts, axis=1))
        gains_ref[i : i + 1, :] = gains[i]
    for side, ref in enumerate((mine_ref, other_ref)):
        for z in range(n // 2):
            inputs = ref[z].astype(F32)
            normed = inputs * inverse_rms(inputs) * gains[0]
            first_ref[rows_at(me_ref[0] ^ (2 * z + side), rows), :] = normed.astype(BF16)
    block = min(256, length)
    for i in range(length // block):
        span = pl.ds(i * block, block)
        raw = dot(first_ref[span, :], w_ref[...])
        cosines, sines = widened(cos_ref[span, :], 2 * heads), widened(sin_ref[span, :], 2 * heads)
        query, key = raw[:, :head_cols], raw[:, head_cols : 2 * head_cols]
        q_ref[span, :] = (query * cosines + turned(query) * sines).astype(BF16)
        k_ref[span, :] = (key * cosines + turned(key) * sines).astype(BF16)
        v_ref[span, :] = raw[:, 2 * head_cols :].astype(BF16)
    for i in range(length // block):
        span, past = pl.ds(i * block, block), pl.ds(0, (i + 1) * block)
        total, starts = None, doc_starts(lengths_ref, i * block, block)
        for h in range(heads):
            probs = masked_probs(head_of(q_ref[span, :], h, heads), k_ref[past, :], starts, i * block)
            mixed = head_of(dot(probs.astype(BF16), v_ref[past, :]), h, heads)
            total = mixed if total is None else total + mixed
        mixed_ref[span, :] = total.astype(BF16)


def attend_back_kernel(reps, lengths_ref, rep_ref, *refs):
    g_ref, first_ref, q_ref, k_ref, v_ref, cos_ref, sin_ref, dqkv_ref = refs[:8]
    piece_refs, (dk_ref, dv_ref, hold_ref) = refs[8 : 8 + reps], refs[8 + reps :]
    length, head_cols = q_ref.shape
    heads = head_cols // HD
    block = min(256, length)
    dk_ref[...] = jnp.zeros_like(dk_ref)
    dv_ref[...] = jnp.zeros_like(dv_ref)
    for i in range(length // block):
        span, past = pl.ds(i * block, block), pl.ds(0, (i + 1) * block)
        total, starts = None, doc_starts(lengths_ref, i * block, block)
        for h in range(heads):
            query = head_of(q_ref[span, :], h, heads)
            grad = head_of(g_ref[span, :], h, heads)
            key = k_ref[past, :]
            probs = masked_probs(query, key, starts, i * block)
            grad_probs = contract_cols(grad, v_ref[past, :])
            delta = jnp.sum(probs * grad_probs, axis=-1, keepdims=True)
            grad_logits = (probs * (grad_probs - delta)).astype(BF16)
            grad_query = head_of(dot(grad_logits, key), h, heads)
            total = grad_query if total is None else total + grad_query
            dv_ref[past, :] += contract_rows(probs.astype(BF16), grad)
            dk_ref[past, :] += contract_rows(grad_logits, query)
        total = total * SCALE
        cosines, sines = widened(cos_ref[span, :], 2 * heads), widened(sin_ref[span, :], 2 * heads)
        back = total * cosines - turned(total) * sines
        dqkv_ref[span, :head_cols] = back.astype(BF16)
    for i in range(length // block):
        span = pl.ds(i * block, block)
        total = dk_ref[span, :] * SCALE
        cosines, sines = widened(cos_ref[span, :], 2 * heads), widened(sin_ref[span, :], 2 * heads)
        back = total * cosines - turned(total) * sines
        dqkv_ref[span, head_cols : 2 * head_cols] = back.astype(BF16)
        dqkv_ref[span, 2 * head_cols :] = dv_ref[span, :].astype(BF16)
    store_pieces(hold_ref, contract_rows(first_ref[...], dqkv_ref[...]))
    for i, ref in enumerate(piece_refs):
        ref[...] = hold_ref[rep_ref[0] ^ i]


def store_pieces(piece_ref, grad):
    reps, n, piece, _ = piece_ref.shape
    for s in range(n):
        for r in range(reps):
            begin = (s * reps + r) * piece
            piece_ref[r, s] = grad[begin : begin + piece].astype(BF16)


def first_grad_kernel(rows, side, core_ref, dqkv_ref, w_ref, out_ref):
    chips = out_ref.shape[0]
    parts = [dqkv_ref[rows_at(2 * z + (core_ref[0] ^ side), rows), :] for z in range(chips)]
    grad = contract_cols(jnp.concatenate(parts, axis=0), w_ref[...]).astype(BF16)
    for z in range(chips):
        out_ref[z] = grad[z * rows : (z + 1) * rows]


def pair_sum_kernel(mine_ref, other_ref, *out_refs):
    for i, ref in enumerate(out_refs):
        ref[...] = (mine_ref[i].astype(F32) + other_ref[i].astype(F32)).astype(BF16)


def pair_sum_whole_kernel(mine_ref, other_ref, out_ref):
    out_ref[...] = (mine_ref[...].astype(F32) + other_ref[...].astype(F32)).astype(BF16)


def middle_kernel(n, tokens_ref, mixed_ref, w_ref, gains_ref, middle_ref, second_ref, attended_ref):
    width = tokens_ref.shape[1]
    attended = jnp.concatenate([mixed_ref[s] for s in range(n)], axis=1)[:, :D]
    attended = to_blocks(attended.astype(F32), n, width).astype(BF16)
    attended_ref[...] = attended
    middle = tokens_ref[...].astype(F32) + dot(attended, w_ref[...])
    middle_ref[...] = middle
    second_ref[...] = (middle * inverse_rms(middle) * gains_ref[1:2, :]).astype(BF16)


def stacked(ref, begin=0, count=None):
    count = ref.shape[0] if count is None else count
    return jnp.concatenate([ref[begin + i] for i in range(count)], axis=0)


def hidden_kernel(second_ref, cot_ref, w_ref, down_ref, grad_ref, grads_ref, hidden_ref):
    reps, rows, _ = second_ref.shape
    units = down_ref.shape[0]
    for i in range(0, reps, 2):
        span = pl.ds(i * rows, 2 * rows)
        both = dot(stacked(second_ref, i, 2), w_ref[...])
        gate, up = both[:, :units], both[:, units:]
        grad_hidden = contract_cols(stacked(cot_ref, i, 2), down_ref[...])
        sigmoid = 1.0 / (1.0 + jnp.exp(-gate))
        silu = gate * sigmoid
        hidden_ref[span, :] = (silu * up).astype(BF16)
        grad_gate = grad_hidden * up * sigmoid * (1.0 + gate * (1.0 - sigmoid))
        grads = jnp.concatenate([grad_gate, grad_hidden * silu], axis=1).astype(BF16)
        grads_ref[span, :] = grads
        grad = contract_cols(grads, w_ref[...]).astype(BF16)
        for j in range(2):
            grad_ref[i + j] = grad[j * rows : (j + 1) * rows]


def hidden_weights_kernel(n, own, each, *refs):
    second_a, second_b, cot_a, cot_b, grads_a, grads_b, hidden_a, hidden_b, *msg_refs = refs
    cols = msg_refs[0].shape[2]
    grad = contract_rows(stacked(second_a), grads_a[...])
    grad = grad + contract_rows(stacked(second_b), grads_b[...])
    down = contract_rows(hidden_a[...], stacked(cot_a)) + contract_rows(hidden_b[...], stacked(cot_b))
    down = from_blocks(down, n, own)
    block = grad.shape[0] // n
    for s in range(n):
        both = grad[s * block : s * block + own]
        message = pack_message(both, down[s * each : (s + 1) * each], cols).astype(BF16)
        split_rows([ref.at[s] for ref in msg_refs], message)


def core_sums_kernel(*refs):
    out_ref = refs[-1]
    for core in range(2):
        sums = [
            sum(part[s].astype(F32) for s in range(core, part.shape[0], 2)) for part in refs[:-1]
        ]
        out_ref[core] = jnp.concatenate(sums, axis=0).astype(BF16)


def hidden_out_kernel(n, reps, each, rep_ref, *refs):
    parts, refs = refs[:reps], refs[reps:]
    gate_w_ref, up_w_ref, gain_ref, gate_ref, up_ref, down_ref, norm_ref, hold_ref = refs
    own = gate_ref.shape[0]
    units = 2 * reps * each
    for i, part in enumerate(parts):
        hold_ref[rep_ref[0] ^ i] = part[...]
    cols = hold_ref.shape[3]
    boths = []
    for f in range(2 * reps):
        _, down = unpack_message(hold_ref[f // 2, f % 2].astype(F32), own, each)
        boths.append(hold_ref[f // 2, f % 2, pl.ds(0, round_up(own, 16)), :])
        down_ref[f * each : (f + 1) * each, :] = down
    total = jnp.zeros((own, 1), F32)
    for begin, w_ref, out_ref in ((0, gate_w_ref, gate_ref), (cols // 2, up_w_ref, up_ref)):
        for s in range(n):
            place = begin + s * each
            rows = jnp.concatenate([part[:, place : place + each] for part in boths], axis=1)
            rows = rows.astype(F32)[:own]
            span = slice(s * units, (s + 1) * units)
            out_ref[:, span] = rows
            total = total + jnp.sum(rows * w_ref[:, span].astype(F32), axis=1, keepdims=True)
    norm_ref[...] = as_row(total) / gain_ref[...]


def down_kernel(hidden_ref, w_ref, out_ref):
    rows = out_ref.shape[1]
    for i in range(0, out_ref.shape[0], 2):
        both = dot(hidden_ref[pl.ds(i * rows, 2 * rows), :], w_ref[...]).astype(BF16)
        for j in range(2):
            out_ref[i + j] = both[j * rows : (j + 1) * rows]


def output_kernel(n, own, middle_ref, *refs):
    total = middle_ref[...]
    for ref in refs[:-1]:
        total = total + ref[...].astype(F32)
    refs[-1][...] = from_blocks(total, n, own).T.astype(BF16)


def middle_grad_kernel(n, own, reps, *refs):
    parts, refs = refs[:reps], refs[reps:]
    cot_ref, middle_ref, gains_ref, w_ref, grad_ref, branch_ref, heads_ref = refs
    rows = middle_ref.shape[0]
    middle = middle_ref[...]
    grad_second = sum(ref[...].astype(F32) for ref in parts)
    grad = cot_ref[...].astype(F32) + norm_backward(
        middle, inverse_rms(middle), gains_ref[1:2, :], grad_second
    )
    grad_ref[...] = grad
    branch = grad.astype(BF16)
    branch_ref[...] = branch
    attended = from_blocks(contract_cols(branch, w_ref[...]), n, own)
    head_cols = heads_ref.shape[2]
    if n * head_cols > D:
        attended = jnp.concatenate([attended, jnp.zeros((rows, n * head_cols - D), F32)], axis=1)
    for s in range(n):
        heads_ref[s] = attended[:, s * head_cols : (s + 1) * head_cols].astype(BF16)


def out_weights_kernel(rep_ref, me_ref, attended_ref, branch_ref, mine_ref, other_ref, hold_ref):
    store_pieces(hold_ref, contract_rows(attended_ref[...], branch_ref[...]))
    for side, ref in enumerate((mine_ref, other_ref)):
        for i in range(ref.shape[0]):
            for z in range(ref.shape[1]):
                ref[i, z] = hold_ref[rep_ref[0] ^ i, me_ref[0] ^ (2 * z + side)]


def chip_sums_kernel(reps, *refs):
    for z, out_ref in enumerate(refs[reps:]):
        out_ref[...] = sum(ref[z].astype(F32) for ref in refs[:reps]).astype(BF16)


def owner_sum_kernel(*refs):
    refs[-1][...] = sum(ref[...].astype(F32) for ref in refs[:-1]).astype(BF16)


def out_out_kernel(n, reps, rep_ref, *refs):
    out_ref, hold_ref = refs[reps:]
    for i in range(reps):
        hold_ref[rep_ref[0] ^ i] = refs[i][...].astype(F32)
    own = out_ref.shape[0]
    rows = jnp.concatenate([hold_ref[r] for r in range(reps)], axis=0)[:own]
    out_ref[...] = from_blocks(rows, n, own)


def attention_out_kernel(n, reps, rep_ref, *refs):
    parts, refs = refs[:reps], refs[reps:]
    q_w_ref, k_w_ref, v_w_ref, gain_ref, q_ref, k_ref, v_ref, norm_ref, hold_ref = refs
    own = q_ref.shape[0]
    cols = parts[0].shape[2]
    head_cols = cols // 3
    heads = head_cols // HD
    for i, part in enumerate(parts):
        for s in range(n):
            hold_ref[rep_ref[0] ^ i, s] = part[s].astype(F32)
    sides = [
        jnp.concatenate([hold_ref[r, s] for r in range(reps)], axis=0)[:own] for s in range(n)
    ]

    def slot(h, kind):
        begin = kind * head_cols + h % heads * HD
        return sides[h // heads][:, begin : begin + HD]

    query = jnp.concatenate([slot(h, 0) for h in range(QH)], axis=1)
    q_ref[...] = query
    total = jnp.sum(query * q_w_ref[...].astype(F32), axis=1, keepdims=True)
    total = as_row(total)
    for kind, w_ref, out_ref in ((1, k_w_ref, k_ref), (2, v_w_ref, v_ref)):
        wide = jnp.concatenate(
            [sum(slot(j * GROUP + g, kind) for g in range(GROUP)) for j in range(KVH)], axis=1
        ).T
        out_ref[...] = wide
        total = total + jnp.sum(wide * w_ref[...].astype(F32), axis=0, keepdims=True)
    norm_ref[...] = total / gain_ref[...]


def input_grad_kernel(n, own, parts_ref, tokens_ref, gains_ref, grad_ref, out_ref):
    inputs = tokens_ref[...].astype(F32)
    grad_first = sum(parts_ref[z].astype(F32) for z in range(parts_ref.shape[0]))
    total = grad_ref[...] + norm_backward(inputs, inverse_rms(inputs), gains_ref[0:1, :], grad_first)
    out_ref[...] = from_blocks(total, n, own).T


def shards(
    tokens,
    lengths,
    norm_one,
    w_query,
    w_key,
    w_value,
    w_out,
    norm_two,
    w_gate,
    w_up,
    w_down,
    cotangent,
):
    n = lax.axis_size("shard")
    reps = lax.axis_size("rep")
    nz = n // 2
    rows = tokens.shape[0]
    length = rows * n
    own = w_query.shape[0]
    held = w_down.shape[0]
    block = round_up(own + 2, 16)
    width = n * block
    piece = block // reps
    heads = -(-QH // n)
    head_cols = heads * HD
    qkv_cols = 3 * head_cols
    each = held // (2 * reps)
    units = n * each
    msg_rows = message_plan(own, each, 2 * units)[-1]
    shard_index = lax.axis_index("shard").astype(jnp.int32)
    me = shard_index.reshape(1)
    core = (shard_index % 2).reshape(1)
    rep = lax.axis_index("rep").astype(jnp.int32).reshape(1)
    own_block = (rows, width)

    (tokens_in,) = call(lambda *r: blocks_kernel(n, *r), "tokens_blocks", [(own_block, BF16)], tokens.T)
    tokens_parts = spread(tokens_in, "shard", 2)
    gains_own = jnp.pad(jnp.stack([norm_one, norm_two]), ((0, 0), (0, qkv_cols - own))).astype(F32)
    (message,) = call(
        lambda *r: attention_message_kernel(n, *r),
        "attention_message",
        [((n, piece, qkv_cols + width // 2), BF16)],
        after(w_query, tokens_in),
        w_key.T,
        w_value.T,
        w_out,
        gains_own,
        scalars=(rep,),
    )
    arrived = exchange(message)
    qkv_piece = arrived[:, :, :qkv_cols]
    qkv_tiled = jnp.broadcast_to(qkv_piece[None], (reps,) + qkv_piece.shape)
    (w_qkv,) = call(
        join_kernel,
        "join_qkv",
        [((n, reps, piece, qkv_cols), BF16)],
        lax.all_to_all(qkv_tiled, "rep", split_axis=0, concat_axis=0, tiled=True),
    )
    w_qkv = w_qkv.reshape(width, qkv_cols)
    position = doc_layout(after(lengths, message)[0], length)
    cosines, sines = rope_tables(position)

    split = round_up(msg_rows // 2, 16)
    part_rows = (split, msg_rows - split) if split < msg_rows else (msg_rows,)
    messages = call(
        lambda *r: hidden_message_kernel(n, reps, *r),
        "hidden_message",
        [((n, part, 2 * units), BF16) for part in part_rows],
        after(w_gate, cosines, sines),
        w_up,
        w_down,
        scalars=(rep,),
    )
    (cot_in,) = call(
        lambda *r: blocks_kernel(n, *r),
        "cot_blocks",
        [(own_block, BF16)],
        after(cotangent.T, messages[0], arrived, *tokens_parts[1:]),
    )
    cot_parts = spread(after(cot_in, w_qkv), "rep", 1)
    tokens_mine, tokens_other = both_cores([after(tokens_parts[0], cot_in)] + tokens_parts[1:])
    hidden_first = exchange(after(messages[0], tokens_mine))

    out_parts = spread(after(arrived, w_qkv)[:, :, qkv_cols:], "rep", 1)

    head_shape = (length, head_cols)
    first_all, query, key, value, gains, mixed = call(
        lambda *r: attend_kernel(rows, n, *r),
        "attend",
        [((length, width), BF16)]
        + [(head_shape, BF16)] * 3
        + [((2, width), F32)]
        + [(head_shape, BF16)],
        tokens_mine,
        tokens_other,
        w_qkv,
        cosines,
        sines,
        scalars=(me, lengths),
    )
    mixed = exchange(after(mixed, hidden_first).reshape(n, rows, head_cols))
    hidden_rest = [exchange(after(message, mixed)) for message in messages[1:]]
    (out_full,) = call(
        lambda *r: join_out_kernel(reps, *r),
        "join_out",
        [((n, reps, piece, width), BF16)],
        *both_cores([after(out_parts[0], gains)] + out_parts[1:]),
        scalars=(rep, core),
    )
    out_full = out_full.reshape(width, width)

    middle, second, attended = call(
        lambda *r: middle_kernel(n, *r),
        "middle",
        [(own_block, F32), (own_block, BF16), (own_block, BF16)],
        tokens_in,
        mixed,
        out_full,
        gains,
    )
    w_hidden, w_down_in = call(
        lambda *r: hidden_weights_in_kernel(n, own, each, *r),
        "hidden_weights_in",
        [((n, block, 2 * units), BF16), ((units, width), BF16)],
        after(hidden_first, second),
        *hidden_rest,
    )
    w_hidden = w_hidden.reshape(width, 2 * units)
    cot_mine, cot_other = both_cores([after(cot_parts[0], out_full)] + cot_parts[1:])

    second_mine, second_other = both_cores(spread(second, "rep", 1))
    side_outs = [
        ((reps, rows, width), BF16),
        ((reps * rows, 2 * units), BF16),
        ((reps * rows, units), BF16),
    ]

    def hidden_side(seconds, cots, name):
        return call(hidden_kernel, name, side_outs, seconds, cots, w_hidden, w_down_in)

    def plane_sums(mine, other):
        sums = call(pair_sum_kernel, "pair_sum", [(own_block, BF16)] * reps, mine, swap(other, "shard", 1))
        return sums, deliver(sums, "rep", 1)

    grad_other, grads_other, hidden_other = hidden_side(second_other, cot_other, "hidden_other")
    grad_mine, grads_mine, hidden_mine = hidden_side(
        after(second_mine, grad_other), cot_mine, "hidden_mine"
    )
    hidden_messages = call(
        lambda *r: hidden_weights_kernel(n, own, each, *r),
        "hidden_weights",
        [((n, part, 2 * units), BF16) for part in part_rows],
        second_mine,
        second_other,
        cot_mine,
        cot_other,
        grads_mine,
        grads_other,
        hidden_mine,
        hidden_other,
    )
    hidden_sums = [exchange(hidden_messages[0])]
    sums, grad_second = plane_sums(after(grad_mine, hidden_messages[0]), grad_other)
    down_other, down_mine = [
        call(
            down_kernel,
            "down",
            [((reps, rows, width), BF16)],
            after(hidden, grad_second[1]),
            w_down_in,
        )[0]
        for hidden in (hidden_other, hidden_mine)
    ]

    grad_middle, grad_branch, grad_heads = call(
        lambda *r: middle_grad_kernel(n, own, reps, *r),
        "middle_grad",
        [(own_block, F32), (own_block, BF16), ((n, rows, head_cols), BF16)],
        *grad_second,
        cot_in,
        after(middle, down_other, down_mine),
        gains,
        out_full,
    )
    grad_heads = exchange(after(grad_heads, *hidden_sums))
    out_pieces = call(
        out_weights_kernel,
        "out_weights",
        [((reps, nz, piece, width), BF16)] * 2,
        attended,
        grad_branch,
        scalars=(rep, me),
        scratch=[((reps, n, piece, width), BF16)],
    )
    out_sums = call(
        pair_sum_kernel,
        "pair_sum",
        [((nz, piece, width), BF16)] * reps,
        out_pieces[0],
        swap(out_pieces[1], "shard", 1),
    )
    out_parts = deliver(out_sums, "rep", 1)
    hidden_sums += [exchange(after(message, grad_heads, out_pieces[0])) for message in hidden_messages[1:]]
    grad_heads = grad_heads.reshape(head_shape)
    grad_qkv, *attention_pieces = call(
        lambda *r: attend_back_kernel(reps, *r),
        "attend_back",
        [((length, qkv_cols), BF16)] + [((n, piece, qkv_cols), BF16)] * reps,
        grad_heads,
        first_all,
        query,
        key,
        value,
        cosines,
        after(sines, out_sums[0]),
        scalars=(lengths, rep),
        scratch=[(head_shape, F32)] * 2 + [((reps, n, piece, qkv_cols), BF16)],
    )

    def first_side(grads, side):
        return call(
            lambda *r: first_grad_kernel(rows, side, *r),
            "first_grad",
            [((nz, rows, width), BF16)],
            grads,
            w_qkv,
            scalars=(core,),
        )[0]

    attention_arrived = deliver(attention_pieces, "rep", 1)
    first_other = first_side(after(grad_qkv, attention_arrived[1], *out_parts[1:], *hidden_sums), 1)
    first_mine = first_side(after(grad_qkv, first_other), 0)
    (attention_summed,) = call(
        owner_sum_kernel,
        "rep_sum",
        [((n, piece, qkv_cols), BF16)],
        after(attention_arrived[0], first_mine),
        *attention_arrived[1:],
    )
    attention_moved = exchange(after(attention_summed, *hidden_sums))
    (core_sums,) = call(
        core_sums_kernel,
        "core_sums",
        [((2, msg_rows, 2 * units), BF16)],
        after(hidden_sums[0], attention_summed),
        *hidden_sums[1:],
    )
    hidden_parts = spread(core_sums, "rep", 1)
    out_summed = call(
        lambda *r: chip_sums_kernel(reps, *r),
        "chip_sums",
        [((piece, width), BF16)] * nz,
        after(out_parts[0], core_sums),
        *out_parts[1:],
    )
    out_moved = deliver(out_summed, "shard", 2)
    (first_sums,) = call(
        pair_sum_whole_kernel,
        "first_sum",
        [((nz, rows, width), BF16)],
        after(first_mine, *out_moved[1:], hidden_parts[1]),
        swap(first_other, "shard", 1),
    )
    first_parts = exchange_z(after(first_sums, attention_moved))
    attention_parts = spread(attention_moved, "rep", 1)
    (out_piece,) = call(
        owner_sum_kernel,
        "owner_sum",
        [((piece, width), BF16)],
        after(out_moved[0], first_sums),
        *out_moved[1:],
    )
    down_sums, down_parts = plane_sums(
        after(down_mine, out_piece, attention_parts[1]), after(down_other, first_sums)
    )

    gain_rows = [gain.astype(F32)[None] for gain in (norm_one, norm_two)]
    grad_w_gate, grad_w_up, grad_w_down, grad_norm_two = call(
        lambda *r: hidden_out_kernel(n, reps, each, *r),
        "hidden_out",
        [(w_gate.shape, F32), (w_up.shape, F32), (w_down.shape, F32), ((1, own), F32)],
        *hidden_parts,
        w_gate,
        w_up,
        after(gain_rows[1], down_sums[0]),
        scalars=(rep,),
        scratch=[((reps, 2, msg_rows, 2 * units), BF16)],
    )

    grad_w_query, grad_w_key, grad_w_value, grad_norm_one = call(
        lambda *r: attention_out_kernel(n, reps, *r),
        "attention_out",
        [(w_query.shape, F32), (w_key.shape[::-1], F32), (w_value.shape[::-1], F32), ((1, own), F32)],
        *attention_parts,
        after(w_query, grad_norm_two),
        w_key.T,
        w_value.T,
        gain_rows[0],
        scalars=(rep,),
        scratch=[((reps, n, piece, qkv_cols), F32)],
    )

    (grad_w_out,) = call(
        lambda *r: out_out_kernel(n, reps, *r),
        "out_out",
        [(w_out.shape, F32)],
        *later(spread(out_piece, "rep", 1), grad_norm_one),
        scalars=(rep,),
        scratch=[((reps, piece, width), F32)],
    )

    (input_grad,) = call(
        lambda *r: input_grad_kernel(n, own, *r),
        "input_grad",
        [((D, rows), F32)],
        first_parts,
        after(tokens_in, grad_w_out),
        gains,
        grad_middle,
    )

    (output,) = call(
        lambda *r: output_kernel(n, own, *r),
        "output",
        [((D, rows), BF16)],
        after(middle, input_grad),
        *down_parts,
    )
    return (
        output.T,
        input_grad.T,
        grad_norm_one[0],
        grad_w_query,
        grad_w_key.T,
        grad_w_value.T,
        grad_w_out,
        grad_norm_two[0],
        grad_w_gate,
        grad_w_up,
        grad_w_down,
    )


def solution(mesh):
    rows = P("shard", None)
    own_tokens = P(("rep", "shard"), None)
    return jax.shard_map(
        shards,
        mesh=mesh,
        in_specs=(
            own_tokens,
            P("rep", None),
            P("shard"),
            rows,
            rows,
            rows,
            rows,
            P("shard"),
            rows,
            rows,
            rows,
            own_tokens,
        ),
        out_specs=(
            own_tokens,
            own_tokens,
            P("shard"),
            rows,
            rows,
            rows,
            rows,
            P("shard"),
            rows,
            rows,
            rows,
        ),
        check_vma=False,
    )
```

```python
import jax
import jax.numpy as jnp
from jax import lax
from jax.experimental import pallas as pl
from jax.experimental.pallas import tpu as pltpu
from jax.sharding import PartitionSpec as P

D = 960
QH = 15
KVH = 5
HD = 64
FF = 2560
GROUP = QH // KVH

EPS = 1e-05
ROPE_BASE = 10000.0
MASKED = -1e30
SCALE = HD ** (-0.5)
BF16 = jnp.bfloat16
F32 = jnp.float32


def doc_layout(lengths_row, length):
    places = jnp.arange(length, dtype=jnp.int32)
    doc_ends = jnp.cumsum(lengths_row)
    passed = places[:, None] >= doc_ends[None, :]
    doc_start = jnp.sum(jnp.where(passed, lengths_row[None, :], 0), axis=1)
    return places - doc_start


def rope_tables(position):
    half_dim = HD // 2
    fraction = jnp.arange(half_dim, dtype=F32) * (2.0 / HD)
    inverse = ROPE_BASE ** (-fraction)
    angles = position.astype(F32)[:, None] * inverse[None, :]
    return (jnp.cos(angles), jnp.sin(angles))


VMEM_LIMIT = 56 * 2**20


def dot(left, right):
    return jnp.dot(left, right, preferred_element_type=F32)


def contract_rows(left, right):
    return lax.dot_general(left, right, (((0,), (0,)), ((), ())), preferred_element_type=F32)


def contract_cols(left, right):
    return lax.dot_general(left, right, (((1,), (1,)), ((), ())), preferred_element_type=F32)


def inverse_rms(values):
    return lax.rsqrt(jnp.sum(values * values, axis=-1, keepdims=True) * (1.0 / D) + EPS)


def norm_backward(values, inverse, gain, grad_norm):
    scaled = grad_norm * gain
    mean = jnp.sum(scaled * values, axis=-1, keepdims=True) * (1.0 / D)
    return inverse * scaled - values * inverse**3 * mean


def round_up(value, step):
    return -(-value // step) * step


def rows_at(index, rows):
    return pl.ds(pl.multiple_of(index * rows, rows), rows)


def to_blocks(values, n, width):
    rows, own = values.shape[0], values.shape[1] // n
    gap = jnp.zeros((rows, width // n - own), values.dtype)
    parts = []
    for s in range(n):
        parts += [values[:, s * own : (s + 1) * own], gap]
    return jnp.concatenate(parts, axis=1)


def from_blocks(values, n, own):
    block = values.shape[1] // n
    return jnp.concatenate([values[:, s * block : s * block + own] for s in range(n)], axis=1)


def swap(block, axis, k):
    count = lax.axis_size(axis)
    return lax.ppermute(block, axis, [(i, i ^ k) for i in range(count)])


def exchange(block):
    return lax.all_to_all(block, "shard", split_axis=0, concat_axis=0, tiled=True)


def spread(block, axis, step):
    return [block] + [swap(block, axis, k) for k in range(step, lax.axis_size(axis), step)]


def deliver(blocks, axis, step):
    return [blocks[0]] + [swap(block, axis, i * step) for i, block in enumerate(blocks) if i]


def exchange_z(blocks):
    groups = [list(range(core, lax.axis_size("shard"), 2)) for core in range(2)]
    return lax.all_to_all(
        blocks, "shard", split_axis=0, concat_axis=0, axis_index_groups=groups, tiled=True
    )


def after(value, *earlier):
    return lax.optimization_barrier((value,) + earlier)[0]


def later(values, *earlier):
    values = tuple(values)
    return list(lax.optimization_barrier(values + earlier)[: len(values)])


def both_cores(parts):
    stacked = jnp.stack(parts)
    return stacked, swap(stacked, "shard", 1)


def call(kernel, name, outs, *operands, scalars=(), scratch=()):
    specs = [pl.BlockSpec(memory_space=pltpu.SMEM)] * len(scalars)
    specs += [pl.BlockSpec(memory_space=pltpu.VMEM)] * len(operands)
    return pl.pallas_call(
        kernel,
        out_shape=[jax.ShapeDtypeStruct(shape, dtype) for shape, dtype in outs],
        in_specs=specs,
        out_specs=[pl.BlockSpec(memory_space=pltpu.VMEM)] * len(outs),
        scratch_shapes=[pltpu.VMEM(shape, dtype) for shape, dtype in scratch],
        compiler_params=pltpu.CompilerParams(vmem_limit_bytes=VMEM_LIMIT),
        name=name,
    )(*scalars, *operands)


def turned(values):
    half = HD // 2
    parts = []
    for begin in range(0, values.shape[1], HD):
        parts.append(-values[:, begin + half : begin + HD])
        parts.append(values[:, begin : begin + half])
    return jnp.concatenate(parts, axis=1)


def widened(values, times):
    return jnp.concatenate([values] * times, axis=1)


def head_of(values, h, heads):
    if heads == 1:
        return values
    lane = lax.broadcasted_iota(jnp.int32, values.shape, 1)
    return jnp.where(lane // HD == h, values, jnp.zeros_like(values))


def doc_starts(lengths_ref, row, rows):
    place = lax.broadcasted_iota(jnp.int32, (rows, 1), 0) + row
    end = lengths_ref[0, 0]
    starts = jnp.where(place >= end, end, 0)
    for slot in range(1, lengths_ref.shape[1]):
        end = end + lengths_ref[0, slot]
        starts = jnp.where(place >= end, end, starts)
    return starts


def masked_probs(query, key, starts, row):
    rows, cols = query.shape[0], key.shape[0]
    logits = contract_cols(query, key) * SCALE
    place = lax.broadcasted_iota(jnp.int32, (rows, cols), 1)
    own = lax.broadcasted_iota(jnp.int32, (rows, cols), 0) + row
    logits = jnp.where((place <= own) & (place >= starts), logits, MASKED)
    raised = jnp.exp(logits - jnp.max(logits, axis=-1, keepdims=True))
    return raised * (1.0 / jnp.sum(raised, axis=-1, keepdims=True))


def blocks_kernel(n, in_ref, *out_refs):
    values = to_blocks(in_ref[...].astype(F32).T, n, out_refs[0].shape[1]).astype(BF16)
    out_refs[0][...] = values
    for ref in out_refs[1:]:
        for i in range(ref.shape[0]):
            ref[i] = values


def attention_message_kernel(n, rep_ref, q_ref, k_ref, v_ref, out_ref, gain_ref, msg_ref):
    own = q_ref.shape[0]
    piece = msg_ref.shape[1]
    cols = gain_ref.shape[1]
    half = msg_ref.shape[2] - cols
    head_cols = cols // 3
    heads = head_cols // HD
    row = lax.broadcasted_iota(jnp.int32, (piece, own), 0) + rep_ref[0] * piece
    pick = jnp.where(row == lax.broadcasted_iota(jnp.int32, (piece, own), 1), 1.0, 0.0).astype(BF16)
    query, key, value = dot(pick, q_ref[...]), contract_cols(pick, k_ref[...]), contract_cols(pick, v_ref[...])
    gap = jnp.zeros((piece, HD), F32)
    wide = lax.broadcasted_iota(jnp.int32, (piece, cols), 0) + rep_ref[0] * piece
    for s in range(n):
        slots = range(s * heads, (s + 1) * heads)
        parts = [query[:, h * HD : (h + 1) * HD] if h < QH else gap for h in slots]
        for array in (key, value):
            for h in slots:
                j = h // GROUP
                parts.append(array[:, j * HD : (j + 1) * HD] if h < QH else gap)
        block = jnp.concatenate(parts, axis=1)
        for i in range(2):
            block = jnp.where(wide == own + i, gain_ref[i : i + 1, :], block)
        msg_ref[s, :, :cols] = block.astype(BF16)
    rows = to_blocks(dot(pick, out_ref[...]), n, 2 * half).astype(BF16)
    for s in range(n):
        msg_ref[s, :, cols:] = rows[:, s % 2 * half : (s % 2 + 1) * half]


def as_row(column):
    return jnp.broadcast_to(column, (column.shape[0], 128)).T[0:1, :]


def join_kernel(in_ref, out_ref):
    for r in range(in_ref.shape[0]):
        out_ref[:, r] = in_ref[r]


def join_out_kernel(reps, rep_ref, core_ref, mine_ref, other_ref, out_ref):
    first = core_ref[0] == 0
    half = mine_ref.shape[3]
    for i in range(reps):
        mine, other = mine_ref[i], other_ref[i]
        out_ref[:, rep_ref[0] ^ i, :, :half] = jnp.where(first, mine, other)
        out_ref[:, rep_ref[0] ^ i, :, half:] = jnp.where(first, other, mine)


def fill_rows(values, rows):
    if values.shape[0] == rows:
        return values
    return jnp.concatenate([values, jnp.zeros((rows - values.shape[0], values.shape[1]), F32)], axis=0)


def fill_cols(values, cols):
    if values.shape[1] == cols:
        return values
    return jnp.concatenate([values, jnp.zeros((values.shape[0], cols - values.shape[1]), F32)], axis=1)


def message_plan(own, each, cols):
    top, rows = round_up(own, 8), round_up(each, 8)
    rest = D % cols
    halved = rest and 2 * rest <= cols
    first = round_up(rows // 2, 8) if halved else rows
    total = top + D // cols * rows + (first if rest else 0)
    return top, rows, rest, halved, first, total


def pack_message(both, down, cols):
    top, rows, rest, halved, first, _ = message_plan(both.shape[0], down.shape[0], cols)
    down = fill_rows(down, rows)
    parts = [fill_rows(both, top)]
    parts += [down[:, j * cols : (j + 1) * cols] for j in range(D // cols)]
    if rest:
        tail = down[:, D - rest :]
        if halved:
            tail = jnp.concatenate([tail[:first], fill_rows(tail[first:], first)], axis=1)
        parts.append(fill_cols(tail, cols))
    return jnp.concatenate(parts, axis=0)


def unpack_message(message, own, each):
    cols = message.shape[1]
    top, rows, rest, halved, first, _ = message_plan(own, each, cols)
    parts = [message[top + j * rows : top + (j + 1) * rows] for j in range(D // cols)]
    if rest:
        tail = message[top + D // cols * rows :][:first]
        if halved:
            tail = jnp.concatenate([tail[:, :rest], tail[: rows - first, rest : 2 * rest]], axis=0)
        parts.append(tail[:, :rest])
    return message[:own], jnp.concatenate(parts, axis=1)[:each]


def hidden_message_kernel(n, reps, rep_ref, gate_ref, up_ref, down_ref, *out_refs):
    own, units = gate_ref.shape
    held = down_ref.shape[0]
    each = held // (2 * reps)
    cols = n * each
    place = lax.broadcasted_iota(jnp.int32, (1, cols), 1)
    row = lax.broadcasted_iota(jnp.int32, (round_up(each, 8), held), 0)
    for i in range(2):
        begin = each * (2 * rep_ref[0] + i)
        unit = place + begin
        for s in range(1, n):
            unit = unit + jnp.where(place >= each * s, held - each, 0)
        pick = jnp.where(lax.broadcasted_iota(jnp.int32, (units, cols), 0) == unit, 1.0, 0.0)
        pick = pick.astype(BF16)
        both = jnp.concatenate([dot(gate_ref[...], pick), dot(up_ref[...], pick)], axis=1)
        take = (lax.broadcasted_iota(jnp.int32, row.shape, 1) == row + begin) & (row < each)
        down = dot(jnp.where(take, 1.0, 0.0).astype(BF16), down_ref[...])
        message = pack_message(both, down[:each], 2 * cols).astype(BF16)
        for z in range(n // 2):
            split_rows([ref.at[2 * z + i] for ref in out_refs], message)


def split_rows(refs, values):
    begin = 0
    for ref in refs:
        rows = ref.shape[0]
        ref[...] = values[begin : begin + rows]
        begin += rows


def hidden_weights_in_kernel(n, own, each, *refs):
    parts, (w_ref, down_ref) = refs[:-2], refs[-2:]
    block = w_ref.shape[1]
    downs = []
    for s in range(n):
        message = jnp.concatenate([part[s].astype(F32) for part in parts], axis=0)
        both, down = unpack_message(message, own, each)
        w_ref[s] = fill_rows(both, block).astype(BF16)
        downs.append(down)
    down_ref[...] = to_blocks(jnp.concatenate(downs, axis=0), n, down_ref.shape[1]).astype(BF16)


def attend_kernel(rows, n, me_ref, lengths_ref, mine_ref, other_ref, *refs):
    w_ref, cos_ref, sin_ref, first_ref, q_ref, k_ref, v_ref, gains_ref, mixed_ref = refs
    length, head_cols = q_ref.shape
    heads = head_cols // HD
    width = first_ref.shape[1]
    block_rows = width // n
    own = D // n
    gap = jnp.zeros((1, block_rows - own), F32)
    gains = []
    for i in range(2):
        parts = []
        for s in range(n):
            group = w_ref[pl.ds(s * block_rows + own // 16 * 16, block_rows - own // 16 * 16), :]
            row = own % 16 + i
            spread_row = group.astype(F32)[row : row + 1, :own]
            parts += [spread_row, gap]
        gains.append(jnp.concatenate(parts, axis=1))
        gains_ref[i : i + 1, :] = gains[i]
    for side, ref in enumerate((mine_ref, other_ref)):
        for z in range(n // 2):
            inputs = ref[z].astype(F32)
            normed = inputs * inverse_rms(inputs) * gains[0]
            first_ref[rows_at(me_ref[0] ^ (2 * z + side), rows), :] = normed.astype(BF16)
    block = min(256, length)
    for i in range(length // block):
        span = pl.ds(i * block, block)
        raw = dot(first_ref[span, :], w_ref[...])
        cosines, sines = widened(cos_ref[span, :], 2 * heads), widened(sin_ref[span, :], 2 * heads)
        query, key = raw[:, :head_cols], raw[:, head_cols : 2 * head_cols]
        q_ref[span, :] = (query * cosines + turned(query) * sines).astype(BF16)
        k_ref[span, :] = (key * cosines + turned(key) * sines).astype(BF16)
        v_ref[span, :] = raw[:, 2 * head_cols :].astype(BF16)
    for i in range(length // block):
        span, past = pl.ds(i * block, block), pl.ds(0, (i + 1) * block)
        total, starts = None, doc_starts(lengths_ref, i * block, block)
        for h in range(heads):
            probs = masked_probs(head_of(q_ref[span, :], h, heads), k_ref[past, :], starts, i * block)
            mixed = head_of(dot(probs.astype(BF16), v_ref[past, :]), h, heads)
            total = mixed if total is None else total + mixed
        mixed_ref[span, :] = total.astype(BF16)


def attend_back_kernel(lengths_ref, *refs):
    g_ref, first_ref, q_ref, k_ref, v_ref, cos_ref, sin_ref, dqkv_ref, piece_ref, dk_ref, dv_ref = refs
    length, head_cols = q_ref.shape
    heads = head_cols // HD
    block = min(256, length)
    dk_ref[...] = jnp.zeros_like(dk_ref)
    dv_ref[...] = jnp.zeros_like(dv_ref)
    for i in range(length // block):
        span, past = pl.ds(i * block, block), pl.ds(0, (i + 1) * block)
        total, starts = None, doc_starts(lengths_ref, i * block, block)
        for h in range(heads):
            query = head_of(q_ref[span, :], h, heads)
            grad = head_of(g_ref[span, :], h, heads)
            key = k_ref[past, :]
            probs = masked_probs(query, key, starts, i * block)
            grad_probs = contract_cols(grad, v_ref[past, :])
            delta = jnp.sum(probs * grad_probs, axis=-1, keepdims=True)
            grad_logits = (probs * (grad_probs - delta)).astype(BF16)
            grad_query = head_of(dot(grad_logits, key), h, heads)
            total = grad_query if total is None else total + grad_query
            dv_ref[past, :] += contract_rows(probs.astype(BF16), grad)
            dk_ref[past, :] += contract_rows(grad_logits, query)
        total = total * SCALE
        cosines, sines = widened(cos_ref[span, :], 2 * heads), widened(sin_ref[span, :], 2 * heads)
        back = total * cosines - turned(total) * sines
        dqkv_ref[span, :head_cols] = back.astype(BF16)
    for i in range(length // block):
        span = pl.ds(i * block, block)
        total = dk_ref[span, :] * SCALE
        cosines, sines = widened(cos_ref[span, :], 2 * heads), widened(sin_ref[span, :], 2 * heads)
        back = total * cosines - turned(total) * sines
        dqkv_ref[span, head_cols : 2 * head_cols] = back.astype(BF16)
        dqkv_ref[span, 2 * head_cols :] = dv_ref[span, :].astype(BF16)
    store_pieces(piece_ref, contract_rows(first_ref[...], dqkv_ref[...]))


def store_pieces(piece_ref, grad):
    reps, n, piece, _ = piece_ref.shape
    for s in range(n):
        for r in range(reps):
            begin = (s * reps + r) * piece
            piece_ref[r, s] = grad[begin : begin + piece].astype(BF16)


def first_grad_kernel(rows, side, core_ref, dqkv_ref, w_ref, out_ref):
    chips = out_ref.shape[0]
    parts = [dqkv_ref[rows_at(2 * z + (core_ref[0] ^ side), rows), :] for z in range(chips)]
    grad = contract_cols(jnp.concatenate(parts, axis=0), w_ref[...]).astype(BF16)
    for z in range(chips):
        out_ref[z] = grad[z * rows : (z + 1) * rows]


def pair_sum_kernel(mine_ref, other_ref, *out_refs):
    for i, ref in enumerate(out_refs):
        ref[...] = (mine_ref[i].astype(F32) + other_ref[i].astype(F32)).astype(BF16)


def pair_sum_whole_kernel(mine_ref, other_ref, out_ref):
    out_ref[...] = (mine_ref[...].astype(F32) + other_ref[...].astype(F32)).astype(BF16)


def middle_kernel(n, tokens_ref, mixed_ref, w_ref, gains_ref, middle_ref, second_ref, attended_ref):
    width = tokens_ref.shape[1]
    attended = jnp.concatenate([mixed_ref[s] for s in range(n)], axis=1)[:, :D]
    attended = to_blocks(attended.astype(F32), n, width).astype(BF16)
    attended_ref[...] = attended
    middle = tokens_ref[...].astype(F32) + dot(attended, w_ref[...])
    middle_ref[...] = middle
    second_ref[...] = (middle * inverse_rms(middle) * gains_ref[1:2, :]).astype(BF16)


def stacked(ref, begin=0, count=None):
    count = ref.shape[0] if count is None else count
    return jnp.concatenate([ref[begin + i] for i in range(count)], axis=0)


def hidden_kernel(second_ref, cot_ref, w_ref, down_ref, grad_ref, grads_ref, hidden_ref):
    reps, rows, _ = second_ref.shape
    units = down_ref.shape[0]
    for i in range(0, reps, 2):
        span = pl.ds(i * rows, 2 * rows)
        both = dot(stacked(second_ref, i, 2), w_ref[...])
        gate, up = both[:, :units], both[:, units:]
        grad_hidden = contract_cols(stacked(cot_ref, i, 2), down_ref[...])
        sigmoid = 1.0 / (1.0 + jnp.exp(-gate))
        silu = gate * sigmoid
        hidden_ref[span, :] = (silu * up).astype(BF16)
        grad_gate = grad_hidden * up * sigmoid * (1.0 + gate * (1.0 - sigmoid))
        grads = jnp.concatenate([grad_gate, grad_hidden * silu], axis=1).astype(BF16)
        grads_ref[span, :] = grads
        grad = contract_cols(grads, w_ref[...]).astype(BF16)
        for j in range(2):
            grad_ref[i + j] = grad[j * rows : (j + 1) * rows]


def hidden_weights_kernel(n, own, each, *refs):
    second_a, second_b, cot_a, cot_b, grads_a, grads_b, hidden_a, hidden_b, *msg_refs = refs
    cols = msg_refs[0].shape[2]
    grad = contract_rows(stacked(second_a), grads_a[...])
    grad = grad + contract_rows(stacked(second_b), grads_b[...])
    down = contract_rows(hidden_a[...], stacked(cot_a)) + contract_rows(hidden_b[...], stacked(cot_b))
    down = from_blocks(down, n, own)
    block = grad.shape[0] // n
    for s in range(n):
        both = grad[s * block : s * block + own]
        message = pack_message(both, down[s * each : (s + 1) * each], cols).astype(BF16)
        split_rows([ref.at[s] for ref in msg_refs], message)


def core_sums_kernel(*refs):
    out_ref = refs[-1]
    for core in range(2):
        sums = [
            sum(part[s].astype(F32) for s in range(core, part.shape[0], 2)) for part in refs[:-1]
        ]
        out_ref[core] = jnp.concatenate(sums, axis=0).astype(BF16)


def hidden_out_kernel(n, reps, each, rep_ref, *refs):
    parts, refs = refs[:reps], refs[reps:]
    gate_w_ref, up_w_ref, gain_ref, gate_ref, up_ref, down_ref, norm_ref, hold_ref = refs
    own = gate_ref.shape[0]
    units = 2 * reps * each
    for i, part in enumerate(parts):
        hold_ref[rep_ref[0] ^ i] = part[...]
    cols = hold_ref.shape[3]
    boths = []
    for f in range(2 * reps):
        _, down = unpack_message(hold_ref[f // 2, f % 2].astype(F32), own, each)
        boths.append(hold_ref[f // 2, f % 2, pl.ds(0, round_up(own, 16)), :])
        down_ref[f * each : (f + 1) * each, :] = down
    total = jnp.zeros((own, 1), F32)
    for begin, w_ref, out_ref in ((0, gate_w_ref, gate_ref), (cols // 2, up_w_ref, up_ref)):
        for s in range(n):
            place = begin + s * each
            rows = jnp.concatenate([part[:, place : place + each] for part in boths], axis=1)
            rows = rows.astype(F32)[:own]
            span = slice(s * units, (s + 1) * units)
            out_ref[:, span] = rows
            total = total + jnp.sum(rows * w_ref[:, span].astype(F32), axis=1, keepdims=True)
    norm_ref[...] = as_row(total) / gain_ref[...]


def down_kernel(hidden_ref, w_ref, out_ref):
    rows = out_ref.shape[1]
    for i in range(0, out_ref.shape[0], 2):
        both = dot(hidden_ref[pl.ds(i * rows, 2 * rows), :], w_ref[...]).astype(BF16)
        for j in range(2):
            out_ref[i + j] = both[j * rows : (j + 1) * rows]


def output_kernel(n, own, middle_ref, *refs):
    total = middle_ref[...]
    for ref in refs[:-1]:
        total = total + ref[...].astype(F32)
    refs[-1][...] = from_blocks(total, n, own).T.astype(BF16)


def middle_grad_kernel(n, own, reps, *refs):
    parts, refs = refs[:reps], refs[reps:]
    cot_ref, middle_ref, gains_ref, w_ref, grad_ref, branch_ref, heads_ref = refs
    rows = middle_ref.shape[0]
    middle = middle_ref[...]
    grad_second = sum(ref[...].astype(F32) for ref in parts)
    grad = cot_ref[...].astype(F32) + norm_backward(
        middle, inverse_rms(middle), gains_ref[1:2, :], grad_second
    )
    grad_ref[...] = grad
    branch = grad.astype(BF16)
    branch_ref[...] = branch
    attended = from_blocks(contract_cols(branch, w_ref[...]), n, own)
    head_cols = heads_ref.shape[2]
    if n * head_cols > D:
        attended = jnp.concatenate([attended, jnp.zeros((rows, n * head_cols - D), F32)], axis=1)
    for s in range(n):
        heads_ref[s] = attended[:, s * head_cols : (s + 1) * head_cols].astype(BF16)


def out_weights_kernel(rep_ref, me_ref, attended_ref, branch_ref, mine_ref, other_ref, hold_ref):
    store_pieces(hold_ref, contract_rows(attended_ref[...], branch_ref[...]))
    for side, ref in enumerate((mine_ref, other_ref)):
        for i in range(ref.shape[0]):
            for z in range(ref.shape[1]):
                ref[i, z] = hold_ref[rep_ref[0] ^ i, me_ref[0] ^ (2 * z + side)]


def rep_sum_kernel(in_ref, out_ref):
    out_ref[...] = sum(in_ref[r].astype(F32) for r in range(in_ref.shape[0])).astype(BF16)


def chip_sums_kernel(reps, *refs):
    for z, out_ref in enumerate(refs[reps:]):
        out_ref[...] = sum(ref[z].astype(F32) for ref in refs[:reps]).astype(BF16)


def owner_sum_kernel(*refs):
    refs[-1][...] = sum(ref[...].astype(F32) for ref in refs[:-1]).astype(BF16)


def out_out_kernel(n, reps, rep_ref, *refs):
    out_ref, hold_ref = refs[reps:]
    for i in range(reps):
        hold_ref[rep_ref[0] ^ i] = refs[i][...].astype(F32)
    own = out_ref.shape[0]
    rows = jnp.concatenate([hold_ref[r] for r in range(reps)], axis=0)[:own]
    out_ref[...] = from_blocks(rows, n, own)


def attention_out_kernel(n, reps, rep_ref, *refs):
    parts, refs = refs[:reps], refs[reps:]
    q_w_ref, k_w_ref, v_w_ref, gain_ref, q_ref, k_ref, v_ref, norm_ref, hold_ref = refs
    own = q_ref.shape[0]
    cols = parts[0].shape[2]
    head_cols = cols // 3
    heads = head_cols // HD
    for i, part in enumerate(parts):
        for s in range(n):
            hold_ref[rep_ref[0] ^ i, s] = part[s].astype(F32)
    sides = [
        jnp.concatenate([hold_ref[r, s] for r in range(reps)], axis=0)[:own] for s in range(n)
    ]

    def slot(h, kind):
        begin = kind * head_cols + h % heads * HD
        return sides[h // heads][:, begin : begin + HD]

    query = jnp.concatenate([slot(h, 0) for h in range(QH)], axis=1)
    q_ref[...] = query
    total = jnp.sum(query * q_w_ref[...].astype(F32), axis=1, keepdims=True)
    total = as_row(total)
    for kind, w_ref, out_ref in ((1, k_w_ref, k_ref), (2, v_w_ref, v_ref)):
        wide = jnp.concatenate(
            [sum(slot(j * GROUP + g, kind) for g in range(GROUP)) for j in range(KVH)], axis=1
        ).T
        out_ref[...] = wide
        total = total + jnp.sum(wide * w_ref[...].astype(F32), axis=0, keepdims=True)
    norm_ref[...] = total / gain_ref[...]


def input_grad_kernel(n, own, parts_ref, tokens_ref, gains_ref, grad_ref, out_ref):
    inputs = tokens_ref[...].astype(F32)
    grad_first = sum(parts_ref[z].astype(F32) for z in range(parts_ref.shape[0]))
    total = grad_ref[...] + norm_backward(inputs, inverse_rms(inputs), gains_ref[0:1, :], grad_first)
    out_ref[...] = from_blocks(total, n, own).T


def shards(
    tokens,
    lengths,
    norm_one,
    w_query,
    w_key,
    w_value,
    w_out,
    norm_two,
    w_gate,
    w_up,
    w_down,
    cotangent,
):
    n = lax.axis_size("shard")
    reps = lax.axis_size("rep")
    nz = n // 2
    rows = tokens.shape[0]
    length = rows * n
    own = w_query.shape[0]
    held = w_down.shape[0]
    block = round_up(own + 2, 16)
    width = n * block
    piece = block // reps
    heads = -(-QH // n)
    head_cols = heads * HD
    qkv_cols = 3 * head_cols
    each = held // (2 * reps)
    units = n * each
    msg_rows = message_plan(own, each, 2 * units)[-1]
    shard_index = lax.axis_index("shard").astype(jnp.int32)
    me = shard_index.reshape(1)
    core = (shard_index % 2).reshape(1)
    rep = lax.axis_index("rep").astype(jnp.int32).reshape(1)
    own_block = (rows, width)

    (tokens_in,) = call(lambda *r: blocks_kernel(n, *r), "tokens_blocks", [(own_block, BF16)], tokens.T)
    tokens_parts = spread(tokens_in, "shard", 2)
    gains_own = jnp.pad(jnp.stack([norm_one, norm_two]), ((0, 0), (0, qkv_cols - own))).astype(F32)
    (message,) = call(
        lambda *r: attention_message_kernel(n, *r),
        "attention_message",
        [((n, piece, qkv_cols + width // 2), BF16)],
        after(w_query, tokens_in),
        w_key.T,
        w_value.T,
        w_out,
        gains_own,
        scalars=(rep,),
    )
    arrived = exchange(message)
    qkv_piece = arrived[:, :, :qkv_cols]
    qkv_tiled = jnp.broadcast_to(qkv_piece[None], (reps,) + qkv_piece.shape)
    (w_qkv,) = call(
        join_kernel,
        "join_qkv",
        [((n, reps, piece, qkv_cols), BF16)],
        lax.all_to_all(qkv_tiled, "rep", split_axis=0, concat_axis=0, tiled=True),
    )
    w_qkv = w_qkv.reshape(width, qkv_cols)
    position = doc_layout(after(lengths, message)[0], length)
    cosines, sines = rope_tables(position)

    split = round_up(msg_rows // 2, 16)
    part_rows = (split, msg_rows - split) if split < msg_rows else (msg_rows,)
    messages = call(
        lambda *r: hidden_message_kernel(n, reps, *r),
        "hidden_message",
        [((n, part, 2 * units), BF16) for part in part_rows],
        after(w_gate, cosines, sines),
        w_up,
        w_down,
        scalars=(rep,),
    )
    (cot_in,) = call(
        lambda *r: blocks_kernel(n, *r),
        "cot_blocks",
        [(own_block, BF16)],
        after(cotangent.T, messages[0], arrived, *tokens_parts[1:]),
    )
    cot_parts = spread(after(cot_in, w_qkv), "rep", 1)
    tokens_mine, tokens_other = both_cores([after(tokens_parts[0], cot_in)] + tokens_parts[1:])
    hidden_first = exchange(after(messages[0], tokens_mine))

    out_parts = spread(after(arrived, w_qkv)[:, :, qkv_cols:], "rep", 1)

    head_shape = (length, head_cols)
    first_all, query, key, value, gains, mixed = call(
        lambda *r: attend_kernel(rows, n, *r),
        "attend",
        [((length, width), BF16)]
        + [(head_shape, BF16)] * 3
        + [((2, width), F32)]
        + [(head_shape, BF16)],
        tokens_mine,
        tokens_other,
        w_qkv,
        cosines,
        sines,
        scalars=(me, lengths),
    )
    mixed = exchange(after(mixed, hidden_first).reshape(n, rows, head_cols))
    hidden_rest = [exchange(after(message, mixed)) for message in messages[1:]]
    (out_full,) = call(
        lambda *r: join_out_kernel(reps, *r),
        "join_out",
        [((n, reps, piece, width), BF16)],
        *both_cores([after(out_parts[0], gains)] + out_parts[1:]),
        scalars=(rep, core),
    )
    out_full = out_full.reshape(width, width)

    middle, second, attended = call(
        lambda *r: middle_kernel(n, *r),
        "middle",
        [(own_block, F32), (own_block, BF16), (own_block, BF16)],
        tokens_in,
        mixed,
        out_full,
        gains,
    )
    w_hidden, w_down_in = call(
        lambda *r: hidden_weights_in_kernel(n, own, each, *r),
        "hidden_weights_in",
        [((n, block, 2 * units), BF16), ((units, width), BF16)],
        after(hidden_first, second),
        *hidden_rest,
    )
    w_hidden = w_hidden.reshape(width, 2 * units)
    cot_mine, cot_other = both_cores([after(cot_parts[0], out_full)] + cot_parts[1:])

    second_mine, second_other = both_cores(spread(second, "rep", 1))
    side_outs = [
        ((reps, rows, width), BF16),
        ((reps * rows, 2 * units), BF16),
        ((reps * rows, units), BF16),
    ]

    def hidden_side(seconds, cots, name):
        return call(hidden_kernel, name, side_outs, seconds, cots, w_hidden, w_down_in)

    def plane_sums(mine, other):
        sums = call(pair_sum_kernel, "pair_sum", [(own_block, BF16)] * reps, mine, swap(other, "shard", 1))
        return sums, deliver(sums, "rep", 1)

    grad_other, grads_other, hidden_other = hidden_side(second_other, cot_other, "hidden_other")
    grad_mine, grads_mine, hidden_mine = hidden_side(
        after(second_mine, grad_other), cot_mine, "hidden_mine"
    )
    hidden_messages = call(
        lambda *r: hidden_weights_kernel(n, own, each, *r),
        "hidden_weights",
        [((n, part, 2 * units), BF16) for part in part_rows],
        second_mine,
        second_other,
        cot_mine,
        cot_other,
        grads_mine,
        grads_other,
        hidden_mine,
        hidden_other,
    )
    hidden_sums = [exchange(hidden_messages[0])]
    sums, grad_second = plane_sums(after(grad_mine, hidden_messages[0]), grad_other)
    down_other, down_mine = [
        call(
            down_kernel,
            "down",
            [((reps, rows, width), BF16)],
            after(hidden, grad_second[1]),
            w_down_in,
        )[0]
        for hidden in (hidden_other, hidden_mine)
    ]

    grad_middle, grad_branch, grad_heads = call(
        lambda *r: middle_grad_kernel(n, own, reps, *r),
        "middle_grad",
        [(own_block, F32), (own_block, BF16), ((n, rows, head_cols), BF16)],
        *grad_second,
        cot_in,
        after(middle, down_other, down_mine),
        gains,
        out_full,
    )
    grad_heads = exchange(after(grad_heads, *hidden_sums))
    out_pieces = call(
        out_weights_kernel,
        "out_weights",
        [((reps, nz, piece, width), BF16)] * 2,
        attended,
        grad_branch,
        scalars=(rep, me),
        scratch=[((reps, n, piece, width), BF16)],
    )
    out_sums = call(
        pair_sum_kernel,
        "pair_sum",
        [((nz, piece, width), BF16)] * reps,
        out_pieces[0],
        swap(out_pieces[1], "shard", 1),
    )
    out_parts = deliver(out_sums, "rep", 1)
    hidden_sums += [exchange(after(message, grad_heads, out_pieces[0])) for message in hidden_messages[1:]]
    grad_heads = grad_heads.reshape(head_shape)
    grad_qkv, attention_pieces = call(
        attend_back_kernel,
        "attend_back",
        [((length, qkv_cols), BF16), ((reps, n, piece, qkv_cols), BF16)],
        grad_heads,
        first_all,
        query,
        key,
        value,
        cosines,
        after(sines, out_sums[0]),
        scalars=(lengths,),
        scratch=[(head_shape, F32)] * 2,
    )

    def first_side(grads, side):
        return call(
            lambda *r: first_grad_kernel(rows, side, *r),
            "first_grad",
            [((nz, rows, width), BF16)],
            grads,
            w_qkv,
            scalars=(core,),
        )[0]

    attention_arrived = lax.all_to_all(
        after(attention_pieces, *hidden_sums), "rep", split_axis=0, concat_axis=0, tiled=True
    )
    (core_sums,) = call(
        core_sums_kernel,
        "core_sums",
        [((2, msg_rows, 2 * units), BF16)],
        after(hidden_sums[0], grad_qkv, *out_parts[1:]),
        *hidden_sums[1:],
    )
    hidden_parts = spread(core_sums, "rep", 1)
    first_other = first_side(after(grad_qkv, core_sums), 1)
    out_summed = call(
        lambda *r: chip_sums_kernel(reps, *r),
        "chip_sums",
        [((piece, width), BF16)] * nz,
        after(out_parts[0], first_other),
        *out_parts[1:],
    )
    out_moved = deliver(out_summed, "shard", 2)
    first_mine = first_side(after(grad_qkv, out_summed[0]), 0)
    (attention_summed,) = call(
        rep_sum_kernel,
        "rep_sum",
        [((n, piece, qkv_cols), BF16)],
        after(attention_arrived, first_mine, *out_moved[1:]),
    )
    attention_moved = exchange(attention_summed)
    (first_sums,) = call(
        pair_sum_whole_kernel,
        "first_sum",
        [((nz, rows, width), BF16)],
        after(first_mine, attention_summed, *hidden_parts[1:3]),
        swap(first_other, "shard", 1),
    )
    first_parts = exchange_z(after(first_sums, attention_moved))
    attention_parts = spread(attention_moved, "rep", 1)
    (out_piece,) = call(
        owner_sum_kernel,
        "owner_sum",
        [((piece, width), BF16)],
        after(out_moved[0], first_sums),
        *out_moved[1:],
    )
    down_sums, down_parts = plane_sums(
        after(down_mine, out_piece, attention_parts[1]), after(down_other, first_sums)
    )

    gain_rows = [gain.astype(F32)[None] for gain in (norm_one, norm_two)]
    grad_w_gate, grad_w_up, grad_w_down, grad_norm_two = call(
        lambda *r: hidden_out_kernel(n, reps, each, *r),
        "hidden_out",
        [(w_gate.shape, F32), (w_up.shape, F32), (w_down.shape, F32), ((1, own), F32)],
        *hidden_parts,
        w_gate,
        w_up,
        after(gain_rows[1], down_sums[0]),
        scalars=(rep,),
        scratch=[((reps, 2, msg_rows, 2 * units), BF16)],
    )

    grad_w_query, grad_w_key, grad_w_value, grad_norm_one = call(
        lambda *r: attention_out_kernel(n, reps, *r),
        "attention_out",
        [(w_query.shape, F32), (w_key.shape[::-1], F32), (w_value.shape[::-1], F32), ((1, own), F32)],
        *attention_parts,
        after(w_query, grad_norm_two),
        w_key.T,
        w_value.T,
        gain_rows[0],
        scalars=(rep,),
        scratch=[((reps, n, piece, qkv_cols), F32)],
    )

    (grad_w_out,) = call(
        lambda *r: out_out_kernel(n, reps, *r),
        "out_out",
        [(w_out.shape, F32)],
        *later(spread(out_piece, "rep", 1), grad_norm_one),
        scalars=(rep,),
        scratch=[((reps, piece, width), F32)],
    )

    (input_grad,) = call(
        lambda *r: input_grad_kernel(n, own, *r),
        "input_grad",
        [((D, rows), F32)],
        first_parts,
        after(tokens_in, grad_w_out),
        gains,
        grad_middle,
    )

    (output,) = call(
        lambda *r: output_kernel(n, own, *r),
        "output",
        [((D, rows), BF16)],
        after(middle, input_grad),
        *down_parts,
    )
    return (
        output.T,
        input_grad.T,
        grad_norm_one[0],
        grad_w_query,
        grad_w_key.T,
        grad_w_value.T,
        grad_w_out,
        grad_norm_two[0],
        grad_w_gate,
        grad_w_up,
        grad_w_down,
    )


def solution(mesh):
    rows = P("shard", None)
    own_tokens = P(("rep", "shard"), None)
    return jax.shard_map(
        shards,
        mesh=mesh,
        in_specs=(
            own_tokens,
            P("rep", None),
            P("shard"),
            rows,
            rows,
            rows,
            rows,
            P("shard"),
            rows,
            rows,
            rows,
            own_tokens,
        ),
        out_specs=(
            own_tokens,
            own_tokens,
            P("shard"),
            rows,
            rows,
            rows,
            rows,
            P("shard"),
            rows,
            rows,
            rows,
        ),
        check_vma=False,
    )
```
